32 devices in a mesh: fsdp: 4 (over z), ctx: 2 (over x), tp: 4 (over y, core).
Axes of the slice: x: 2, y: 2, z: 4, core: 2. Of those that a mesh axis runs over, the one named last changes fastest.
Arguments:
- tokens: bfloat16 [8192, 2048], P(('fsdp', 'ctx')), may hold values from -6 to 6
- q_weight: bfloat16 [2048, 2048], P('fsdp', 'tp'), may hold values from -0.25 to 0.25
- k_weight: bfloat16 [2048, 512], P('fsdp', 'tp'), may hold values from -0.125 to 0.125
- v_weight: bfloat16 [2048, 512], P('fsdp', 'tp'), may hold values from -0.125 to 0.125
- o_weight: bfloat16 [2048, 2048], P('fsdp', 'tp'), may hold values from -0.5 to 0.5
- attn_gain: bfloat16 [2048], P('fsdp'), may hold values from 0.099609375 to 1.8984375
- gate_weight: bfloat16 [2048, 8192], P('fsdp', 'tp'), may hold values from -0.125 to 0.125
- up_weight: bfloat16 [2048, 8192], P('fsdp', 'tp'), may hold values from -0.125 to 0.125
- down_weight: bfloat16 [2048, 8192], P('fsdp', 'tp'), may hold values from -0.125 to 0.125
- ffn_gain: bfloat16 [2048], P('fsdp'), may hold values from 0.099609375 to 1.8984375
- lengths: int32 [4, 6], P('fsdp'), may hold values from 1 to 1024, as said below
- deal: int32 [4, 4], P('fsdp'), may hold values from 0 to 3, as said below
- cotangent: bfloat16 [8192, 2048], P(('fsdp', 'ctx')), may hold values from -6 to 6
Outputs:
- output: bfloat16 [8192, 2048], P(('fsdp', 'ctx'))
- tokens_grad: bfloat16 [8192, 2048], P(('fsdp', 'ctx'))
- q_grad: float32 [2048, 2048], P('fsdp', 'tp')
- k_grad: float32 [2048, 512], P('fsdp', 'tp')
- v_grad: float32 [2048, 512], P('fsdp', 'tp')
- o_grad: float32 [2048, 2048], P('fsdp', 'tp')
- attn_gain_grad: float32 [2048], P('fsdp')
- gate_grad: float32 [2048, 8192], P('fsdp', 'tp')
- up_grad: float32 [2048, 8192], P('fsdp', 'tp')
- down_grad: float32 [2048, 8192], P('fsdp', 'tp')
- ffn_gain_grad: float32 [2048], P('fsdp')
The draws below stay inside these ranges and needn't reach their ends.
Inputs may be any that keep to these rules, and one draw needn't show every extreme that they name: Each group's lengths add up to 2048, so that no row is padding; exactly one of them equals 1024, and it is the first or the last of the group's list. `deal`: each row is a permutation of the group's 4 spans; for each c, places 2c and 2c+1 hold one span of the first half and one of the second half of the packed order.
All inputs are finite; a program needn't handle non-finite values.
Results may differ from the reference program's by a relative error of at most 0.025.
Values may be sent and summed in bfloat16 or wider, within the bound.
No kernel may reach another device: no remote copies, remote signals or barrier semaphores. Data moves between devices by JAX's collectives and lax.ppermute only.
A program may use at most 448 MiB of HBM per device.

```python
import math
import jax
import jax.numpy as jnp
from jax import lax

D = 2048
FF = 8192
HEADS = 32
KV_HEADS = 8
HEAD_DIM = 64
SEQS = 6
GROUPS = 4
GROUP_TOK = 2048
TOKENS = 8192
MAXLEN = 1024
SPANS = 4
SPAN = 512


def draw_lengths(key, part):
    key = jax.random.fold_in(key, 11)
    cut_key, side_key = jax.random.split(key)
    spare = GROUP_TOK - MAXLEN - (SEQS - 1)
    cuts = jnp.sort(jax.random.randint(cut_key, (GROUPS, SEQS - 2), 0, spare + 1), axis=1)
    edges = jnp.concatenate([jnp.zeros((GROUPS, 1), jnp.int32), cuts, jnp.full((GROUPS, 1), spare, jnp.int32)], axis=1)
    others = edges[:, 1:] - edges[:, :-1] + 1
    longest = jnp.full((GROUPS, 1), MAXLEN, jnp.int32)
    first_side = jax.random.randint(side_key, (GROUPS, 1), 0, 2) == 1
    return jnp.where(first_side, jnp.concatenate([longest, others], axis=1), jnp.concatenate([others, longest], axis=1)).astype(jnp.int32)


def draw_deal(key, part):
    key = jax.random.fold_in(key, 23)
    half_count = SPANS // 2

    def deal_group(group_key):
        early_key, late_key = jax.random.split(group_key)
        early = jax.random.permutation(early_key, half_count)
        late = jax.random.permutation(late_key, half_count) + half_count
        return jnp.stack([early, late], axis=1).reshape(SPANS)
    return jax.vmap(deal_group)(jax.random.split(key, GROUPS)).astype(jnp.int32)


def with_spikes(drawn, own_key, source, target, blocks, factor):
    owner, partner = [(jnp.arange(drawn.shape[axis_at]) // (drawn.shape[axis_at] // blocks)).reshape([-1 if axis == axis_at else 1 for axis in range(drawn.ndim)]) for axis_at in (source, target)]
    chosen = jax.random.permutation(own_key, blocks)[partner]
    strong = (owner == chosen) | (owner == (partner + blocks // 2) % blocks)
    return jnp.where(strong, factor * drawn, drawn)


def level_of(stream_key, extent, cuts, least, top_value):
    gain = 1.0
    for dim, parts in cuts:
        steps = jax.random.uniform(jax.random.fold_in(jax.random.fold_in(stream_key, 6), dim), (parts,), jnp.float32, least / len(cuts), top_value / len(cuts))
        gain = gain * jnp.repeat(jnp.exp(steps), extent[dim] // parts).reshape((-1,) + (1,) * (len(extent) - 1 - dim))
    return gain


def scatter_about(stream_key, shape, spread, reach, cuts=(), kind=jnp.bfloat16):
    result = spread * jax.random.normal(stream_key, shape, jnp.float32)
    if cuts:
        result = result * level_of(stream_key, shape, cuts, -0.22, 0.18)
    return jnp.clip(result, -reach, reach).astype(kind)


def heavy_noise(rng, dims, width, bound, pieces, heavy, kind=jnp.bfloat16):
    values = width * jax.random.normal(rng, dims, jnp.float32)
    if pieces:
        values = values * level_of(rng, dims, pieces, -0.22, 0.18)
    return jnp.clip(with_spikes(values, jax.random.fold_in(rng, 3), *heavy), -bound, bound).astype(kind)


def setup_inputs(seed: int = 0) -> dict:
    splits = jax.random.split(jax.random.key(seed), 14)
    return {
        "tokens": heavy_noise(splits[0], (TOKENS, D), 1.0, 6.0, ((0, 8),), (0, 1, 8, 2.0)),
        "q_weight": scatter_about(splits[1], (D, D), (D // 4) ** -0.5, 0.25, ((0, 4), (1, 4))),
        "k_weight": scatter_about(splits[2], (D, KV_HEADS * HEAD_DIM), D ** -0.5, 0.125, ((0, 4), (1, 4))),
        "v_weight": scatter_about(splits[3], (D, KV_HEADS * HEAD_DIM), D ** -0.5, 0.125, ((0, 4), (1, 4))),
        "o_weight": scatter_about(splits[4], (D, D), (D // 16) ** -0.5, 0.5, ((0, 4), (1, 4))),
        "attn_gain": jnp.clip(1.0 + 0.18 * jax.random.normal(splits[5], (D,), jnp.float32), 0.099609375, 1.8984375).astype(jnp.bfloat16),
        "gate_weight": scatter_about(splits[6], (D, FF), D ** -0.5, 0.125, ((0, 4), (1, 4))),
        "up_weight": scatter_about(splits[7], (D, FF), D ** -0.5, 0.125, ((0, 4), (1, 4))),
        "down_weight": scatter_about(splits[8], (D, FF), (FF // 4) ** -0.5, 0.125, ((0, 4), (1, 4))),
        "ffn_gain": jnp.clip(1.0 + 0.18 * jax.random.normal(splits[9], (D,), jnp.float32), 0.099609375, 1.8984375).astype(jnp.bfloat16),
        "lengths": draw_lengths(jax.random.fold_in(splits[13], 71), 0),
        "deal": draw_deal(jax.random.fold_in(splits[13], 71), 0),
        "cotangent": scatter_about(splits[12], (TOKENS, D), 1.0, 6.0, ((0, 8),)),
    }


EPSILON = 1e-05
ROPE_BASE = 500000.0
MASKED = -1e+30
HIGHEST = lax.Precision.HIGHEST

@jax.custom_vjp
def low(v):
    return lax.optimization_barrier(v.astype(jnp.bfloat16)).astype(jnp.float32)

@jax.custom_vjp
def low_back(v):
    return v

def low_keep(v):
    return (low(v), None)

def low_pass(kept, grad):
    return (grad,)

def back_keep(v):
    return (v, None)

def back_low(kept, grad):
    return (low(grad),)
low.defvjp(low_keep, low_pass)
low_back.defvjp(back_keep, back_low)

def rms_scale(hidden, gain_row):
    mean_square = lax.optimization_barrier(jnp.mean(hidden * hidden, axis=-1, keepdims=True))
    return hidden * lax.rsqrt(mean_square + EPSILON) * gain_row

def rotate(values, cos_table, sin_table):
    half_dim = values.shape[-1] // 2
    turned = jnp.concatenate([-values[..., half_dim:], values[..., :half_dim]], axis=-1)
    return values * cos_table + turned * sin_table

def angle_tables(position, head_dim):
    half_dim = head_dim // 2
    inverse = jnp.exp(jnp.arange(half_dim, dtype=jnp.float32) * (-2.0 * math.log(ROPE_BASE) / head_dim))
    angles = position.astype(jnp.float32)[:, None] * inverse[None, :]
    both_halves = jnp.concatenate([angles, angles], axis=-1)[:, None, :]
    return (jnp.cos(both_halves), jnp.sin(both_halves))

def token_places(length_row, deal_row, span_size):
    natural = (deal_row[:, None] * span_size + jnp.arange(span_size, dtype=jnp.int32)[None, :]).reshape(-1)
    seq_ends = jnp.cumsum(length_row, dtype=jnp.int32)
    seq_starts = seq_ends - length_row
    segment = lax.optimization_barrier(jnp.sum((natural[None, :] >= seq_ends[:, None]).astype(jnp.int32), axis=0, dtype=jnp.int32))
    member = segment[None, :] == jnp.arange(length_row.shape[0], dtype=jnp.int32)[:, None]
    position = natural - lax.optimization_barrier(jnp.sum(jnp.where(member, seq_starts[:, None], 0), axis=0, dtype=jnp.int32))
    return (natural, segment, position)

def block_mask(segment_rows, natural_rows, segment_all, natural_all):
    return (segment_rows[:, None] == segment_all[None, :]) & (natural_all[None, :] <= natural_rows[:, None])

def attend_block(query_block, key_all, value_all, segment_rows, natural_rows, segment_all, natural_all):
    score_scale = query_block.shape[-1] ** (-0.5)
    raw_scores = low_back(jnp.einsum('qhgd,khd->hgqk', query_block, key_all, precision=HIGHEST) * score_scale)
    allowed = block_mask(segment_rows, natural_rows, segment_all, natural_all)
    scores = jnp.where(allowed[None, None], raw_scores, MASKED)
    row_top = lax.optimization_barrier(jnp.max(scores, axis=-1, keepdims=True))
    exp_scores = jnp.exp(scores - row_top)
    probs = exp_scores / lax.optimization_barrier(jnp.sum(exp_scores, axis=-1, keepdims=True))
    return jnp.einsum('hgqk,khd->qhgd', low(probs), value_all, precision=HIGHEST)

def layer(inputs, q_weight, k_weight, v_weight, o_weight, attn_gain, gate_weight, up_weight, down_weight, ffn_gain, natural, segment, position):
    row_count = inputs.shape[0]
    per_kv = HEADS // KV_HEADS
    normed = low(rms_scale(inputs, attn_gain))
    q_raw = low_back(jnp.dot(normed, q_weight, precision=HIGHEST)).reshape(row_count, HEADS, HEAD_DIM)
    k_raw = low_back(jnp.dot(normed, k_weight, precision=HIGHEST)).reshape(row_count, KV_HEADS, HEAD_DIM)
    v_all = low(low_back(jnp.dot(normed, v_weight, precision=HIGHEST))).reshape(row_count, KV_HEADS, HEAD_DIM)
    cos_table, sin_table = angle_tables(position, HEAD_DIM)
    q_all = low(rotate(q_raw, cos_table, sin_table)).reshape(row_count, KV_HEADS, per_kv, HEAD_DIM)
    k_all = low(rotate(k_raw, cos_table, sin_table))
    block_rows = min(512, row_count)

    def one_block(block_index):
        first_row = block_index * block_rows
        query_block = lax.dynamic_slice_in_dim(q_all, first_row, block_rows, 0)
        segment_rows = lax.dynamic_slice_in_dim(segment, first_row, block_rows, 0)
        natural_rows = lax.dynamic_slice_in_dim(natural, first_row, block_rows, 0)
        return attend_block(query_block, k_all, v_all, segment_rows, natural_rows, segment, natural)
    heads_out = lax.map(jax.checkpoint(one_block), jnp.arange(row_count // block_rows, dtype=jnp.int32))
    heads_low = low(low_back(heads_out.reshape(row_count, HEADS * HEAD_DIM)))
    attn_out = low_back(jnp.dot(heads_low, o_weight.T, precision=HIGHEST))
    hidden_one = inputs + attn_out
    normed_two = low(rms_scale(hidden_one, ffn_gain))
    gate_raw = low_back(jnp.dot(normed_two, gate_weight, precision=HIGHEST))
    up_raw = low_back(jnp.dot(normed_two, up_weight, precision=HIGHEST))
    mixed = low(jax.nn.silu(gate_raw) * up_raw)
    ffn_out = low_back(jnp.dot(mixed, down_weight.T, precision=HIGHEST))
    return hidden_one + ffn_out

def reference(tokens, q_weight, k_weight, v_weight, o_weight, attn_gain, gate_weight, up_weight, down_weight, ffn_gain, lengths, deal, cotangent):
    weights = tuple((item.astype(jnp.float32) for item in (q_weight, k_weight, v_weight, o_weight, attn_gain, gate_weight, up_weight, down_weight, ffn_gain)))
    token_groups = tokens.astype(jnp.float32).reshape(GROUPS, GROUP_TOK, D)
    cot_groups = cotangent.astype(jnp.float32).reshape(GROUPS, GROUP_TOK, D)

    def per_group(totals, items):
        group_in, group_cot, length_row, deal_row = items
        natural, segment, position = token_places(length_row, deal_row, SPAN)

        def forward(group_tokens, wq_in, wk_in, wv_in, wo_in, ga_in, wg_in, wu_in, wd_in, gf_in):
            return layer(group_tokens, wq_in, wk_in, wv_in, wo_in, ga_in, wg_in, wu_in, wd_in, gf_in, natural, segment, position)
        group_out, pull_back = jax.vjp(forward, group_in, *weights)
        grads = pull_back(group_cot)
        totals = tuple((total + grad for total, grad in zip(totals, grads[1:])))
        return (totals, (group_out.astype(jnp.bfloat16), grads[0].astype(jnp.bfloat16)))
    start = tuple((jnp.zeros_like(item) for item in weights))
    totals, (outs, input_grads) = lax.scan(per_group, start, (token_groups, cot_groups, lengths, deal))
    return (outs.reshape(TOKENS, D), input_grads.reshape(TOKENS, D), totals[0], totals[1], totals[2], totals[3], totals[4], totals[5], totals[6], totals[7], totals[8])
```

```python
import functools
import math

import jax
import jax.numpy as jnp
from jax import lax
from jax.experimental import pallas as pl
from jax.experimental.pallas import tpu as pltpu
from jax.sharding import PartitionSpec as P

HEAD_DIM = 64
EPSILON = 1e-05
ROPE_BASE = 500000.0
MASKED = -1e30
LOG2_E = 1.4426950408889634
BLOCK = 256
CHUNKS = 2
VMEM = 56 * 2**20

F32 = jnp.float32
BF16 = jnp.bfloat16

PAIR = [(0, 1), (1, 0)]
CORE = [(0, 1), (1, 0), (2, 3), (3, 2)]
ACROSS = [(0, 2), (2, 0), (1, 3), (3, 1)]


def joint_pairs(x_core):
    pairs = []
    for ctx in range(2):
        for tp in range(4):
            there = (1 - ctx) * 4 + tp if tp % 2 == x_core else ctx * 4 + (tp ^ 2)
            pairs.append((ctx * 4 + tp, there))
    return pairs


FIRST = joint_pairs(0)
SECOND = joint_pairs(1)


def swap_core(v):
    return lax.ppermute(v, "tp", CORE)


def swap_y(v):
    return lax.ppermute(v, "tp", ACROSS)


def swap_x(v):
    return lax.ppermute(v, "ctx", PAIR)


def swap_first(v):
    return lax.ppermute(v, ("ctx", "tp"), FIRST)


def swap_second(v):
    return lax.ppermute(v, ("ctx", "tp"), SECOND)


def after(value, *others):
    return lax.optimization_barrier((value,) + others)[0]


def params(*semantics):
    return pltpu.CompilerParams(vmem_limit_bytes=VMEM)


def cost(flops, read, exps=0):
    return pl.CostEstimate(flops=int(flops), bytes_accessed=int(read), transcendentals=int(exps))


def inv_rms(hidden):
    return lax.rsqrt(jnp.mean(hidden * hidden, axis=-1, keepdims=True) + EPSILON)


def rms_back(hidden, gain, grad):
    scale = inv_rms(hidden)
    weighted = grad * gain
    inner = jnp.mean(weighted * hidden, axis=-1, keepdims=True)
    return scale * weighted - hidden * (scale * scale * scale) * inner


def turn_lanes(u, first):
    return jnp.where(first, pltpu.roll(u, 96, 1), pltpu.roll(u, 32, 1))


def two_halves(step, width, halves):
    return [
        pl.BlockSpec((step, width), lambda i: (jnp.minimum(i, halves - 1), 0)),
        pl.BlockSpec((step, width), lambda i: (jnp.maximum(i - halves, 0), 0)),
    ]


def either(halves, body, low_refs, high_refs):
    @pl.when(pl.program_id(0) < halves)
    def _():
        body(*low_refs)

    @pl.when(pl.program_id(0) >= halves)
    def _():
        body(*high_refs)


def qkv_kernel(halves, low_ref, high_ref, wq_ref, wkv_ref, cos_ref, sin_ref, o_ref):
    cos, sin = cos_ref[...], sin_ref[...]
    lane = lax.broadcasted_iota(jnp.int32, cos.shape, 1)
    first = (lane % 64) < 32

    def body(x_ref):
        x = x_ref[...]
        raw = jnp.dot(x, wq_ref[...], preferred_element_type=F32)
        tiles = raw.shape[1] // 128
        for tile in range(tiles):
            u = raw[:, tile * 128 : (tile + 1) * 128]
            turned = u * cos + turn_lanes(u, first) * sin
            o_ref[:, tile * 128 : (tile + 1) * 128] = turned.astype(BF16)
        u = jnp.dot(x, wkv_ref[...], preferred_element_type=F32)
        turned = u * cos + turn_lanes(u, first) * sin
        o_ref[:, tiles * 128 :] = jnp.where(lane < 64, turned, u).astype(BF16)

    either(halves, body, (low_ref,), (high_ref,))


def project_qkv(x, w, q_width, cos, sin):
    half_rows, depth = x[0].shape
    rows = 2 * half_rows
    width = q_width + 128
    step = min(512, half_rows)
    return pl.pallas_call(
        functools.partial(qkv_kernel, half_rows // step),
        out_shape=jax.ShapeDtypeStruct((rows, width), BF16),
        grid=(rows // step,),
        in_specs=two_halves(step, depth, half_rows // step)
        + [
            pl.BlockSpec((depth, q_width), lambda i: (0, 1)),
            pl.BlockSpec((depth, 128), lambda i: (0, 2 * q_width // 128)),
            pl.BlockSpec((step, 128), lambda i: (i, 0)),
            pl.BlockSpec((step, 128), lambda i: (i, 0)),
        ],
        out_specs=pl.BlockSpec((step, width), lambda i: (i, 0)),
        compiler_params=params(),
        cost_estimate=cost(2 * rows * depth * width, 2 * (rows * depth + depth * width)),
        name="qkv",
    )(*x, w, w, cos, sin)


def ffn_kernel(halves, xl_ref, xh_ref, cl_ref, ch_ref, w_ref, o_ref):
    n = w_ref.shape[1] // 3

    def body(x_ref, c_ref):
        x = x_ref[...]
        gate = jnp.dot(x, w_ref[:, :n], preferred_element_type=F32)
        up = jnp.dot(x, w_ref[:, n : 2 * n], preferred_element_type=F32)
        d_mixed = jnp.dot(c_ref[...], w_ref[:, 2 * n :], preferred_element_type=F32)
        sig = 1.0 / (1.0 + jnp.exp(-gate))
        silu = gate * sig
        o_ref[:, :n] = (d_mixed * up * (sig * (1.0 + gate * (1.0 - sig)))).astype(BF16)
        o_ref[:, n : 2 * n] = (d_mixed * silu).astype(BF16)
        o_ref[:, 2 * n :] = (silu * up).astype(BF16)

    either(halves, body, (xl_ref, cl_ref), (xh_ref, ch_ref))


def ffn_chunk(x, cot, w):
    half_rows, depth = x[0].shape
    rows = 2 * half_rows
    width = w.shape[1]
    step = min(512, half_rows)
    halves = half_rows // step
    return pl.pallas_call(
        functools.partial(ffn_kernel, halves),
        out_shape=jax.ShapeDtypeStruct((rows, width), BF16),
        grid=(rows // step,),
        in_specs=two_halves(step, depth, halves)
        + two_halves(step, depth, halves)
        + [pl.BlockSpec((depth, width), lambda i: (0, 0))],
        out_specs=pl.BlockSpec((step, width), lambda i: (i, 0)),
        compiler_params=params(),
        cost_estimate=cost(2 * rows * depth * width, 4 * rows * depth + 4 * depth * width),
        name="ffn",
    )(*x, *cot, w)


DOWN = (((0,), (0,)), ((), ()))


def grads_kernel(split, xl_ref, xh_ref, yl_ref, yh_ref, a_ref, b_ref, o_ref):
    half_rows = xl_ref.shape[0]

    def both(low_ref, high_ref, right_ref, columns):
        low = right_ref[:half_rows, columns].astype(BF16)
        high = right_ref[half_rows:, columns].astype(BF16)
        total = lax.dot_general(low_ref[...], low, DOWN, preferred_element_type=F32)
        return total + lax.dot_general(high_ref[...], high, DOWN, preferred_element_type=F32)

    o_ref[:, :split] = both(xl_ref, xh_ref, a_ref, slice(None)).astype(BF16)
    o_ref[:, split:] = both(yl_ref, yh_ref, b_ref, slice(None)).astype(BF16)


def weight_grads(x, a, a_width, a_column, y, b, b_width, b_column):
    half_rows, depth = x[0].shape
    rows = 2 * half_rows
    width = a_width + b_width
    step = 512
    tall = pl.BlockSpec((half_rows, step), lambda i: (0, i))
    return pl.pallas_call(
        functools.partial(grads_kernel, a_width),
        out_shape=jax.ShapeDtypeStruct((depth, width), BF16),
        grid=(depth // step,),
        in_specs=[tall] * 4
        + [
            pl.BlockSpec((rows, a_width), lambda i: (0, a_column)),
            pl.BlockSpec((rows, b_width), lambda i: (0, b_column)),
        ],
        out_specs=pl.BlockSpec((step, width), lambda i: (i, 0)),
        compiler_params=params(),
        cost_estimate=cost(2 * rows * depth * width, 4 * rows * depth + 4 * depth * width),
        name="weight_grads",
    )(*x, *y, a, b)


def back_kernel(*refs):
    o_ref = refs[-1]
    count = (len(refs) - 1) // 2
    total = None
    for part in range(count):
        term = lax.dot_general(
            refs[part][...].astype(BF16),
            refs[count + part][...],
            (((1,), (1,)), ((), ())),
            preferred_element_type=F32,
        )
        total = term if total is None else total + term
    o_ref[...] = total.astype(BF16)


def back_product(terms):
    rows = terms[0][0].shape[0]
    depth = terms[0][2].shape[0]
    step = 512
    total = sum(term[4] for term in terms)
    return pl.pallas_call(
        back_kernel,
        out_shape=jax.ShapeDtypeStruct((rows, depth), BF16),
        grid=(rows // step,),
        in_specs=[
            pl.BlockSpec((step, term[4]), lambda i, column=term[1]: (i, column)) for term in terms
        ]
        + [pl.BlockSpec((depth, term[4]), lambda i, column=term[3]: (0, column)) for term in terms],
        out_specs=pl.BlockSpec((step, depth), lambda i: (i, 0)),
        compiler_params=params(),
        cost_estimate=cost(2 * rows * depth * total, 2 * rows * depth),
        name="back",
    )(*[term[0] for term in terms], *[term[2] for term in terms])


def front_kernel(halves, low_ref, high_ref, w_ref, o_ref):
    def body(x_ref):
        o_ref[...] = jnp.dot(x_ref[...], w_ref[...], preferred_element_type=F32).astype(BF16)

    either(halves, body, (low_ref,), (high_ref,))


def front_product(x, w, width, column):
    half_rows, depth = x[0].shape
    rows = 2 * half_rows
    step = min(512, half_rows)
    halves = half_rows // step
    return pl.pallas_call(
        functools.partial(front_kernel, halves),
        out_shape=jax.ShapeDtypeStruct((rows, width), BF16),
        grid=(rows // step,),
        in_specs=two_halves(step, depth, halves)
        + [pl.BlockSpec((depth, width), lambda i: (0, column))],
        out_specs=pl.BlockSpec((step, width), lambda i: (i, 0)),
        compiler_params=params(),
        cost_estimate=cost(2 * rows * depth * width, 2 * rows * depth),
        name="front",
    )(*x, w)


def stack_heads(block):
    count = block.shape[1] // HEAD_DIM
    return jnp.concatenate(
        [block[:, h * HEAD_DIM : (h + 1) * HEAD_DIM] for h in range(count)], axis=0
    )


def unstack_heads(stacked):
    count = stacked.shape[0] // BLOCK
    return jnp.concatenate([stacked[h * BLOCK : (h + 1) * BLOCK] for h in range(count)], axis=1)


def allowed_of(i, j, start):
    row = i * BLOCK + lax.broadcasted_iota(jnp.int32, (BLOCK, BLOCK), 0)
    col = j * BLOCK + lax.broadcasted_iota(jnp.int32, (BLOCK, BLOCK), 1)
    return (col <= row) & (col >= start)


def attend_kernel(place, first, q_ref, kv_ref, start_ref, o_ref):
    i = pl.program_id(0)
    q = stack_heads(q_ref[...])
    heads = q.shape[0] // BLOCK
    start = start_ref[...]

    def step(j, carry):
        top, total, acc = carry
        at = pl.multiple_of(place[j] * BLOCK, BLOCK)
        kv = kv_ref[pl.ds(at, BLOCK), :]
        raw = lax.dot_general(
            q, kv[:, :HEAD_DIM], (((1,), (1,)), ((), ())), preferred_element_type=F32
        ) * (HEAD_DIM**-0.5 * LOG2_E)
        allowed = allowed_of(i, j, start)
        scores = jnp.where(allowed[None], raw.reshape(heads, BLOCK, BLOCK), MASKED).reshape(
            heads * BLOCK, BLOCK
        )
        new_top = jnp.maximum(top, jnp.max(scores, axis=-1, keepdims=True))
        keep = jnp.exp2(top - new_top)
        probs = jnp.exp2(scores - new_top)
        total = total * keep + jnp.sum(probs, axis=-1, keepdims=True)
        acc = acc * keep + jnp.dot(probs.astype(BF16), kv, preferred_element_type=F32)
        return (new_top, total, acc)

    size = heads * BLOCK
    top, total, acc = lax.fori_loop(
        first[i],
        i + 1,
        step,
        (
            jnp.full((size, 1), MASKED, F32),
            jnp.zeros((size, 1), F32),
            jnp.zeros((size, 2 * HEAD_DIM), F32),
        ),
    )
    out = acc[:, HEAD_DIM:] / total
    q_width = q_ref.shape[1]
    o_ref[:, :q_width] = unstack_heads(out)
    lse = top + jnp.log2(total)
    lane = lax.broadcasted_iota(jnp.int32, (BLOCK, 128), 1)
    packed = jnp.zeros((BLOCK, 128), F32)
    for h in range(heads):
        packed = jnp.where(lane == h, lse[h * BLOCK : (h + 1) * BLOCK], packed)
    o_ref[:, q_width:] = packed


def attend(qkv, place, first, start, q_width):
    rows = qkv.shape[0]
    blocks = rows // BLOCK
    return pl.pallas_call(
        attend_kernel,
        out_shape=jax.ShapeDtypeStruct((rows, q_width + 128), F32),
        grid_spec=pltpu.PrefetchScalarGridSpec(
            num_scalar_prefetch=2,
            grid=(blocks,),
            in_specs=[
                pl.BlockSpec((BLOCK, q_width), lambda i, place, first: (place[i], 0)),
                pl.BlockSpec((rows, 128), lambda i, place, first: (0, q_width // 128)),
                pl.BlockSpec((BLOCK, 1), lambda i, place, first: (i, 0)),
            ],
            out_specs=pl.BlockSpec((BLOCK, q_width + 128), lambda i, place, first: (place[i], 0)),
        ),
        compiler_params=params(),
        cost_estimate=cost(16e9, 4e6, rows * 1024 * 4),
        name="attend",
    )(place, first, qkv, qkv, start)


def attend_back_kernel(
    place,
    first,
    q_ref,
    d_ref,
    h_ref,
    kv_ref,
    start_ref,
    cos_ref,
    sin_ref,
    o_ref,
    dkv_ref,
):
    i = pl.program_id(0)
    blocks = pl.num_programs(0)
    score_scale = HEAD_DIM**-0.5
    q_width = q_ref.shape[1]

    @pl.when(i == 0)
    def _():
        dkv_ref[...] = jnp.zeros_like(dkv_ref)

    q = stack_heads(q_ref[...])
    d_out = stack_heads(d_ref[...])
    heads = q.shape[0] // BLOCK
    out = stack_heads(h_ref[:, :q_width])
    delta = jnp.sum(d_out.astype(F32) * out, axis=-1, keepdims=True)
    lse_block = h_ref[:, q_width:]
    lse = jnp.concatenate([lse_block[:, h : h + 1] for h in range(heads)], axis=0)
    start = start_ref[...]

    def step(j, d_q):
        at = pl.multiple_of(place[j] * BLOCK, BLOCK)
        kv = kv_ref[pl.ds(at, BLOCK), :]
        k, v = kv[:, :HEAD_DIM], kv[:, HEAD_DIM:]
        across = (((1,), (1,)), ((), ()))
        down = (((0,), (0,)), ((), ()))
        raw = lax.dot_general(q, k, across, preferred_element_type=F32) * (score_scale * LOG2_E)
        allowed = allowed_of(i, j, start)
        scores = jnp.where(allowed[None], raw.reshape(heads, BLOCK, BLOCK), MASKED).reshape(
            heads * BLOCK, BLOCK
        )
        probs = jnp.exp2(scores - lse)
        d_probs = lax.dot_general(d_out, v, across, preferred_element_type=F32)
        d_scores = (probs * (d_probs - delta)).astype(BF16)
        d_k = lax.dot_general(d_scores, q, down, preferred_element_type=F32) * score_scale
        d_v = lax.dot_general(probs.astype(BF16), d_out, down, preferred_element_type=F32)
        here = pl.ds(pl.multiple_of(j * BLOCK, BLOCK), BLOCK)
        dkv_ref[here, :] += jnp.concatenate([d_k, d_v], axis=1)
        return d_q + jnp.dot(d_scores, k, preferred_element_type=F32)

    d_q = lax.fori_loop(first[i], i + 1, step, jnp.zeros((heads * BLOCK, HEAD_DIM), F32))
    d_q = unstack_heads(d_q * score_scale)
    lane = lax.broadcasted_iota(jnp.int32, (BLOCK, 128), 1)
    front = (lane % 64) < 32
    mine = pl.ds(pl.multiple_of(place[i] * BLOCK, BLOCK), BLOCK)
    cos, sin = cos_ref[mine, :], sin_ref[mine, :]
    for tile in range(q_width // 128):
        u = d_q[:, tile * 128 : (tile + 1) * 128]
        o_ref[mine, tile * 128 : (tile + 1) * 128] = (u * cos - turn_lanes(u, front) * sin).astype(
            BF16
        )

    @pl.when(i == blocks - 1)
    def _():
        for b in range(dkv_ref.shape[0] // BLOCK):
            there = pl.ds(pl.multiple_of(place[b] * BLOCK, BLOCK), BLOCK)
            u = dkv_ref[b * BLOCK : (b + 1) * BLOCK, :]
            turned = u * cos_ref[there, :] - turn_lanes(u, front) * sin_ref[there, :]
            o_ref[there, q_width:] = jnp.where(lane < HEAD_DIM, turned, u).astype(BF16)


def attend_back(qkv, d_heads, heads, place, first, start, cos, sin):
    rows, width = qkv.shape
    q_width = d_heads.shape[1]
    blocks = rows // BLOCK
    by_place = lambda i, place, first: (place[i], 0)
    whole = lambda i, place, first: (0, 0)
    return pl.pallas_call(
        attend_back_kernel,
        out_shape=jax.ShapeDtypeStruct((rows, width), BF16),
        grid_spec=pltpu.PrefetchScalarGridSpec(
            num_scalar_prefetch=2,
            grid=(blocks,),
            in_specs=[
                pl.BlockSpec((BLOCK, q_width), by_place),
                pl.BlockSpec((BLOCK, q_width), by_place),
                pl.BlockSpec((BLOCK, q_width + 128), by_place),
                pl.BlockSpec((rows, 128), lambda i, place, first: (0, q_width // 128)),
                pl.BlockSpec((BLOCK, 1), lambda i, place, first: (i, 0)),
                pl.BlockSpec((rows, 128), whole),
                pl.BlockSpec((rows, 128), whole),
            ],
            out_specs=pl.BlockSpec((rows, width), whole),
            scratch_shapes=[pltpu.VMEM((rows, 128), F32)],
        ),
        compiler_params=params(),
        cost_estimate=cost(40e9, 6e6, rows * 1024 * 4),
        name="attend_back",
    )(place, first, qkv, d_heads, heads, qkv, start, cos, sin)


def sum_to_owner(part):
    rows = part.shape[0] // 8
    arrived = swap_core(part[4 * rows :])
    arrived = part[2 * rows : 4 * rows] + arrived[2 * rows :], part[: 2 * rows] + arrived[: 2 * rows]
    pair = arrived[1] + swap_second(arrived[0])
    return pair[:rows].astype(F32) + swap_first(pair[rows:]).astype(F32)


def share_rows(own):
    two = jnp.concatenate([own, swap_first(own)])
    four = jnp.concatenate([two, swap_second(two)])
    return four, swap_core(four)


def share_in_ctx(own, y, core):
    pair = jnp.stack([own, swap_y(own)])
    four = jnp.stack([pair, swap_core(pair)])
    four = jnp.where(y == 1, four[:, ::-1], four)
    four = jnp.where(core == 1, four[::-1], four)
    return four.transpose(1, 0, 2, 3).reshape(-1, own.shape[1])


def sum_all(v):
    v = v + swap_core(v)
    v = v + swap_y(v)
    return v + swap_x(v)


def both_halves(own, other, ctx):
    low = jnp.where(ctx == 0, own, other).astype(F32)
    high = jnp.where(ctx == 0, other, own).astype(F32)
    return low, high


def shards(
    tokens,
    q_weight,
    k_weight,
    v_weight,
    o_weight,
    attn_gain,
    gate_weight,
    up_weight,
    down_weight,
    ffn_gain,
    lengths,
    deal,
    cotangent,
):
    ctx = lax.axis_index("ctx")
    tp = lax.axis_index("tp")
    y, core = tp // 2, tp % 2
    row_count, depth = tokens.shape
    group_rows = row_count * lax.axis_size("ctx")
    own_rows = row_count // lax.axis_size("tp")

    def half(weight):
        width = weight.shape[1] // 2
        return lax.dynamic_slice_in_dim(weight, ctx * width, width, 1)

    q_half, k_half, v_half, o_half = map(half, (q_weight, k_weight, v_weight, o_weight))
    q_width, kv_width = q_half.shape[1], k_half.shape[1]
    attn_shard = jnp.concatenate([o_half, q_half, k_half, v_half], axis=1)
    attn_full = lax.all_gather(attn_shard, "fsdp", axis=0, tiled=True)
    gains = lax.all_gather(jnp.stack([attn_gain, ffn_gain]), "fsdp", axis=1, tiled=True)
    gain_one = gains[0].astype(F32)[None]
    gain_two = gains[1].astype(F32)[None]
    ff_half = gate_weight.shape[1] // 2
    chunk = ff_half // CHUNKS
    ffn_shards = []
    for part in range(CHUNKS):
        at = ctx * ff_half + part * chunk
        ffn_shards.append(
            jnp.concatenate(
                [
                    lax.dynamic_slice_in_dim(weight, at, chunk, 1)
                    for weight in (gate_weight, up_weight, down_weight)
                ],
                axis=1,
            )
        )
    ffn_full = []
    before = attn_full
    for part in range(CHUNKS):
        before = lax.all_gather(after(ffn_shards[part], before), "fsdp", axis=0, tiled=True)
        ffn_full.append(before)

    length_row, deal_row = lengths[0], deal[0]
    spans = deal_row.shape[0]
    span_rows = group_rows // spans
    ends = jnp.cumsum(length_row, dtype=jnp.int32)
    starts = ends - length_row
    natural = jnp.arange(group_rows, dtype=jnp.int32)
    inside = (natural[:, None] >= starts[None]) & (natural[:, None] < ends[None])
    start_of = jnp.sum(jnp.where(inside, starts[None], 0), axis=1, dtype=jnp.int32)
    first = start_of[::BLOCK] // BLOCK
    rel = jnp.arange(group_rows // own_rows, dtype=jnp.int32)
    rel_core = core ^ (rel // 4)
    by_first, by_second = rel % 2, (rel // 2) % 2
    rel_ctx = ctx ^ jnp.where(rel_core == 0, by_first, by_second)
    rel_y = y ^ jnp.where(rel_core == 0, by_second, by_first)
    dealt_block = rel_ctx * (row_count // own_rows) + rel_y * 2 + rel_core
    per_span = span_rows // own_rows
    span_of = jnp.sum(
        jnp.where(
            (dealt_block // per_span)[:, None] == jnp.arange(spans, dtype=jnp.int32)[None],
            deal_row[None],
            0,
        ),
        axis=1,
        dtype=jnp.int32,
    )
    natural_block = span_of * per_span + dealt_block % per_span
    place = jnp.sum(
        jnp.where(natural_block[None, :] == rel[:, None], rel[None, :], 0), axis=1, dtype=jnp.int32
    )
    natural_rel = (
        natural_block[:, None] * own_rows + jnp.arange(own_rows, dtype=jnp.int32)[None]
    ).reshape(-1)
    inside_rel = (natural_rel[:, None] >= starts[None]) & (natural_rel[:, None] < ends[None])
    position = natural_rel - jnp.sum(
        jnp.where(inside_rel, starts[None], 0), axis=1, dtype=jnp.int32
    )
    lane = jnp.arange(128, dtype=jnp.int32)
    inverse = jnp.exp((lane % 32).astype(F32) * (-2.0 * math.log(ROPE_BASE) / HEAD_DIM))
    angles = position.astype(F32)[:, None] * inverse[None]
    cos = jnp.cos(angles)
    sin = jnp.where((lane % 64 < 32)[None], -jnp.sin(angles), jnp.sin(angles))
    start_column = start_of[:, None]

    tokens_own = lax.dynamic_slice_in_dim(tokens, tp * own_rows, own_rows, 0).astype(F32)
    cot_low = lax.dynamic_slice_in_dim(cotangent, tp * own_rows, own_rows, 0)
    cot_own = cot_low.astype(F32)
    normed = share_rows((tokens_own * inv_rms(tokens_own) * gain_one).astype(BF16))
    cot = share_rows(after(cot_low, normed[0]))
    qkv = project_qkv(normed, attn_full, q_width, cos, sin)
    heads = attend(qkv, place, first, start_column, q_width)
    heads = after(heads, *cot)
    attn_part = back_product([(heads, 0, attn_full, 0, q_width)])
    hidden = tokens_own + sum_to_owner(attn_part)
    normed_two = share_rows((hidden * inv_rms(hidden) * gain_two).astype(BF16))

    acts = []
    grad_parts = []
    for part in range(CHUNKS):
        acts.append(ffn_chunk(normed_two, cot, ffn_full[part]))
        grad_parts.append(
            weight_grads(normed_two, acts[part], 2 * chunk, 0, cot, acts[part], chunk, 2)
        )
    d_norm_part = back_product(
        [(acts[part], 0, ffn_full[part], 0, 2 * chunk) for part in range(CHUNKS)]
    )
    ffn_part = back_product([(acts[part], 2, ffn_full[part], 2, chunk) for part in range(CHUNKS)])
    d_normed_two = sum_to_owner(d_norm_part)
    d_hidden = cot_own + rms_back(hidden, gain_two, d_normed_two)
    d_attn = share_rows(d_hidden.astype(BF16))
    result_own = (hidden + sum_to_owner(ffn_part)).astype(BF16)
    result = share_in_ctx(result_own, y, core)

    d_heads = front_product(d_attn, attn_full, q_width, 0)
    d_qkv = attend_back(qkv, d_heads, heads, place, first, start_column, cos, sin)
    d_normed_part = back_product(
        [
            (d_qkv, 0, attn_full, 1, q_width),
            (d_qkv, q_width // 128, attn_full, 2 * q_width // 128, 128),
        ]
    )
    attn_grad = weight_grads(
        d_attn, heads, q_width, 0, normed, d_qkv, q_width + 128, 0
    )
    d_normed = sum_to_owner(d_normed_part)
    tokens_grad_own = (d_hidden + rms_back(tokens_own, gain_one, d_normed)).astype(BF16)
    tokens_grad = share_in_ctx(tokens_grad_own, y, core)

    reduced = [
        lax.psum_scatter(part, "fsdp", scatter_dimension=0, tiled=True) for part in grad_parts
    ]
    attn_reduced = lax.psum_scatter(attn_grad, "fsdp", scatter_dimension=0, tiled=True)

    def gain_grad(pairs, gain):
        products = sum(
            jnp.sum(mine.astype(F32) * grad.astype(F32), axis=1) for mine, grad in pairs
        )
        return sum_all(products) / gain.astype(F32)

    attn_gain_grad = gain_grad([(attn_shard[:, q_width:], attn_reduced[:, q_width:])], attn_gain)
    ffn_gain_grad = gain_grad(
        [
            (ffn_shards[part][:, : 2 * chunk], reduced[part][:, : 2 * chunk])
            for part in range(CHUNKS)
        ],
        ffn_gain,
    )

    other_reduced = [swap_x(part) for part in reduced]
    halves = [both_halves(mine, other, ctx) for mine, other in zip(reduced, other_reduced)]

    def ffn_out(which):
        return jnp.concatenate(
            [
                halves[part][side][:, which * chunk : (which + 1) * chunk]
                for side in range(2)
                for part in range(CHUNKS)
            ],
            axis=1,
        )

    attn_low, attn_high = both_halves(attn_reduced, swap_x(attn_reduced), ctx)

    def attn_out(begin, end):
        return jnp.concatenate([attn_low[:, begin:end], attn_high[:, begin:end]], axis=1)

    q_end, k_end = 2 * q_width, 2 * q_width + kv_width
    return (
        result,
        tokens_grad,
        attn_out(q_width, q_end),
        attn_out(q_end, k_end),
        attn_out(k_end, k_end + kv_width),
        attn_out(0, q_width),
        attn_gain_grad,
        ffn_out(0),
        ffn_out(1),
        ffn_out(2),
        ffn_gain_grad,
    )


def solution(mesh):
    rows = P(("fsdp", "ctx"), None)
    matrix = P("fsdp", "tp")
    vector = P("fsdp")
    return jax.shard_map(
        shards,
        mesh=mesh,
        in_specs=(
            rows,
            matrix,
            matrix,
            matrix,
            matrix,
            vector,
            matrix,
            matrix,
            matrix,
            vector,
            P("fsdp", None),
            P("fsdp", None),
            rows,
        ),
        out_specs=(
            rows,
            rows,
            matrix,
            matrix,
            matrix,
            matrix,
            vector,
            matrix,
            matrix,
            matrix,
            vector,
        ),
        check_vma=False,
    )
```

```python
import functools
import math

import jax
import jax.numpy as jnp
from jax import lax
from jax.experimental import pallas as pl
from jax.experimental.pallas import tpu as pltpu
from jax.sharding import PartitionSpec as P

HEAD_DIM = 64
EPSILON = 1e-05
ROPE_BASE = 500000.0
MASKED = -1e30
LOG2_E = 1.4426950408889634
BLOCK = 256
CHUNKS = 2
VMEM = 56 * 2**20

F32 = jnp.float32
BF16 = jnp.bfloat16

PAIR = [(0, 1), (1, 0)]
CORE = [(0, 1), (1, 0), (2, 3), (3, 2)]
ACROSS = [(0, 2), (2, 0), (1, 3), (3, 1)]


def joint_pairs(x_core):
    pairs = []
    for ctx in range(2):
        for tp in range(4):
            there = (1 - ctx) * 4 + tp if tp % 2 == x_core else ctx * 4 + (tp ^ 2)
            pairs.append((ctx * 4 + tp, there))
    return pairs


FIRST = joint_pairs(0)
SECOND = joint_pairs(1)


def swap_core(v, pieces=1):
    if pieces == 1:
        return lax.ppermute(v, "tp", CORE)
    rows = v.shape[0] // pieces
    return jnp.concatenate(
        [lax.ppermute(v[at * rows : (at + 1) * rows], "tp", CORE) for at in range(pieces)]
    )


def swap_y(v):
    return lax.ppermute(v, "tp", ACROSS)


def swap_x(v):
    return lax.ppermute(v, "ctx", PAIR)


def swap_first(v):
    return lax.ppermute(v, ("ctx", "tp"), FIRST)


def swap_second(v):
    return lax.ppermute(v, ("ctx", "tp"), SECOND)


def after(value, *others):
    return lax.optimization_barrier((value,) + others)[0]


def params(*semantics):
    return pltpu.CompilerParams(vmem_limit_bytes=VMEM)


def cost(gigaflops=0):
    return pl.CostEstimate(flops=int(gigaflops * 1e9) + 1, bytes_accessed=1, transcendentals=0)


def inv_rms(hidden):
    return lax.rsqrt(jnp.mean(hidden * hidden, axis=-1, keepdims=True) + EPSILON)


def rms_back(hidden, gain, grad):
    scale = inv_rms(hidden)
    weighted = grad * gain
    inner = jnp.mean(weighted * hidden, axis=-1, keepdims=True)
    return scale * weighted - hidden * (scale * scale * scale) * inner


def turn_lanes(u, first):
    return jnp.where(first, pltpu.roll(u, 96, 1), pltpu.roll(u, 32, 1))


def two_halves(step, width, halves):
    return [
        pl.BlockSpec((step, width), lambda i: (jnp.minimum(i, halves - 1), 0)),
        pl.BlockSpec((step, width), lambda i: (jnp.maximum(i - halves, 0), 0)),
    ]


def either(halves, body, low_refs, high_refs):
    @pl.when(pl.program_id(0) < halves)
    def _():
        body(*low_refs)

    @pl.when(pl.program_id(0) >= halves)
    def _():
        body(*high_refs)


def qkv_kernel(halves, low_ref, high_ref, wq_ref, wkv_ref, cos_ref, sin_ref, o_ref):
    cos, sin = cos_ref[...], sin_ref[...]
    lane = lax.broadcasted_iota(jnp.int32, cos.shape, 1)
    first = (lane % 64) < 32

    def body(x_ref):
        x = x_ref[...]
        raw = jnp.dot(x, wq_ref[...], preferred_element_type=F32)
        tiles = raw.shape[1] // 128
        for tile in range(tiles):
            u = raw[:, tile * 128 : (tile + 1) * 128]
            turned = u * cos + turn_lanes(u, first) * sin
            o_ref[:, tile * 128 : (tile + 1) * 128] = turned.astype(BF16)
        u = jnp.dot(x, wkv_ref[...], preferred_element_type=F32)
        turned = u * cos + turn_lanes(u, first) * sin
        o_ref[:, tiles * 128 :] = jnp.where(lane < 64, turned, u).astype(BF16)

    either(halves, body, (low_ref,), (high_ref,))


def project_qkv(x, w, q_width, cos, sin):
    half_rows, depth = x[0].shape
    rows = 2 * half_rows
    width = q_width + 128
    step = min(512, half_rows)
    return pl.pallas_call(
        functools.partial(qkv_kernel, half_rows // step),
        out_shape=jax.ShapeDtypeStruct((rows, width), BF16),
        grid=(rows // step,),
        in_specs=two_halves(step, depth, half_rows // step)
        + [
            pl.BlockSpec((depth, q_width), lambda i: (0, 1)),
            pl.BlockSpec((depth, 128), lambda i: (0, 2 * q_width // 128)),
            pl.BlockSpec((step, 128), lambda i: (i, 0)),
            pl.BlockSpec((step, 128), lambda i: (i, 0)),
        ],
        out_specs=pl.BlockSpec((step, width), lambda i: (i, 0)),
        compiler_params=params(),
        cost_estimate=cost(),
        name="qkv",
    )(*x, w, w, cos, sin)


def ffn_kernel(halves, xl_ref, xh_ref, cl_ref, ch_ref, w_ref, o_ref):
    n = w_ref.shape[1] // 3

    def body(x_ref, c_ref):
        x = x_ref[...]
        gate = jnp.dot(x, w_ref[:, :n], preferred_element_type=F32)
        up = jnp.dot(x, w_ref[:, n : 2 * n], preferred_element_type=F32)
        d_mixed = jnp.dot(c_ref[...], w_ref[:, 2 * n :], preferred_element_type=F32)
        sig = 1.0 / (1.0 + jnp.exp(-gate))
        silu = gate * sig
        o_ref[:, :n] = (d_mixed * up * (sig * (1.0 + gate * (1.0 - sig)))).astype(BF16)
        o_ref[:, n : 2 * n] = (d_mixed * silu).astype(BF16)
        o_ref[:, 2 * n :] = (silu * up).astype(BF16)

    either(halves, body, (xl_ref, cl_ref), (xh_ref, ch_ref))


def ffn_chunk(x, cot, w):
    half_rows, depth = x[0].shape
    rows = 2 * half_rows
    width = w.shape[1]
    step = min(512, half_rows)
    halves = half_rows // step
    return pl.pallas_call(
        functools.partial(ffn_kernel, halves),
        out_shape=jax.ShapeDtypeStruct((rows, width), BF16),
        grid=(rows // step,),
        in_specs=two_halves(step, depth, halves)
        + two_halves(step, depth, halves)
        + [pl.BlockSpec((depth, width), lambda i: (0, 0))],
        out_specs=pl.BlockSpec((step, width), lambda i: (i, 0)),
        compiler_params=params(),
        cost_estimate=cost(),
        name="ffn",
    )(*x, *cot, w)


DOWN = (((0,), (0,)), ((), ()))


def grads_kernel(split, xl_ref, xh_ref, yl_ref, yh_ref, a_ref, b_ref, o_ref):
    half_rows = xl_ref.shape[0]

    def both(low_ref, high_ref, right_ref, columns):
        low = right_ref[:half_rows, columns].astype(BF16)
        high = right_ref[half_rows:, columns].astype(BF16)
        total = lax.dot_general(low_ref[...], low, DOWN, preferred_element_type=F32)
        return total + lax.dot_general(high_ref[...], high, DOWN, preferred_element_type=F32)

    o_ref[:, :split] = both(xl_ref, xh_ref, a_ref, slice(None)).astype(BF16)
    o_ref[:, split:] = both(yl_ref, yh_ref, b_ref, slice(None)).astype(BF16)


def weight_grads(x, a, a_width, a_column, y, b, b_width, b_column):
    half_rows, depth = x[0].shape
    rows = 2 * half_rows
    width = a_width + b_width
    step = 512
    tall = pl.BlockSpec((half_rows, step), lambda i: (0, i))
    return pl.pallas_call(
        functools.partial(grads_kernel, a_width),
        out_shape=jax.ShapeDtypeStruct((depth, width), BF16),
        grid=(depth // step,),
        in_specs=[tall] * 4
        + [
            pl.BlockSpec((rows, a_width), lambda i: (0, a_column)),
            pl.BlockSpec((rows, b_width), lambda i: (0, b_column)),
        ],
        out_specs=pl.BlockSpec((step, width), lambda i: (i, 0)),
        compiler_params=params(),
        cost_estimate=cost(),
        name="weight_grads",
    )(*x, *y, a, b)


def back_kernel(*refs):
    o_ref = refs[-1]
    count = (len(refs) - 1) // 2
    total = None
    for part in range(count):
        term = lax.dot_general(
            refs[part][...].astype(BF16),
            refs[count + part][...],
            (((1,), (1,)), ((), ())),
            preferred_element_type=F32,
        )
        total = term if total is None else total + term
    o_ref[...] = total.astype(BF16)


def back_product(terms):
    rows = terms[0][0].shape[0]
    depth = terms[0][2].shape[0]
    step = 512
    total = sum(term[4] for term in terms)
    return pl.pallas_call(
        back_kernel,
        out_shape=jax.ShapeDtypeStruct((rows, depth), BF16),
        grid=(rows // step,),
        in_specs=[
            pl.BlockSpec((step, term[4]), lambda i, column=term[1]: (i, column)) for term in terms
        ]
        + [pl.BlockSpec((depth, term[4]), lambda i, column=term[3]: (0, column)) for term in terms],
        out_specs=pl.BlockSpec((step, depth), lambda i: (i, 0)),
        compiler_params=params(),
        cost_estimate=cost(),
        name="back",
    )(*[term[0] for term in terms], *[term[2] for term in terms])


def front_kernel(halves, low_ref, high_ref, w_ref, o_ref):
    def body(x_ref):
        o_ref[...] = jnp.dot(x_ref[...], w_ref[...], preferred_element_type=F32).astype(BF16)

    either(halves, body, (low_ref,), (high_ref,))


def front_product(x, w, width, column):
    half_rows, depth = x[0].shape
    rows = 2 * half_rows
    step = min(512, half_rows)
    halves = half_rows // step
    return pl.pallas_call(
        functools.partial(front_kernel, halves),
        out_shape=jax.ShapeDtypeStruct((rows, width), BF16),
        grid=(rows // step,),
        in_specs=two_halves(step, depth, halves)
        + [pl.BlockSpec((depth, width), lambda i: (0, column))],
        out_specs=pl.BlockSpec((step, width), lambda i: (i, 0)),
        compiler_params=params(),
        cost_estimate=cost(),
        name="front",
    )(*x, w)


def stack_heads(block):
    count = block.shape[1] // HEAD_DIM
    return jnp.concatenate(
        [block[:, h * HEAD_DIM : (h + 1) * HEAD_DIM] for h in range(count)], axis=0
    )


def unstack_heads(stacked):
    count = stacked.shape[0] // BLOCK
    return jnp.concatenate([stacked[h * BLOCK : (h + 1) * BLOCK] for h in range(count)], axis=1)


def allowed_of(i, j, start):
    row = i * BLOCK + lax.broadcasted_iota(jnp.int32, (BLOCK, BLOCK), 0)
    col = j * BLOCK + lax.broadcasted_iota(jnp.int32, (BLOCK, BLOCK), 1)
    return (col <= row) & (col >= start)


def attend_kernel(place, first, q_ref, kv_ref, start_ref, o_ref):
    i = pl.program_id(0)
    q = stack_heads(q_ref[...])
    heads = q.shape[0] // BLOCK
    start = start_ref[...]

    def step(j, carry):
        top, total, acc = carry
        at = pl.multiple_of(place[j] * BLOCK, BLOCK)
        kv = kv_ref[pl.ds(at, BLOCK), :]
        raw = lax.dot_general(
            q, kv[:, :HEAD_DIM], (((1,), (1,)), ((), ())), preferred_element_type=F32
        ) * (HEAD_DIM**-0.5 * LOG2_E)
        allowed = allowed_of(i, j, start)
        scores = jnp.where(allowed[None], raw.reshape(heads, BLOCK, BLOCK), MASKED).reshape(
            heads * BLOCK, BLOCK
        )
        new_top = jnp.maximum(top, jnp.max(scores, axis=-1, keepdims=True))
        keep = jnp.exp2(top - new_top)
        probs = jnp.exp2(scores - new_top)
        total = total * keep + jnp.sum(probs, axis=-1, keepdims=True)
        acc = acc * keep + jnp.dot(probs.astype(BF16), kv, preferred_element_type=F32)
        return (new_top, total, acc)

    size = heads * BLOCK
    top, total, acc = lax.fori_loop(
        first[i],
        i + 1,
        step,
        (
            jnp.full((size, 1), MASKED, F32),
            jnp.zeros((size, 1), F32),
            jnp.zeros((size, 2 * HEAD_DIM), F32),
        ),
    )
    out = acc[:, HEAD_DIM:] / total
    q_width = q_ref.shape[1]
    o_ref[:, :q_width] = unstack_heads(out)
    lse = top + jnp.log2(total)
    lane = lax.broadcasted_iota(jnp.int32, (BLOCK, 128), 1)
    packed = jnp.zeros((BLOCK, 128), F32)
    for h in range(heads):
        packed = jnp.where(lane == h, lse[h * BLOCK : (h + 1) * BLOCK], packed)
    o_ref[:, q_width:] = packed


def attend(qkv, place, first, start, q_width):
    rows = qkv.shape[0]
    blocks = rows // BLOCK
    return pl.pallas_call(
        attend_kernel,
        out_shape=jax.ShapeDtypeStruct((rows, q_width + 128), F32),
        grid_spec=pltpu.PrefetchScalarGridSpec(
            num_scalar_prefetch=2,
            grid=(blocks,),
            in_specs=[
                pl.BlockSpec((BLOCK, q_width), lambda i, place, first: (place[i], 0)),
                pl.BlockSpec((rows, 128), lambda i, place, first: (0, q_width // 128)),
                pl.BlockSpec((BLOCK, 1), lambda i, place, first: (i, 0)),
            ],
            out_specs=pl.BlockSpec((BLOCK, q_width + 128), lambda i, place, first: (place[i], 0)),
        ),
        compiler_params=params(),
        cost_estimate=cost(),
        name="attend",
    )(place, first, qkv, qkv, start)


def attend_back_kernel(
    place,
    first,
    q_ref,
    d_ref,
    h_ref,
    kv_ref,
    start_ref,
    cos_ref,
    sin_ref,
    o_ref,
    dkv_ref,
):
    i = pl.program_id(0)
    blocks = pl.num_programs(0)
    score_scale = HEAD_DIM**-0.5
    q_width = q_ref.shape[1]

    @pl.when(i == 0)
    def _():
        dkv_ref[...] = jnp.zeros_like(dkv_ref)

    q = stack_heads(q_ref[...])
    d_out = stack_heads(d_ref[...])
    heads = q.shape[0] // BLOCK
    out = stack_heads(h_ref[:, :q_width])
    delta = jnp.sum(d_out.astype(F32) * out, axis=-1, keepdims=True)
    lse_block = h_ref[:, q_width:]
    lse = jnp.concatenate([lse_block[:, h : h + 1] for h in range(heads)], axis=0)
    start = start_ref[...]

    def step(j, d_q):
        at = pl.multiple_of(place[j] * BLOCK, BLOCK)
        kv = kv_ref[pl.ds(at, BLOCK), :]
        k, v = kv[:, :HEAD_DIM], kv[:, HEAD_DIM:]
        across = (((1,), (1,)), ((), ()))
        down = (((0,), (0,)), ((), ()))
        raw = lax.dot_general(q, k, across, preferred_element_type=F32) * (score_scale * LOG2_E)
        allowed = allowed_of(i, j, start)
        scores = jnp.where(allowed[None], raw.reshape(heads, BLOCK, BLOCK), MASKED).reshape(
            heads * BLOCK, BLOCK
        )
        probs = jnp.exp2(scores - lse)
        d_probs = lax.dot_general(d_out, v, across, preferred_element_type=F32)
        d_scores = (probs * (d_probs - delta)).astype(BF16)
        d_k = lax.dot_general(d_scores, q, down, preferred_element_type=F32) * score_scale
        d_v = lax.dot_general(probs.astype(BF16), d_out, down, preferred_element_type=F32)
        here = pl.ds(pl.multiple_of(j * BLOCK, BLOCK), BLOCK)
        dkv_ref[here, :] += jnp.concatenate([d_k, d_v], axis=1)
        return d_q + jnp.dot(d_scores, k, preferred_element_type=F32)

    d_q = lax.fori_loop(first[i], i + 1, step, jnp.zeros((heads * BLOCK, HEAD_DIM), F32))
    d_q = unstack_heads(d_q * score_scale)
    lane = lax.broadcasted_iota(jnp.int32, (BLOCK, 128), 1)
    front = (lane % 64) < 32
    mine = pl.ds(pl.multiple_of(place[i] * BLOCK, BLOCK), BLOCK)
    cos, sin = cos_ref[mine, :], sin_ref[mine, :]
    for tile in range(q_width // 128):
        u = d_q[:, tile * 128 : (tile + 1) * 128]
        o_ref[mine, tile * 128 : (tile + 1) * 128] = (u * cos - turn_lanes(u, front) * sin).astype(
            BF16
        )

    @pl.when(i == blocks - 1)
    def _():
        for b in range(dkv_ref.shape[0] // BLOCK):
            there = pl.ds(pl.multiple_of(place[b] * BLOCK, BLOCK), BLOCK)
            u = dkv_ref[b * BLOCK : (b + 1) * BLOCK, :]
            turned = u * cos_ref[there, :] - turn_lanes(u, front) * sin_ref[there, :]
            o_ref[there, q_width:] = jnp.where(lane < HEAD_DIM, turned, u).astype(BF16)


def attend_back(qkv, d_heads, heads, place, first, start, cos, sin):
    rows, width = qkv.shape
    q_width = d_heads.shape[1]
    blocks = rows // BLOCK
    by_place = lambda i, place, first: (place[i], 0)
    whole = lambda i, place, first: (0, 0)
    return pl.pallas_call(
        attend_back_kernel,
        out_shape=jax.ShapeDtypeStruct((rows, width), BF16),
        grid_spec=pltpu.PrefetchScalarGridSpec(
            num_scalar_prefetch=2,
            grid=(blocks,),
            in_specs=[
                pl.BlockSpec((BLOCK, q_width), by_place),
                pl.BlockSpec((BLOCK, q_width), by_place),
                pl.BlockSpec((BLOCK, q_width + 128), by_place),
                pl.BlockSpec((rows, 128), lambda i, place, first: (0, q_width // 128)),
                pl.BlockSpec((BLOCK, 1), lambda i, place, first: (i, 0)),
                pl.BlockSpec((rows, 128), whole),
                pl.BlockSpec((rows, 128), whole),
            ],
            out_specs=pl.BlockSpec((rows, width), whole),
            scratch_shapes=[pltpu.VMEM((rows, 128), F32)],
        ),
        compiler_params=params(),
        cost_estimate=cost(),
        name="attend_back",
    )(place, first, qkv, d_heads, heads, qkv, start, cos, sin)


def sum_cores(part):
    rows = part.shape[0] // 8
    arrived = [lax.ppermute(part[at * rows : (at + 1) * rows], "tp", CORE) for at in range(4, 8)]
    far = part[2 * rows : 4 * rows] + jnp.concatenate(arrived[2:])
    near = part[: 2 * rows] + jnp.concatenate(arrived[:2])
    return far, near


def sum_chips(far, near, behind=(), beside=()):
    rows = near.shape[0] // 2
    near = near + after(swap_second(far), *behind)
    near = after(near, *beside)
    return near[:rows].astype(F32) + swap_first(near[rows:]).astype(F32)


def sum_to_owner(part, beside=()):
    return sum_chips(*sum_cores(part), beside=beside)


def share_rows(own, beside=()):
    beside = list(beside) + [()] * (2 - len(beside))
    two = jnp.concatenate([own, after(swap_first(own), *beside[0])])
    four = jnp.concatenate([two, after(swap_second(two), *beside[1])])
    return four, swap_core(four, 4)


def ring_over(shard, count):
    cycle = [(at, (at + 1) % count) for at in range(count)]
    pieces = [shard]
    for _ in range(count - 1):
        pieces.append(lax.ppermute(pieces[-1], "fsdp", cycle))
    return pieces


def in_place(pieces, axis):
    count, size = len(pieces), pieces[0].shape[axis]
    here = lax.axis_index("fsdp")
    shape = list(pieces[0].shape)
    shape[axis] *= count
    whole = jnp.zeros(shape, pieces[0].dtype)
    for back, piece in enumerate(pieces):
        owner = lax.rem(here + count - back, count)
        whole = lax.dynamic_update_slice_in_dim(whole, piece, owner * size, axis)
    return whole


def shifts_over(shard, count):
    return [shard] + [
        lax.ppermute(shard, "fsdp", [(at, (at + by) % count) for at in range(count)])
        for by in range(1, count)
    ]


def share_in_ctx(own, y, core):
    pair = jnp.stack([own, swap_y(own)])
    four = jnp.stack([pair, swap_core(pair)])
    four = jnp.where(y == 1, four[:, ::-1], four)
    four = jnp.where(core == 1, four[::-1], four)
    return four.transpose(1, 0, 2, 3).reshape(-1, own.shape[1])


def sum_all(v):
    v = v + swap_core(v)
    v = v + swap_y(v)
    return v + swap_x(v)


def both_halves(own, other, ctx):
    low = jnp.where(ctx == 0, own, other).astype(F32)
    high = jnp.where(ctx == 0, other, own).astype(F32)
    return low, high


def shards(
    tokens,
    q_weight,
    k_weight,
    v_weight,
    o_weight,
    attn_gain,
    gate_weight,
    up_weight,
    down_weight,
    ffn_gain,
    lengths,
    deal,
    cotangent,
):
    ctx = lax.axis_index("ctx")
    tp = lax.axis_index("tp")
    y, core = tp // 2, tp % 2
    row_count, depth = tokens.shape
    group_rows = row_count * lax.axis_size("ctx")
    own_rows = row_count // lax.axis_size("tp")

    def half(weight):
        width = weight.shape[1] // 2
        return lax.dynamic_slice_in_dim(weight, ctx * width, width, 1)

    q_half, k_half, v_half, o_half = map(half, (q_weight, k_weight, v_weight, o_weight))
    q_width, kv_width = q_half.shape[1], k_half.shape[1]
    attn_shard = jnp.concatenate([o_half, q_half, k_half, v_half], axis=1)
    fsdp = lax.axis_size("fsdp")
    attn_ring = ring_over(attn_shard, fsdp)
    attn_full = in_place(attn_ring, 0)
    gains = in_place(shifts_over(jnp.stack([attn_gain, ffn_gain]), fsdp), 1)
    gain_one = gains[0].astype(F32)[None]
    gain_two = gains[1].astype(F32)[None]
    ff_half = gate_weight.shape[1] // 2
    chunk = ff_half // CHUNKS
    ffn_shards = []
    for part in range(CHUNKS):
        at = ctx * ff_half + part * chunk
        ffn_shards.append(
            jnp.concatenate(
                [
                    lax.dynamic_slice_in_dim(weight, at, chunk, 1)
                    for weight in (gate_weight, up_weight, down_weight)
                ],
                axis=1,
            )
        )
    length_row, deal_row = lengths[0], deal[0]
    spans = deal_row.shape[0]
    span_rows = group_rows // spans
    ends = jnp.cumsum(length_row, dtype=jnp.int32)
    starts = ends - length_row
    natural = jnp.arange(group_rows, dtype=jnp.int32)
    inside = (natural[:, None] >= starts[None]) & (natural[:, None] < ends[None])
    start_of = jnp.sum(jnp.where(inside, starts[None], 0), axis=1, dtype=jnp.int32)
    first = start_of[::BLOCK] // BLOCK
    rel = jnp.arange(group_rows // own_rows, dtype=jnp.int32)
    rel_core = core ^ (rel // 4)
    by_first, by_second = rel % 2, (rel // 2) % 2
    rel_ctx = ctx ^ jnp.where(rel_core == 0, by_first, by_second)
    rel_y = y ^ jnp.where(rel_core == 0, by_second, by_first)
    dealt_block = rel_ctx * (row_count // own_rows) + rel_y * 2 + rel_core
    per_span = span_rows // own_rows
    span_of = jnp.sum(
        jnp.where(
            (dealt_block // per_span)[:, None] == jnp.arange(spans, dtype=jnp.int32)[None],
            deal_row[None],
            0,
        ),
        axis=1,
        dtype=jnp.int32,
    )
    natural_block = span_of * per_span + dealt_block % per_span
    place = jnp.sum(
        jnp.where(natural_block[None, :] == rel[:, None], rel[None, :], 0), axis=1, dtype=jnp.int32
    )
    natural_rel = (
        natural_block[:, None] * own_rows + jnp.arange(own_rows, dtype=jnp.int32)[None]
    ).reshape(-1)
    inside_rel = (natural_rel[:, None] >= starts[None]) & (natural_rel[:, None] < ends[None])
    position = natural_rel - jnp.sum(
        jnp.where(inside_rel, starts[None], 0), axis=1, dtype=jnp.int32
    )
    lane = jnp.arange(128, dtype=jnp.int32)
    inverse = jnp.exp((lane % 32).astype(F32) * (-2.0 * math.log(ROPE_BASE) / HEAD_DIM))
    angles = position.astype(F32)[:, None] * inverse[None]
    cos = jnp.cos(angles)
    sin = jnp.where((lane % 64 < 32)[None], -jnp.sin(angles), jnp.sin(angles))
    start_column = start_of[:, None]

    tokens_own = lax.dynamic_slice_in_dim(tokens, tp * own_rows, own_rows, 0).astype(F32)
    cot_low = lax.dynamic_slice_in_dim(cotangent, tp * own_rows, own_rows, 0)
    cot_own = cot_low.astype(F32)
    normed = share_rows(
        (tokens_own * inv_rms(tokens_own) * gain_one).astype(BF16), [[piece] for piece in attn_ring[1:3]]
    )
    attn_full, first_shard, cot_low, cos, sin, *normed = lax.optimization_barrier(
        (attn_full, after(ffn_shards[0], attn_ring[-1]), cot_low, cos, sin, *normed)
    )
    qkv = project_qkv(normed, attn_full, q_width, cos, sin)
    heads = attend(qkv, place, first, start_column, q_width)
    cot = share_rows(cot_low, [[qkv], [heads]])
    ffn_full = [
        lax.all_gather(shard, "fsdp", axis=0, tiled=True)
        for shard in (first_shard, after(ffn_shards[1], heads))
    ]
    heads = after(heads, *cot)
    attn_part = back_product([(heads, 0, attn_full, 0, q_width)])
    hidden = tokens_own + sum_to_owner(attn_part, ffn_full[:1])
    normed_two = share_rows((hidden * inv_rms(hidden) * gain_two).astype(BF16))

    acts = []
    grad_parts = []
    for part in range(CHUNKS):
        acts.append(ffn_chunk(after(normed_two, *grad_parts), cot, ffn_full[part]))
        grad_parts.append(
            weight_grads(normed_two, acts[part], 2 * chunk, 0, cot, acts[part], chunk, 2)
        )
    reduced = [
        lax.psum_scatter(part, "fsdp", scatter_dimension=0, tiled=True) for part in grad_parts
    ]
    d_norm_part = back_product(
        [(acts[part], 0, ffn_full[part], 0, 2 * chunk) for part in range(CHUNKS)]
    )
    ffn_part = back_product([(acts[part], 2, ffn_full[part], 2, chunk) for part in range(CHUNKS)])
    d_normed_two = sum_to_owner(d_norm_part, grad_parts)
    d_hidden = cot_own + rms_back(hidden, gain_two, d_normed_two)
    d_attn = share_rows(d_hidden.astype(BF16), [[ffn_part, reduced[0]]])

    d_heads = front_product(d_attn, attn_full, q_width, 0)
    ffn_far, ffn_near = sum_cores(after(ffn_part, d_attn[1]))
    d_heads, ffn_far, reduced[0] = lax.optimization_barrier((d_heads, ffn_far, reduced[0]))
    other_reduced = [swap_x(reduced[0])]
    d_qkv = attend_back(qkv, d_heads, heads, place, first, start_column, cos, sin)
    d_normed_part = back_product(
        [
            (d_qkv, 0, attn_full, 1, q_width),
            (d_qkv, q_width // 128, attn_full, 2 * q_width // 128, 128),
        ]
    )
    attn_grad = weight_grads(
        d_attn, heads, q_width, 0, normed, d_qkv, q_width + 128, 0
    )
    normed_far, normed_near = sum_cores(d_normed_part)
    for part in range(1, CHUNKS):
        reduced[part] = after(reduced[part], attn_grad)
    d_normed = sum_chips(normed_far, normed_near, beside=[attn_grad, *reduced[1:]])
    for part in range(1, CHUNKS):
        reduced[part] = after(reduced[part], d_normed)
        other_reduced.append(swap_x(reduced[part]))
    result_own = (hidden + sum_chips(ffn_far, ffn_near, behind=[normed_far])).astype(BF16)
    result = share_in_ctx(result_own, y, core)
    tokens_grad_own = (d_hidden + rms_back(tokens_own, gain_one, d_normed)).astype(BF16)
    tokens_grad = share_in_ctx(tokens_grad_own, y, core)

    attn_reduced = lax.psum_scatter(attn_grad, "fsdp", scatter_dimension=0, tiled=True)
    attn_reduced = after(attn_reduced, tokens_grad)

    def gain_grad(pairs, gain):
        products = sum(
            jnp.sum(mine.astype(F32) * grad.astype(F32), axis=1) for mine, grad in pairs
        )
        return sum_all(products) / gain.astype(F32)

    attn_gain_grad = gain_grad([(attn_shard[:, q_width:], attn_reduced[:, q_width:])], attn_gain)
    ffn_gain_grad = gain_grad(
        [
            (ffn_shards[part][:, : 2 * chunk], reduced[part][:, : 2 * chunk])
            for part in range(CHUNKS)
        ],
        ffn_gain,
    )

    halves = [both_halves(mine, other, ctx) for mine, other in zip(reduced, other_reduced)]

    def ffn_out(which):
        return jnp.concatenate(
            [
                halves[part][side][:, which * chunk : (which + 1) * chunk]
                for side in range(2)
                for part in range(CHUNKS)
            ],
            axis=1,
        )

    attn_low, attn_high = both_halves(attn_reduced, swap_x(attn_reduced), ctx)

    def attn_out(begin, end):
        return jnp.concatenate([attn_low[:, begin:end], attn_high[:, begin:end]], axis=1)

    q_end, k_end = 2 * q_width, 2 * q_width + kv_width
    return (
        result,
        tokens_grad,
        attn_out(q_width, q_end),
        attn_out(q_end, k_end),
        attn_out(k_end, k_end + kv_width),
        attn_out(0, q_width),
        attn_gain_grad,
        ffn_out(0),
        ffn_out(1),
        ffn_out(2),
        ffn_gain_grad,
    )


def solution(mesh):
    rows = P(("fsdp", "ctx"), None)
    matrix = P("fsdp", "tp")
    vector = P("fsdp")
    return jax.shard_map(
        shards,
        mesh=mesh,
        in_specs=(
            rows,
            matrix,
            matrix,
            matrix,
            matrix,
            vector,
            matrix,
            matrix,
            matrix,
            vector,
            P("fsdp", None),
            P("fsdp", None),
            rows,
        ),
        out_specs=(
            rows,
            rows,
            matrix,
            matrix,
            matrix,
            matrix,
            vector,
            matrix,
            matrix,
            matrix,
            vector,
        ),
        check_vma=False,
    )
```

```python
import functools
import math

import jax
import jax.numpy as jnp
from jax import lax
from jax.experimental import pallas as pl
from jax.experimental.pallas import tpu as pltpu
from jax.sharding import PartitionSpec as P

HEAD_DIM = 64
EPSILON = 1e-05
ROPE_BASE = 500000.0
MASKED = -1e30
LOG2_E = 1.4426950408889634
BLOCK = 256
CHUNKS = 2
VMEM = 56 * 2**20

F32 = jnp.float32
BF16 = jnp.bfloat16

PAIR = [(0, 1), (1, 0)]
CORE = [(0, 1), (1, 0), (2, 3), (3, 2)]
ACROSS = [(0, 2), (2, 0), (1, 3), (3, 1)]


def joint_pairs(x_core):
    pairs = []
    for ctx in range(2):
        for tp in range(4):
            there = (1 - ctx) * 4 + tp if tp % 2 == x_core else ctx * 4 + (tp ^ 2)
            pairs.append((ctx * 4 + tp, there))
    return pairs


FIRST = joint_pairs(0)
SECOND = joint_pairs(1)


def swap_core(v):
    return lax.ppermute(v, "tp", CORE)


def swap_y(v):
    return lax.ppermute(v, "tp", ACROSS)


def swap_x(v):
    return lax.ppermute(v, "ctx", PAIR)


def swap_first(v):
    return lax.ppermute(v, ("ctx", "tp"), FIRST)


def swap_second(v):
    return lax.ppermute(v, ("ctx", "tp"), SECOND)


def after(value, *others):
    return lax.optimization_barrier((value,) + others)[0]


def params(*semantics):
    return pltpu.CompilerParams(vmem_limit_bytes=VMEM)


def cost(gigaflops=0):
    return pl.CostEstimate(flops=int(gigaflops * 1e9) + 1, bytes_accessed=1, transcendentals=0)


def inv_rms(hidden):
    return lax.rsqrt(jnp.mean(hidden * hidden, axis=-1, keepdims=True) + EPSILON)


def rms_back(hidden, gain, grad):
    scale = inv_rms(hidden)
    weighted = grad * gain
    inner = jnp.mean(weighted * hidden, axis=-1, keepdims=True)
    return scale * weighted - hidden * (scale * scale * scale) * inner


def turn_lanes(u, first):
    return jnp.where(first, pltpu.roll(u, 96, 1), pltpu.roll(u, 32, 1))


def two_halves(step, width, halves):
    return [
        pl.BlockSpec((step, width), lambda i: (jnp.minimum(i, halves - 1), 0)),
        pl.BlockSpec((step, width), lambda i: (jnp.maximum(i - halves, 0), 0)),
    ]


def either(halves, body, low_refs, high_refs):
    @pl.when(pl.program_id(0) < halves)
    def _():
        body(*low_refs)

    @pl.when(pl.program_id(0) >= halves)
    def _():
        body(*high_refs)


def qkv_kernel(halves, low_ref, high_ref, gain_ref, wq_ref, wkv_ref, cos_ref, sin_ref, o_ref):
    cos, sin = cos_ref[...], sin_ref[...]
    lane = lax.broadcasted_iota(jnp.int32, cos.shape, 1)
    first = (lane % 64) < 32

    def body(x_ref):
        x = x_ref[...].astype(F32)
        x = (x * inv_rms(x) * gain_ref[...]).astype(BF16)
        raw = jnp.dot(x, wq_ref[...], preferred_element_type=F32)
        tiles = raw.shape[1] // 128
        for tile in range(tiles):
            u = raw[:, tile * 128 : (tile + 1) * 128]
            turned = u * cos + turn_lanes(u, first) * sin
            o_ref[:, tile * 128 : (tile + 1) * 128] = turned.astype(BF16)
        u = jnp.dot(x, wkv_ref[...], preferred_element_type=F32)
        turned = u * cos + turn_lanes(u, first) * sin
        o_ref[:, tiles * 128 :] = jnp.where(lane < 64, turned, u).astype(BF16)

    either(halves, body, (low_ref,), (high_ref,))


def project_qkv(x, gain, w, q_width, cos, sin):
    half_rows, depth = x[0].shape
    rows = 2 * half_rows
    width = q_width + 128
    step = min(512, half_rows)
    return pl.pallas_call(
        functools.partial(qkv_kernel, half_rows // step),
        out_shape=jax.ShapeDtypeStruct((rows, width), BF16),
        grid=(rows // step,),
        in_specs=two_halves(step, depth, half_rows // step)
        + [
            pl.BlockSpec((1, depth), lambda i: (0, 0)),
            pl.BlockSpec((depth, q_width), lambda i: (0, 1)),
            pl.BlockSpec((depth, 128), lambda i: (0, 2 * q_width // 128)),
            pl.BlockSpec((step, 128), lambda i: (i, 0)),
            pl.BlockSpec((step, 128), lambda i: (i, 0)),
        ],
        out_specs=pl.BlockSpec((step, width), lambda i: (i, 0)),
        compiler_params=params(),
        cost_estimate=cost(),
        name="qkv",
    )(*x, gain, w, w, cos, sin)


def ffn_kernel(halves, xl_ref, xh_ref, cl_ref, ch_ref, w_ref, o_ref):
    n = w_ref.shape[1] // 3

    def body(x_ref, c_ref):
        x = x_ref[...]
        gate = jnp.dot(x, w_ref[:, :n], preferred_element_type=F32)
        up = jnp.dot(x, w_ref[:, n : 2 * n], preferred_element_type=F32)
        d_mixed = jnp.dot(c_ref[...], w_ref[:, 2 * n :], preferred_element_type=F32)
        sig = 1.0 / (1.0 + jnp.exp(-gate))
        silu = gate * sig
        o_ref[:, :n] = (d_mixed * up * (sig * (1.0 + gate * (1.0 - sig)))).astype(BF16)
        o_ref[:, n : 2 * n] = (d_mixed * silu).astype(BF16)
        o_ref[:, 2 * n :] = (silu * up).astype(BF16)

    either(halves, body, (xl_ref, cl_ref), (xh_ref, ch_ref))


def ffn_chunk(x, cot, w):
    half_rows, depth = x[0].shape
    rows = 2 * half_rows
    width = w.shape[1]
    step = min(512, half_rows)
    halves = half_rows // step
    return pl.pallas_call(
        functools.partial(ffn_kernel, halves),
        out_shape=jax.ShapeDtypeStruct((rows, width), BF16),
        grid=(rows // step,),
        in_specs=two_halves(step, depth, halves)
        + two_halves(step, depth, halves)
        + [pl.BlockSpec((depth, width), lambda i: (0, 0))],
        out_specs=pl.BlockSpec((step, width), lambda i: (i, 0)),
        compiler_params=params(),
        cost_estimate=cost(),
        name="ffn",
    )(*x, *cot, w)


DOWN = (((0,), (0,)), ((), ()))


def grads_kernel(split, xl_ref, xh_ref, yl_ref, yh_ref, a_ref, b_ref, o_ref):
    half_rows = xl_ref.shape[0]

    def both(low_ref, high_ref, right_ref, columns):
        low = right_ref[:half_rows, columns].astype(BF16)
        high = right_ref[half_rows:, columns].astype(BF16)
        total = lax.dot_general(low_ref[...], low, DOWN, preferred_element_type=F32)
        return total + lax.dot_general(high_ref[...], high, DOWN, preferred_element_type=F32)

    o_ref[:, :split] = both(xl_ref, xh_ref, a_ref, slice(None)).astype(BF16)
    o_ref[:, split:] = both(yl_ref, yh_ref, b_ref, slice(None)).astype(BF16)


def weight_grads(x, a, a_width, a_column, y, b, b_width, b_column):
    half_rows, depth = x[0].shape
    rows = 2 * half_rows
    width = a_width + b_width
    step = 512
    tall = pl.BlockSpec((half_rows, step), lambda i: (0, i))
    return pl.pallas_call(
        functools.partial(grads_kernel, a_width),
        out_shape=jax.ShapeDtypeStruct((depth, width), BF16),
        grid=(depth // step,),
        in_specs=[tall] * 4
        + [
            pl.BlockSpec((rows, a_width), lambda i: (0, a_column)),
            pl.BlockSpec((rows, b_width), lambda i: (0, b_column)),
        ],
        out_specs=pl.BlockSpec((step, width), lambda i: (i, 0)),
        compiler_params=params(),
        cost_estimate=cost(),
        name="weight_grads",
    )(*x, *y, a, b)


def back_kernel(*refs):
    o_ref = refs[-1]
    count = (len(refs) - 1) // 2
    total = None
    for part in range(count):
        term = lax.dot_general(
            refs[part][...].astype(BF16),
            refs[count + part][...],
            (((1,), (1,)), ((), ())),
            preferred_element_type=F32,
        )
        total = term if total is None else total + term
    o_ref[...] = total.astype(BF16)


def back_product(terms, part, parts):
    rows = terms[0][0].shape[0] // parts
    depth = terms[0][2].shape[0]
    step = min(512, rows)
    ahead = part * (rows // step)
    return pl.pallas_call(
        back_kernel,
        out_shape=jax.ShapeDtypeStruct((rows, depth), BF16),
        grid=(rows // step,),
        in_specs=[
            pl.BlockSpec((step, term[4]), lambda i, column=term[1]: (i + ahead, column))
            for term in terms
        ]
        + [pl.BlockSpec((depth, term[4]), lambda i, column=term[3]: (0, column)) for term in terms],
        out_specs=pl.BlockSpec((step, depth), lambda i: (i, 0)),
        compiler_params=params(),
        cost_estimate=cost(),
        name="back",
    )(*[term[0] for term in terms], *[term[2] for term in terms])


def front_kernel(halves, low_ref, high_ref, w_ref, o_ref):
    def body(x_ref):
        o_ref[...] = jnp.dot(x_ref[...], w_ref[...], preferred_element_type=F32).astype(BF16)

    either(halves, body, (low_ref,), (high_ref,))


def front_product(x, w, width, column):
    half_rows, depth = x[0].shape
    rows = 2 * half_rows
    step = min(512, half_rows)
    halves = half_rows // step
    return pl.pallas_call(
        functools.partial(front_kernel, halves),
        out_shape=jax.ShapeDtypeStruct((rows, width), BF16),
        grid=(rows // step,),
        in_specs=two_halves(step, depth, halves)
        + [pl.BlockSpec((depth, width), lambda i: (0, column))],
        out_specs=pl.BlockSpec((step, width), lambda i: (i, 0)),
        compiler_params=params(),
        cost_estimate=cost(),
        name="front",
    )(*x, w)


def stack_heads(block):
    count = block.shape[1] // HEAD_DIM
    return jnp.concatenate(
        [block[:, h * HEAD_DIM : (h + 1) * HEAD_DIM] for h in range(count)], axis=0
    )


def unstack_heads(stacked):
    count = stacked.shape[0] // BLOCK
    return jnp.concatenate([stacked[h * BLOCK : (h + 1) * BLOCK] for h in range(count)], axis=1)


def allowed_of(i, j, start):
    row = i * BLOCK + lax.broadcasted_iota(jnp.int32, (BLOCK, BLOCK), 0)
    col = j * BLOCK + lax.broadcasted_iota(jnp.int32, (BLOCK, BLOCK), 1)
    return (col <= row) & (col >= start)


def attend_kernel(place, first, q_ref, kv_ref, start_ref, o_ref):
    i = pl.program_id(0)
    q = stack_heads(q_ref[...])
    heads = q.shape[0] // BLOCK
    start = start_ref[...]

    def step(j, carry):
        top, total, acc = carry
        at = pl.multiple_of(place[j] * BLOCK, BLOCK)
        kv = kv_ref[pl.ds(at, BLOCK), :]
        raw = lax.dot_general(
            q, kv[:, :HEAD_DIM], (((1,), (1,)), ((), ())), preferred_element_type=F32
        ) * (HEAD_DIM**-0.5 * LOG2_E)
        allowed = allowed_of(i, j, start)
        scores = jnp.where(allowed[None], raw.reshape(heads, BLOCK, BLOCK), MASKED).reshape(
            heads * BLOCK, BLOCK
        )
        new_top = jnp.maximum(top, jnp.max(scores, axis=-1, keepdims=True))
        keep = jnp.exp2(top - new_top)
        probs = jnp.exp2(scores - new_top)
        total = total * keep + jnp.sum(probs, axis=-1, keepdims=True)
        acc = acc * keep + jnp.dot(probs.astype(BF16), kv, preferred_element_type=F32)
        return (new_top, total, acc)

    size = heads * BLOCK
    top, total, acc = lax.fori_loop(
        first[i],
        i + 1,
        step,
        (
            jnp.full((size, 1), MASKED, F32),
            jnp.zeros((size, 1), F32),
            jnp.zeros((size, 2 * HEAD_DIM), F32),
        ),
    )
    out = acc[:, HEAD_DIM:] / total
    q_width = q_ref.shape[1]
    o_ref[:, :q_width] = unstack_heads(out)
    lse = top + jnp.log2(total)
    lane = lax.broadcasted_iota(jnp.int32, (BLOCK, 128), 1)
    packed = jnp.zeros((BLOCK, 128), F32)
    for h in range(heads):
        packed = jnp.where(lane == h, lse[h * BLOCK : (h + 1) * BLOCK], packed)
    o_ref[:, q_width:] = packed


def attend(qkv, place, first, start, q_width):
    rows = qkv.shape[0]
    blocks = rows // BLOCK
    return pl.pallas_call(
        attend_kernel,
        out_shape=jax.ShapeDtypeStruct((rows, q_width + 128), F32),
        grid_spec=pltpu.PrefetchScalarGridSpec(
            num_scalar_prefetch=2,
            grid=(blocks,),
            in_specs=[
                pl.BlockSpec((BLOCK, q_width), lambda i, place, first: (place[i], 0)),
                pl.BlockSpec((rows, 128), lambda i, place, first: (0, q_width // 128)),
                pl.BlockSpec((BLOCK, 1), lambda i, place, first: (i, 0)),
            ],
            out_specs=pl.BlockSpec((BLOCK, q_width + 128), lambda i, place, first: (place[i], 0)),
        ),
        compiler_params=params(),
        cost_estimate=cost(),
        name="attend",
    )(place, first, qkv, qkv, start)


def attend_back_kernel(
    place,
    first,
    q_ref,
    d_ref,
    h_ref,
    kv_ref,
    start_ref,
    cos_ref,
    sin_ref,
    o_ref,
    dkv_ref,
):
    i = pl.program_id(0)
    blocks = pl.num_programs(0)
    score_scale = HEAD_DIM**-0.5
    q_width = q_ref.shape[1]

    @pl.when(i == 0)
    def _():
        dkv_ref[...] = jnp.zeros_like(dkv_ref)

    q = stack_heads(q_ref[...])
    d_out = stack_heads(d_ref[...])
    heads = q.shape[0] // BLOCK
    out = stack_heads(h_ref[:, :q_width])
    delta = jnp.sum(d_out.astype(F32) * out, axis=-1, keepdims=True)
    lse_block = h_ref[:, q_width:]
    lse = jnp.concatenate([lse_block[:, h : h + 1] for h in range(heads)], axis=0)
    start = start_ref[...]

    def step(j, d_q):
        at = pl.multiple_of(place[j] * BLOCK, BLOCK)
        kv = kv_ref[pl.ds(at, BLOCK), :]
        k, v = kv[:, :HEAD_DIM], kv[:, HEAD_DIM:]
        across = (((1,), (1,)), ((), ()))
        down = (((0,), (0,)), ((), ()))
        raw = lax.dot_general(q, k, across, preferred_element_type=F32) * (score_scale * LOG2_E)
        allowed = allowed_of(i, j, start)
        scores = jnp.where(allowed[None], raw.reshape(heads, BLOCK, BLOCK), MASKED).reshape(
            heads * BLOCK, BLOCK
        )
        probs = jnp.exp2(scores - lse)
        d_probs = lax.dot_general(d_out, v, across, preferred_element_type=F32)
        d_scores = (probs * (d_probs - delta)).astype(BF16)
        d_k = lax.dot_general(d_scores, q, down, preferred_element_type=F32) * score_scale
        d_v = lax.dot_general(probs.astype(BF16), d_out, down, preferred_element_type=F32)
        here = pl.ds(pl.multiple_of(j * BLOCK, BLOCK), BLOCK)
        dkv_ref[here, :] += jnp.concatenate([d_k, d_v], axis=1)
        return d_q + jnp.dot(d_scores, k, preferred_element_type=F32)

    d_q = lax.fori_loop(first[i], i + 1, step, jnp.zeros((heads * BLOCK, HEAD_DIM), F32))
    d_q = unstack_heads(d_q * score_scale)
    lane = lax.broadcasted_iota(jnp.int32, (BLOCK, 128), 1)
    front = (lane % 64) < 32
    mine = pl.ds(pl.multiple_of(place[i] * BLOCK, BLOCK), BLOCK)
    cos, sin = cos_ref[mine, :], sin_ref[mine, :]
    for tile in range(q_width // 128):
        u = d_q[:, tile * 128 : (tile + 1) * 128]
        o_ref[mine, tile * 128 : (tile + 1) * 128] = (u * cos - turn_lanes(u, front) * sin).astype(
            BF16
        )

    @pl.when(i == blocks - 1)
    def _():
        for b in range(dkv_ref.shape[0] // BLOCK):
            there = pl.ds(pl.multiple_of(place[b] * BLOCK, BLOCK), BLOCK)
            u = dkv_ref[b * BLOCK : (b + 1) * BLOCK, :]
            turned = u * cos_ref[there, :] - turn_lanes(u, front) * sin_ref[there, :]
            o_ref[there, q_width:] = jnp.where(lane < HEAD_DIM, turned, u).astype(BF16)


def attend_back(qkv, d_heads, heads, place, first, start, cos, sin):
    rows, width = qkv.shape
    q_width = d_heads.shape[1]
    blocks = rows // BLOCK
    by_place = lambda i, place, first: (place[i], 0)
    whole = lambda i, place, first: (0, 0)
    return pl.pallas_call(
        attend_back_kernel,
        out_shape=jax.ShapeDtypeStruct((rows, width), BF16),
        grid_spec=pltpu.PrefetchScalarGridSpec(
            num_scalar_prefetch=2,
            grid=(blocks,),
            in_specs=[
                pl.BlockSpec((BLOCK, q_width), by_place),
                pl.BlockSpec((BLOCK, q_width), by_place),
                pl.BlockSpec((BLOCK, q_width + 128), by_place),
                pl.BlockSpec((rows, 128), lambda i, place, first: (0, q_width // 128)),
                pl.BlockSpec((BLOCK, 1), lambda i, place, first: (i, 0)),
                pl.BlockSpec((rows, 128), whole),
                pl.BlockSpec((rows, 128), whole),
            ],
            out_specs=pl.BlockSpec((rows, width), whole),
            scratch_shapes=[pltpu.VMEM((rows, 128), F32)],
        ),
        compiler_params=params(),
        cost_estimate=cost(),
        name="attend_back",
    )(place, first, qkv, d_heads, heads, qkv, start, cos, sin)


def sum_cores(terms, pieces=2, *held):
    sent = [back_product(terms, 2 * pieces - 1 - at, 2 * pieces) for at in range(pieces)]
    arrived = [swap_core(after(piece, *held)) for piece in sent]
    mine = back_product(terms, 0, 2)
    rows = mine.shape[0] // 2
    if pieces == 1:
        return mine[rows:] + arrived[0][rows:], mine[:rows] + arrived[0][:rows]
    return mine[rows:] + arrived[0], mine[:rows] + arrived[1]


def y_first(far, near, core):
    rows = near.shape[0] // 2
    first, second = near[rows:], far[:rows]
    return (
        jnp.concatenate([jnp.where(core == 0, second, first), far[rows:]]),
        jnp.concatenate([near[:rows], jnp.where(core == 0, first, second)]),
    )


def sum_pairs(far, near, *behind):
    return near + after(swap_second(far), *behind)


def sum_last(near, *beside):
    rows = near.shape[0] // 2
    near = after(near, *beside)
    return near[:rows].astype(F32) + swap_first(near[rows:]).astype(F32)


def share_rows(own, beside=()):
    beside = list(beside) + [()] * (2 - len(beside))
    one = after(swap_first(own), *beside[0])
    parts = (own, one, swap_second(own), after(swap_second(one), *beside[1]))
    return jnp.concatenate(parts), jnp.concatenate([swap_core(part) for part in parts])


def ring_over(shard, count):
    cycle = [(at, (at + 1) % count) for at in range(count)]
    pieces = [shard]
    for _ in range(count - 1):
        pieces.append(lax.ppermute(pieces[-1], "fsdp", cycle))
    return pieces


def in_place(pieces, axis):
    count, size = len(pieces), pieces[0].shape[axis]
    here = lax.axis_index("fsdp")
    shape = list(pieces[0].shape)
    shape[axis] *= count
    whole = jnp.zeros(shape, pieces[0].dtype)
    for back, piece in enumerate(pieces):
        owner = lax.rem(here + count - back, count)
        whole = lax.dynamic_update_slice_in_dim(whole, piece, owner * size, axis)
    return whole


def shifts_over(shard, count):
    return [shard] + [
        lax.ppermute(shard, "fsdp", [(at, (at + by) % count) for at in range(count)])
        for by in range(1, count)
    ]


def share_in_ctx(own, beside, y, core):
    pair = jnp.stack([own, beside])
    other = jnp.stack([swap_core(own), swap_core(beside)])
    four = jnp.stack([pair, other])
    four = jnp.where(y == 1, four[:, ::-1], four)
    four = jnp.where(core == 1, four[::-1], four)
    return four.transpose(1, 0, 2, 3).reshape(-1, own.shape[1])


def sum_all(v):
    v = v + swap_core(v)
    v = v + swap_y(v)
    return v + swap_x(v)


def both_halves(own, other, ctx):
    low = jnp.where(ctx == 0, own, other).astype(F32)
    high = jnp.where(ctx == 0, other, own).astype(F32)
    return low, high


def shards(
    tokens,
    q_weight,
    k_weight,
    v_weight,
    o_weight,
    attn_gain,
    gate_weight,
    up_weight,
    down_weight,
    ffn_gain,
    lengths,
    deal,
    cotangent,
):
    ctx = lax.axis_index("ctx")
    tp = lax.axis_index("tp")
    y, core = tp // 2, tp % 2
    row_count, depth = tokens.shape
    group_rows = row_count * lax.axis_size("ctx")
    own_rows = row_count // lax.axis_size("tp")

    def half(weight):
        width = weight.shape[1] // 2
        return lax.dynamic_slice_in_dim(weight, ctx * width, width, 1)

    q_half, k_half, v_half, o_half = map(half, (q_weight, k_weight, v_weight, o_weight))
    q_width, kv_width = q_half.shape[1], k_half.shape[1]
    attn_shard = jnp.concatenate([o_half, q_half, k_half, v_half], axis=1)
    fsdp = lax.axis_size("fsdp")
    attn_ring = ring_over(attn_shard, fsdp)
    attn_full = in_place(attn_ring, 0)
    gains = in_place(shifts_over(jnp.stack([attn_gain, ffn_gain]), fsdp), 1)
    gain_one = gains[0].astype(F32)[None]
    gain_two = gains[1].astype(F32)[None]
    ff_half = gate_weight.shape[1] // 2
    chunk = ff_half // CHUNKS
    ffn_shards = []
    for part in range(CHUNKS):
        at = ctx * ff_half + part * chunk
        ffn_shards.append(
            jnp.concatenate(
                [
                    lax.dynamic_slice_in_dim(weight, at, chunk, 1)
                    for weight in (gate_weight, up_weight, down_weight)
                ],
                axis=1,
            )
        )
    length_row, deal_row = lengths[0], deal[0]
    spans = deal_row.shape[0]
    span_rows = group_rows // spans
    ends = jnp.cumsum(length_row, dtype=jnp.int32)
    starts = ends - length_row
    natural = jnp.arange(group_rows, dtype=jnp.int32)
    inside = (natural[:, None] >= starts[None]) & (natural[:, None] < ends[None])
    start_of = jnp.sum(jnp.where(inside, starts[None], 0), axis=1, dtype=jnp.int32)
    first = start_of[::BLOCK] // BLOCK
    rel = jnp.arange(group_rows // own_rows, dtype=jnp.int32)
    rel_core = core ^ (rel // 4)
    by_first, by_second = rel % 2, (rel // 2) % 2
    rel_ctx = ctx ^ jnp.where(rel_core == 0, by_first, by_second)
    rel_y = y ^ jnp.where(rel_core == 0, by_second, by_first)
    dealt_block = rel_ctx * (row_count // own_rows) + rel_y * 2 + rel_core
    per_span = span_rows // own_rows
    span_of = jnp.sum(
        jnp.where(
            (dealt_block // per_span)[:, None] == jnp.arange(spans, dtype=jnp.int32)[None],
            deal_row[None],
            0,
        ),
        axis=1,
        dtype=jnp.int32,
    )
    natural_block = span_of * per_span + dealt_block % per_span
    place = jnp.sum(
        jnp.where(natural_block[None, :] == rel[:, None], rel[None, :], 0), axis=1, dtype=jnp.int32
    )
    natural_rel = (
        natural_block[:, None] * own_rows + jnp.arange(own_rows, dtype=jnp.int32)[None]
    ).reshape(-1)
    inside_rel = (natural_rel[:, None] >= starts[None]) & (natural_rel[:, None] < ends[None])
    position = natural_rel - jnp.sum(
        jnp.where(inside_rel, starts[None], 0), axis=1, dtype=jnp.int32
    )
    lane = jnp.arange(128, dtype=jnp.int32)
    inverse = jnp.exp((lane % 32).astype(F32) * (-2.0 * math.log(ROPE_BASE) / HEAD_DIM))
    angles = position.astype(F32)[:, None] * inverse[None]
    cos = jnp.cos(angles)
    sin = jnp.where((lane % 64 < 32)[None], -jnp.sin(angles), jnp.sin(angles))
    start_column = start_of[:, None]

    tokens_low = lax.dynamic_slice_in_dim(tokens, tp * own_rows, own_rows, 0)
    cot_low = lax.dynamic_slice_in_dim(cotangent, tp * own_rows, own_rows, 0)
    tokens_own, cot_own = tokens_low.astype(F32), cot_low.astype(F32)
    group_tokens = share_rows(tokens_low, [[piece] for piece in attn_ring[1:3]])
    attn_full, first_shard, cot_low, cos, sin, gain_one, *group_tokens = lax.optimization_barrier(
        (attn_full, ffn_shards[0], cot_low, cos, sin, gain_one, *group_tokens)
    )
    qkv = project_qkv(group_tokens, gain_one, attn_full, q_width, cos, sin)
    heads = attend(qkv, place, first, start_column, q_width)
    cot = share_rows(cot_low, [[qkv], [heads]])
    ffn_full = [
        lax.all_gather(shard, "fsdp", axis=0, tiled=True)
        for shard in (first_shard, after(ffn_shards[1], heads))
    ]
    heads = after(heads, *cot)
    attn_sum = sum_last(
        sum_pairs(*sum_cores([(heads, 0, attn_full, 0, q_width)])), ffn_full[0]
    )
    hidden = tokens_own + attn_sum
    normed_two = share_rows((hidden * inv_rms(hidden) * gain_two).astype(BF16))

    acts = []
    grad_parts = []
    for part in range(CHUNKS):
        acts.append(ffn_chunk(after(normed_two, *grad_parts), cot, ffn_full[part]))
        grad_parts.append(
            weight_grads(normed_two, acts[part], 2 * chunk, 0, cot, acts[part], chunk, 2)
        )
    reduced = [
        lax.psum_scatter(part, "fsdp", scatter_dimension=0, tiled=True) for part in grad_parts
    ]
    d_norm_terms = [(acts[part], 0, ffn_full[part], 0, 2 * chunk) for part in range(CHUNKS)]
    ffn_terms = [(acts[part], 2, ffn_full[part], 2, chunk) for part in range(CHUNKS)]
    d_normed_two = sum_last(sum_pairs(*sum_cores(d_norm_terms, 1)), *grad_parts)
    d_hidden = cot_own + rms_back(hidden, gain_two, d_normed_two)
    ffn_sent = [back_product(ffn_terms, at, 4) for at in (3, 2)]
    ffn_mine = back_product(ffn_terms, 0, 2)
    d_attn = share_rows(d_hidden.astype(BF16), [[reduced[0]], [*ffn_sent, ffn_mine]])

    d_heads = front_product(d_attn, attn_full, q_width, 0)
    arrived = [swap_core(after(piece, d_attn[1])) for piece in ffn_sent]
    half_rows = ffn_mine.shape[0] // 2
    ffn_far, ffn_near = y_first(
        ffn_mine[half_rows:] + arrived[0], ffn_mine[:half_rows] + arrived[1], core
    )
    d_heads, ffn_far, reduced[0] = lax.optimization_barrier((d_heads, ffn_far, reduced[0]))
    other_reduced = [swap_x(reduced[0])]
    d_qkv = attend_back(qkv, d_heads, heads, place, first, start_column, cos, sin)
    ffn_near = ffn_near + after(swap_y(ffn_far), d_qkv)
    d_qkv = after(d_qkv, ffn_near, other_reduced[0])
    normed = []
    for part in group_tokens:
        wide = part.astype(F32)
        normed.append((wide * inv_rms(wide) * gain_one).astype(BF16))
    normed_far, normed_near = sum_cores(
        [
            (d_qkv, 0, attn_full, 1, q_width),
            (d_qkv, q_width // 128, attn_full, 2 * q_width // 128, 128),
        ]
    )
    attn_grad = weight_grads(
        d_attn, heads, q_width, 0, normed, d_qkv, q_width + 128, 0
    )
    for part in range(1, CHUNKS):
        reduced[part] = after(reduced[part], attn_grad)
    d_normed = sum_last(sum_pairs(normed_far, normed_near), attn_grad, *reduced[1:])
    for part in range(1, CHUNKS):
        reduced[part] = after(reduced[part], d_normed)
        other_reduced.append(swap_x(reduced[part]))
    ffn_near = after(ffn_near, normed_far)
    ffn_sum = ffn_near[:own_rows].astype(F32) + swap_x(ffn_near[own_rows:]).astype(F32)
    result_own = (hidden + ffn_sum).astype(BF16)
    result = share_in_ctx(result_own, swap_y(result_own), y, core)
    tokens_grad_own = (d_hidden + rms_back(tokens_own, gain_one, d_normed)).astype(BF16)
    tokens_grad_beside = swap_y(tokens_grad_own)
    tokens_grad = share_in_ctx(tokens_grad_own, tokens_grad_beside, y, core)

    attn_reduced = lax.psum_scatter(attn_grad, "fsdp", scatter_dimension=0, tiled=True)
    attn_reduced = after(attn_reduced, tokens_grad_beside)

    def gain_part(pairs):
        return sum(jnp.sum(mine.astype(F32) * grad.astype(F32), axis=1) for mine, grad in pairs)

    gain_sums = sum_all(
        jnp.stack(
            [
                gain_part([(attn_shard[:, q_width:], attn_reduced[:, q_width:])]),
                gain_part(
                    [
                        (ffn_shards[part][:, : 2 * chunk], reduced[part][:, : 2 * chunk])
                        for part in range(CHUNKS)
                    ]
                ),
            ]
        )
    )
    attn_gain_grad = gain_sums[0] / attn_gain.astype(F32)
    ffn_gain_grad = gain_sums[1] / ffn_gain.astype(F32)

    halves = [both_halves(mine, other, ctx) for mine, other in zip(reduced, other_reduced)]

    def ffn_out(which):
        return jnp.concatenate(
            [
                halves[part][side][:, which * chunk : (which + 1) * chunk]
                for side in range(2)
                for part in range(CHUNKS)
            ],
            axis=1,
        )

    attn_low, attn_high = both_halves(attn_reduced, swap_x(attn_reduced), ctx)

    def attn_out(begin, end):
        return jnp.concatenate([attn_low[:, begin:end], attn_high[:, begin:end]], axis=1)

    q_end, k_end = 2 * q_width, 2 * q_width + kv_width
    return (
        result,
        tokens_grad,
        attn_out(q_width, q_end),
        attn_out(q_end, k_end),
        attn_out(k_end, k_end + kv_width),
        attn_out(0, q_width),
        attn_gain_grad,
        ffn_out(0),
        ffn_out(1),
        ffn_out(2),
        ffn_gain_grad,
    )


def solution(mesh):
    rows = P(("fsdp", "ctx"), None)
    matrix = P("fsdp", "tp")
    vector = P("fsdp")
    return jax.shard_map(
        shards,
        mesh=mesh,
        in_specs=(
            rows,
            matrix,
            matrix,
            matrix,
            matrix,
            vector,
            matrix,
            matrix,
            matrix,
            vector,
            P("fsdp", None),
            P("fsdp", None),
            rows,
        ),
        out_specs=(
            rows,
            rows,
            matrix,
            matrix,
            matrix,
            matrix,
            vector,
            matrix,
            matrix,
            matrix,
            vector,
        ),
        check_vma=False,
    )
```

```python
import functools
import math

import jax
import jax.numpy as jnp
from jax import lax
from jax.experimental import pallas as pl
from jax.experimental.pallas import tpu as pltpu
from jax.sharding import PartitionSpec as P

HEAD_DIM = 64
EPSILON = 1e-05
ROPE_BASE = 500000.0
MASKED = -1e30
LOG2_E = 1.4426950408889634
BLOCK = 256
CHUNKS = 2
VMEM = 56 * 2**20

F32 = jnp.float32
BF16 = jnp.bfloat16

PAIR = [(0, 1), (1, 0)]
CORE = [(0, 1), (1, 0), (2, 3), (3, 2)]
ACROSS = [(0, 2), (2, 0), (1, 3), (3, 1)]


def joint_pairs(x_core):
    pairs = []
    for ctx in range(2):
        for tp in range(4):
            there = (1 - ctx) * 4 + tp if tp % 2 == x_core else ctx * 4 + (tp ^ 2)
            pairs.append((ctx * 4 + tp, there))
    return pairs


FIRST = joint_pairs(0)
SECOND = joint_pairs(1)


def swap_core(v):
    return lax.ppermute(v, "tp", CORE)


def swap_y(v):
    return lax.ppermute(v, "tp", ACROSS)


def swap_x(v):
    return lax.ppermute(v, "ctx", PAIR)


def swap_first(v):
    return lax.ppermute(v, ("ctx", "tp"), FIRST)


def swap_second(v):
    return lax.ppermute(v, ("ctx", "tp"), SECOND)


def after(value, *others):
    return lax.optimization_barrier((value,) + others)[0]


def params(*semantics):
    return pltpu.CompilerParams(vmem_limit_bytes=VMEM)


def cost(gigaflops=0):
    return pl.CostEstimate(flops=int(gigaflops * 1e9) + 1, bytes_accessed=1, transcendentals=0)


def inv_rms(hidden):
    return lax.rsqrt(jnp.mean(hidden * hidden, axis=-1, keepdims=True) + EPSILON)


def rms_back(hidden, gain, grad):
    scale = inv_rms(hidden)
    weighted = grad * gain
    inner = jnp.mean(weighted * hidden, axis=-1, keepdims=True)
    return scale * weighted - hidden * (scale * scale * scale) * inner


def turn_lanes(u, first):
    return jnp.where(first, pltpu.roll(u, 96, 1), pltpu.roll(u, 32, 1))


def stream_scratch(count, rows, depth):
    return [pltpu.VMEM((2, rows, depth), BF16), pltpu.SemaphoreType.DMA((2,))] * count


def next_piece(refs, buffer, sems):
    i = pl.program_id(0)

    def copy_of(piece):
        return pltpu.make_async_copy(refs[piece], buffer.at[piece % 2], sems.at[piece % 2])

    @pl.when(i == 0)
    def _():
        copy_of(0).start()

    for piece in range(1, len(refs)):

        @pl.when(i == piece - 1)
        def _(piece=piece):
            copy_of(piece).start()

    for piece in range(len(refs)):

        @pl.when(i == piece)
        def _(piece=piece):
            copy_of(piece).wait()

    return buffer[lax.rem(i, 2)]


def qkv_kernel(count, *refs):
    gain_ref, wq_ref, wkv_ref, cos_ref, sin_ref, o_ref, buffer, sems = refs[count:]
    cos, sin = cos_ref[...], sin_ref[...]
    depth = gain_ref.shape[1]
    lane = lax.broadcasted_iota(jnp.int32, cos.shape, 1)
    first = (lane % 64) < 32
    x = next_piece(refs[:count], buffer, sems).astype(F32)
    x = (x * inv_rms(x) * gain_ref[...]).astype(BF16)
    o_ref[:, :depth] = x
    raw = jnp.dot(x, wq_ref[...], preferred_element_type=F32)
    tiles = raw.shape[1] // 128
    for tile in range(tiles):
        u = raw[:, tile * 128 : (tile + 1) * 128]
        turned = u * cos + turn_lanes(u, first) * sin
        o_ref[:, depth + tile * 128 : depth + (tile + 1) * 128] = turned.astype(BF16)
    u = jnp.dot(x, wkv_ref[...], preferred_element_type=F32)
    turned = u * cos + turn_lanes(u, first) * sin
    o_ref[:, depth + tiles * 128 :] = jnp.where(lane < 64, turned, u).astype(BF16)


def project_qkv(x, gain, w, q_width, cos, sin):
    step, depth = x[0].shape
    rows = len(x) * step
    width = depth + q_width + 128
    return pl.pallas_call(
        functools.partial(qkv_kernel, len(x)),
        out_shape=jax.ShapeDtypeStruct((rows, width), BF16),
        grid=(len(x),),
        in_specs=[pl.BlockSpec(memory_space=pl.ANY)] * len(x)
        + [
            pl.BlockSpec((1, depth), lambda i: (0, 0)),
            pl.BlockSpec((depth, q_width), lambda i: (0, 1)),
            pl.BlockSpec((depth, 128), lambda i: (0, 2 * q_width // 128)),
            pl.BlockSpec((step, 128), lambda i: (i, 0)),
            pl.BlockSpec((step, 128), lambda i: (i, 0)),
        ],
        out_specs=pl.BlockSpec((step, width), lambda i: (i, 0)),
        scratch_shapes=stream_scratch(1, step, depth),
        compiler_params=params(),
        cost_estimate=cost(),
        name="qkv",
    )(*x, gain, w, w, cos, sin)


def ffn_kernel(count, *refs):
    w_ref, o_ref, x_buffer, x_sems, c_buffer, c_sems = refs[2 * count :]
    n = w_ref.shape[1] // 3
    x = next_piece(refs[:count], x_buffer, x_sems)
    c = next_piece(refs[count : 2 * count], c_buffer, c_sems)
    gate = jnp.dot(x, w_ref[:, :n], preferred_element_type=F32)
    up = jnp.dot(x, w_ref[:, n : 2 * n], preferred_element_type=F32)
    d_mixed = jnp.dot(c, w_ref[:, 2 * n :], preferred_element_type=F32)
    sig = 1.0 / (1.0 + jnp.exp(-gate))
    silu = gate * sig
    o_ref[:, :n] = (d_mixed * up * (sig * (1.0 + gate * (1.0 - sig)))).astype(BF16)
    o_ref[:, n : 2 * n] = (d_mixed * silu).astype(BF16)
    o_ref[:, 2 * n :] = (silu * up).astype(BF16)


def ffn_chunk(x, cot, w):
    step, depth = x[0].shape
    rows = len(x) * step
    width = w.shape[1]
    return pl.pallas_call(
        functools.partial(ffn_kernel, len(x)),
        out_shape=jax.ShapeDtypeStruct((rows, width), BF16),
        grid=(len(x),),
        in_specs=[pl.BlockSpec(memory_space=pl.ANY)] * (2 * len(x))
        + [pl.BlockSpec((depth, width), lambda i: (0, 0))],
        out_specs=pl.BlockSpec((step, width), lambda i: (i, 0)),
        scratch_shapes=stream_scratch(2, step, depth),
        compiler_params=params(),
        cost_estimate=cost(),
        name="ffn",
    )(*x, *cot, w)


DOWN = (((0,), (0,)), ((), ()))


def grads_kernel(x_count, y_count, *refs):
    a_ref, b_ref, o_ref = refs[x_count + y_count :]
    split = a_ref.shape[1]

    def product(tall_refs, right_ref):
        tall = jnp.concatenate([ref[...] for ref in tall_refs], axis=0)
        return lax.dot_general(
            tall, right_ref[...].astype(BF16), DOWN, preferred_element_type=F32
        ).astype(BF16)

    o_ref[:, :split] = product(refs[:x_count], a_ref)
    o_ref[:, split:] = product(refs[x_count : x_count + y_count], b_ref)


def weight_grads(x, a, a_width, a_column, y, b, b_width, b_column):
    depth = x[0].shape[1]
    rows = a.shape[0]
    width = a_width + b_width
    step = 512
    return pl.pallas_call(
        functools.partial(grads_kernel, len(x), len(y)),
        out_shape=jax.ShapeDtypeStruct((depth, width), BF16),
        grid=(depth // step,),
        in_specs=[pl.BlockSpec((piece.shape[0], step), lambda i: (0, i)) for piece in (*x, *y)]
        + [
            pl.BlockSpec((rows, a_width), lambda i: (0, a_column)),
            pl.BlockSpec((rows, b_width), lambda i: (0, b_column)),
        ],
        out_specs=pl.BlockSpec((step, width), lambda i: (i, 0)),
        compiler_params=params(),
        cost_estimate=cost(),
        name="weight_grads",
    )(*x, *y, a, b)


def back_kernel(*refs):
    o_ref = refs[-1]
    count = (len(refs) - 1) // 2
    total = None
    for part in range(count):
        term = lax.dot_general(
            refs[part][...].astype(BF16),
            refs[count + part][...],
            (((1,), (1,)), ((), ())),
            preferred_element_type=F32,
        )
        total = term if total is None else total + term
    o_ref[...] = total.astype(BF16)


def back_product(terms, part, parts):
    rows = terms[0][0].shape[0] // parts
    depth = terms[0][2].shape[0]
    step = min(512, rows)
    ahead = part * (rows // step)
    return pl.pallas_call(
        back_kernel,
        out_shape=jax.ShapeDtypeStruct((rows, depth), BF16),
        grid=(rows // step,),
        in_specs=[
            pl.BlockSpec((step, term[4]), lambda i, column=term[1]: (i + ahead, column))
            for term in terms
        ]
        + [pl.BlockSpec((depth, term[4]), lambda i, column=term[3]: (0, column)) for term in terms],
        out_specs=pl.BlockSpec((step, depth), lambda i: (i, 0)),
        compiler_params=params(),
        cost_estimate=cost(),
        name="back",
    )(*[term[0] for term in terms], *[term[2] for term in terms])


def front_kernel(count, *refs):
    w_ref, o_ref, buffer, sems = refs[count:]
    x = next_piece(refs[:count], buffer, sems)
    o_ref[...] = jnp.dot(x, w_ref[...], preferred_element_type=F32).astype(BF16)


def front_product(x, w, width, column):
    step, depth = x[0].shape
    rows = len(x) * step
    return pl.pallas_call(
        functools.partial(front_kernel, len(x)),
        out_shape=jax.ShapeDtypeStruct((rows, width), BF16),
        grid=(len(x),),
        in_specs=[pl.BlockSpec(memory_space=pl.ANY)] * len(x)
        + [pl.BlockSpec((depth, width), lambda i: (0, column))],
        out_specs=pl.BlockSpec((step, width), lambda i: (i, 0)),
        scratch_shapes=stream_scratch(1, step, depth),
        compiler_params=params(),
        cost_estimate=cost(),
        name="front",
    )(*x, w)


def stack_heads(block):
    count = block.shape[1] // HEAD_DIM
    return jnp.concatenate(
        [block[:, h * HEAD_DIM : (h + 1) * HEAD_DIM] for h in range(count)], axis=0
    )


def unstack_heads(stacked):
    count = stacked.shape[0] // BLOCK
    return jnp.concatenate([stacked[h * BLOCK : (h + 1) * BLOCK] for h in range(count)], axis=1)


def allowed_of(i, j, start):
    row = i * BLOCK + lax.broadcasted_iota(jnp.int32, (BLOCK, BLOCK), 0)
    col = j * BLOCK + lax.broadcasted_iota(jnp.int32, (BLOCK, BLOCK), 1)
    return (col <= row) & (col >= start)


def attend_kernel(place, first, q_ref, kv_ref, start_ref, o_ref):
    i = pl.program_id(0)
    q = stack_heads(q_ref[...])
    heads = q.shape[0] // BLOCK
    start = start_ref[...]

    def step(j, carry):
        top, total, acc = carry
        at = pl.multiple_of(place[j] * BLOCK, BLOCK)
        kv = kv_ref[pl.ds(at, BLOCK), :]
        raw = lax.dot_general(
            q, kv[:, :HEAD_DIM], (((1,), (1,)), ((), ())), preferred_element_type=F32
        ) * (HEAD_DIM**-0.5 * LOG2_E)
        allowed = allowed_of(i, j, start)
        scores = jnp.where(allowed[None], raw.reshape(heads, BLOCK, BLOCK), MASKED).reshape(
            heads * BLOCK, BLOCK
        )
        new_top = jnp.maximum(top, jnp.max(scores, axis=-1, keepdims=True))
        keep = jnp.exp2(top - new_top)
        probs = jnp.exp2(scores - new_top)
        total = total * keep + jnp.sum(probs, axis=-1, keepdims=True)
        acc = acc * keep + jnp.dot(probs.astype(BF16), kv, preferred_element_type=F32)
        return (new_top, total, acc)

    size = heads * BLOCK
    top, total, acc = lax.fori_loop(
        first[i],
        i + 1,
        step,
        (
            jnp.full((size, 1), MASKED, F32),
            jnp.zeros((size, 1), F32),
            jnp.zeros((size, 2 * HEAD_DIM), F32),
        ),
    )
    out = acc[:, HEAD_DIM:] / total
    q_width = q_ref.shape[1]
    o_ref[:, :q_width] = unstack_heads(out)
    lse = top + jnp.log2(total)
    lane = lax.broadcasted_iota(jnp.int32, (BLOCK, 128), 1)
    packed = jnp.zeros((BLOCK, 128), F32)
    for h in range(heads):
        packed = jnp.where(lane == h, lse[h * BLOCK : (h + 1) * BLOCK], packed)
    o_ref[:, q_width:] = packed


def attend(qkv, depth, place, first, start, q_width):
    rows = qkv.shape[0]
    blocks = rows // BLOCK
    return pl.pallas_call(
        attend_kernel,
        out_shape=jax.ShapeDtypeStruct((rows, q_width + 128), F32),
        grid_spec=pltpu.PrefetchScalarGridSpec(
            num_scalar_prefetch=2,
            grid=(blocks,),
            in_specs=[
                pl.BlockSpec((BLOCK, q_width), lambda i, place, first: (place[i], depth // q_width)),
                pl.BlockSpec((rows, 128), lambda i, place, first: (0, (depth + q_width) // 128)),
                pl.BlockSpec((BLOCK, 1), lambda i, place, first: (i, 0)),
            ],
            out_specs=pl.BlockSpec((BLOCK, q_width + 128), lambda i, place, first: (place[i], 0)),
        ),
        compiler_params=params(),
        cost_estimate=cost(),
        name="attend",
    )(place, first, qkv, qkv, start)


def attend_back_kernel(
    place,
    first,
    q_ref,
    d_ref,
    h_ref,
    kv_ref,
    start_ref,
    cos_ref,
    sin_ref,
    o_ref,
    dkv_ref,
):
    i = pl.program_id(0)
    blocks = pl.num_programs(0)
    score_scale = HEAD_DIM**-0.5
    q_width = q_ref.shape[1]

    @pl.when(i == 0)
    def _():
        dkv_ref[...] = jnp.zeros_like(dkv_ref)

    q = stack_heads(q_ref[...])
    d_out = stack_heads(d_ref[...])
    heads = q.shape[0] // BLOCK
    out = stack_heads(h_ref[:, :q_width])
    delta = jnp.sum(d_out.astype(F32) * out, axis=-1, keepdims=True)
    lse_block = h_ref[:, q_width:]
    lse = jnp.concatenate([lse_block[:, h : h + 1] for h in range(heads)], axis=0)
    start = start_ref[...]

    def step(j, d_q):
        at = pl.multiple_of(place[j] * BLOCK, BLOCK)
        kv = kv_ref[pl.ds(at, BLOCK), :]
        k, v = kv[:, :HEAD_DIM], kv[:, HEAD_DIM:]
        across = (((1,), (1,)), ((), ()))
        down = (((0,), (0,)), ((), ()))
        raw = lax.dot_general(q, k, across, preferred_element_type=F32) * (score_scale * LOG2_E)
        allowed = allowed_of(i, j, start)
        scores = jnp.where(allowed[None], raw.reshape(heads, BLOCK, BLOCK), MASKED).reshape(
            heads * BLOCK, BLOCK
        )
        probs = jnp.exp2(scores - lse)
        d_probs = lax.dot_general(d_out, v, across, preferred_element_type=F32)
        d_scores = (probs * (d_probs - delta)).astype(BF16)
        d_k = lax.dot_general(d_scores, q, down, preferred_element_type=F32) * score_scale
        d_v = lax.dot_general(probs.astype(BF16), d_out, down, preferred_element_type=F32)
        here = pl.ds(pl.multiple_of(j * BLOCK, BLOCK), BLOCK)
        dkv_ref[here, :] += jnp.concatenate([d_k, d_v], axis=1)
        return d_q + jnp.dot(d_scores, k, preferred_element_type=F32)

    d_q = lax.fori_loop(first[i], i + 1, step, jnp.zeros((heads * BLOCK, HEAD_DIM), F32))
    d_q = unstack_heads(d_q * score_scale)
    lane = lax.broadcasted_iota(jnp.int32, (BLOCK, 128), 1)
    front = (lane % 64) < 32
    mine = pl.ds(pl.multiple_of(place[i] * BLOCK, BLOCK), BLOCK)
    cos, sin = cos_ref[mine, :], sin_ref[mine, :]
    for tile in range(q_width // 128):
        u = d_q[:, tile * 128 : (tile + 1) * 128]
        o_ref[mine, tile * 128 : (tile + 1) * 128] = (u * cos - turn_lanes(u, front) * sin).astype(
            BF16
        )

    @pl.when(i == blocks - 1)
    def _():
        for b in range(dkv_ref.shape[0] // BLOCK):
            there = pl.ds(pl.multiple_of(place[b] * BLOCK, BLOCK), BLOCK)
            u = dkv_ref[b * BLOCK : (b + 1) * BLOCK, :]
            turned = u * cos_ref[there, :] - turn_lanes(u, front) * sin_ref[there, :]
            o_ref[there, q_width:] = jnp.where(lane < HEAD_DIM, turned, u).astype(BF16)


def attend_back(qkv, depth, d_heads, heads, place, first, start, cos, sin):
    rows, q_width = d_heads.shape
    width = q_width + 128
    blocks = rows // BLOCK
    by_place = lambda i, place, first: (place[i], 0)
    whole = lambda i, place, first: (0, 0)
    return pl.pallas_call(
        attend_back_kernel,
        out_shape=jax.ShapeDtypeStruct((rows, width), BF16),
        grid_spec=pltpu.PrefetchScalarGridSpec(
            num_scalar_prefetch=2,
            grid=(blocks,),
            in_specs=[
                pl.BlockSpec((BLOCK, q_width), lambda i, place, first: (place[i], depth // q_width)),
                pl.BlockSpec((BLOCK, q_width), by_place),
                pl.BlockSpec((BLOCK, q_width + 128), by_place),
                pl.BlockSpec((rows, 128), lambda i, place, first: (0, (depth + q_width) // 128)),
                pl.BlockSpec((BLOCK, 1), lambda i, place, first: (i, 0)),
                pl.BlockSpec((rows, 128), whole),
                pl.BlockSpec((rows, 128), whole),
            ],
            out_specs=pl.BlockSpec((rows, width), whole),
            scratch_shapes=[pltpu.VMEM((rows, 128), F32)],
        ),
        compiler_params=params(),
        cost_estimate=cost(),
        name="attend_back",
    )(place, first, qkv, d_heads, heads, qkv, start, cos, sin)


def sum_cores(terms, pieces=2, *held):
    sent = [back_product(terms, 2 * pieces - 1 - at, 2 * pieces) for at in range(pieces)]
    arrived = [swap_core(after(piece, *held)) for piece in sent]
    mine = back_product(terms, 0, 2)
    rows = mine.shape[0] // 2
    if pieces == 1:
        return mine[rows:] + arrived[0][rows:], mine[:rows] + arrived[0][:rows]
    return mine[rows:] + arrived[0], mine[:rows] + arrived[1]


def y_first(far, near, core):
    rows = near.shape[0] // 2
    first, second = near[rows:], far[:rows]
    return (
        jnp.concatenate([jnp.where(core == 0, second, first), far[rows:]]),
        jnp.concatenate([near[:rows], jnp.where(core == 0, first, second)]),
    )


def sum_pairs(far, near, *behind):
    return near + after(swap_second(far), *behind)


def sum_last(near, *beside):
    rows = near.shape[0] // 2
    near = after(near, *beside)
    return near[:rows].astype(F32) + swap_first(near[rows:]).astype(F32)


def share_rows(own, beside=()):
    beside = list(beside) + [()] * (2 - len(beside))
    one, two, *_ = lax.optimization_barrier((swap_first(own), swap_second(own), *beside[0]))
    early = tuple(swap_core(part) for part in (own, one, two))
    last = after(swap_second(one), *early, *beside[1])
    return (own, one, two, last, *early, swap_core(last))


def ring_over(shard, count, held):
    cycle = [(at, (at + 1) % count) for at in range(count)]
    pieces = [shard]
    for step in range(count - 1):
        sent = after(pieces[-1], held) if step == 1 else pieces[-1]
        pieces.append(lax.ppermute(sent, "fsdp", cycle))
    return pieces


def in_place(pieces, axis):
    count, size = len(pieces), pieces[0].shape[axis]
    here = lax.axis_index("fsdp")
    shape = list(pieces[0].shape)
    shape[axis] *= count
    whole = jnp.zeros(shape, pieces[0].dtype)
    for back, piece in enumerate(pieces):
        owner = lax.rem(here + count - back, count)
        whole = lax.dynamic_update_slice_in_dim(whole, piece, owner * size, axis)
    return whole


def share_in_ctx(own, beside, y, core):
    pair = jnp.stack([own, beside])
    other = jnp.stack([swap_core(own), swap_core(beside)])
    four = jnp.stack([pair, other])
    four = jnp.where(y == 1, four[:, ::-1], four)
    four = jnp.where(core == 1, four[::-1], four)
    return four.transpose(1, 0, 2, 3).reshape(-1, own.shape[1])


def sum_all(v):
    v = v + swap_core(v)
    v = v + swap_y(v)
    return v + swap_x(v)


def both_halves(own, other, ctx):
    low = jnp.where(ctx == 0, own, other).astype(F32)
    high = jnp.where(ctx == 0, other, own).astype(F32)
    return low, high


def shards(
    tokens,
    q_weight,
    k_weight,
    v_weight,
    o_weight,
    attn_gain,
    gate_weight,
    up_weight,
    down_weight,
    ffn_gain,
    lengths,
    deal,
    cotangent,
):
    ctx = lax.axis_index("ctx")
    tp = lax.axis_index("tp")
    y, core = tp // 2, tp % 2
    row_count, depth = tokens.shape
    group_rows = row_count * lax.axis_size("ctx")
    own_rows = row_count // lax.axis_size("tp")

    def half(weight):
        width = weight.shape[1] // 2
        return lax.dynamic_slice_in_dim(weight, ctx * width, width, 1)

    q_half, k_half, v_half, o_half = map(half, (q_weight, k_weight, v_weight, o_weight))
    q_width, kv_width = q_half.shape[1], k_half.shape[1]
    attn_shard = jnp.concatenate([o_half, q_half, k_half, v_half], axis=1)
    fsdp = lax.axis_size("fsdp")
    gain_rows = jnp.stack([attn_gain, ffn_gain])
    gain_width = attn_gain.shape[0]
    extra = ((0, 14), (0, attn_shard.shape[1] - gain_width))
    tokens_low = lax.dynamic_slice_in_dim(tokens, tp * own_rows, own_rows, 0)
    tokens_one = swap_first(tokens_low)
    attn_ring = ring_over(jnp.concatenate([attn_shard, jnp.pad(gain_rows, extra)]), fsdp, tokens_one)
    own_depth = attn_shard.shape[0]
    attn_full = in_place([piece[:own_depth] for piece in attn_ring], 0)
    gains = in_place([piece[own_depth : own_depth + 2, :gain_width] for piece in attn_ring], 1)
    gain_one = gains[0].astype(F32)[None]
    gain_two = gains[1].astype(F32)[None]
    ff_half = gate_weight.shape[1] // 2
    chunk = ff_half // CHUNKS
    ffn_shards = []
    for part in range(CHUNKS):
        at = ctx * ff_half + part * chunk
        ffn_shards.append(
            jnp.concatenate(
                [
                    lax.dynamic_slice_in_dim(weight, at, chunk, 1)
                    for weight in (gate_weight, up_weight, down_weight)
                ],
                axis=1,
            )
        )
    length_row, deal_row = lengths[0], deal[0]
    spans = deal_row.shape[0]
    span_rows = group_rows // spans
    ends = jnp.cumsum(length_row, dtype=jnp.int32)
    starts = ends - length_row
    natural = jnp.arange(group_rows, dtype=jnp.int32)
    inside = (natural[:, None] >= starts[None]) & (natural[:, None] < ends[None])
    start_of = jnp.sum(jnp.where(inside, starts[None], 0), axis=1, dtype=jnp.int32)
    first = start_of[::BLOCK] // BLOCK
    rel = jnp.arange(group_rows // own_rows, dtype=jnp.int32)
    rel_core = core ^ (rel // 4)
    by_first, by_second = rel % 2, (rel // 2) % 2
    rel_ctx = ctx ^ jnp.where(rel_core == 0, by_first, by_second)
    rel_y = y ^ jnp.where(rel_core == 0, by_second, by_first)
    dealt_block = rel_ctx * (row_count // own_rows) + rel_y * 2 + rel_core
    per_span = span_rows // own_rows
    span_of = jnp.sum(
        jnp.where(
            (dealt_block // per_span)[:, None] == jnp.arange(spans, dtype=jnp.int32)[None],
            deal_row[None],
            0,
        ),
        axis=1,
        dtype=jnp.int32,
    )
    natural_block = span_of * per_span + dealt_block % per_span
    place = jnp.sum(
        jnp.where(natural_block[None, :] == rel[:, None], rel[None, :], 0), axis=1, dtype=jnp.int32
    )
    natural_rel = (
        natural_block[:, None] * own_rows + jnp.arange(own_rows, dtype=jnp.int32)[None]
    ).reshape(-1)
    inside_rel = (natural_rel[:, None] >= starts[None]) & (natural_rel[:, None] < ends[None])
    position = natural_rel - jnp.sum(
        jnp.where(inside_rel, starts[None], 0), axis=1, dtype=jnp.int32
    )
    lane = jnp.arange(128, dtype=jnp.int32)
    inverse = jnp.exp((lane % 32).astype(F32) * (-2.0 * math.log(ROPE_BASE) / HEAD_DIM))
    angles = position.astype(F32)[:, None] * inverse[None]
    cos = jnp.cos(angles)
    sin = jnp.where((lane % 64 < 32)[None], -jnp.sin(angles), jnp.sin(angles))
    start_column = start_of[:, None]

    cot_low = lax.dynamic_slice_in_dim(cotangent, tp * own_rows, own_rows, 0)
    tokens_own, cot_own = tokens_low.astype(F32), cot_low.astype(F32)
    group_tokens = (tokens_low, tokens_one, swap_second(tokens_low), swap_second(tokens_one))
    first_shard = after(ffn_shards[0], attn_ring[-1], *group_tokens[2:])
    group_tokens = group_tokens + tuple(swap_core(part) for part in group_tokens)
    attn_full, cot_low, cos, sin, gain_one, *group_tokens = lax.optimization_barrier(
        (attn_full, cot_low, cos, sin, gain_one, *group_tokens)
    )
    qkv = project_qkv(group_tokens, gain_one, attn_full, q_width, cos, sin)
    heads = attend(qkv, depth, place, first, start_column, q_width)
    cot = share_rows(cot_low, [[qkv], [heads]])
    ffn_full = [
        lax.all_gather(shard, "fsdp", axis=0, tiled=True)
        for shard in (first_shard, after(ffn_shards[1], heads))
    ]
    heads = after(heads, *cot)
    attn_sum = sum_last(
        sum_pairs(*sum_cores([(heads, 0, attn_full, 0, q_width)])), ffn_full[0]
    )
    hidden = tokens_own + attn_sum
    normed_two = share_rows((hidden * inv_rms(hidden) * gain_two).astype(BF16))

    acts = []
    grad_parts = []
    for part in range(CHUNKS):
        normed_two = (after(normed_two[0], *grad_parts), *normed_two[1:])
        acts.append(ffn_chunk(normed_two, cot, ffn_full[part]))
        grad_parts.append(
            weight_grads(normed_two, acts[part], 2 * chunk, 0, cot, acts[part], chunk, 2)
        )
    reduced = [
        lax.psum_scatter(part, "fsdp", scatter_dimension=0, tiled=True) for part in grad_parts
    ]
    d_norm_terms = [(acts[part], 0, ffn_full[part], 0, 2 * chunk) for part in range(CHUNKS)]
    ffn_terms = [(acts[part], 2, ffn_full[part], 2, chunk) for part in range(CHUNKS)]
    d_normed_two = sum_last(sum_pairs(*sum_cores(d_norm_terms, 1)), *grad_parts)
    d_hidden = cot_own + rms_back(hidden, gain_two, d_normed_two)
    ffn_sent = [back_product(ffn_terms, at, 4) for at in (3, 2)]
    ffn_mine = back_product(ffn_terms, 0, 2)
    d_attn = share_rows(d_hidden.astype(BF16), [[*ffn_sent, ffn_mine], [reduced[0]]])

    d_heads = front_product(d_attn, attn_full, q_width, 0)
    arrived = [swap_core(after(piece, *d_attn[4:])) for piece in ffn_sent]
    half_rows = ffn_mine.shape[0] // 2
    ffn_far, ffn_near = y_first(
        ffn_mine[half_rows:] + arrived[0], ffn_mine[:half_rows] + arrived[1], core
    )
    d_heads, ffn_far, reduced[0] = lax.optimization_barrier((d_heads, ffn_far, reduced[0]))
    other_reduced = [swap_x(reduced[0])]
    d_qkv = attend_back(qkv, depth, d_heads, heads, place, first, start_column, cos, sin)
    ffn_near = ffn_near + after(swap_y(ffn_far), d_qkv)
    d_qkv = after(d_qkv, ffn_near, other_reduced[0], *reduced[1:])
    ffn_sum = ffn_near[:own_rows].astype(F32) + swap_x(ffn_near[own_rows:]).astype(F32)
    result_own = (hidden + ffn_sum).astype(BF16)
    normed_far, normed_near = sum_cores(
        [
            (d_qkv, 0, attn_full, 1, q_width),
            (d_qkv, q_width // 128, attn_full, 2 * q_width // 128, 128),
        ]
    )
    normed_far = after(normed_far, result_own)
    attn_grad = weight_grads(
        d_attn, heads, q_width, 0, (qkv,), d_qkv, q_width + 128, 0
    )
    d_normed = sum_last(sum_pairs(normed_far, normed_near), attn_grad)
    tokens_grad_own = (d_hidden + rms_back(tokens_own, gain_one, d_normed)).astype(BF16)
    for part in range(1, CHUNKS):
        reduced[part] = after(reduced[part], attn_grad, tokens_grad_own)
        other_reduced.append(swap_x(reduced[part]))
    tokens_grad_beside = swap_y(tokens_grad_own)
    tokens_grad = share_in_ctx(tokens_grad_own, tokens_grad_beside, y, core)
    result_own = after(result_own, tokens_grad_own)
    result = share_in_ctx(result_own, swap_y(result_own), y, core)

    attn_reduced = lax.psum_scatter(attn_grad, "fsdp", scatter_dimension=0, tiled=True)
    attn_reduced = after(attn_reduced, tokens_grad_beside, *other_reduced)

    def gain_part(pairs):
        return sum(jnp.sum(mine.astype(F32) * grad.astype(F32), axis=1) for mine, grad in pairs)

    gain_sums = sum_all(
        jnp.stack(
            [
                gain_part([(attn_shard[:, q_width:], attn_reduced[:, q_width:])]),
                gain_part(
                    [
                        (ffn_shards[part][:, : 2 * chunk], reduced[part][:, : 2 * chunk])
                        for part in range(CHUNKS)
                    ]
                ),
            ]
        )
    )
    attn_gain_grad = gain_sums[0] / attn_gain.astype(F32)
    ffn_gain_grad = gain_sums[1] / ffn_gain.astype(F32)

    halves = [both_halves(mine, other, ctx) for mine, other in zip(reduced, other_reduced)]

    def ffn_out(which):
        return jnp.concatenate(
            [
                halves[part][side][:, which * chunk : (which + 1) * chunk]
                for side in range(2)
                for part in range(CHUNKS)
            ],
            axis=1,
        )

    attn_low, attn_high = both_halves(attn_reduced, swap_x(attn_reduced), ctx)

    def attn_out(begin, end):
        return jnp.concatenate([attn_low[:, begin:end], attn_high[:, begin:end]], axis=1)

    q_end, k_end = 2 * q_width, 2 * q_width + kv_width
    return (
        result,
        tokens_grad,
        attn_out(q_width, q_end),
        attn_out(q_end, k_end),
        attn_out(k_end, k_end + kv_width),
        attn_out(0, q_width),
        attn_gain_grad,
        ffn_out(0),
        ffn_out(1),
        ffn_out(2),
        ffn_gain_grad,
    )


def solution(mesh):
    rows = P(("fsdp", "ctx"), None)
    matrix = P("fsdp", "tp")
    vector = P("fsdp")
    return jax.shard_map(
        shards,
        mesh=mesh,
        in_specs=(
            rows,
            matrix,
            matrix,
            matrix,
            matrix,
            vector,
            matrix,
            matrix,
            matrix,
            vector,
            P("fsdp", None),
            P("fsdp", None),
            rows,
        ),
        out_specs=(
            rows,
            rows,
            matrix,
            matrix,
            matrix,
            matrix,
            vector,
            matrix,
            matrix,
            matrix,
            vector,
        ),
        check_vma=False,
    )
```

```python
import functools
import math

import jax
import jax.numpy as jnp
from jax import lax
from jax.experimental import pallas as pl
from jax.experimental.pallas import tpu as pltpu
from jax.sharding import PartitionSpec as P

HEAD_DIM = 64
EPSILON = 1e-05
ROPE_BASE = 500000.0
MASKED = -1e30
LOG2_E = 1.4426950408889634
BLOCK = 256
SPLIT = (5, 3)
VMEM = 56 * 2**20

F32 = jnp.float32
BF16 = jnp.bfloat16

PAIR = [(0, 1), (1, 0)]
CORE = [(0, 1), (1, 0), (2, 3), (3, 2)]
ACROSS = [(0, 2), (2, 0), (1, 3), (3, 1)]


def joint_pairs(x_core):
    pairs = []
    for ctx in range(2):
        for tp in range(4):
            there = (1 - ctx) * 4 + tp if tp % 2 == x_core else ctx * 4 + (tp ^ 2)
            pairs.append((ctx * 4 + tp, there))
    return pairs


FIRST = joint_pairs(0)
SECOND = joint_pairs(1)


def swap_core(v):
    return lax.ppermute(v, "tp", CORE)


def swap_y(v):
    return lax.ppermute(v, "tp", ACROSS)


def swap_x(v):
    return lax.ppermute(v, "ctx", PAIR)


def swap_first(v):
    return lax.ppermute(v, ("ctx", "tp"), FIRST)


def swap_second(v):
    return lax.ppermute(v, ("ctx", "tp"), SECOND)


def after(value, *others):
    return lax.optimization_barrier((value,) + others)[0]


def params(*semantics):
    return pltpu.CompilerParams(vmem_limit_bytes=VMEM)


def cost(gigaflops=0):
    return pl.CostEstimate(flops=int(gigaflops * 1e9) + 1, bytes_accessed=1, transcendentals=0)


def inv_rms(hidden):
    return lax.rsqrt(jnp.mean(hidden * hidden, axis=-1, keepdims=True) + EPSILON)


def rms_back(hidden, gain, grad):
    scale = inv_rms(hidden)
    weighted = grad * gain
    inner = jnp.mean(weighted * hidden, axis=-1, keepdims=True)
    return scale * weighted - hidden * (scale * scale * scale) * inner


def turn_lanes(u, first):
    return jnp.where(first, pltpu.roll(u, 96, 1), pltpu.roll(u, 32, 1))


def stream_scratch(count, rows, depth):
    return [pltpu.VMEM((2, rows, depth), BF16), pltpu.SemaphoreType.DMA((2,))] * count


def next_piece(refs, buffer, sems):
    i = pl.program_id(0)

    def copy_of(piece):
        return pltpu.make_async_copy(refs[piece], buffer.at[piece % 2], sems.at[piece % 2])

    @pl.when(i == 0)
    def _():
        copy_of(0).start()

    for piece in range(1, len(refs)):

        @pl.when(i == piece - 1)
        def _(piece=piece):
            copy_of(piece).start()

    for piece in range(len(refs)):

        @pl.when(i == piece)
        def _(piece=piece):
            copy_of(piece).wait()

    return buffer[lax.rem(i, 2)]


def qkv_kernel(count, *refs):
    gain_ref, wq_ref, wkv_ref, cos_ref, sin_ref, o_ref, buffer, sems = refs[count:]
    cos, sin = cos_ref[...], sin_ref[...]
    depth = gain_ref.shape[1]
    lane = lax.broadcasted_iota(jnp.int32, cos.shape, 1)
    first = (lane % 64) < 32
    x = next_piece(refs[:count], buffer, sems).astype(F32)
    x = (x * inv_rms(x) * gain_ref[...]).astype(BF16)
    o_ref[:, :depth] = x
    raw = jnp.dot(x, wq_ref[...], preferred_element_type=F32)
    tiles = raw.shape[1] // 128
    for tile in range(tiles):
        u = raw[:, tile * 128 : (tile + 1) * 128]
        turned = u * cos + turn_lanes(u, first) * sin
        o_ref[:, depth + tile * 128 : depth + (tile + 1) * 128] = turned.astype(BF16)
    u = jnp.dot(x, wkv_ref[...], preferred_element_type=F32)
    turned = u * cos + turn_lanes(u, first) * sin
    o_ref[:, depth + tiles * 128 :] = jnp.where(lane < 64, turned, u).astype(BF16)


def project_qkv(x, gain, w, q_width, cos, sin):
    step, depth = x[0].shape
    rows = len(x) * step
    width = depth + q_width + 128
    return pl.pallas_call(
        functools.partial(qkv_kernel, len(x)),
        out_shape=jax.ShapeDtypeStruct((rows, width), BF16),
        grid=(len(x),),
        in_specs=[pl.BlockSpec(memory_space=pl.ANY)] * len(x)
        + [
            pl.BlockSpec((1, depth), lambda i: (0, 0)),
            pl.BlockSpec((depth, q_width), lambda i: (0, 1)),
            pl.BlockSpec((depth, 128), lambda i: (0, 2 * q_width // 128)),
            pl.BlockSpec((step, 128), lambda i: (i, 0)),
            pl.BlockSpec((step, 128), lambda i: (i, 0)),
        ],
        out_specs=pl.BlockSpec((step, width), lambda i: (i, 0)),
        scratch_shapes=stream_scratch(1, step, depth),
        compiler_params=params(),
        cost_estimate=cost(),
        name="qkv",
    )(*x, gain, w, w, cos, sin)


def ffn_kernel(count, *refs):
    w_ref, o_ref, x_buffer, x_sems, c_buffer, c_sems = refs[2 * count :]
    n = w_ref.shape[1] // 3
    x = next_piece(refs[:count], x_buffer, x_sems)
    c = next_piece(refs[count : 2 * count], c_buffer, c_sems)
    gate = jnp.dot(x, w_ref[:, :n], preferred_element_type=F32)
    up = jnp.dot(x, w_ref[:, n : 2 * n], preferred_element_type=F32)
    d_mixed = jnp.dot(c, w_ref[:, 2 * n :], preferred_element_type=F32)
    sig = 1.0 / (1.0 + jnp.exp(-gate))
    silu = gate * sig
    o_ref[:, :n] = (d_mixed * up * (sig * (1.0 + gate * (1.0 - sig)))).astype(BF16)
    o_ref[:, n : 2 * n] = (d_mixed * silu).astype(BF16)
    o_ref[:, 2 * n :] = (silu * up).astype(BF16)


def ffn_chunk(x, cot, w):
    step, depth = x[0].shape
    rows = len(x) * step
    width = w.shape[1]
    return pl.pallas_call(
        functools.partial(ffn_kernel, len(x)),
        out_shape=jax.ShapeDtypeStruct((rows, width), BF16),
        grid=(len(x),),
        in_specs=[pl.BlockSpec(memory_space=pl.ANY)] * (2 * len(x))
        + [pl.BlockSpec((depth, width), lambda i: (0, 0))],
        out_specs=pl.BlockSpec((step, width), lambda i: (i, 0)),
        scratch_shapes=stream_scratch(2, step, depth),
        compiler_params=params(),
        cost_estimate=cost(),
        name="ffn",
    )(*x, *cot, w)


DOWN = (((0,), (0,)), ((), ()))


def grads_kernel(x_count, y_count, *refs):
    a_ref, b_ref, o_ref = refs[x_count + y_count :]
    split = a_ref.shape[1]

    def product(tall_refs, right_ref):
        tall = jnp.concatenate([ref[...] for ref in tall_refs], axis=0)
        return lax.dot_general(
            tall, right_ref[...].astype(BF16), DOWN, preferred_element_type=F32
        ).astype(BF16)

    o_ref[:, :split] = product(refs[:x_count], a_ref)
    o_ref[:, split:] = product(refs[x_count : x_count + y_count], b_ref)


def weight_grads(x, a, a_width, a_column, y, b, b_width, b_column):
    depth = x[0].shape[1]
    rows = a.shape[0]
    width = a_width + b_width
    step = 512
    return pl.pallas_call(
        functools.partial(grads_kernel, len(x), len(y)),
        out_shape=jax.ShapeDtypeStruct((depth, width), BF16),
        grid=(depth // step,),
        in_specs=[pl.BlockSpec((piece.shape[0], step), lambda i: (0, i)) for piece in (*x, *y)]
        + [
            pl.BlockSpec((rows, a_width), lambda i: (0, a_column)),
            pl.BlockSpec((rows, b_width), lambda i: (0, b_column)),
        ],
        out_specs=pl.BlockSpec((step, width), lambda i: (i, 0)),
        compiler_params=params(),
        cost_estimate=cost(),
        name="weight_grads",
    )(*x, *y, a, b)


def back_kernel(*refs):
    o_ref = refs[-1]
    count = (len(refs) - 1) // 2
    total = None
    for part in range(count):
        term = lax.dot_general(
            refs[part][...].astype(BF16),
            refs[count + part][...],
            (((1,), (1,)), ((), ())),
            preferred_element_type=F32,
        )
        total = term if total is None else total + term
    o_ref[...] = total.astype(BF16)


def back_product(terms, part, parts):
    rows = terms[0][0].shape[0] // parts
    depth = terms[0][2].shape[0]
    step = min(512, rows)
    ahead = part * (rows // step)
    return pl.pallas_call(
        back_kernel,
        out_shape=jax.ShapeDtypeStruct((rows, depth), BF16),
        grid=(rows // step,),
        in_specs=[
            pl.BlockSpec((step, term[4]), lambda i, column=term[1]: (i + ahead, column))
            for term in terms
        ]
        + [pl.BlockSpec((depth, term[4]), lambda i, column=term[3]: (0, column)) for term in terms],
        out_specs=pl.BlockSpec((step, depth), lambda i: (i, 0)),
        compiler_params=params(),
        cost_estimate=cost(),
        name="back",
    )(*[term[0] for term in terms], *[term[2] for term in terms])


def front_kernel(count, *refs):
    w_ref, o_ref, buffer, sems = refs[count:]
    x = next_piece(refs[:count], buffer, sems)
    o_ref[...] = jnp.dot(x, w_ref[...], preferred_element_type=F32).astype(BF16)


def front_product(x, w, width, column):
    step, depth = x[0].shape
    rows = len(x) * step
    return pl.pallas_call(
        functools.partial(front_kernel, len(x)),
        out_shape=jax.ShapeDtypeStruct((rows, width), BF16),
        grid=(len(x),),
        in_specs=[pl.BlockSpec(memory_space=pl.ANY)] * len(x)
        + [pl.BlockSpec((depth, width), lambda i: (0, column))],
        out_specs=pl.BlockSpec((step, width), lambda i: (i, 0)),
        scratch_shapes=stream_scratch(1, step, depth),
        compiler_params=params(),
        cost_estimate=cost(),
        name="front",
    )(*x, w)


def stack_heads(block):
    count = block.shape[1] // HEAD_DIM
    return jnp.concatenate(
        [block[:, h * HEAD_DIM : (h + 1) * HEAD_DIM] for h in range(count)], axis=0
    )


def unstack_heads(stacked):
    count = stacked.shape[0] // BLOCK
    return jnp.concatenate([stacked[h * BLOCK : (h + 1) * BLOCK] for h in range(count)], axis=1)


def allowed_of(i, j, start):
    row = i * BLOCK + lax.broadcasted_iota(jnp.int32, (BLOCK, BLOCK), 0)
    col = j * BLOCK + lax.broadcasted_iota(jnp.int32, (BLOCK, BLOCK), 1)
    return (col <= row) & (col >= start)


def attend_kernel(place, first, q_ref, kv_ref, start_ref, o_ref):
    i = pl.program_id(0)
    q = stack_heads(q_ref[...])
    heads = q.shape[0] // BLOCK
    start = start_ref[...]

    def step(j, carry):
        top, total, acc = carry
        at = pl.multiple_of(place[j] * BLOCK, BLOCK)
        kv = kv_ref[pl.ds(at, BLOCK), :]
        raw = lax.dot_general(
            q, kv[:, :HEAD_DIM], (((1,), (1,)), ((), ())), preferred_element_type=F32
        ) * (HEAD_DIM**-0.5 * LOG2_E)
        allowed = allowed_of(i, j, start)
        scores = jnp.where(allowed[None], raw.reshape(heads, BLOCK, BLOCK), MASKED).reshape(
            heads * BLOCK, BLOCK
        )
        new_top = jnp.maximum(top, jnp.max(scores, axis=-1, keepdims=True))
        keep = jnp.exp2(top - new_top)
        probs = jnp.exp2(scores - new_top)
        total = total * keep + jnp.sum(probs, axis=-1, keepdims=True)
        acc = acc * keep + jnp.dot(probs.astype(BF16), kv, preferred_element_type=F32)
        return (new_top, total, acc)

    size = heads * BLOCK
    top, total, acc = lax.fori_loop(
        first[i],
        i + 1,
        step,
        (
            jnp.full((size, 1), MASKED, F32),
            jnp.zeros((size, 1), F32),
            jnp.zeros((size, 2 * HEAD_DIM), F32),
        ),
    )
    out = acc[:, HEAD_DIM:] / total
    q_width = q_ref.shape[1]
    o_ref[:, :q_width] = unstack_heads(out)
    lse = top + jnp.log2(total)
    lane = lax.broadcasted_iota(jnp.int32, (BLOCK, 128), 1)
    packed = jnp.zeros((BLOCK, 128), F32)
    for h in range(heads):
        packed = jnp.where(lane == h, lse[h * BLOCK : (h + 1) * BLOCK], packed)
    o_ref[:, q_width:] = packed


def attend(qkv, depth, place, first, start, q_width):
    rows = qkv.shape[0]
    blocks = rows // BLOCK
    return pl.pallas_call(
        attend_kernel,
        out_shape=jax.ShapeDtypeStruct((rows, q_width + 128), F32),
        grid_spec=pltpu.PrefetchScalarGridSpec(
            num_scalar_prefetch=2,
            grid=(blocks,),
            in_specs=[
                pl.BlockSpec((BLOCK, q_width), lambda i, place, first: (place[i], depth // q_width)),
                pl.BlockSpec((rows, 128), lambda i, place, first: (0, (depth + q_width) // 128)),
                pl.BlockSpec((BLOCK, 1), lambda i, place, first: (i, 0)),
            ],
            out_specs=pl.BlockSpec((BLOCK, q_width + 128), lambda i, place, first: (place[i], 0)),
        ),
        compiler_params=params(),
        cost_estimate=cost(),
        name="attend",
    )(place, first, qkv, qkv, start)


def attend_back_kernel(
    place,
    first,
    q_ref,
    d_ref,
    h_ref,
    kv_ref,
    start_ref,
    cos_ref,
    sin_ref,
    o_ref,
    dkv_ref,
):
    i = pl.program_id(0)
    blocks = pl.num_programs(0)
    score_scale = HEAD_DIM**-0.5
    q_width = q_ref.shape[1]

    @pl.when(i == 0)
    def _():
        dkv_ref[...] = jnp.zeros_like(dkv_ref)

    q = stack_heads(q_ref[...])
    d_out = stack_heads(d_ref[...])
    heads = q.shape[0] // BLOCK
    out = stack_heads(h_ref[:, :q_width])
    delta = jnp.sum(d_out.astype(F32) * out, axis=-1, keepdims=True)
    lse_block = h_ref[:, q_width:]
    lse = jnp.concatenate([lse_block[:, h : h + 1] for h in range(heads)], axis=0)
    start = start_ref[...]

    def step(j, d_q):
        at = pl.multiple_of(place[j] * BLOCK, BLOCK)
        kv = kv_ref[pl.ds(at, BLOCK), :]
        k, v = kv[:, :HEAD_DIM], kv[:, HEAD_DIM:]
        across = (((1,), (1,)), ((), ()))
        down = (((0,), (0,)), ((), ()))
        raw = lax.dot_general(q, k, across, preferred_element_type=F32) * (score_scale * LOG2_E)
        allowed = allowed_of(i, j, start)
        scores = jnp.where(allowed[None], raw.reshape(heads, BLOCK, BLOCK), MASKED).reshape(
            heads * BLOCK, BLOCK
        )
        probs = jnp.exp2(scores - lse)
        d_probs = lax.dot_general(d_out, v, across, preferred_element_type=F32)
        d_scores = (probs * (d_probs - delta)).astype(BF16)
        d_k = lax.dot_general(d_scores, q, down, preferred_element_type=F32) * score_scale
        d_v = lax.dot_general(probs.astype(BF16), d_out, down, preferred_element_type=F32)
        here = pl.ds(pl.multiple_of(j * BLOCK, BLOCK), BLOCK)
        dkv_ref[here, :] += jnp.concatenate([d_k, d_v], axis=1)
        return d_q + jnp.dot(d_scores, k, preferred_element_type=F32)

    d_q = lax.fori_loop(first[i], i + 1, step, jnp.zeros((heads * BLOCK, HEAD_DIM), F32))
    d_q = unstack_heads(d_q * score_scale)
    lane = lax.broadcasted_iota(jnp.int32, (BLOCK, 128), 1)
    front = (lane % 64) < 32
    mine = pl.ds(pl.multiple_of(place[i] * BLOCK, BLOCK), BLOCK)
    cos, sin = cos_ref[mine, :], sin_ref[mine, :]
    for tile in range(q_width // 128):
        u = d_q[:, tile * 128 : (tile + 1) * 128]
        o_ref[mine, tile * 128 : (tile + 1) * 128] = (u * cos - turn_lanes(u, front) * sin).astype(
            BF16
        )

    @pl.when(i == blocks - 1)
    def _():
        for b in range(dkv_ref.shape[0] // BLOCK):
            there = pl.ds(pl.multiple_of(place[b] * BLOCK, BLOCK), BLOCK)
            u = dkv_ref[b * BLOCK : (b + 1) * BLOCK, :]
            turned = u * cos_ref[there, :] - turn_lanes(u, front) * sin_ref[there, :]
            o_ref[there, q_width:] = jnp.where(lane < HEAD_DIM, turned, u).astype(BF16)


def attend_back(qkv, depth, d_heads, heads, place, first, start, cos, sin):
    rows, q_width = d_heads.shape
    width = q_width + 128
    blocks = rows // BLOCK
    by_place = lambda i, place, first: (place[i], 0)
    whole = lambda i, place, first: (0, 0)
    return pl.pallas_call(
        attend_back_kernel,
        out_shape=jax.ShapeDtypeStruct((rows, width), BF16),
        grid_spec=pltpu.PrefetchScalarGridSpec(
            num_scalar_prefetch=2,
            grid=(blocks,),
            in_specs=[
                pl.BlockSpec((BLOCK, q_width), lambda i, place, first: (place[i], depth // q_width)),
                pl.BlockSpec((BLOCK, q_width), by_place),
                pl.BlockSpec((BLOCK, q_width + 128), by_place),
                pl.BlockSpec((rows, 128), lambda i, place, first: (0, (depth + q_width) // 128)),
                pl.BlockSpec((BLOCK, 1), lambda i, place, first: (i, 0)),
                pl.BlockSpec((rows, 128), whole),
                pl.BlockSpec((rows, 128), whole),
            ],
            out_specs=pl.BlockSpec((rows, width), whole),
            scratch_shapes=[pltpu.VMEM((rows, 128), F32)],
        ),
        compiler_params=params(),
        cost_estimate=cost(),
        name="attend_back",
    )(place, first, qkv, d_heads, heads, qkv, start, cos, sin)


def sum_cores(terms, pieces=2, *held):
    sent = [back_product(terms, 2 * pieces - 1 - at, 2 * pieces) for at in range(pieces)]
    arrived = [swap_core(after(piece, *held)) for piece in sent]
    mine = back_product(terms, 0, 2)
    rows = mine.shape[0] // 2
    if pieces == 1:
        return mine[rows:] + arrived[0][rows:], mine[:rows] + arrived[0][:rows]
    return mine[rows:] + arrived[0], mine[:rows] + arrived[1]


def y_first(far, near, core):
    rows = near.shape[0] // 2
    first, second = near[rows:], far[:rows]
    return (
        jnp.concatenate([jnp.where(core == 0, second, first), far[rows:]]),
        jnp.concatenate([near[:rows], jnp.where(core == 0, first, second)]),
    )


def sum_pairs(far, near, *behind):
    return near + after(swap_second(far), *behind)


def sum_last(near, *beside):
    rows = near.shape[0] // 2
    near = after(near, *beside)
    return near[:rows].astype(F32) + swap_first(near[rows:]).astype(F32)


def share_rows(own, beside=()):
    beside = list(beside) + [()] * (2 - len(beside))
    one, two, *_ = lax.optimization_barrier((swap_first(own), swap_second(own), *beside[0]))
    early = tuple(swap_core(part) for part in (own, one, two))
    last = after(swap_second(one), *early, *beside[1])
    return (own, one, two, last, *early, swap_core(last))


def ring_over(shard, count, held):
    cycle = [(at, (at + 1) % count) for at in range(count)]
    pieces = [shard]
    for step in range(count - 1):
        sent = after(pieces[-1], *held) if step == 1 else pieces[-1]
        pieces.append(lax.ppermute(sent, "fsdp", cycle))
    return pieces


def in_place(pieces, axis):
    count, size = len(pieces), pieces[0].shape[axis]
    here = lax.axis_index("fsdp")
    shape = list(pieces[0].shape)
    shape[axis] *= count
    whole = jnp.zeros(shape, pieces[0].dtype)
    for back, piece in enumerate(pieces):
        owner = lax.rem(here + count - back, count)
        whole = lax.dynamic_update_slice_in_dim(whole, piece, owner * size, axis)
    return whole


def share_in_ctx(own, beside, y, core):
    pair = jnp.stack([own, beside])
    other = jnp.stack([swap_core(own), swap_core(beside)])
    four = jnp.stack([pair, other])
    four = jnp.where(y == 1, four[:, ::-1], four)
    four = jnp.where(core == 1, four[::-1], four)
    return four.transpose(1, 0, 2, 3).reshape(-1, own.shape[1])


def sum_all(v):
    v = v + swap_core(v)
    v = v + swap_y(v)
    return v + swap_x(v)


def both_halves(own, other, ctx):
    low = jnp.where(ctx == 0, own, other).astype(F32)
    high = jnp.where(ctx == 0, other, own).astype(F32)
    return low, high


def shards(
    tokens,
    q_weight,
    k_weight,
    v_weight,
    o_weight,
    attn_gain,
    gate_weight,
    up_weight,
    down_weight,
    ffn_gain,
    lengths,
    deal,
    cotangent,
):
    ctx = lax.axis_index("ctx")
    tp = lax.axis_index("tp")
    y, core = tp // 2, tp % 2
    row_count, depth = tokens.shape
    group_rows = row_count * lax.axis_size("ctx")
    own_rows = row_count // lax.axis_size("tp")

    def half(weight):
        width = weight.shape[1] // 2
        return lax.dynamic_slice_in_dim(weight, ctx * width, width, 1)

    length_row, deal_row = lengths[0], deal[0]
    spans = deal_row.shape[0]
    span_rows = group_rows // spans
    ends = jnp.cumsum(length_row, dtype=jnp.int32)
    starts = ends - length_row
    natural = jnp.arange(group_rows, dtype=jnp.int32)
    inside = (natural[:, None] >= starts[None]) & (natural[:, None] < ends[None])
    start_of = jnp.sum(jnp.where(inside, starts[None], 0), axis=1, dtype=jnp.int32)
    first = start_of[::BLOCK] // BLOCK
    rel = jnp.arange(group_rows // own_rows, dtype=jnp.int32)
    rel_core = core ^ (rel // 4)
    by_first, by_second = rel % 2, (rel // 2) % 2
    rel_ctx = ctx ^ jnp.where(rel_core == 0, by_first, by_second)
    rel_y = y ^ jnp.where(rel_core == 0, by_second, by_first)
    dealt_block = rel_ctx * (row_count // own_rows) + rel_y * 2 + rel_core
    per_span = span_rows // own_rows
    span_of = jnp.sum(
        jnp.where(
            (dealt_block // per_span)[:, None] == jnp.arange(spans, dtype=jnp.int32)[None],
            deal_row[None],
            0,
        ),
        axis=1,
        dtype=jnp.int32,
    )
    natural_block = span_of * per_span + dealt_block % per_span
    place = jnp.sum(
        jnp.where(natural_block[None, :] == rel[:, None], rel[None, :], 0), axis=1, dtype=jnp.int32
    )
    natural_rel = (
        natural_block[:, None] * own_rows + jnp.arange(own_rows, dtype=jnp.int32)[None]
    ).reshape(-1)
    inside_rel = (natural_rel[:, None] >= starts[None]) & (natural_rel[:, None] < ends[None])
    position = natural_rel - jnp.sum(
        jnp.where(inside_rel, starts[None], 0), axis=1, dtype=jnp.int32
    )
    lane = jnp.arange(128, dtype=jnp.int32)
    inverse = jnp.exp((lane % 32).astype(F32) * (-2.0 * math.log(ROPE_BASE) / HEAD_DIM))
    angles = position.astype(F32)[:, None] * inverse[None]
    cos = jnp.cos(angles)
    sin = jnp.where((lane % 64 < 32)[None], -jnp.sin(angles), jnp.sin(angles))
    start_column = start_of[:, None]

    q_half, k_half, v_half, o_half = map(half, (q_weight, k_weight, v_weight, o_weight))
    q_width, kv_width = q_half.shape[1], k_half.shape[1]
    attn_shard = jnp.concatenate([o_half, q_half, k_half, v_half], axis=1)
    fsdp = lax.axis_size("fsdp")
    gain_rows = jnp.stack([attn_gain, ffn_gain])
    gain_width = attn_gain.shape[0]
    extra = ((0, 14), (0, attn_shard.shape[1] - gain_width))
    tokens_low = lax.dynamic_slice_in_dim(tokens, tp * own_rows, own_rows, 0)
    cot_low = lax.dynamic_slice_in_dim(cotangent, tp * own_rows, own_rows, 0)
    tokens_one = swap_first(tokens_low)
    attn_ring = ring_over(
        jnp.concatenate([attn_shard, jnp.pad(gain_rows, extra)]),
        fsdp,
        (tokens_one, cos, sin, cot_low, place, first, start_column),
    )
    own_depth = attn_shard.shape[0]
    attn_full = in_place([piece[:own_depth] for piece in attn_ring], 0)
    gains = in_place([piece[own_depth : own_depth + 2, :gain_width] for piece in attn_ring], 1)
    gain_one = gains[0].astype(F32)[None]
    gain_two = gains[1].astype(F32)[None]
    ff_half = gate_weight.shape[1] // 2
    chunks = [ff_half * share // sum(SPLIT) for share in SPLIT]
    ffn_shards = []
    for part, chunk in enumerate(chunks):
        at = ctx * ff_half + sum(chunks[:part])
        ffn_shards.append(
            jnp.concatenate(
                [
                    lax.dynamic_slice_in_dim(weight, at, chunk, 1)
                    for weight in (gate_weight, up_weight, down_weight)
                ],
                axis=1,
            )
        )
    tokens_own, cot_own = tokens_low.astype(F32), cot_low.astype(F32)
    group_tokens = (tokens_low, tokens_one, swap_second(tokens_low), swap_second(tokens_one))
    first_shard = after(ffn_shards[0], attn_ring[-1], *group_tokens[2:])
    group_tokens = group_tokens + tuple(swap_core(part) for part in group_tokens)
    attn_full, cot_low, cos, sin, gain_one, *group_tokens = lax.optimization_barrier(
        (attn_full, cot_low, cos, sin, gain_one, *group_tokens)
    )
    qkv = project_qkv(group_tokens, gain_one, attn_full, q_width, cos, sin)
    heads = attend(qkv, depth, place, first, start_column, q_width)
    cot = share_rows(cot_low, [[qkv], [heads]])
    ffn_full = [
        lax.all_gather(shard, "fsdp", axis=0, tiled=True)
        for shard in (first_shard, after(ffn_shards[1], heads))
    ]
    heads = after(heads, *cot)
    attn_sum = sum_last(
        sum_pairs(*sum_cores([(heads, 0, attn_full, 0, q_width)])), ffn_full[0]
    )
    hidden = tokens_own + attn_sum
    normed_two = share_rows((hidden * inv_rms(hidden) * gain_two).astype(BF16))

    acts = []
    grad_parts = []
    for part, chunk in enumerate(chunks):
        normed_two = (after(normed_two[0], *grad_parts), *normed_two[1:])
        acts.append(ffn_chunk(normed_two, cot, ffn_full[part]))
        grad_parts.append(
            weight_grads(normed_two, acts[part], 2 * chunk, 0, cot, acts[part], chunk, 2)
        )
    reduced = [
        lax.psum_scatter(part, "fsdp", scatter_dimension=0, tiled=True) for part in grad_parts
    ]
    d_norm_terms = [
        (acts[part], 0, ffn_full[part], 0, 2 * chunk) for part, chunk in enumerate(chunks)
    ]
    ffn_terms = [
        (acts[part], 2, ffn_full[part], 2, chunk) for part, chunk in enumerate(chunks)
    ]
    d_normed_two = sum_last(sum_pairs(*sum_cores(d_norm_terms, 1)), *grad_parts)
    d_hidden = cot_own + rms_back(hidden, gain_two, d_normed_two)
    ffn_sent = [back_product(ffn_terms, at, 4) for at in (3, 2)]
    ffn_mine = back_product(ffn_terms, 0, 2)
    d_own = d_hidden.astype(BF16)
    d_one, d_two, ffn_mine, *ffn_sent = lax.optimization_barrier(
        (swap_first(d_own), swap_second(d_own), ffn_mine, *ffn_sent)
    )
    d_early = [swap_core(part) for part in (d_own, d_one, d_two)]
    arrived = [swap_core(piece) for piece in ffn_sent]
    half_rows = ffn_mine.shape[0] // 2
    ffn_far, ffn_near = y_first(
        ffn_mine[half_rows:] + arrived[0], ffn_mine[:half_rows] + arrived[1], core
    )
    d_last = after(swap_second(d_one), *d_early, ffn_far, ffn_near, reduced[0])
    d_attn = (d_own, d_one, d_two, d_last, *d_early, swap_core(d_last))

    d_heads = front_product(d_attn, attn_full, q_width, 0)
    other_reduced = [swap_x(reduced[0])]
    d_qkv = attend_back(qkv, depth, d_heads, heads, place, first, start_column, cos, sin)
    ffn_near = ffn_near + after(swap_y(ffn_far), d_qkv)
    d_qkv = after(d_qkv, ffn_near, other_reduced[0])
    ffn_sum = ffn_near[:own_rows].astype(F32) + swap_x(ffn_near[own_rows:]).astype(F32)
    result_own = (hidden + ffn_sum).astype(BF16)
    normed_far, normed_near = sum_cores(
        [
            (d_qkv, 0, attn_full, 1, q_width),
            (d_qkv, q_width // 128, attn_full, 2 * q_width // 128, 128),
        ]
    )
    normed_far = after(normed_far, *reduced[1:])
    attn_grad = weight_grads(
        d_attn, heads, q_width, 0, (qkv,), d_qkv, q_width + 128, 0
    )
    d_normed = sum_last(sum_pairs(normed_far, normed_near), attn_grad, result_own)
    tokens_grad_own = (d_hidden + rms_back(tokens_own, gain_one, d_normed)).astype(BF16)
    for part in range(1, len(chunks)):
        reduced[part] = after(reduced[part], attn_grad, tokens_grad_own)
        other_reduced.append(swap_x(reduced[part]))
    tokens_grad_beside = swap_y(tokens_grad_own)
    tokens_grad = share_in_ctx(tokens_grad_own, tokens_grad_beside, y, core)
    result_own = after(result_own, tokens_grad_own)
    result = share_in_ctx(result_own, swap_y(result_own), y, core)

    attn_reduced = lax.psum_scatter(attn_grad, "fsdp", scatter_dimension=0, tiled=True)
    attn_reduced = after(attn_reduced, tokens_grad_beside, *other_reduced)

    def gain_part(pairs):
        return sum(jnp.sum(mine.astype(F32) * grad.astype(F32), axis=1) for mine, grad in pairs)

    gain_sums = sum_all(
        jnp.stack(
            [
                gain_part([(attn_shard[:, q_width:], attn_reduced[:, q_width:])]),
                gain_part(
                    [
                        (ffn_shards[part][:, : 2 * chunk], reduced[part][:, : 2 * chunk])
                        for part, chunk in enumerate(chunks)
                    ]
                ),
            ]
        )
    )
    attn_gain_grad = gain_sums[0] / attn_gain.astype(F32)
    ffn_gain_grad = gain_sums[1] / ffn_gain.astype(F32)

    halves = [both_halves(mine, other, ctx) for mine, other in zip(reduced, other_reduced)]

    def ffn_out(which):
        return jnp.concatenate(
            [
                halves[part][side][:, which * chunk : (which + 1) * chunk]
                for side in range(2)
                for part, chunk in enumerate(chunks)
            ],
            axis=1,
        )

    attn_low, attn_high = both_halves(attn_reduced, swap_x(attn_reduced), ctx)

    def attn_out(begin, end):
        return jnp.concatenate([attn_low[:, begin:end], attn_high[:, begin:end]], axis=1)

    q_end, k_end = 2 * q_width, 2 * q_width + kv_width
    return (
        result,
        tokens_grad,
        attn_out(q_width, q_end),
        attn_out(q_end, k_end),
        attn_out(k_end, k_end + kv_width),
        attn_out(0, q_width),
        attn_gain_grad,
        ffn_out(0),
        ffn_out(1),
        ffn_out(2),
        ffn_gain_grad,
    )


def solution(mesh):
    rows = P(("fsdp", "ctx"), None)
    matrix = P("fsdp", "tp")
    vector = P("fsdp")
    return jax.shard_map(
        shards,
        mesh=mesh,
        in_specs=(
            rows,
            matrix,
            matrix,
            matrix,
            matrix,
            vector,
            matrix,
            matrix,
            matrix,
            vector,
            P("fsdp", None),
            P("fsdp", None),
            rows,
        ),
        out_specs=(
            rows,
            rows,
            matrix,
            matrix,
            matrix,
            matrix,
            vector,
            matrix,
            matrix,
            matrix,
            vector,
        ),
        check_vma=False,
    )
```

```python
import functools
import math

import jax
import jax.numpy as jnp
from jax import lax
from jax.experimental import pallas as pl
from jax.experimental.pallas import tpu as pltpu
from jax.sharding import PartitionSpec as P

HEAD_DIM = 64
EPSILON = 1e-05
ROPE_BASE = 500000.0
MASKED = -1e30
LOG2_E = 1.4426950408889634
BLOCK = 256
SPLIT = (1, 1)
VMEM = 56 * 2**20

F32 = jnp.float32
BF16 = jnp.bfloat16

PAIR = [(0, 1), (1, 0)]
CORE = [(0, 1), (1, 0), (2, 3), (3, 2)]
ACROSS = [(0, 2), (2, 0), (1, 3), (3, 1)]


def joint_pairs(x_core):
    pairs = []
    for ctx in range(2):
        for tp in range(4):
            there = (1 - ctx) * 4 + tp if tp % 2 == x_core else ctx * 4 + (tp ^ 2)
            pairs.append((ctx * 4 + tp, there))
    return pairs


FIRST = joint_pairs(0)
SECOND = joint_pairs(1)


def swap_core(v):
    return lax.ppermute(v, "tp", CORE)


def swap_y(v):
    return lax.ppermute(v, "tp", ACROSS)


def swap_x(v):
    return lax.ppermute(v, "ctx", PAIR)


def swap_first(v):
    return lax.ppermute(v, ("ctx", "tp"), FIRST)


def swap_second(v):
    return lax.ppermute(v, ("ctx", "tp"), SECOND)


def after(value, *others):
    return lax.optimization_barrier((value,) + others)[0]


def params(*semantics):
    return pltpu.CompilerParams(vmem_limit_bytes=VMEM)


def cost(gigaflops=0):
    return pl.CostEstimate(flops=int(gigaflops * 1e9) + 1, bytes_accessed=1, transcendentals=0)


def inv_rms(hidden):
    return lax.rsqrt(jnp.mean(hidden * hidden, axis=-1, keepdims=True) + EPSILON)


def rms_back(hidden, gain, grad):
    scale = inv_rms(hidden)
    weighted = grad * gain
    inner = jnp.mean(weighted * hidden, axis=-1, keepdims=True)
    return scale * weighted - hidden * (scale * scale * scale) * inner


def turn_lanes(u, first):
    return jnp.where(first, pltpu.roll(u, 96, 1), pltpu.roll(u, 32, 1))


def stream_scratch(count, rows, depth):
    return [pltpu.VMEM((2, rows, depth), BF16), pltpu.SemaphoreType.DMA((2,))] * count


def next_piece(refs, buffer, sems):
    i = pl.program_id(0)

    def copy_of(piece):
        return pltpu.make_async_copy(refs[piece], buffer.at[piece % 2], sems.at[piece % 2])

    @pl.when(i == 0)
    def _():
        copy_of(0).start()

    for piece in range(1, len(refs)):

        @pl.when(i == piece - 1)
        def _(piece=piece):
            copy_of(piece).start()

    for piece in range(len(refs)):

        @pl.when(i == piece)
        def _(piece=piece):
            copy_of(piece).wait()

    return buffer[lax.rem(i, 2)]


def qkv_kernel(count, *refs):
    gain_ref, wq_ref, wkv_ref, cos_ref, sin_ref, o_ref, buffer, sems = refs[count:]
    cos, sin = cos_ref[...], sin_ref[...]
    depth = gain_ref.shape[1]
    lane = lax.broadcasted_iota(jnp.int32, cos.shape, 1)
    first = (lane % 64) < 32
    x = next_piece(refs[:count], buffer, sems).astype(F32)
    x = (x * inv_rms(x) * gain_ref[...]).astype(BF16)
    o_ref[:, :depth] = x
    raw = jnp.dot(x, wq_ref[...], preferred_element_type=F32)
    tiles = raw.shape[1] // 128
    for tile in range(tiles):
        u = raw[:, tile * 128 : (tile + 1) * 128]
        turned = u * cos + turn_lanes(u, first) * sin
        o_ref[:, depth + tile * 128 : depth + (tile + 1) * 128] = turned.astype(BF16)
    u = jnp.dot(x, wkv_ref[...], preferred_element_type=F32)
    turned = u * cos + turn_lanes(u, first) * sin
    o_ref[:, depth + tiles * 128 :] = jnp.where(lane < 64, turned, u).astype(BF16)


def project_qkv(x, gain, w, q_width, cos, sin):
    step, depth = x[0].shape
    rows = len(x) * step
    width = depth + q_width + 128
    return pl.pallas_call(
        functools.partial(qkv_kernel, len(x)),
        out_shape=jax.ShapeDtypeStruct((rows, width), BF16),
        grid=(len(x),),
        in_specs=[pl.BlockSpec(memory_space=pl.ANY)] * len(x)
        + [
            pl.BlockSpec((1, depth), lambda i: (0, 0)),
            pl.BlockSpec((depth, q_width), lambda i: (0, 1)),
            pl.BlockSpec((depth, 128), lambda i: (0, 2 * q_width // 128)),
            pl.BlockSpec((step, 128), lambda i: (i, 0)),
            pl.BlockSpec((step, 128), lambda i: (i, 0)),
        ],
        out_specs=pl.BlockSpec((step, width), lambda i: (i, 0)),
        scratch_shapes=stream_scratch(1, step, depth),
        compiler_params=params(),
        cost_estimate=cost(),
        name="qkv",
    )(*x, gain, w, w, cos, sin)


def ffn_kernel(count, *refs):
    w_ref, o_ref, x_buffer, x_sems, c_buffer, c_sems = refs[2 * count :]
    n = w_ref.shape[1] // 3
    x = next_piece(refs[:count], x_buffer, x_sems)
    c = next_piece(refs[count : 2 * count], c_buffer, c_sems)
    gate = jnp.dot(x, w_ref[:, :n], preferred_element_type=F32)
    up = jnp.dot(x, w_ref[:, n : 2 * n], preferred_element_type=F32)
    d_mixed = jnp.dot(c, w_ref[:, 2 * n :], preferred_element_type=F32)
    sig = 1.0 / (1.0 + jnp.exp(-gate))
    silu = gate * sig
    o_ref[:, :n] = (d_mixed * up * (sig * (1.0 + gate * (1.0 - sig)))).astype(BF16)
    o_ref[:, n : 2 * n] = (d_mixed * silu).astype(BF16)
    o_ref[:, 2 * n :] = (silu * up).astype(BF16)


def ffn_chunk(x, cot, w):
    step, depth = x[0].shape
    rows = len(x) * step
    width = w.shape[1]
    return pl.pallas_call(
        functools.partial(ffn_kernel, len(x)),
        out_shape=jax.ShapeDtypeStruct((rows, width), BF16),
        grid=(len(x),),
        in_specs=[pl.BlockSpec(memory_space=pl.ANY)] * (2 * len(x))
        + [pl.BlockSpec((depth, width), lambda i: (0, 0))],
        out_specs=pl.BlockSpec((step, width), lambda i: (i, 0)),
        scratch_shapes=stream_scratch(2, step, depth),
        compiler_params=params(),
        cost_estimate=cost(),
        name="ffn",
    )(*x, *cot, w)


DOWN = (((0,), (0,)), ((), ()))


def grads_kernel(x_count, y_count, *refs):
    a_ref, b_ref, o_ref = refs[x_count + y_count :]
    split = a_ref.shape[1]

    def product(tall_refs, right_ref):
        tall = jnp.concatenate([ref[...] for ref in tall_refs], axis=0)
        return lax.dot_general(
            tall, right_ref[...].astype(BF16), DOWN, preferred_element_type=F32
        ).astype(BF16)

    o_ref[:, :split] = product(refs[:x_count], a_ref)
    o_ref[:, split:] = product(refs[x_count : x_count + y_count], b_ref)


def weight_grads(x, a, a_width, a_column, y, b, b_width, b_column):
    depth = x[0].shape[1]
    rows = a.shape[0]
    width = a_width + b_width
    step = 512
    return pl.pallas_call(
        functools.partial(grads_kernel, len(x), len(y)),
        out_shape=jax.ShapeDtypeStruct((depth, width), BF16),
        grid=(depth // step,),
        in_specs=[pl.BlockSpec((piece.shape[0], step), lambda i: (0, i)) for piece in (*x, *y)]
        + [
            pl.BlockSpec((rows, a_width), lambda i: (0, a_column)),
            pl.BlockSpec((rows, b_width), lambda i: (0, b_column)),
        ],
        out_specs=pl.BlockSpec((step, width), lambda i: (i, 0)),
        compiler_params=params(),
        cost_estimate=cost(),
        name="weight_grads",
    )(*x, *y, a, b)


def back_kernel(*refs):
    o_ref = refs[-1]
    count = (len(refs) - 1) // 2
    total = None
    for part in range(count):
        term = lax.dot_general(
            refs[part][...].astype(BF16),
            refs[count + part][...],
            (((1,), (1,)), ((), ())),
            preferred_element_type=F32,
        )
        total = term if total is None else total + term
    o_ref[...] = total.astype(BF16)


def back_product(terms, part, parts):
    rows = terms[0][0].shape[0] // parts
    depth = terms[0][2].shape[0]
    step = min(512, rows)
    ahead = part * (rows // step)
    return pl.pallas_call(
        back_kernel,
        out_shape=jax.ShapeDtypeStruct((rows, depth), BF16),
        grid=(rows // step,),
        in_specs=[
            pl.BlockSpec((step, term[4]), lambda i, column=term[1]: (i + ahead, column))
            for term in terms
        ]
        + [pl.BlockSpec((depth, term[4]), lambda i, column=term[3]: (0, column)) for term in terms],
        out_specs=pl.BlockSpec((step, depth), lambda i: (i, 0)),
        compiler_params=params(),
        cost_estimate=cost(),
        name="back",
    )(*[term[0] for term in terms], *[term[2] for term in terms])


def front_kernel(count, *refs):
    w_ref, o_ref, buffer, sems = refs[count:]
    x = next_piece(refs[:count], buffer, sems)
    o_ref[...] = jnp.dot(x, w_ref[...], preferred_element_type=F32).astype(BF16)


def front_product(x, w, width, column):
    step, depth = x[0].shape
    rows = len(x) * step
    return pl.pallas_call(
        functools.partial(front_kernel, len(x)),
        out_shape=jax.ShapeDtypeStruct((rows, width), BF16),
        grid=(len(x),),
        in_specs=[pl.BlockSpec(memory_space=pl.ANY)] * len(x)
        + [pl.BlockSpec((depth, width), lambda i: (0, column))],
        out_specs=pl.BlockSpec((step, width), lambda i: (i, 0)),
        scratch_shapes=stream_scratch(1, step, depth),
        compiler_params=params(),
        cost_estimate=cost(),
        name="front",
    )(*x, w)


def stack_heads(block):
    count = block.shape[1] // HEAD_DIM
    return jnp.concatenate(
        [block[:, h * HEAD_DIM : (h + 1) * HEAD_DIM] for h in range(count)], axis=0
    )


def unstack_heads(stacked):
    count = stacked.shape[0] // BLOCK
    return jnp.concatenate([stacked[h * BLOCK : (h + 1) * BLOCK] for h in range(count)], axis=1)


def allowed_of(i, j, start):
    row = i * BLOCK + lax.broadcasted_iota(jnp.int32, (BLOCK, BLOCK), 0)
    col = j * BLOCK + lax.broadcasted_iota(jnp.int32, (BLOCK, BLOCK), 1)
    return (col <= row) & (col >= start)


def attend_kernel(place, first, q_ref, kv_ref, start_ref, o_ref):
    i = pl.program_id(0)
    q = stack_heads(q_ref[...])
    heads = q.shape[0] // BLOCK
    start = start_ref[...]

    def step(j, carry):
        top, total, acc = carry
        at = pl.multiple_of(place[j] * BLOCK, BLOCK)
        kv = kv_ref[pl.ds(at, BLOCK), :]
        raw = lax.dot_general(
            q, kv[:, :HEAD_DIM], (((1,), (1,)), ((), ())), preferred_element_type=F32
        ) * (HEAD_DIM**-0.5 * LOG2_E)
        allowed = allowed_of(i, j, start)
        scores = jnp.where(allowed[None], raw.reshape(heads, BLOCK, BLOCK), MASKED).reshape(
            heads * BLOCK, BLOCK
        )
        new_top = jnp.maximum(top, jnp.max(scores, axis=-1, keepdims=True))
        keep = jnp.exp2(top - new_top)
        probs = jnp.exp2(scores - new_top)
        total = total * keep + jnp.sum(probs, axis=-1, keepdims=True)
        acc = acc * keep + jnp.dot(probs.astype(BF16), kv, preferred_element_type=F32)
        return (new_top, total, acc)

    size = heads * BLOCK
    top, total, acc = lax.fori_loop(
        first[i],
        i + 1,
        step,
        (
            jnp.full((size, 1), MASKED, F32),
            jnp.zeros((size, 1), F32),
            jnp.zeros((size, 2 * HEAD_DIM), F32),
        ),
    )
    out = acc[:, HEAD_DIM:] / total
    q_width = q_ref.shape[1]
    o_ref[:, :q_width] = unstack_heads(out)
    lse = top + jnp.log2(total)
    lane = lax.broadcasted_iota(jnp.int32, (BLOCK, 128), 1)
    packed = jnp.zeros((BLOCK, 128), F32)
    for h in range(heads):
        packed = jnp.where(lane == h, lse[h * BLOCK : (h + 1) * BLOCK], packed)
    o_ref[:, q_width:] = packed


def attend(qkv, depth, place, first, start, q_width):
    rows = qkv.shape[0]
    blocks = rows // BLOCK
    return pl.pallas_call(
        attend_kernel,
        out_shape=jax.ShapeDtypeStruct((rows, q_width + 128), F32),
        grid_spec=pltpu.PrefetchScalarGridSpec(
            num_scalar_prefetch=2,
            grid=(blocks,),
            in_specs=[
                pl.BlockSpec((BLOCK, q_width), lambda i, place, first: (place[i], depth // q_width)),
                pl.BlockSpec((rows, 128), lambda i, place, first: (0, (depth + q_width) // 128)),
                pl.BlockSpec((BLOCK, 1), lambda i, place, first: (i, 0)),
            ],
            out_specs=pl.BlockSpec((BLOCK, q_width + 128), lambda i, place, first: (place[i], 0)),
        ),
        compiler_params=params(),
        cost_estimate=cost(),
        name="attend",
    )(place, first, qkv, qkv, start)


def attend_back_kernel(
    place,
    first,
    q_ref,
    d_ref,
    h_ref,
    kv_ref,
    start_ref,
    cos_ref,
    sin_ref,
    o_ref,
    dkv_ref,
):
    i = pl.program_id(0)
    blocks = pl.num_programs(0)
    score_scale = HEAD_DIM**-0.5
    q_width = q_ref.shape[1]

    @pl.when(i == 0)
    def _():
        dkv_ref[...] = jnp.zeros_like(dkv_ref)

    q = stack_heads(q_ref[...])
    d_out = stack_heads(d_ref[...])
    heads = q.shape[0] // BLOCK
    out = stack_heads(h_ref[:, :q_width])
    delta = jnp.sum(d_out.astype(F32) * out, axis=-1, keepdims=True)
    lse_block = h_ref[:, q_width:]
    lse = jnp.concatenate([lse_block[:, h : h + 1] for h in range(heads)], axis=0)
    start = start_ref[...]

    def step(j, d_q):
        at = pl.multiple_of(place[j] * BLOCK, BLOCK)
        kv = kv_ref[pl.ds(at, BLOCK), :]
        k, v = kv[:, :HEAD_DIM], kv[:, HEAD_DIM:]
        across = (((1,), (1,)), ((), ()))
        down = (((0,), (0,)), ((), ()))
        raw = lax.dot_general(q, k, across, preferred_element_type=F32) * (score_scale * LOG2_E)
        allowed = allowed_of(i, j, start)
        scores = jnp.where(allowed[None], raw.reshape(heads, BLOCK, BLOCK), MASKED).reshape(
            heads * BLOCK, BLOCK
        )
        probs = jnp.exp2(scores - lse)
        d_probs = lax.dot_general(d_out, v, across, preferred_element_type=F32)
        d_scores = (probs * (d_probs - delta)).astype(BF16)
        d_k = lax.dot_general(d_scores, q, down, preferred_element_type=F32) * score_scale
        d_v = lax.dot_general(probs.astype(BF16), d_out, down, preferred_element_type=F32)
        here = pl.ds(pl.multiple_of(j * BLOCK, BLOCK), BLOCK)
        dkv_ref[here, :] += jnp.concatenate([d_k, d_v], axis=1)
        return d_q + jnp.dot(d_scores, k, preferred_element_type=F32)

    d_q = lax.fori_loop(first[i], i + 1, step, jnp.zeros((heads * BLOCK, HEAD_DIM), F32))
    d_q = unstack_heads(d_q * score_scale)
    lane = lax.broadcasted_iota(jnp.int32, (BLOCK, 128), 1)
    front = (lane % 64) < 32
    mine = pl.ds(pl.multiple_of(place[i] * BLOCK, BLOCK), BLOCK)
    cos, sin = cos_ref[mine, :], sin_ref[mine, :]
    for tile in range(q_width // 128):
        u = d_q[:, tile * 128 : (tile + 1) * 128]
        o_ref[mine, tile * 128 : (tile + 1) * 128] = (u * cos - turn_lanes(u, front) * sin).astype(
            BF16
        )

    @pl.when(i == blocks - 1)
    def _():
        for b in range(dkv_ref.shape[0] // BLOCK):
            there = pl.ds(pl.multiple_of(place[b] * BLOCK, BLOCK), BLOCK)
            u = dkv_ref[b * BLOCK : (b + 1) * BLOCK, :]
            turned = u * cos_ref[there, :] - turn_lanes(u, front) * sin_ref[there, :]
            o_ref[there, q_width:] = jnp.where(lane < HEAD_DIM, turned, u).astype(BF16)


def attend_back(qkv, depth, d_heads, heads, place, first, start, cos, sin):
    rows, q_width = d_heads.shape
    width = q_width + 128
    blocks = rows // BLOCK
    by_place = lambda i, place, first: (place[i], 0)
    whole = lambda i, place, first: (0, 0)
    return pl.pallas_call(
        attend_back_kernel,
        out_shape=jax.ShapeDtypeStruct((rows, width), BF16),
        grid_spec=pltpu.PrefetchScalarGridSpec(
            num_scalar_prefetch=2,
            grid=(blocks,),
            in_specs=[
                pl.BlockSpec((BLOCK, q_width), lambda i, place, first: (place[i], depth // q_width)),
                pl.BlockSpec((BLOCK, q_width), by_place),
                pl.BlockSpec((BLOCK, q_width + 128), by_place),
                pl.BlockSpec((rows, 128), lambda i, place, first: (0, (depth + q_width) // 128)),
                pl.BlockSpec((BLOCK, 1), lambda i, place, first: (i, 0)),
                pl.BlockSpec((rows, 128), whole),
                pl.BlockSpec((rows, 128), whole),
            ],
            out_specs=pl.BlockSpec((rows, width), whole),
            scratch_shapes=[pltpu.VMEM((rows, 128), F32)],
        ),
        compiler_params=params(),
        cost_estimate=cost(),
        name="attend_back",
    )(place, first, qkv, d_heads, heads, qkv, start, cos, sin)


def sum_cores(terms, pieces=2):
    sent = [back_product(terms, 2 * pieces - 1 - at, 2 * pieces) for at in range(pieces)]
    arrived = [swap_core(piece) for piece in sent]
    return add_blocks(back_product(terms, 0, 2), arrived)


def add_blocks(mine, arrived):
    rows = mine.shape[0] // 4
    each = 4 // len(arrived)
    blocks = []
    for at in range(4):
        other = arrived[len(arrived) - 1 - at // each]
        begin = (at % each) * rows
        blocks.append(mine[at * rows : (at + 1) * rows] + other[begin : begin + rows])
    return blocks


def sum_first(blocks, early=()):
    own, along_a, along_b, both = blocks
    along_a = along_a + after(swap_second(both), *early)
    return (own, *lax.optimization_barrier((along_a, along_b)))


def sum_last(own, along_a, along_b, beside=()):
    from_a = after(swap_first(along_a), *beside)
    return own.astype(F32) + swap_second(along_b).astype(F32) + from_a.astype(F32)


def sum_wide(terms, between, beside):
    arrived = swap_core(back_product(terms, 1, 2))
    mine = back_product(terms, 0, 2)
    rows = mine.shape[0] // 4
    far, near = mine[2 * rows :] + arrived[2 * rows :], mine[: 2 * rows] + arrived[: 2 * rows]
    near = after(near + swap_second(far), *between)
    from_a = after(swap_first(near[rows:]), *beside)
    return near[:rows].astype(F32) + from_a.astype(F32)


def share_rows(own, beside=()):
    beside = list(beside) + [()] * (2 - len(beside))
    one, two, *_ = lax.optimization_barrier((swap_first(own), swap_second(own), *beside[0]))
    early = tuple(swap_core(part) for part in (own, one, two))
    last = after(swap_second(one), *early, *beside[1])
    return (own, one, two, last, *early, swap_core(last))


def ring_over(shard, count, held):
    cycle = [(at, (at + 1) % count) for at in range(count)]
    pieces = [shard]
    for step in range(count - 1):
        sent = after(pieces[-1], *held) if step == 1 else pieces[-1]
        pieces.append(lax.ppermute(sent, "fsdp", cycle))
    return pieces


def in_place(pieces, axis):
    count, size = len(pieces), pieces[0].shape[axis]
    here = lax.axis_index("fsdp")
    shape = list(pieces[0].shape)
    shape[axis] *= count
    whole = jnp.zeros(shape, pieces[0].dtype)
    for back, piece in enumerate(pieces):
        owner = lax.rem(here + count - back, count)
        whole = lax.dynamic_update_slice_in_dim(whole, piece, owner * size, axis)
    return whole


def share_in_ctx(own, beside, y, core):
    pair = jnp.stack([own, beside])
    other = jnp.stack([swap_core(own), swap_core(beside)])
    four = jnp.stack([pair, other])
    four = jnp.where(y == 1, four[:, ::-1], four)
    four = jnp.where(core == 1, four[::-1], four)
    return four.transpose(1, 0, 2, 3).reshape(-1, own.shape[1])


def sum_all(v):
    v = v + swap_core(v)
    v = v + swap_y(v)
    return v + swap_x(v)


def both_halves(own, other, ctx):
    low = jnp.where(ctx == 0, own, other).astype(F32)
    high = jnp.where(ctx == 0, other, own).astype(F32)
    return low, high


def shards(
    tokens,
    q_weight,
    k_weight,
    v_weight,
    o_weight,
    attn_gain,
    gate_weight,
    up_weight,
    down_weight,
    ffn_gain,
    lengths,
    deal,
    cotangent,
):
    ctx = lax.axis_index("ctx")
    tp = lax.axis_index("tp")
    y, core = tp // 2, tp % 2
    row_count, depth = tokens.shape
    group_rows = row_count * lax.axis_size("ctx")
    own_rows = row_count // lax.axis_size("tp")

    def half(weight):
        width = weight.shape[1] // 2
        return lax.dynamic_slice_in_dim(weight, ctx * width, width, 1)

    length_row, deal_row = lengths[0], deal[0]
    spans = deal_row.shape[0]
    span_rows = group_rows // spans
    ends = jnp.cumsum(length_row, dtype=jnp.int32)
    starts = ends - length_row
    natural = jnp.arange(group_rows, dtype=jnp.int32)
    inside = (natural[:, None] >= starts[None]) & (natural[:, None] < ends[None])
    start_of = jnp.sum(jnp.where(inside, starts[None], 0), axis=1, dtype=jnp.int32)
    first = start_of[::BLOCK] // BLOCK
    rel = jnp.arange(group_rows // own_rows, dtype=jnp.int32)
    rel_core = core ^ (rel // 4)
    by_first, by_second = rel % 2, (rel // 2) % 2
    rel_ctx = ctx ^ jnp.where(rel_core == 0, by_first, by_second)
    rel_y = y ^ jnp.where(rel_core == 0, by_second, by_first)
    dealt_block = rel_ctx * (row_count // own_rows) + rel_y * 2 + rel_core
    per_span = span_rows // own_rows
    span_of = jnp.sum(
        jnp.where(
            (dealt_block // per_span)[:, None] == jnp.arange(spans, dtype=jnp.int32)[None],
            deal_row[None],
            0,
        ),
        axis=1,
        dtype=jnp.int32,
    )
    natural_block = span_of * per_span + dealt_block % per_span
    place = jnp.sum(
        jnp.where(natural_block[None, :] == rel[:, None], rel[None, :], 0), axis=1, dtype=jnp.int32
    )
    natural_rel = (
        natural_block[:, None] * own_rows + jnp.arange(own_rows, dtype=jnp.int32)[None]
    ).reshape(-1)
    inside_rel = (natural_rel[:, None] >= starts[None]) & (natural_rel[:, None] < ends[None])
    position = natural_rel - jnp.sum(
        jnp.where(inside_rel, starts[None], 0), axis=1, dtype=jnp.int32
    )
    lane = jnp.arange(128, dtype=jnp.int32)
    inverse = jnp.exp((lane % 32).astype(F32) * (-2.0 * math.log(ROPE_BASE) / HEAD_DIM))
    angles = position.astype(F32)[:, None] * inverse[None]
    cos = jnp.cos(angles)
    sin = jnp.where((lane % 64 < 32)[None], -jnp.sin(angles), jnp.sin(angles))
    start_column = start_of[:, None]

    q_half, k_half, v_half, o_half = map(half, (q_weight, k_weight, v_weight, o_weight))
    q_width, kv_width = q_half.shape[1], k_half.shape[1]
    attn_shard = jnp.concatenate([o_half, q_half, k_half, v_half], axis=1)
    fsdp = lax.axis_size("fsdp")
    gain_rows = jnp.stack([attn_gain, ffn_gain])
    gain_width = attn_gain.shape[0]
    extra = ((0, 14), (0, attn_shard.shape[1] - gain_width))
    tokens_low = lax.dynamic_slice_in_dim(tokens, tp * own_rows, own_rows, 0)
    cot_low = lax.dynamic_slice_in_dim(cotangent, tp * own_rows, own_rows, 0)
    tokens_one = swap_first(tokens_low)
    attn_ring = ring_over(
        jnp.concatenate([attn_shard, jnp.pad(gain_rows, extra)]),
        fsdp,
        (tokens_one, cos, sin, cot_low, place, first, start_column),
    )
    own_depth = attn_shard.shape[0]
    attn_full = in_place([piece[:own_depth] for piece in attn_ring], 0)
    gains = in_place([piece[own_depth : own_depth + 2, :gain_width] for piece in attn_ring], 1)
    gain_one = gains[0].astype(F32)[None]
    gain_two = gains[1].astype(F32)[None]
    ff_half = gate_weight.shape[1] // 2
    chunks = [ff_half * share // sum(SPLIT) for share in SPLIT]
    ffn_shards = []
    for part, chunk in enumerate(chunks):
        at = ctx * ff_half + sum(chunks[:part])
        ffn_shards.append(
            jnp.concatenate(
                [
                    lax.dynamic_slice_in_dim(weight, at, chunk, 1)
                    for weight in (gate_weight, up_weight, down_weight)
                ],
                axis=1,
            )
        )
    tokens_own, cot_own = tokens_low.astype(F32), cot_low.astype(F32)
    group_tokens = (tokens_low, tokens_one, swap_second(tokens_low), swap_second(tokens_one))
    first_shard = after(ffn_shards[0], attn_ring[-1], *group_tokens[2:])
    group_tokens = group_tokens + tuple(swap_core(part) for part in group_tokens)
    attn_full, cot_low, cos, sin, gain_one, *group_tokens = lax.optimization_barrier(
        (attn_full, cot_low, cos, sin, gain_one, *group_tokens)
    )
    qkv = project_qkv(group_tokens, gain_one, attn_full, q_width, cos, sin)
    heads = attend(qkv, depth, place, first, start_column, q_width)
    cot = share_rows(cot_low, [[qkv], [heads]])
    ffn_full = [
        lax.all_gather(shard, "fsdp", axis=0, tiled=True)
        for shard in (first_shard, after(ffn_shards[1], heads))
    ]
    heads = after(heads, *cot)
    attn_blocks = sum_cores([(heads, 0, attn_full, 0, q_width)])
    attn_sum = sum_last(*sum_first(attn_blocks), beside=ffn_full[:1])
    hidden = tokens_own + attn_sum
    normed_two = share_rows((hidden * inv_rms(hidden) * gain_two).astype(BF16))

    acts = []
    grad_parts = []

    def chunk_grads(part, held=()):
        chunk = chunks[part]
        act = after(acts[part], *held)
        grad_parts.append(weight_grads(normed_two, act, 2 * chunk, 0, cot, act, chunk, 2))

    last = len(chunks) - 1
    for part in range(len(chunks)):
        normed_two = (after(normed_two[0], *grad_parts), *normed_two[1:])
        acts.append(ffn_chunk(normed_two, cot, ffn_full[part]))
        if part < last:
            chunk_grads(part)
    d_norm_terms = [
        (acts[part], 0, ffn_full[part], 0, 2 * chunk) for part, chunk in enumerate(chunks)
    ]
    ffn_terms = [(acts[part], 2, ffn_full[part], 2, chunk) for part, chunk in enumerate(chunks)]
    ffn_sent = [back_product(ffn_terms, at, 4) for at in (3, 2)]
    ffn_mine = back_product(ffn_terms, 0, 2)
    chunk_grads(last)
    reduced = [
        lax.psum_scatter(part, "fsdp", scatter_dimension=0, tiled=True) for part in grad_parts
    ]
    d_normed_two = sum_wide(d_norm_terms, grad_parts, ffn_sent[:1])
    d_hidden = cot_own + rms_back(hidden, gain_two, d_normed_two)
    d_own = d_hidden.astype(BF16)
    ffn_own, ffn_a, ffn_b, ffn_both = add_blocks(ffn_mine, [swap_core(piece) for piece in ffn_sent])
    ffn_x, ffn_y = jnp.where(core == 0, ffn_a, ffn_b), jnp.where(core == 0, ffn_b, ffn_a)
    d_one, d_two, ffn_own, ffn_x, ffn_y, ffn_both = lax.optimization_barrier(
        (swap_first(d_own), swap_second(d_own), ffn_own, ffn_x, ffn_y, ffn_both)
    )
    d_early = [swap_core(part) for part in (d_own, d_one, d_two)]
    d_last = after(swap_second(d_one), *d_early, reduced[0])
    d_attn = (d_own, d_one, d_two, d_last, *d_early, swap_core(d_last))

    d_heads = front_product(d_attn, attn_full, q_width, 0)
    other_reduced = [swap_x(after(reduced[0], d_last))]
    d_qkv = attend_back(qkv, depth, d_heads, heads, place, first, start_column, cos, sin)
    y_both, y_own, d_qkv, other_reduced[0] = lax.optimization_barrier(
        (swap_y(ffn_both), swap_y(ffn_y), d_qkv, other_reduced[0])
    )
    ffn_x, ffn_own, d_qkv = lax.optimization_barrier((ffn_x + y_both, ffn_own + y_own, d_qkv))
    result_own = (hidden + (ffn_own.astype(F32) + swap_x(ffn_x).astype(F32))).astype(BF16)
    result_beside = swap_y(result_own)
    normed_blocks = sum_cores(
        [
            (d_qkv, 0, attn_full, 1, q_width),
            (d_qkv, q_width // 128, attn_full, 2 * q_width // 128, 128),
        ]
    )
    attn_grad = weight_grads(
        d_attn, heads, q_width, 0, (qkv,), after(d_qkv, result_own), q_width + 128, 0
    )
    d_normed = sum_last(*sum_first(normed_blocks, [attn_grad]), beside=reduced[1:])
    tokens_grad_own = (d_hidden + rms_back(tokens_own, gain_one, d_normed)).astype(BF16)
    for part in range(1, len(chunks)):
        reduced[part] = after(reduced[part], tokens_grad_own)
        other_reduced.append(swap_x(reduced[part]))
    attn_reduced = lax.psum_scatter(attn_grad, "fsdp", scatter_dimension=0, tiled=True)
    attn_reduced = after(attn_reduced, tokens_grad_own)
    tokens_grad_beside = after(swap_y(tokens_grad_own), attn_reduced)
    tokens_grad = share_in_ctx(tokens_grad_own, tokens_grad_beside, y, core)
    result_own, result_beside, _ = lax.optimization_barrier(
        (result_own, result_beside, tokens_grad_own)
    )
    result = share_in_ctx(result_own, result_beside, y, core)

    attn_late = after(attn_reduced, tokens_grad_beside)

    def gain_part(pairs):
        return sum(jnp.sum(mine.astype(F32) * grad.astype(F32), axis=1) for mine, grad in pairs)

    gain_sums = sum_all(
        jnp.stack(
            [
                gain_part([(attn_shard[:, q_width:], attn_late[:, q_width:])]),
                gain_part(
                    [
                        (ffn_shards[part][:, : 2 * chunk], reduced[part][:, : 2 * chunk])
                        for part, chunk in enumerate(chunks)
                    ]
                ),
            ]
        )
    )
    attn_gain_grad = gain_sums[0] / attn_gain.astype(F32)
    ffn_gain_grad = gain_sums[1] / ffn_gain.astype(F32)

    halves = [both_halves(mine, other, ctx) for mine, other in zip(reduced, other_reduced)]

    def ffn_out(which):
        return jnp.concatenate(
            [
                halves[part][side][:, which * chunk : (which + 1) * chunk]
                for side in range(2)
                for part, chunk in enumerate(chunks)
            ],
            axis=1,
        )

    attn_low, attn_high = both_halves(
        attn_reduced, swap_x(after(attn_reduced, *other_reduced[1:])), ctx
    )

    def attn_out(begin, end):
        return jnp.concatenate([attn_low[:, begin:end], attn_high[:, begin:end]], axis=1)

    q_end, k_end = 2 * q_width, 2 * q_width + kv_width
    return (
        result,
        tokens_grad,
        attn_out(q_width, q_end),
        attn_out(q_end, k_end),
        attn_out(k_end, k_end + kv_width),
        attn_out(0, q_width),
        attn_gain_grad,
        ffn_out(0),
        ffn_out(1),
        ffn_out(2),
        ffn_gain_grad,
    )


def solution(mesh):
    rows = P(("fsdp", "ctx"), None)
    matrix = P("fsdp", "tp")
    vector = P("fsdp")
    return jax.shard_map(
        shards,
        mesh=mesh,
        in_specs=(
            rows,
            matrix,
            matrix,
            matrix,
            matrix,
            vector,
            matrix,
            matrix,
            matrix,
            vector,
            P("fsdp", None),
            P("fsdp", None),
            rows,
        ),
        out_specs=(
            rows,
            rows,
            matrix,
            matrix,
            matrix,
            matrix,
            vector,
            matrix,
            matrix,
            matrix,
            vector,
        ),
        check_vma=False,
    )
```

```python
import functools
import math

import jax
import jax.numpy as jnp
from jax import lax
from jax.experimental import pallas as pl
from jax.experimental.pallas import tpu as pltpu
from jax.sharding import PartitionSpec as P

HEAD_DIM = 64
EPSILON = 1e-05
ROPE_BASE = 500000.0
MASKED = -1e30
LOG2_E = 1.4426950408889634
BLOCK = 256
SPLIT = (1, 1)
VMEM = 56 * 2**20

F32 = jnp.float32
BF16 = jnp.bfloat16

PAIR = [(0, 1), (1, 0)]
CORE = [(0, 1), (1, 0), (2, 3), (3, 2)]
ACROSS = [(0, 2), (2, 0), (1, 3), (3, 1)]


def joint_pairs(x_core):
    pairs = []
    for ctx in range(2):
        for tp in range(4):
            there = (1 - ctx) * 4 + tp if tp % 2 == x_core else ctx * 4 + (tp ^ 2)
            pairs.append((ctx * 4 + tp, there))
    return pairs


FIRST = joint_pairs(0)
SECOND = joint_pairs(1)


def swap_core(v):
    return lax.ppermute(v, "tp", CORE)


def swap_y(v):
    return lax.ppermute(v, "tp", ACROSS)


def swap_x(v):
    return lax.ppermute(v, "ctx", PAIR)


def swap_first(v):
    return lax.ppermute(v, ("ctx", "tp"), FIRST)


def swap_second(v):
    return lax.ppermute(v, ("ctx", "tp"), SECOND)


def after(value, *others):
    return lax.optimization_barrier((value,) + others)[0]


def params(*semantics):
    return pltpu.CompilerParams(vmem_limit_bytes=VMEM)


def cost(gigaflops=0):
    return pl.CostEstimate(flops=int(gigaflops * 1e9) + 1, bytes_accessed=1, transcendentals=0)


def inv_rms(hidden):
    return lax.rsqrt(jnp.mean(hidden * hidden, axis=-1, keepdims=True) + EPSILON)


def rms_back(hidden, gain, grad):
    scale = inv_rms(hidden)
    weighted = grad * gain
    inner = jnp.mean(weighted * hidden, axis=-1, keepdims=True)
    return scale * weighted - hidden * (scale * scale * scale) * inner


def turn_lanes(u, first):
    return jnp.where(first, pltpu.roll(u, 96, 1), pltpu.roll(u, 32, 1))


def stream_scratch(count, rows, depth):
    return [pltpu.VMEM((2, rows, depth), BF16), pltpu.SemaphoreType.DMA((2,))] * count


def next_piece(refs, buffer, sems):
    i = pl.program_id(0)

    def copy_of(piece):
        return pltpu.make_async_copy(refs[piece], buffer.at[piece % 2], sems.at[piece % 2])

    @pl.when(i == 0)
    def _():
        copy_of(0).start()

    for piece in range(1, len(refs)):

        @pl.when(i == piece - 1)
        def _(piece=piece):
            copy_of(piece).start()

    for piece in range(len(refs)):

        @pl.when(i == piece)
        def _(piece=piece):
            copy_of(piece).wait()

    return buffer[lax.rem(i, 2)]


def qkv_kernel(count, *refs):
    gain_ref, wq_ref, wkv_ref, cos_ref, sin_ref, o_ref, buffer, sems = refs[count:]
    cos, sin = cos_ref[...], sin_ref[...]
    depth = gain_ref.shape[1]
    lane = lax.broadcasted_iota(jnp.int32, cos.shape, 1)
    first = (lane % 64) < 32
    x = next_piece(refs[:count], buffer, sems).astype(F32)
    x = (x * inv_rms(x) * gain_ref[...]).astype(BF16)
    o_ref[:, :depth] = x
    raw = jnp.dot(x, wq_ref[...], preferred_element_type=F32)
    tiles = raw.shape[1] // 128
    for tile in range(tiles):
        u = raw[:, tile * 128 : (tile + 1) * 128]
        turned = u * cos + turn_lanes(u, first) * sin
        o_ref[:, depth + tile * 128 : depth + (tile + 1) * 128] = turned.astype(BF16)
    u = jnp.dot(x, wkv_ref[...], preferred_element_type=F32)
    turned = u * cos + turn_lanes(u, first) * sin
    o_ref[:, depth + tiles * 128 :] = jnp.where(lane < 64, turned, u).astype(BF16)


def project_qkv(x, gain, w, q_width, cos, sin):
    step, depth = x[0].shape
    rows = len(x) * step
    width = depth + q_width + 128
    return pl.pallas_call(
        functools.partial(qkv_kernel, len(x)),
        out_shape=jax.ShapeDtypeStruct((rows, width), BF16),
        grid=(len(x),),
        in_specs=[pl.BlockSpec(memory_space=pl.ANY)] * len(x)
        + [
            pl.BlockSpec((1, depth), lambda i: (0, 0)),
            pl.BlockSpec((depth, q_width), lambda i: (0, 1)),
            pl.BlockSpec((depth, 128), lambda i: (0, 2 * q_width // 128)),
            pl.BlockSpec((step, 128), lambda i: (i, 0)),
            pl.BlockSpec((step, 128), lambda i: (i, 0)),
        ],
        out_specs=pl.BlockSpec((step, width), lambda i: (i, 0)),
        scratch_shapes=stream_scratch(1, step, depth),
        compiler_params=params(),
        cost_estimate=cost(),
        name="qkv",
    )(*x, gain, w, w, cos, sin)


def ffn_kernel(count, *refs):
    w_ref, o_ref, x_buffer, x_sems, c_buffer, c_sems = refs[2 * count :]
    n = w_ref.shape[1] // 3
    x = next_piece(refs[:count], x_buffer, x_sems)
    c = next_piece(refs[count : 2 * count], c_buffer, c_sems)
    gate = jnp.dot(x, w_ref[:, :n], preferred_element_type=F32)
    up = jnp.dot(x, w_ref[:, n : 2 * n], preferred_element_type=F32)
    d_mixed = jnp.dot(c, w_ref[:, 2 * n :], preferred_element_type=F32)
    sig = 1.0 / (1.0 + jnp.exp(-gate))
    silu = gate * sig
    o_ref[:, :n] = (d_mixed * up * (sig * (1.0 + gate * (1.0 - sig)))).astype(BF16)
    o_ref[:, n : 2 * n] = (d_mixed * silu).astype(BF16)
    o_ref[:, 2 * n :] = (silu * up).astype(BF16)


def ffn_chunk(x, cot, w):
    step, depth = x[0].shape
    rows = len(x) * step
    width = w.shape[1]
    return pl.pallas_call(
        functools.partial(ffn_kernel, len(x)),
        out_shape=jax.ShapeDtypeStruct((rows, width), BF16),
        grid=(len(x),),
        in_specs=[pl.BlockSpec(memory_space=pl.ANY)] * (2 * len(x))
        + [pl.BlockSpec((depth, width), lambda i: (0, 0))],
        out_specs=pl.BlockSpec((step, width), lambda i: (i, 0)),
        scratch_shapes=stream_scratch(2, step, depth),
        compiler_params=params(),
        cost_estimate=cost(),
        name="ffn",
    )(*x, *cot, w)


DOWN = (((0,), (0,)), ((), ()))


def grads_kernel(x_count, y_count, *refs):
    a_ref, b_ref, o_ref = refs[x_count + y_count :]
    split = a_ref.shape[1]

    def product(tall_refs, right_ref):
        tall = jnp.concatenate([ref[...] for ref in tall_refs], axis=0)
        return lax.dot_general(
            tall, right_ref[...].astype(BF16), DOWN, preferred_element_type=F32
        ).astype(BF16)

    o_ref[:, :split] = product(refs[:x_count], a_ref)
    o_ref[:, split:] = product(refs[x_count : x_count + y_count], b_ref)


def weight_grads(x, a, a_width, a_column, y, b, b_width, b_column):
    depth = x[0].shape[1]
    rows = a.shape[0]
    width = a_width + b_width
    step = 512
    return pl.pallas_call(
        functools.partial(grads_kernel, len(x), len(y)),
        out_shape=jax.ShapeDtypeStruct((depth, width), BF16),
        grid=(depth // step,),
        in_specs=[pl.BlockSpec((piece.shape[0], step), lambda i: (0, i)) for piece in (*x, *y)]
        + [
            pl.BlockSpec((rows, a_width), lambda i: (0, a_column)),
            pl.BlockSpec((rows, b_width), lambda i: (0, b_column)),
        ],
        out_specs=pl.BlockSpec((step, width), lambda i: (i, 0)),
        compiler_params=params(),
        cost_estimate=cost(20),
        name="weight_grads",
    )(*x, *y, a, b)


def back_kernel(count, *refs):
    o_ref = refs[-1]
    total = refs[2 * count][...].astype(F32) if len(refs) > 2 * count + 1 else None
    for part in range(count):
        term = lax.dot_general(
            refs[part][...].astype(BF16),
            refs[count + part][...],
            (((1,), (1,)), ((), ())),
            preferred_element_type=F32,
        )
        total = term if total is None else total + term
    o_ref[...] = total.astype(BF16)


def back_product(terms, part=0, parts=1, plus=()):
    rows = terms[0][0].shape[0] // parts
    depth = terms[0][2].shape[0]
    step = min(512, rows)
    ahead = part * (rows // step)
    return pl.pallas_call(
        functools.partial(back_kernel, len(terms)),
        out_shape=jax.ShapeDtypeStruct((rows, depth), BF16),
        grid=(rows // step,),
        in_specs=[
            pl.BlockSpec((step, term[4]), lambda i, column=term[1]: (i + ahead, column))
            for term in terms
        ]
        + [pl.BlockSpec((depth, term[4]), lambda i, column=term[3]: (0, column)) for term in terms]
        + [pl.BlockSpec((step, depth), lambda i: (i + ahead, 0))] * len(plus),
        out_specs=pl.BlockSpec((step, depth), lambda i: (i, 0)),
        compiler_params=params(),
        cost_estimate=cost(),
        name="back",
    )(*[term[0] for term in terms], *[term[2] for term in terms], *plus)


def front_kernel(count, *refs):
    w_ref, o_ref, buffer, sems = refs[count:]
    x = next_piece(refs[:count], buffer, sems)
    o_ref[...] = jnp.dot(x, w_ref[...], preferred_element_type=F32).astype(BF16)


def front_product(x, w, width, column):
    step, depth = x[0].shape
    rows = len(x) * step
    return pl.pallas_call(
        functools.partial(front_kernel, len(x)),
        out_shape=jax.ShapeDtypeStruct((rows, width), BF16),
        grid=(len(x),),
        in_specs=[pl.BlockSpec(memory_space=pl.ANY)] * len(x)
        + [pl.BlockSpec((depth, width), lambda i: (0, column))],
        out_specs=pl.BlockSpec((step, width), lambda i: (i, 0)),
        scratch_shapes=stream_scratch(1, step, depth),
        compiler_params=params(),
        cost_estimate=cost(),
        name="front",
    )(*x, w)


def stack_heads(block):
    count = block.shape[1] // HEAD_DIM
    return jnp.concatenate(
        [block[:, h * HEAD_DIM : (h + 1) * HEAD_DIM] for h in range(count)], axis=0
    )


def unstack_heads(stacked):
    count = stacked.shape[0] // BLOCK
    return jnp.concatenate([stacked[h * BLOCK : (h + 1) * BLOCK] for h in range(count)], axis=1)


def allowed_of(i, j, start):
    row = i * BLOCK + lax.broadcasted_iota(jnp.int32, (BLOCK, BLOCK), 0)
    col = j * BLOCK + lax.broadcasted_iota(jnp.int32, (BLOCK, BLOCK), 1)
    return (col <= row) & (col >= start)


def attend_kernel(place, first, q_ref, kv_ref, start_ref, o_ref):
    i = pl.program_id(0)
    q = stack_heads(q_ref[...])
    heads = q.shape[0] // BLOCK
    start = start_ref[...]

    def step(j, carry):
        top, total, acc = carry
        at = pl.multiple_of(place[j] * BLOCK, BLOCK)
        kv = kv_ref[pl.ds(at, BLOCK), :]
        raw = lax.dot_general(
            q, kv[:, :HEAD_DIM], (((1,), (1,)), ((), ())), preferred_element_type=F32
        ) * (HEAD_DIM**-0.5 * LOG2_E)
        allowed = allowed_of(i, j, start)
        scores = jnp.where(allowed[None], raw.reshape(heads, BLOCK, BLOCK), MASKED).reshape(
            heads * BLOCK, BLOCK
        )
        new_top = jnp.maximum(top, jnp.max(scores, axis=-1, keepdims=True))
        keep = jnp.exp2(top - new_top)
        probs = jnp.exp2(scores - new_top)
        total = total * keep + jnp.sum(probs, axis=-1, keepdims=True)
        acc = acc * keep + jnp.dot(probs.astype(BF16), kv, preferred_element_type=F32)
        return (new_top, total, acc)

    size = heads * BLOCK
    top, total, acc = lax.fori_loop(
        first[i],
        i + 1,
        step,
        (
            jnp.full((size, 1), MASKED, F32),
            jnp.zeros((size, 1), F32),
            jnp.zeros((size, 2 * HEAD_DIM), F32),
        ),
    )
    out = acc[:, HEAD_DIM:] / total
    q_width = q_ref.shape[1]
    o_ref[:, :q_width] = unstack_heads(out)
    lse = top + jnp.log2(total)
    lane = lax.broadcasted_iota(jnp.int32, (BLOCK, 128), 1)
    packed = jnp.zeros((BLOCK, 128), F32)
    for h in range(heads):
        packed = jnp.where(lane == h, lse[h * BLOCK : (h + 1) * BLOCK], packed)
    o_ref[:, q_width:] = packed


def attend(qkv, depth, place, first, start, q_width):
    rows = qkv.shape[0]
    blocks = rows // BLOCK
    return pl.pallas_call(
        attend_kernel,
        out_shape=jax.ShapeDtypeStruct((rows, q_width + 128), F32),
        grid_spec=pltpu.PrefetchScalarGridSpec(
            num_scalar_prefetch=2,
            grid=(blocks,),
            in_specs=[
                pl.BlockSpec((BLOCK, q_width), lambda i, place, first: (place[i], depth // q_width)),
                pl.BlockSpec((rows, 128), lambda i, place, first: (0, (depth + q_width) // 128)),
                pl.BlockSpec((BLOCK, 1), lambda i, place, first: (i, 0)),
            ],
            out_specs=pl.BlockSpec((BLOCK, q_width + 128), lambda i, place, first: (place[i], 0)),
        ),
        compiler_params=params(),
        cost_estimate=cost(),
        name="attend",
    )(place, first, qkv, qkv, start)


def attend_back_kernel(
    place,
    first,
    q_ref,
    d_ref,
    h_ref,
    kv_ref,
    start_ref,
    cos_ref,
    sin_ref,
    o_ref,
    dkv_ref,
):
    i = pl.program_id(0)
    blocks = pl.num_programs(0)
    score_scale = HEAD_DIM**-0.5
    q_width = q_ref.shape[1]

    @pl.when(i == 0)
    def _():
        dkv_ref[...] = jnp.zeros_like(dkv_ref)

    q = stack_heads(q_ref[...])
    d_out = stack_heads(d_ref[...])
    heads = q.shape[0] // BLOCK
    out = stack_heads(h_ref[:, :q_width])
    delta = jnp.sum(d_out.astype(F32) * out, axis=-1, keepdims=True)
    lse_block = h_ref[:, q_width:]
    lse = jnp.concatenate([lse_block[:, h : h + 1] for h in range(heads)], axis=0)
    start = start_ref[...]

    def step(j, d_q):
        at = pl.multiple_of(place[j] * BLOCK, BLOCK)
        kv = kv_ref[pl.ds(at, BLOCK), :]
        k, v = kv[:, :HEAD_DIM], kv[:, HEAD_DIM:]
        across = (((1,), (1,)), ((), ()))
        down = (((0,), (0,)), ((), ()))
        raw = lax.dot_general(q, k, across, preferred_element_type=F32) * (score_scale * LOG2_E)
        allowed = allowed_of(i, j, start)
        scores = jnp.where(allowed[None], raw.reshape(heads, BLOCK, BLOCK), MASKED).reshape(
            heads * BLOCK, BLOCK
        )
        probs = jnp.exp2(scores - lse)
        d_probs = lax.dot_general(d_out, v, across, preferred_element_type=F32)
        d_scores = (probs * (d_probs - delta)).astype(BF16)
        d_k = lax.dot_general(d_scores, q, down, preferred_element_type=F32) * score_scale
        d_v = lax.dot_general(probs.astype(BF16), d_out, down, preferred_element_type=F32)
        here = pl.ds(pl.multiple_of(j * BLOCK, BLOCK), BLOCK)
        dkv_ref[here, :] += jnp.concatenate([d_k, d_v], axis=1)
        return d_q + jnp.dot(d_scores, k, preferred_element_type=F32)

    d_q = lax.fori_loop(first[i], i + 1, step, jnp.zeros((heads * BLOCK, HEAD_DIM), F32))
    d_q = unstack_heads(d_q * score_scale)
    lane = lax.broadcasted_iota(jnp.int32, (BLOCK, 128), 1)
    front = (lane % 64) < 32
    mine = pl.ds(pl.multiple_of(place[i] * BLOCK, BLOCK), BLOCK)
    cos, sin = cos_ref[mine, :], sin_ref[mine, :]
    for tile in range(q_width // 128):
        u = d_q[:, tile * 128 : (tile + 1) * 128]
        o_ref[mine, tile * 128 : (tile + 1) * 128] = (u * cos - turn_lanes(u, front) * sin).astype(
            BF16
        )

    @pl.when(i == blocks - 1)
    def _():
        for b in range(dkv_ref.shape[0] // BLOCK):
            there = pl.ds(pl.multiple_of(place[b] * BLOCK, BLOCK), BLOCK)
            u = dkv_ref[b * BLOCK : (b + 1) * BLOCK, :]
            turned = u * cos_ref[there, :] - turn_lanes(u, front) * sin_ref[there, :]
            o_ref[there, q_width:] = jnp.where(lane < HEAD_DIM, turned, u).astype(BF16)


def attend_back(qkv, depth, d_heads, heads, place, first, start, cos, sin):
    rows, q_width = d_heads.shape
    width = q_width + 128
    blocks = rows // BLOCK
    by_place = lambda i, place, first: (place[i], 0)
    whole = lambda i, place, first: (0, 0)
    return pl.pallas_call(
        attend_back_kernel,
        out_shape=jax.ShapeDtypeStruct((rows, width), BF16),
        grid_spec=pltpu.PrefetchScalarGridSpec(
            num_scalar_prefetch=2,
            grid=(blocks,),
            in_specs=[
                pl.BlockSpec((BLOCK, q_width), lambda i, place, first: (place[i], depth // q_width)),
                pl.BlockSpec((BLOCK, q_width), by_place),
                pl.BlockSpec((BLOCK, q_width + 128), by_place),
                pl.BlockSpec((rows, 128), lambda i, place, first: (0, (depth + q_width) // 128)),
                pl.BlockSpec((BLOCK, 1), lambda i, place, first: (i, 0)),
                pl.BlockSpec((rows, 128), whole),
                pl.BlockSpec((rows, 128), whole),
            ],
            out_specs=pl.BlockSpec((rows, width), whole),
            scratch_shapes=[pltpu.VMEM((rows, 128), F32)],
        ),
        compiler_params=params(),
        cost_estimate=cost(),
        name="attend_back",
    )(place, first, qkv, d_heads, heads, qkv, start, cos, sin)


def sum_cores(terms, pieces=2):
    sent = [back_product(terms, 2 * pieces - 1 - at, 2 * pieces) for at in range(pieces)]
    arrived = [swap_core(piece) for piece in sent]
    return add_blocks(back_product(terms, 0, 2), arrived)


def add_blocks(mine, arrived):
    rows = mine.shape[0] // 4
    each = 4 // len(arrived)
    blocks = []
    for at in range(4):
        other = arrived[len(arrived) - 1 - at // each]
        begin = (at % each) * rows
        blocks.append(mine[at * rows : (at + 1) * rows] + other[begin : begin + rows])
    return blocks


def sum_first(blocks, early=()):
    own, along_a, along_b, both = blocks
    along_a = along_a + after(swap_second(both), *early)
    return (own, *lax.optimization_barrier((along_a, along_b)))


def sum_last(own, along_a, along_b, beside=()):
    from_a = after(swap_first(along_a), *beside)
    return own.astype(F32) + swap_second(along_b).astype(F32) + from_a.astype(F32)


def halves_of_cores(terms, plus):
    arrived = swap_core(back_product(terms, 1, 2, plus))
    mine = back_product(terms, 0, 2, plus)
    rows = mine.shape[0] // 4
    return mine[2 * rows :] + arrived[2 * rows :], mine[: 2 * rows] + arrived[: 2 * rows]


def sum_wide(far, near, between, beside):
    rows = near.shape[0] // 2
    near = after(near + swap_second(far), *between)
    from_a = after(swap_first(near[rows:]), *beside)
    return near[:rows].astype(F32) + from_a.astype(F32)


def share_rows(own, beside=()):
    beside = list(beside) + [()] * (2 - len(beside))
    one, two, *_ = lax.optimization_barrier((swap_first(own), swap_second(own), *beside[0]))
    early = tuple(swap_core(part) for part in (own, one, two))
    last = after(swap_second(one), *early, *beside[1])
    return (own, one, two, last, *early, swap_core(last))


def ring_over(shard, count, held):
    cycle = [(at, (at + 1) % count) for at in range(count)]
    pieces = [shard]
    for step in range(count - 1):
        sent = after(pieces[-1], *held) if step == 1 else pieces[-1]
        pieces.append(lax.ppermute(sent, "fsdp", cycle))
    return pieces


def in_place(pieces, axis):
    count, size = len(pieces), pieces[0].shape[axis]
    here = lax.axis_index("fsdp")
    shape = list(pieces[0].shape)
    shape[axis] *= count
    whole = jnp.zeros(shape, pieces[0].dtype)
    for back, piece in enumerate(pieces):
        owner = lax.rem(here + count - back, count)
        whole = lax.dynamic_update_slice_in_dim(whole, piece, owner * size, axis)
    return whole


def share_in_ctx(own, beside, y, core):
    pair = jnp.stack([own, beside])
    other = jnp.stack([swap_core(own), swap_core(beside)])
    four = jnp.stack([pair, other])
    four = jnp.where(y == 1, four[:, ::-1], four)
    four = jnp.where(core == 1, four[::-1], four)
    return four.transpose(1, 0, 2, 3).reshape(-1, own.shape[1])


def sum_all(v):
    v = v + swap_core(v)
    v = v + swap_y(v)
    return v + swap_x(v)


def both_halves(own, other, ctx):
    low = jnp.where(ctx == 0, own, other).astype(F32)
    high = jnp.where(ctx == 0, other, own).astype(F32)
    return low, high


def shards(
    tokens,
    q_weight,
    k_weight,
    v_weight,
    o_weight,
    attn_gain,
    gate_weight,
    up_weight,
    down_weight,
    ffn_gain,
    lengths,
    deal,
    cotangent,
):
    ctx = lax.axis_index("ctx")
    tp = lax.axis_index("tp")
    y, core = tp // 2, tp % 2
    row_count, depth = tokens.shape
    group_rows = row_count * lax.axis_size("ctx")
    own_rows = row_count // lax.axis_size("tp")

    def half(weight):
        width = weight.shape[1] // 2
        return lax.dynamic_slice_in_dim(weight, ctx * width, width, 1)

    length_row, deal_row = lengths[0], deal[0]
    spans = deal_row.shape[0]
    span_rows = group_rows // spans
    ends = jnp.cumsum(length_row, dtype=jnp.int32)
    starts = ends - length_row
    natural = jnp.arange(group_rows, dtype=jnp.int32)
    inside = (natural[:, None] >= starts[None]) & (natural[:, None] < ends[None])
    start_of = jnp.sum(jnp.where(inside, starts[None], 0), axis=1, dtype=jnp.int32)
    first = start_of[::BLOCK] // BLOCK
    rel = jnp.arange(group_rows // own_rows, dtype=jnp.int32)
    rel_core = core ^ (rel // 4)
    by_first, by_second = rel % 2, (rel // 2) % 2
    rel_ctx = ctx ^ jnp.where(rel_core == 0, by_first, by_second)
    rel_y = y ^ jnp.where(rel_core == 0, by_second, by_first)
    dealt_block = rel_ctx * (row_count // own_rows) + rel_y * 2 + rel_core
    per_span = span_rows // own_rows
    span_of = jnp.sum(
        jnp.where(
            (dealt_block // per_span)[:, None] == jnp.arange(spans, dtype=jnp.int32)[None],
            deal_row[None],
            0,
        ),
        axis=1,
        dtype=jnp.int32,
    )
    natural_block = span_of * per_span + dealt_block % per_span
    place = jnp.sum(
        jnp.where(natural_block[None, :] == rel[:, None], rel[None, :], 0), axis=1, dtype=jnp.int32
    )
    natural_rel = (
        natural_block[:, None] * own_rows + jnp.arange(own_rows, dtype=jnp.int32)[None]
    ).reshape(-1)
    inside_rel = (natural_rel[:, None] >= starts[None]) & (natural_rel[:, None] < ends[None])
    position = natural_rel - jnp.sum(
        jnp.where(inside_rel, starts[None], 0), axis=1, dtype=jnp.int32
    )
    lane = jnp.arange(128, dtype=jnp.int32)
    inverse = jnp.exp((lane % 32).astype(F32) * (-2.0 * math.log(ROPE_BASE) / HEAD_DIM))
    angles = position.astype(F32)[:, None] * inverse[None]
    cos = jnp.cos(angles)
    sin = jnp.where((lane % 64 < 32)[None], -jnp.sin(angles), jnp.sin(angles))
    start_column = start_of[:, None]

    q_half, k_half, v_half, o_half = map(half, (q_weight, k_weight, v_weight, o_weight))
    q_width, kv_width = q_half.shape[1], k_half.shape[1]
    attn_shard = jnp.concatenate([o_half, q_half, k_half, v_half], axis=1)
    fsdp = lax.axis_size("fsdp")
    gain_rows = jnp.stack([attn_gain, ffn_gain])
    gain_width = attn_gain.shape[0]
    extra = ((0, 14), (0, attn_shard.shape[1] - gain_width))
    tokens_low = lax.dynamic_slice_in_dim(tokens, tp * own_rows, own_rows, 0)
    cot_low = lax.dynamic_slice_in_dim(cotangent, tp * own_rows, own_rows, 0)
    tokens_one = swap_first(tokens_low)
    attn_ring = ring_over(
        jnp.concatenate([attn_shard, jnp.pad(gain_rows, extra)]),
        fsdp,
        (tokens_one, cos, sin, cot_low, place, first, start_column),
    )
    own_depth = attn_shard.shape[0]
    attn_full = in_place([piece[:own_depth] for piece in attn_ring], 0)
    gains = in_place([piece[own_depth : own_depth + 2, :gain_width] for piece in attn_ring], 1)
    gain_one = gains[0].astype(F32)[None]
    gain_two = gains[1].astype(F32)[None]
    ff_half = gate_weight.shape[1] // 2
    chunks = [ff_half * share // sum(SPLIT) for share in SPLIT]
    ffn_shards = []
    for part, chunk in enumerate(chunks):
        at = ctx * ff_half + sum(chunks[:part])
        ffn_shards.append(
            jnp.concatenate(
                [
                    lax.dynamic_slice_in_dim(weight, at, chunk, 1)
                    for weight in (gate_weight, up_weight, down_weight)
                ],
                axis=1,
            )
        )
    tokens_own, cot_own = tokens_low.astype(F32), cot_low.astype(F32)
    group_tokens = (tokens_low, tokens_one, swap_second(tokens_low), swap_second(tokens_one))
    first_shard = after(ffn_shards[0], attn_ring[-1], *group_tokens[2:])
    group_tokens = group_tokens + tuple(swap_core(part) for part in group_tokens)
    attn_full, cot_low, cos, sin, gain_one, *group_tokens = lax.optimization_barrier(
        (attn_full, cot_low, cos, sin, gain_one, *group_tokens)
    )
    qkv = project_qkv(group_tokens, gain_one, attn_full, q_width, cos, sin)
    heads = attend(qkv, depth, place, first, start_column, q_width)
    cot = share_rows(cot_low, [[qkv], [heads]])
    ffn_full = [
        lax.all_gather(shard, "fsdp", axis=0, tiled=True)
        for shard in (first_shard, after(ffn_shards[1], heads))
    ]
    heads = after(heads, *cot)
    attn_blocks = sum_cores([(heads, 0, attn_full, 0, q_width)])
    attn_sum = sum_last(*sum_first(attn_blocks), beside=ffn_full[:1])
    hidden = tokens_own + attn_sum
    normed_two = share_rows((hidden * inv_rms(hidden) * gain_two).astype(BF16))

    acts = []
    grad_parts = []
    d_norm_partial = ()

    def chunk_grads(part, held=()):
        chunk = chunks[part]
        act = after(acts[part], *held)
        grad_parts.append(weight_grads(normed_two, act, 2 * chunk, 0, cot, act, chunk, 2))

    last = len(chunks) - 1
    for part in range(len(chunks)):
        normed_two = (after(normed_two[0], *grad_parts, *d_norm_partial), *normed_two[1:])
        acts.append(ffn_chunk(normed_two, cot, ffn_full[part]))
        d_norm_term = (acts[part], 0, ffn_full[part], 0, 2 * chunks[part])
        if part < last:
            chunk_grads(part)
            d_norm_partial = (back_product([d_norm_term], plus=d_norm_partial),)
    ffn_terms = [(acts[part], 2, ffn_full[part], 2, chunk) for part, chunk in enumerate(chunks)]
    ffn_sent = [back_product(ffn_terms, at, 4) for at in (3, 2)]
    ffn_mine = back_product(ffn_terms, 0, 2)
    d_norm_far, d_norm_near = halves_of_cores([d_norm_term], d_norm_partial)
    chunk_grads(last)
    reduced = [
        lax.psum_scatter(part, "fsdp", scatter_dimension=0, tiled=True) for part in grad_parts
    ]
    d_normed_two = sum_wide(d_norm_far, d_norm_near, grad_parts, ffn_sent[:1])
    d_hidden = cot_own + rms_back(hidden, gain_two, d_normed_two)
    d_own = d_hidden.astype(BF16)
    ffn_own, ffn_a, ffn_b, ffn_both = add_blocks(ffn_mine, [swap_core(piece) for piece in ffn_sent])
    ffn_x, ffn_y = jnp.where(core == 0, ffn_a, ffn_b), jnp.where(core == 0, ffn_b, ffn_a)
    d_one, d_two, ffn_own, ffn_x, ffn_y, ffn_both = lax.optimization_barrier(
        (swap_first(d_own), swap_second(d_own), ffn_own, ffn_x, ffn_y, ffn_both)
    )
    d_early = [swap_core(part) for part in (d_own, d_one, d_two)]
    d_last = after(swap_second(d_one), *d_early, reduced[0])
    d_attn = (d_own, d_one, d_two, d_last, *d_early, swap_core(d_last))

    d_heads = front_product(d_attn, attn_full, q_width, 0)
    other_reduced = [swap_x(after(reduced[0], d_last))]
    d_qkv = attend_back(qkv, depth, d_heads, heads, place, first, start_column, cos, sin)
    y_both, y_own, d_qkv, other_reduced[0] = lax.optimization_barrier(
        (swap_y(ffn_both), swap_y(ffn_y), d_qkv, other_reduced[0])
    )
    ffn_x, ffn_own, d_qkv = lax.optimization_barrier((ffn_x + y_both, ffn_own + y_own, d_qkv))
    ffn_far = swap_x(ffn_x)
    normed_blocks = sum_cores(
        [
            (d_qkv, 0, attn_full, 1, q_width),
            (d_qkv, q_width // 128, attn_full, 2 * q_width // 128, 128),
        ]
    )
    attn_grad = weight_grads(
        d_attn, heads, q_width, 0, (qkv,), after(d_qkv, normed_blocks[3]), q_width + 128, 0
    )
    ffn_far = after(ffn_far, attn_grad)
    result_own = (hidden + (ffn_own.astype(F32) + ffn_far.astype(F32))).astype(BF16)
    result_beside = swap_y(result_own)
    normed_first = sum_first(normed_blocks, [attn_grad, result_own])
    d_normed = sum_last(*normed_first, beside=[result_beside])
    tokens_grad_own = (d_hidden + rms_back(tokens_own, gain_one, d_normed)).astype(BF16)
    for part in range(1, len(chunks)):
        reduced[part] = after(reduced[part], tokens_grad_own)
        other_reduced.append(swap_x(reduced[part]))
    attn_reduced = lax.psum_scatter(attn_grad, "fsdp", scatter_dimension=0, tiled=True)
    attn_reduced = after(attn_reduced, tokens_grad_own)
    tokens_grad_beside, other_reduced[1:] = lax.optimization_barrier(
        (swap_y(tokens_grad_own), other_reduced[1:], attn_reduced)
    )[:2]
    tokens_grad = share_in_ctx(tokens_grad_own, tokens_grad_beside, y, core)
    result_own, result_beside, _ = lax.optimization_barrier(
        (result_own, result_beside, tokens_grad_beside)
    )
    result = share_in_ctx(result_own, result_beside, y, core)

    attn_late = after(attn_reduced, tokens_grad)

    def gain_part(pairs):
        return sum(jnp.sum(mine.astype(F32) * grad.astype(F32), axis=1) for mine, grad in pairs)

    gain_sums = sum_all(
        jnp.stack(
            [
                gain_part([(attn_shard[:, q_width:], attn_late[:, q_width:])]),
                gain_part(
                    [
                        (ffn_shards[part][:, : 2 * chunk], reduced[part][:, : 2 * chunk])
                        for part, chunk in enumerate(chunks)
                    ]
                ),
            ]
        )
    )
    attn_gain_grad = gain_sums[0] / attn_gain.astype(F32)
    ffn_gain_grad = gain_sums[1] / ffn_gain.astype(F32)

    halves = [both_halves(mine, other, ctx) for mine, other in zip(reduced, other_reduced)]

    def ffn_out(which):
        return jnp.concatenate(
            [
                halves[part][side][:, which * chunk : (which + 1) * chunk]
                for side in range(2)
                for part, chunk in enumerate(chunks)
            ],
            axis=1,
        )

    attn_low, attn_high = both_halves(attn_reduced, swap_x(attn_reduced), ctx)

    def attn_out(begin, end):
        return jnp.concatenate([attn_low[:, begin:end], attn_high[:, begin:end]], axis=1)

    q_end, k_end = 2 * q_width, 2 * q_width + kv_width
    return (
        result,
        tokens_grad,
        attn_out(q_width, q_end),
        attn_out(q_end, k_end),
        attn_out(k_end, k_end + kv_width),
        attn_out(0, q_width),
        attn_gain_grad,
        ffn_out(0),
        ffn_out(1),
        ffn_out(2),
        ffn_gain_grad,
    )


def solution(mesh):
    rows = P(("fsdp", "ctx"), None)
    matrix = P("fsdp", "tp")
    vector = P("fsdp")
    return jax.shard_map(
        shards,
        mesh=mesh,
        in_specs=(
            rows,
            matrix,
            matrix,
            matrix,
            matrix,
            vector,
            matrix,
            matrix,
            matrix,
            vector,
            P("fsdp", None),
            P("fsdp", None),
            rows,
        ),
        out_specs=(
            rows,
            rows,
            matrix,
            matrix,
            matrix,
            matrix,
            vector,
            matrix,
            matrix,
            matrix,
            vector,
        ),
        check_vma=False,
    )
```

```python
import functools
import math

import jax
import jax.numpy as jnp
from jax import lax
from jax.experimental import pallas as pl
from jax.experimental.pallas import tpu as pltpu
from jax.sharding import PartitionSpec as P

HEAD_DIM = 64
EPSILON = 1e-05
ROPE_BASE = 500000.0
MASKED = -1e30
LOG2_E = 1.4426950408889634
BLOCK = 256
SPLIT = (1, 1)
VMEM = 56 * 2**20

F32 = jnp.float32
BF16 = jnp.bfloat16

PAIR = [(0, 1), (1, 0)]
CORE = [(0, 1), (1, 0), (2, 3), (3, 2)]
ACROSS = [(0, 2), (2, 0), (1, 3), (3, 1)]


def joint_pairs(x_core):
    pairs = []
    for ctx in range(2):
        for tp in range(4):
            there = (1 - ctx) * 4 + tp if tp % 2 == x_core else ctx * 4 + (tp ^ 2)
            pairs.append((ctx * 4 + tp, there))
    return pairs


FIRST = joint_pairs(0)
SECOND = joint_pairs(1)


def swap_core(v):
    return lax.ppermute(v, "tp", CORE)


def swap_y(v):
    return lax.ppermute(v, "tp", ACROSS)


def swap_x(v):
    return lax.ppermute(v, "ctx", PAIR)


def swap_first(v):
    return lax.ppermute(v, ("ctx", "tp"), FIRST)


def swap_second(v):
    return lax.ppermute(v, ("ctx", "tp"), SECOND)


def after(value, *others):
    return lax.optimization_barrier((value,) + others)[0]


def params(*semantics):
    return pltpu.CompilerParams(vmem_limit_bytes=VMEM)


def cost(gigaflops=0):
    return pl.CostEstimate(flops=int(gigaflops * 1e9) + 1, bytes_accessed=1, transcendentals=0)


def inv_rms(hidden):
    return lax.rsqrt(jnp.mean(hidden * hidden, axis=-1, keepdims=True) + EPSILON)


def rms_back(hidden, gain, grad):
    scale = inv_rms(hidden)
    weighted = grad * gain
    inner = jnp.mean(weighted * hidden, axis=-1, keepdims=True)
    return scale * weighted - hidden * (scale * scale * scale) * inner


def norm_back_kernel(count, *refs):
    hidden_ref, gain_ref, kept_ref, o_ref = refs[count:]
    grad = sum(ref[...].astype(F32) for ref in refs[:count])
    back = rms_back(hidden_ref[...].astype(F32), gain_ref[...], grad)
    o_ref[...] = (kept_ref[...].astype(F32) + back).astype(BF16)


def norm_back(parts, hidden, gain, kept):
    rows, depth = hidden.shape
    step = min(64, rows)
    block = pl.BlockSpec((step, depth), lambda i: (i, 0))
    return pl.pallas_call(
        functools.partial(norm_back_kernel, len(parts)),
        out_shape=jax.ShapeDtypeStruct((rows, depth), BF16),
        grid=(rows // step,),
        in_specs=[block] * (len(parts) + 1)
        + [pl.BlockSpec((1, depth), lambda i: (0, 0)), block],
        out_specs=block,
        compiler_params=params(),
        cost_estimate=cost(),
        name="norm_back",
    )(*parts, hidden, gain, kept)


def turn_lanes(u, first):
    return jnp.where(first, pltpu.roll(u, 96, 1), pltpu.roll(u, 32, 1))


def stream_scratch(count, rows, depth):
    return [pltpu.VMEM((2, rows, depth), BF16), pltpu.SemaphoreType.DMA((2,))] * count


def next_piece(refs, buffer, sems):
    i = pl.program_id(0)

    def copy_of(piece):
        return pltpu.make_async_copy(refs[piece], buffer.at[piece % 2], sems.at[piece % 2])

    @pl.when(i == 0)
    def _():
        copy_of(0).start()

    for piece in range(1, len(refs)):

        @pl.when(i == piece - 1)
        def _(piece=piece):
            copy_of(piece).start()

    for piece in range(len(refs)):

        @pl.when(i == piece)
        def _(piece=piece):
            copy_of(piece).wait()

    return buffer[lax.rem(i, 2)]


def qkv_kernel(count, *refs):
    gain_ref, wq_ref, wkv_ref, cos_ref, sin_ref, o_ref, buffer, sems = refs[count:]
    cos, sin = cos_ref[...], sin_ref[...]
    depth = gain_ref.shape[1]
    lane = lax.broadcasted_iota(jnp.int32, cos.shape, 1)
    first = (lane % 64) < 32
    x = next_piece(refs[:count], buffer, sems).astype(F32)
    x = (x * inv_rms(x) * gain_ref[...]).astype(BF16)
    o_ref[:, :depth] = x
    raw = jnp.dot(x, wq_ref[...], preferred_element_type=F32)
    tiles = raw.shape[1] // 128
    for tile in range(tiles):
        u = raw[:, tile * 128 : (tile + 1) * 128]
        turned = u * cos + turn_lanes(u, first) * sin
        o_ref[:, depth + tile * 128 : depth + (tile + 1) * 128] = turned.astype(BF16)
    u = jnp.dot(x, wkv_ref[...], preferred_element_type=F32)
    turned = u * cos + turn_lanes(u, first) * sin
    o_ref[:, depth + tiles * 128 :] = jnp.where(lane < 64, turned, u).astype(BF16)


def project_qkv(x, gain, w, q_width, cos, sin):
    step, depth = x[0].shape
    rows = len(x) * step
    width = depth + q_width + 128
    return pl.pallas_call(
        functools.partial(qkv_kernel, len(x)),
        out_shape=jax.ShapeDtypeStruct((rows, width), BF16),
        grid=(len(x),),
        in_specs=[pl.BlockSpec(memory_space=pl.ANY)] * len(x)
        + [
            pl.BlockSpec((1, depth), lambda i: (0, 0)),
            pl.BlockSpec((depth, q_width), lambda i: (0, 1)),
            pl.BlockSpec((depth, 128), lambda i: (0, 2 * q_width // 128)),
            pl.BlockSpec((step, 128), lambda i: (i, 0)),
            pl.BlockSpec((step, 128), lambda i: (i, 0)),
        ],
        out_specs=pl.BlockSpec((step, width), lambda i: (i, 0)),
        scratch_shapes=stream_scratch(1, step, depth),
        compiler_params=params(),
        cost_estimate=cost(),
        name="qkv",
    )(*x, gain, w, w, cos, sin)


def ffn_kernel(count, *refs):
    w_ref, o_ref, x_buffer, x_sems, c_buffer, c_sems = refs[2 * count :]
    n = w_ref.shape[1] // 3
    x = next_piece(refs[:count], x_buffer, x_sems)
    c = next_piece(refs[count : 2 * count], c_buffer, c_sems)
    gate = jnp.dot(x, w_ref[:, :n], preferred_element_type=F32)
    up = jnp.dot(x, w_ref[:, n : 2 * n], preferred_element_type=F32)
    d_mixed = jnp.dot(c, w_ref[:, 2 * n :], preferred_element_type=F32)
    sig = 1.0 / (1.0 + jnp.exp(-gate))
    silu = gate * sig
    o_ref[:, :n] = (d_mixed * up * (sig * (1.0 + gate * (1.0 - sig)))).astype(BF16)
    o_ref[:, n : 2 * n] = (d_mixed * silu).astype(BF16)
    o_ref[:, 2 * n :] = (silu * up).astype(BF16)


def ffn_chunk(x, cot, w):
    step, depth = x[0].shape
    rows = len(x) * step
    width = w.shape[1]
    return pl.pallas_call(
        functools.partial(ffn_kernel, len(x)),
        out_shape=jax.ShapeDtypeStruct((rows, width), BF16),
        grid=(len(x),),
        in_specs=[pl.BlockSpec(memory_space=pl.ANY)] * (2 * len(x))
        + [pl.BlockSpec((depth, width), lambda i: (0, 0))],
        out_specs=pl.BlockSpec((step, width), lambda i: (i, 0)),
        scratch_shapes=stream_scratch(2, step, depth),
        compiler_params=params(),
        cost_estimate=cost(),
        name="ffn",
    )(*x, *cot, w)


DOWN = (((0,), (0,)), ((), ()))


def grads_kernel(x_count, y_count, *refs):
    a_ref, b_ref, o_ref = refs[x_count + y_count :]
    split = a_ref.shape[1]

    def product(tall_refs, right_ref):
        tall = jnp.concatenate([ref[...] for ref in tall_refs], axis=0)
        return lax.dot_general(
            tall, right_ref[...].astype(BF16), DOWN, preferred_element_type=F32
        ).astype(BF16)

    o_ref[:, :split] = product(refs[:x_count], a_ref)
    o_ref[:, split:] = product(refs[x_count : x_count + y_count], b_ref)


def weight_grads(x, a, a_width, a_column, y, b, b_width, b_column):
    depth = x[0].shape[1]
    rows = a.shape[0]
    width = a_width + b_width
    step = 512
    return pl.pallas_call(
        functools.partial(grads_kernel, len(x), len(y)),
        out_shape=jax.ShapeDtypeStruct((depth, width), BF16),
        grid=(depth // step,),
        in_specs=[pl.BlockSpec((piece.shape[0], step), lambda i: (0, i)) for piece in (*x, *y)]
        + [
            pl.BlockSpec((rows, a_width), lambda i: (0, a_column)),
            pl.BlockSpec((rows, b_width), lambda i: (0, b_column)),
        ],
        out_specs=pl.BlockSpec((step, width), lambda i: (i, 0)),
        compiler_params=params(),
        cost_estimate=cost(20),
        name="weight_grads",
    )(*x, *y, a, b)


def back_kernel(count, *refs):
    o_ref = refs[-1]
    total = refs[2 * count][...].astype(F32) if len(refs) > 2 * count + 1 else None
    for part in range(count):
        term = lax.dot_general(
            refs[part][...].astype(BF16),
            refs[count + part][...],
            (((1,), (1,)), ((), ())),
            preferred_element_type=F32,
        )
        total = term if total is None else total + term
    o_ref[...] = total.astype(BF16)


def back_product(terms, part=0, parts=1, plus=(), work=0):
    rows = terms[0][0].shape[0] // parts
    depth = terms[0][2].shape[0]
    step = min(512, rows)
    ahead = part * (rows // step)
    return pl.pallas_call(
        functools.partial(back_kernel, len(terms)),
        out_shape=jax.ShapeDtypeStruct((rows, depth), BF16),
        grid=(rows // step,),
        in_specs=[
            pl.BlockSpec((step, term[4]), lambda i, column=term[1]: (i + ahead, column))
            for term in terms
        ]
        + [pl.BlockSpec((depth, term[4]), lambda i, column=term[3]: (0, column)) for term in terms]
        + [pl.BlockSpec((step, depth), lambda i: (i + ahead, 0))] * len(plus),
        out_specs=pl.BlockSpec((step, depth), lambda i: (i, 0)),
        compiler_params=params(),
        cost_estimate=cost(work),
        name="back",
    )(*[term[0] for term in terms], *[term[2] for term in terms], *plus)


def front_kernel(count, *refs):
    w_ref, o_ref, buffer, sems = refs[count:]
    x = next_piece(refs[:count], buffer, sems)
    o_ref[...] = jnp.dot(x, w_ref[...], preferred_element_type=F32).astype(BF16)


def front_product(x, w, width, column):
    step, depth = x[0].shape
    rows = len(x) * step
    return pl.pallas_call(
        functools.partial(front_kernel, len(x)),
        out_shape=jax.ShapeDtypeStruct((rows, width), BF16),
        grid=(len(x),),
        in_specs=[pl.BlockSpec(memory_space=pl.ANY)] * len(x)
        + [pl.BlockSpec((depth, width), lambda i: (0, column))],
        out_specs=pl.BlockSpec((step, width), lambda i: (i, 0)),
        scratch_shapes=stream_scratch(1, step, depth),
        compiler_params=params(),
        cost_estimate=cost(),
        name="front",
    )(*x, w)


def stack_heads(block):
    count = block.shape[1] // HEAD_DIM
    return jnp.concatenate(
        [block[:, h * HEAD_DIM : (h + 1) * HEAD_DIM] for h in range(count)], axis=0
    )


def unstack_heads(stacked):
    count = stacked.shape[0] // BLOCK
    return jnp.concatenate([stacked[h * BLOCK : (h + 1) * BLOCK] for h in range(count)], axis=1)


def allowed_of(i, j, start):
    row = i * BLOCK + lax.broadcasted_iota(jnp.int32, (BLOCK, BLOCK), 0)
    col = j * BLOCK + lax.broadcasted_iota(jnp.int32, (BLOCK, BLOCK), 1)
    return (col <= row) & (col >= start)


def attend_kernel(place, first, q_ref, kv_ref, start_ref, o_ref):
    i = pl.program_id(0)
    q = stack_heads(q_ref[...])
    heads = q.shape[0] // BLOCK
    start = start_ref[...]

    def step(j, carry):
        top, total, acc = carry
        at = pl.multiple_of(place[j] * BLOCK, BLOCK)
        kv = kv_ref[pl.ds(at, BLOCK), :]
        raw = lax.dot_general(
            q, kv[:, :HEAD_DIM], (((1,), (1,)), ((), ())), preferred_element_type=F32
        ) * (HEAD_DIM**-0.5 * LOG2_E)
        allowed = allowed_of(i, j, start)
        scores = jnp.where(allowed[None], raw.reshape(heads, BLOCK, BLOCK), MASKED).reshape(
            heads * BLOCK, BLOCK
        )
        new_top = jnp.maximum(top, jnp.max(scores, axis=-1, keepdims=True))
        keep = jnp.exp2(top - new_top)
        probs = jnp.exp2(scores - new_top)
        total = total * keep + jnp.sum(probs, axis=-1, keepdims=True)
        acc = acc * keep + jnp.dot(probs.astype(BF16), kv, preferred_element_type=F32)
        return (new_top, total, acc)

    size = heads * BLOCK
    top, total, acc = lax.fori_loop(
        first[i],
        i + 1,
        step,
        (
            jnp.full((size, 1), MASKED, F32),
            jnp.zeros((size, 1), F32),
            jnp.zeros((size, 2 * HEAD_DIM), F32),
        ),
    )
    out = acc[:, HEAD_DIM:] / total
    q_width = q_ref.shape[1]
    o_ref[:, :q_width] = unstack_heads(out)
    lse = top + jnp.log2(total)
    lane = lax.broadcasted_iota(jnp.int32, (BLOCK, 128), 1)
    packed = jnp.zeros((BLOCK, 128), F32)
    for h in range(heads):
        packed = jnp.where(lane == h, lse[h * BLOCK : (h + 1) * BLOCK], packed)
    o_ref[:, q_width:] = packed


def attend(qkv, depth, place, first, start, q_width):
    rows = qkv.shape[0]
    blocks = rows // BLOCK
    return pl.pallas_call(
        attend_kernel,
        out_shape=jax.ShapeDtypeStruct((rows, q_width + 128), F32),
        grid_spec=pltpu.PrefetchScalarGridSpec(
            num_scalar_prefetch=2,
            grid=(blocks,),
            in_specs=[
                pl.BlockSpec((BLOCK, q_width), lambda i, place, first: (place[i], depth // q_width)),
                pl.BlockSpec((rows, 128), lambda i, place, first: (0, (depth + q_width) // 128)),
                pl.BlockSpec((BLOCK, 1), lambda i, place, first: (i, 0)),
            ],
            out_specs=pl.BlockSpec((BLOCK, q_width + 128), lambda i, place, first: (place[i], 0)),
        ),
        compiler_params=params(),
        cost_estimate=cost(),
        name="attend",
    )(place, first, qkv, qkv, start)


def attend_back_kernel(
    place,
    first,
    q_ref,
    d_ref,
    h_ref,
    kv_ref,
    start_ref,
    cos_ref,
    sin_ref,
    o_ref,
    dkv_ref,
):
    i = pl.program_id(0)
    blocks = pl.num_programs(0)
    score_scale = HEAD_DIM**-0.5
    q_width = q_ref.shape[1]

    @pl.when(i == 0)
    def _():
        dkv_ref[...] = jnp.zeros_like(dkv_ref)

    q = stack_heads(q_ref[...])
    d_out = stack_heads(d_ref[...])
    heads = q.shape[0] // BLOCK
    out = stack_heads(h_ref[:, :q_width])
    delta = jnp.sum(d_out.astype(F32) * out, axis=-1, keepdims=True)
    lse_block = h_ref[:, q_width:]
    lse = jnp.concatenate([lse_block[:, h : h + 1] for h in range(heads)], axis=0)
    start = start_ref[...]

    def step(j, d_q):
        at = pl.multiple_of(place[j] * BLOCK, BLOCK)
        kv = kv_ref[pl.ds(at, BLOCK), :]
        k, v = kv[:, :HEAD_DIM], kv[:, HEAD_DIM:]
        across = (((1,), (1,)), ((), ()))
        down = (((0,), (0,)), ((), ()))
        raw = lax.dot_general(q, k, across, preferred_element_type=F32) * (score_scale * LOG2_E)
        allowed = allowed_of(i, j, start)
        scores = jnp.where(allowed[None], raw.reshape(heads, BLOCK, BLOCK), MASKED).reshape(
            heads * BLOCK, BLOCK
        )
        probs = jnp.exp2(scores - lse)
        d_probs = lax.dot_general(d_out, v, across, preferred_element_type=F32)
        d_scores = (probs * (d_probs - delta)).astype(BF16)
        d_k = lax.dot_general(d_scores, q, down, preferred_element_type=F32) * score_scale
        d_v = lax.dot_general(probs.astype(BF16), d_out, down, preferred_element_type=F32)
        here = pl.ds(pl.multiple_of(j * BLOCK, BLOCK), BLOCK)
        dkv_ref[here, :] += jnp.concatenate([d_k, d_v], axis=1)
        return d_q + jnp.dot(d_scores, k, preferred_element_type=F32)

    d_q = lax.fori_loop(first[i], i + 1, step, jnp.zeros((heads * BLOCK, HEAD_DIM), F32))
    d_q = unstack_heads(d_q * score_scale)
    lane = lax.broadcasted_iota(jnp.int32, (BLOCK, 128), 1)
    front = (lane % 64) < 32
    mine = pl.ds(pl.multiple_of(place[i] * BLOCK, BLOCK), BLOCK)
    cos, sin = cos_ref[mine, :], sin_ref[mine, :]
    for tile in range(q_width // 128):
        u = d_q[:, tile * 128 : (tile + 1) * 128]
        o_ref[mine, tile * 128 : (tile + 1) * 128] = (u * cos - turn_lanes(u, front) * sin).astype(
            BF16
        )

    @pl.when(i == blocks - 1)
    def _():
        for b in range(dkv_ref.shape[0] // BLOCK):
            there = pl.ds(pl.multiple_of(place[b] * BLOCK, BLOCK), BLOCK)
            u = dkv_ref[b * BLOCK : (b + 1) * BLOCK, :]
            turned = u * cos_ref[there, :] - turn_lanes(u, front) * sin_ref[there, :]
            o_ref[there, q_width:] = jnp.where(lane < HEAD_DIM, turned, u).astype(BF16)


def attend_back(qkv, depth, d_heads, heads, place, first, start, cos, sin):
    rows, q_width = d_heads.shape
    width = q_width + 128
    blocks = rows // BLOCK
    by_place = lambda i, place, first: (place[i], 0)
    whole = lambda i, place, first: (0, 0)
    return pl.pallas_call(
        attend_back_kernel,
        out_shape=jax.ShapeDtypeStruct((rows, width), BF16),
        grid_spec=pltpu.PrefetchScalarGridSpec(
            num_scalar_prefetch=2,
            grid=(blocks,),
            in_specs=[
                pl.BlockSpec((BLOCK, q_width), lambda i, place, first: (place[i], depth // q_width)),
                pl.BlockSpec((BLOCK, q_width), by_place),
                pl.BlockSpec((BLOCK, q_width + 128), by_place),
                pl.BlockSpec((rows, 128), lambda i, place, first: (0, (depth + q_width) // 128)),
                pl.BlockSpec((BLOCK, 1), lambda i, place, first: (i, 0)),
                pl.BlockSpec((rows, 128), whole),
                pl.BlockSpec((rows, 128), whole),
            ],
            out_specs=pl.BlockSpec((rows, width), whole),
            scratch_shapes=[pltpu.VMEM((rows, 128), F32)],
        ),
        compiler_params=params(),
        cost_estimate=cost(),
        name="attend_back",
    )(place, first, qkv, d_heads, heads, qkv, start, cos, sin)


def sum_cores(terms, pieces=2):
    sent = [back_product(terms, 2 * pieces - 1 - at, 2 * pieces) for at in range(pieces)]
    arrived = [swap_core(piece) for piece in sent]
    return add_blocks(back_product(terms, 0, 2), arrived)


def add_blocks(mine, arrived):
    rows = mine.shape[0] // 4
    each = 4 // len(arrived)
    blocks = []
    for at in range(4):
        other = arrived[len(arrived) - 1 - at // each]
        begin = (at % each) * rows
        blocks.append(mine[at * rows : (at + 1) * rows] + other[begin : begin + rows])
    return blocks


def sum_first(blocks, early=()):
    own, along_a, along_b, both = blocks
    along_a = along_a + after(swap_second(both), *early)
    return (own, *lax.optimization_barrier((along_a, along_b)))


def last_parts(own, along_a, along_b, beside=()):
    return own, swap_second(along_b), after(swap_first(along_a), *beside)


def halves_of_cores(terms, plus):
    arrived = swap_core(back_product(terms, 1, 2, plus))
    mine = back_product(terms, 0, 2, plus)
    rows = mine.shape[0] // 4
    return mine[2 * rows :] + arrived[2 * rows :], mine[: 2 * rows] + arrived[: 2 * rows]


def wide_first(far, near, between):
    return after(near + swap_second(far), *between)


def wide_last(near, beside):
    return near, after(swap_first(near[near.shape[0] // 2 :]), *beside)


def share_rows(own, beside=()):
    beside = list(beside) + [()] * (2 - len(beside))
    one, two, *_ = lax.optimization_barrier((swap_first(own), swap_second(own), *beside[0]))
    early = tuple(swap_core(part) for part in (own, one, two))
    last = after(swap_second(one), *early, *beside[1])
    return (own, one, two, last, *early, swap_core(last))


def ring_over(shard, count, held):
    cycle = [(at, (at + 1) % count) for at in range(count)]
    pieces = [shard]
    for step in range(count - 1):
        sent = after(pieces[-1], *held) if step == 1 else pieces[-1]
        pieces.append(lax.ppermute(sent, "fsdp", cycle))
    return pieces


def in_place(pieces, axis):
    count, size = len(pieces), pieces[0].shape[axis]
    here = lax.axis_index("fsdp")
    shape = list(pieces[0].shape)
    shape[axis] *= count
    whole = jnp.zeros(shape, pieces[0].dtype)
    for back, piece in enumerate(pieces):
        owner = lax.rem(here + count - back, count)
        whole = lax.dynamic_update_slice_in_dim(whole, piece, owner * size, axis)
    return whole


def share_in_ctx(own, beside, y, core):
    pair = jnp.stack([own, beside])
    other = jnp.stack([swap_core(own), swap_core(beside)])
    four = jnp.stack([pair, other])
    four = jnp.where(y == 1, four[:, ::-1], four)
    four = jnp.where(core == 1, four[::-1], four)
    return four.transpose(1, 0, 2, 3).reshape(-1, own.shape[1])


def both_halves(own, other, ctx):
    low = jnp.where(ctx == 0, own, other).astype(F32)
    high = jnp.where(ctx == 0, other, own).astype(F32)
    return low, high


def shards(
    tokens,
    q_weight,
    k_weight,
    v_weight,
    o_weight,
    attn_gain,
    gate_weight,
    up_weight,
    down_weight,
    ffn_gain,
    lengths,
    deal,
    cotangent,
):
    ctx = lax.axis_index("ctx")
    tp = lax.axis_index("tp")
    y, core = tp // 2, tp % 2
    row_count, depth = tokens.shape
    group_rows = row_count * lax.axis_size("ctx")
    own_rows = row_count // lax.axis_size("tp")

    def half(weight):
        width = weight.shape[1] // 2
        return lax.dynamic_slice_in_dim(weight, ctx * width, width, 1)

    length_row, deal_row = lengths[0], deal[0]
    spans = deal_row.shape[0]
    span_rows = group_rows // spans
    ends = jnp.cumsum(length_row, dtype=jnp.int32)
    starts = ends - length_row
    natural = jnp.arange(group_rows, dtype=jnp.int32)
    inside = (natural[:, None] >= starts[None]) & (natural[:, None] < ends[None])
    start_of = jnp.sum(jnp.where(inside, starts[None], 0), axis=1, dtype=jnp.int32)
    first = start_of[::BLOCK] // BLOCK
    rel = jnp.arange(group_rows // own_rows, dtype=jnp.int32)
    rel_core = core ^ (rel // 4)
    by_first, by_second = rel % 2, (rel // 2) % 2
    rel_ctx = ctx ^ jnp.where(rel_core == 0, by_first, by_second)
    rel_y = y ^ jnp.where(rel_core == 0, by_second, by_first)
    dealt_block = rel_ctx * (row_count // own_rows) + rel_y * 2 + rel_core
    per_span = span_rows // own_rows
    span_of = jnp.sum(
        jnp.where(
            (dealt_block // per_span)[:, None] == jnp.arange(spans, dtype=jnp.int32)[None],
            deal_row[None],
            0,
        ),
        axis=1,
        dtype=jnp.int32,
    )
    natural_block = span_of * per_span + dealt_block % per_span
    place = jnp.sum(
        jnp.where(natural_block[None, :] == rel[:, None], rel[None, :], 0), axis=1, dtype=jnp.int32
    )
    natural_rel = (
        natural_block[:, None] * own_rows + jnp.arange(own_rows, dtype=jnp.int32)[None]
    ).reshape(-1)
    inside_rel = (natural_rel[:, None] >= starts[None]) & (natural_rel[:, None] < ends[None])
    position = natural_rel - jnp.sum(
        jnp.where(inside_rel, starts[None], 0), axis=1, dtype=jnp.int32
    )
    lane = jnp.arange(128, dtype=jnp.int32)
    inverse = jnp.exp((lane % 32).astype(F32) * (-2.0 * math.log(ROPE_BASE) / HEAD_DIM))
    angles = position.astype(F32)[:, None] * inverse[None]
    cos = jnp.cos(angles)
    sin = jnp.where((lane % 64 < 32)[None], -jnp.sin(angles), jnp.sin(angles))
    start_column = start_of[:, None]

    q_half, k_half, v_half, o_half = map(half, (q_weight, k_weight, v_weight, o_weight))
    q_width, kv_width = q_half.shape[1], k_half.shape[1]
    attn_shard = jnp.concatenate([o_half, q_half, k_half, v_half], axis=1)
    fsdp = lax.axis_size("fsdp")
    gain_rows = jnp.stack([attn_gain, ffn_gain])
    gain_width = attn_gain.shape[0]
    extra = ((0, 14), (0, attn_shard.shape[1] - gain_width))
    tokens_low = lax.dynamic_slice_in_dim(tokens, tp * own_rows, own_rows, 0)
    cot_low = lax.dynamic_slice_in_dim(cotangent, tp * own_rows, own_rows, 0)
    tokens_one = swap_first(tokens_low)
    attn_ring = ring_over(
        jnp.concatenate([attn_shard, jnp.pad(gain_rows, extra)]),
        fsdp,
        (tokens_one, cos, sin, cot_low, place, first, start_column),
    )
    own_depth = attn_shard.shape[0]
    attn_full = in_place([piece[:own_depth] for piece in attn_ring], 0)
    gains = in_place([piece[own_depth : own_depth + 2, :gain_width] for piece in attn_ring], 1)
    gain_one = gains[0].astype(F32)[None]
    gain_two = gains[1].astype(F32)[None]
    ff_half = gate_weight.shape[1] // 2
    chunks = [ff_half * share // sum(SPLIT) for share in SPLIT]
    ffn_shards = []
    for part, chunk in enumerate(chunks):
        at = ctx * ff_half + sum(chunks[:part])
        ffn_shards.append(
            jnp.concatenate(
                [
                    lax.dynamic_slice_in_dim(weight, at, chunk, 1)
                    for weight in (gate_weight, up_weight, down_weight)
                ],
                axis=1,
            )
        )
    tokens_own, cot_own = tokens_low.astype(F32), cot_low.astype(F32)
    group_tokens = (tokens_low, tokens_one, swap_second(tokens_low), swap_second(tokens_one))
    first_shard = after(ffn_shards[0], attn_ring[-1], *group_tokens[2:])
    group_tokens = group_tokens + tuple(swap_core(part) for part in group_tokens)
    attn_full, cot_low, cos, sin, gain_one, *group_tokens = lax.optimization_barrier(
        (attn_full, cot_low, cos, sin, gain_one, *group_tokens)
    )
    qkv = project_qkv(group_tokens, gain_one, attn_full, q_width, cos, sin)
    heads = attend(qkv, depth, place, first, start_column, q_width)
    cot = share_rows(cot_low, [[qkv], [heads]])
    ffn_full = [
        lax.all_gather(shard, "fsdp", axis=0, tiled=True)
        for shard in (first_shard, after(ffn_shards[1], heads))
    ]
    heads = after(heads, *cot)
    attn_blocks = sum_cores([(heads, 0, attn_full, 0, q_width)])
    attn_parts = last_parts(*sum_first(attn_blocks), beside=ffn_full[:1])
    attn_sum = sum(part.astype(F32) for part in attn_parts)
    hidden = tokens_own + attn_sum
    normed_two = share_rows((hidden * inv_rms(hidden) * gain_two).astype(BF16))

    acts = []
    grad_parts = []
    d_norm_partial = ()

    def chunk_grads(part, held=()):
        chunk = chunks[part]
        act = after(acts[part], *held)
        grad_parts.append(weight_grads(normed_two, act, 2 * chunk, 0, cot, act, chunk, 2))

    last = len(chunks) - 1
    for part in range(len(chunks)):
        normed_two = (after(normed_two[0], *grad_parts, *d_norm_partial), *normed_two[1:])
        acts.append(ffn_chunk(normed_two, cot, ffn_full[part]))
        d_norm_term = (acts[part], 0, ffn_full[part], 0, 2 * chunks[part])
        if part < last:
            chunk_grads(part)
            d_norm_partial = (back_product([d_norm_term], plus=d_norm_partial),)
    ffn_terms = [(acts[part], 2, ffn_full[part], 2, chunk) for part, chunk in enumerate(chunks)]
    d_norm_far, d_norm_near = halves_of_cores([d_norm_term], d_norm_partial)
    chunk_grads(last, (d_norm_far,))
    reduced = [
        lax.psum_scatter(part, "fsdp", scatter_dimension=0, tiled=True) for part in grad_parts
    ]
    d_norm_near = wide_first(d_norm_far, d_norm_near, grad_parts)

    def ffn_rows(part, parts, held):
        (act, *rest), *others = ffn_terms
        return back_product([(after(act, held), *rest), *others], part, parts, work=7)

    ffn_sent = [ffn_rows(3, 4, d_norm_near)]
    d_own = norm_back(wide_last(d_norm_near, ffn_sent), hidden, gain_two, cot_low)
    ffn_sent.append(ffn_rows(2, 4, d_own))
    ffn_mine = ffn_rows(0, 2, d_own)
    ffn_own, ffn_a, ffn_b, ffn_both = add_blocks(ffn_mine, [swap_core(piece) for piece in ffn_sent])
    ffn_x, ffn_y = jnp.where(core == 0, ffn_a, ffn_b), jnp.where(core == 0, ffn_b, ffn_a)
    d_one, d_two, ffn_own, ffn_x, ffn_y, ffn_both = lax.optimization_barrier(
        (swap_first(d_own), swap_second(d_own), ffn_own, ffn_x, ffn_y, ffn_both)
    )
    d_early = [swap_core(part) for part in (d_own, d_one, d_two)]
    d_last = after(swap_second(d_one), *d_early, reduced[0])
    d_attn = (d_own, d_one, d_two, d_last, *d_early, swap_core(d_last))

    d_heads = front_product(d_attn, attn_full, q_width, 0)
    other_reduced = [swap_x(after(reduced[0], d_last))]
    d_qkv = attend_back(qkv, depth, d_heads, heads, place, first, start_column, cos, sin)
    y_both, y_own, d_qkv, other_reduced[0] = lax.optimization_barrier(
        (swap_y(ffn_both), swap_y(ffn_y), d_qkv, other_reduced[0])
    )
    ffn_x, ffn_own, d_qkv = lax.optimization_barrier((ffn_x + y_both, ffn_own + y_own, d_qkv))
    ffn_far = swap_x(ffn_x)
    normed_blocks = sum_cores(
        [
            (d_qkv, 0, attn_full, 1, q_width),
            (d_qkv, q_width // 128, attn_full, 2 * q_width // 128, 128),
        ]
    )
    attn_grad = weight_grads(
        d_attn, heads, q_width, 0, (qkv,), after(d_qkv, normed_blocks[3]), q_width + 128, 0
    )
    ffn_far = after(ffn_far, attn_grad)
    result_own = (hidden + (ffn_own.astype(F32) + ffn_far.astype(F32))).astype(BF16)
    result_beside = swap_y(result_own)
    normed_first = sum_first(normed_blocks, [attn_grad, result_own])
    for part in range(1, len(chunks)):
        reduced[part] = after(reduced[part], normed_first[1])
        other_reduced.append(swap_x(reduced[part]))
    normed_parts = last_parts(*normed_first, beside=[result_beside, *other_reduced[1:]])
    tokens_grad_own = norm_back(normed_parts, tokens_low, gain_one, d_own)
    attn_reduced = lax.psum_scatter(attn_grad, "fsdp", scatter_dimension=0, tiled=True)
    attn_reduced = after(attn_reduced, tokens_grad_own)
    other_attn = swap_x(attn_reduced)
    result_own, result_beside, _ = lax.optimization_barrier(
        (result_own, result_beside, tokens_grad_own)
    )
    result = share_in_ctx(result_own, result_beside, y, core)

    def gain_part(pairs):
        return sum(jnp.sum(mine.astype(F32) * grad.astype(F32), axis=1) for mine, grad in pairs)

    gain_sums = jnp.stack(
        [
            gain_part([(attn_shard[:, q_width:], attn_reduced[:, q_width:])]),
            gain_part(
                [
                    (ffn_shards[part][:, : 2 * chunk], reduced[part][:, : 2 * chunk])
                    for part, chunk in enumerate(chunks)
                ]
            ),
        ]
    )
    gain_sums = gain_sums + swap_core(gain_sums)

    halves = [both_halves(mine, other, ctx) for mine, other in zip(reduced, other_reduced)]

    def ffn_out(which):
        return jnp.concatenate(
            [
                halves[part][side][:, which * chunk : (which + 1) * chunk]
                for side in range(2)
                for part, chunk in enumerate(chunks)
            ],
            axis=1,
        )

    ffn_grads = [ffn_out(which) for which in range(3)]
    tokens_grad_beside, gain_sums, other_attn, result, *ffn_grads = lax.optimization_barrier(
        (swap_y(tokens_grad_own), gain_sums, other_attn, result, *ffn_grads)
    )
    tokens_grad = share_in_ctx(tokens_grad_own, tokens_grad_beside, y, core)
    gain_sums = gain_sums + swap_y(gain_sums)
    gain_sums = gain_sums + swap_x(gain_sums)
    attn_gain_grad = gain_sums[0] / attn_gain.astype(F32)
    ffn_gain_grad = gain_sums[1] / ffn_gain.astype(F32)
    attn_low, attn_high = both_halves(attn_reduced, other_attn, ctx)

    def attn_out(begin, end):
        return jnp.concatenate([attn_low[:, begin:end], attn_high[:, begin:end]], axis=1)

    q_end, k_end = 2 * q_width, 2 * q_width + kv_width
    return (
        result,
        tokens_grad,
        attn_out(q_width, q_end),
        attn_out(q_end, k_end),
        attn_out(k_end, k_end + kv_width),
        attn_out(0, q_width),
        attn_gain_grad,
        *ffn_grads,
        ffn_gain_grad,
    )


def solution(mesh):
    rows = P(("fsdp", "ctx"), None)
    matrix = P("fsdp", "tp")
    vector = P("fsdp")
    return jax.shard_map(
        shards,
        mesh=mesh,
        in_specs=(
            rows,
            matrix,
            matrix,
            matrix,
            matrix,
            vector,
            matrix,
            matrix,
            matrix,
            vector,
            P("fsdp", None),
            P("fsdp", None),
            rows,
        ),
        out_specs=(
            rows,
            rows,
            matrix,
            matrix,
            matrix,
            matrix,
            vector,
            matrix,
            matrix,
            matrix,
            vector,
        ),
        check_vma=False,
    )
```

```python
import functools
import math

import jax
import jax.numpy as jnp
from jax import lax
from jax.experimental import pallas as pl
from jax.experimental.pallas import tpu as pltpu
from jax.sharding import PartitionSpec as P

HEAD_DIM = 64
EPSILON = 1e-05
ROPE_BASE = 500000.0
MASKED = -1e30
LOG2_E = 1.4426950408889634
BLOCK = 256
SPLIT = (1, 1)
VMEM = 56 * 2**20

F32 = jnp.float32
BF16 = jnp.bfloat16

PAIR = [(0, 1), (1, 0)]
CORE = [(0, 1), (1, 0), (2, 3), (3, 2)]
ACROSS = [(0, 2), (2, 0), (1, 3), (3, 1)]


def joint_pairs(x_core):
    pairs = []
    for ctx in range(2):
        for tp in range(4):
            there = (1 - ctx) * 4 + tp if tp % 2 == x_core else ctx * 4 + (tp ^ 2)
            pairs.append((ctx * 4 + tp, there))
    return pairs


FIRST = joint_pairs(0)
SECOND = joint_pairs(1)


def swap_core(v):
    return lax.ppermute(v, "tp", CORE)


def swap_y(v):
    return lax.ppermute(v, "tp", ACROSS)


def swap_x(v):
    return lax.ppermute(v, "ctx", PAIR)


def swap_first(v):
    return lax.ppermute(v, ("ctx", "tp"), FIRST)


def swap_second(v):
    return lax.ppermute(v, ("ctx", "tp"), SECOND)


def after(value, *others):
    return lax.optimization_barrier((value,) + others)[0]


def params(*semantics):
    return pltpu.CompilerParams(vmem_limit_bytes=VMEM)


def cost(gigaflops=0):
    return pl.CostEstimate(flops=int(gigaflops * 1e9) + 1, bytes_accessed=1, transcendentals=0)


def inv_rms(hidden):
    return lax.rsqrt(jnp.mean(hidden * hidden, axis=-1, keepdims=True) + EPSILON)


def rms_back(hidden, gain, grad):
    scale = inv_rms(hidden)
    weighted = grad * gain
    inner = jnp.mean(weighted * hidden, axis=-1, keepdims=True)
    return scale * weighted - hidden * (scale * scale * scale) * inner


def norm_back_kernel(count, *refs):
    hidden_ref, gain_ref, kept_ref, o_ref = refs[count:]
    grad = sum(ref[...].astype(F32) for ref in refs[:count])
    back = rms_back(hidden_ref[...].astype(F32), gain_ref[...], grad)
    o_ref[...] = (kept_ref[...].astype(F32) + back).astype(BF16)


def norm_back(parts, hidden, gain, kept):
    rows, depth = hidden.shape
    step = min(64, rows)
    block = pl.BlockSpec((step, depth), lambda i: (i, 0))
    return pl.pallas_call(
        functools.partial(norm_back_kernel, len(parts)),
        out_shape=jax.ShapeDtypeStruct((rows, depth), BF16),
        grid=(rows // step,),
        in_specs=[block] * (len(parts) + 1)
        + [pl.BlockSpec((1, depth), lambda i: (0, 0)), block],
        out_specs=block,
        compiler_params=params(),
        cost_estimate=cost(),
        name="norm_back",
    )(*parts, hidden, gain, kept)


def turn_lanes(u, first):
    return jnp.where(first, pltpu.roll(u, 96, 1), pltpu.roll(u, 32, 1))


def stream_scratch(count, rows, depth):
    return [pltpu.VMEM((2, rows, depth), BF16), pltpu.SemaphoreType.DMA((2,))] * count


def next_piece(refs, buffer, sems):
    i = pl.program_id(0)

    def copy_of(piece):
        return pltpu.make_async_copy(refs[piece], buffer.at[piece % 2], sems.at[piece % 2])

    @pl.when(i == 0)
    def _():
        copy_of(0).start()

    for piece in range(1, len(refs)):

        @pl.when(i == piece - 1)
        def _(piece=piece):
            copy_of(piece).start()

    for piece in range(len(refs)):

        @pl.when(i == piece)
        def _(piece=piece):
            copy_of(piece).wait()

    return buffer[lax.rem(i, 2)]


def qkv_kernel(count, *refs):
    gain_ref, wq_ref, wkv_ref, cos_ref, sin_ref, o_ref, buffer, sems = refs[count:]
    cos, sin = cos_ref[...], sin_ref[...]
    depth = gain_ref.shape[1]
    lane = lax.broadcasted_iota(jnp.int32, cos.shape, 1)
    first = (lane % 64) < 32
    x = next_piece(refs[:count], buffer, sems).astype(F32)
    x = (x * inv_rms(x) * gain_ref[...]).astype(BF16)
    o_ref[:, :depth] = x
    raw = jnp.dot(x, wq_ref[...], preferred_element_type=F32)
    tiles = raw.shape[1] // 128
    for tile in range(tiles):
        u = raw[:, tile * 128 : (tile + 1) * 128]
        turned = u * cos + turn_lanes(u, first) * sin
        o_ref[:, depth + tile * 128 : depth + (tile + 1) * 128] = turned.astype(BF16)
    u = jnp.dot(x, wkv_ref[...], preferred_element_type=F32)
    turned = u * cos + turn_lanes(u, first) * sin
    o_ref[:, depth + tiles * 128 :] = jnp.where(lane < 64, turned, u).astype(BF16)


def project_qkv(x, gain, w, q_width, cos, sin):
    step, depth = x[0].shape
    rows = len(x) * step
    width = depth + q_width + 128
    return pl.pallas_call(
        functools.partial(qkv_kernel, len(x)),
        out_shape=jax.ShapeDtypeStruct((rows, width), BF16),
        grid=(len(x),),
        in_specs=[pl.BlockSpec(memory_space=pl.ANY)] * len(x)
        + [
            pl.BlockSpec((1, depth), lambda i: (0, 0)),
            pl.BlockSpec((depth, q_width), lambda i: (0, 1)),
            pl.BlockSpec((depth, 128), lambda i: (0, 2 * q_width // 128)),
            pl.BlockSpec((step, 128), lambda i: (i, 0)),
            pl.BlockSpec((step, 128), lambda i: (i, 0)),
        ],
        out_specs=pl.BlockSpec((step, width), lambda i: (i, 0)),
        scratch_shapes=stream_scratch(1, step, depth),
        compiler_params=params(),
        cost_estimate=cost(),
        name="qkv",
    )(*x, gain, w, w, cos, sin)


def ffn_kernel(count, *refs):
    w_ref, o_ref, x_buffer, x_sems, c_buffer, c_sems = refs[2 * count :]
    n = w_ref.shape[1] // 3
    x = next_piece(refs[:count], x_buffer, x_sems)
    c = next_piece(refs[count : 2 * count], c_buffer, c_sems)
    gate = jnp.dot(x, w_ref[:, :n], preferred_element_type=F32)
    up = jnp.dot(x, w_ref[:, n : 2 * n], preferred_element_type=F32)
    d_mixed = jnp.dot(c, w_ref[:, 2 * n :], preferred_element_type=F32)
    sig = 1.0 / (1.0 + jnp.exp(-gate))
    silu = gate * sig
    o_ref[:, :n] = (d_mixed * up * (sig * (1.0 + gate * (1.0 - sig)))).astype(BF16)
    o_ref[:, n : 2 * n] = (d_mixed * silu).astype(BF16)
    o_ref[:, 2 * n :] = (silu * up).astype(BF16)


def ffn_chunk(x, cot, w):
    step, depth = x[0].shape
    rows = len(x) * step
    width = w.shape[1]
    return pl.pallas_call(
        functools.partial(ffn_kernel, len(x)),
        out_shape=jax.ShapeDtypeStruct((rows, width), BF16),
        grid=(len(x),),
        in_specs=[pl.BlockSpec(memory_space=pl.ANY)] * (2 * len(x))
        + [pl.BlockSpec((depth, width), lambda i: (0, 0))],
        out_specs=pl.BlockSpec((step, width), lambda i: (i, 0)),
        scratch_shapes=stream_scratch(2, step, depth),
        compiler_params=params(),
        cost_estimate=cost(),
        name="ffn",
    )(*x, *cot, w)


DOWN = (((0,), (0,)), ((), ()))


def grads_kernel(x_count, y_count, *refs):
    a_ref, b_ref, o_ref = refs[x_count + y_count :]
    split = a_ref.shape[1]

    def product(tall_refs, right_ref):
        tall = jnp.concatenate([ref[...] for ref in tall_refs], axis=0)
        return lax.dot_general(
            tall, right_ref[...].astype(BF16), DOWN, preferred_element_type=F32
        ).astype(BF16)

    o_ref[:, :split] = product(refs[:x_count], a_ref)
    o_ref[:, split:] = product(refs[x_count : x_count + y_count], b_ref)


def weight_grads(x, a, a_width, a_column, y, b, b_width, b_column):
    depth = x[0].shape[1]
    rows = a.shape[0]
    width = a_width + b_width
    step = 512
    return pl.pallas_call(
        functools.partial(grads_kernel, len(x), len(y)),
        out_shape=jax.ShapeDtypeStruct((depth, width), BF16),
        grid=(depth // step,),
        in_specs=[pl.BlockSpec((piece.shape[0], step), lambda i: (0, i)) for piece in (*x, *y)]
        + [
            pl.BlockSpec((rows, a_width), lambda i: (0, a_column)),
            pl.BlockSpec((rows, b_width), lambda i: (0, b_column)),
        ],
        out_specs=pl.BlockSpec((step, width), lambda i: (i, 0)),
        compiler_params=params(),
        cost_estimate=cost(20),
        name="weight_grads",
    )(*x, *y, a, b)


def back_kernel(count, *refs):
    o_ref = refs[-1]
    total = refs[2 * count][...].astype(F32) if len(refs) > 2 * count + 1 else None
    for part in range(count):
        term = lax.dot_general(
            refs[part][...].astype(BF16),
            refs[count + part][...],
            (((1,), (1,)), ((), ())),
            preferred_element_type=F32,
        )
        total = term if total is None else total + term
    o_ref[...] = total.astype(BF16)


def back_product(terms, part=0, parts=1, plus=(), work=0):
    rows = terms[0][0].shape[0] // parts
    depth = terms[0][2].shape[0]
    step = min(512, rows)
    ahead = part * (rows // step)
    return pl.pallas_call(
        functools.partial(back_kernel, len(terms)),
        out_shape=jax.ShapeDtypeStruct((rows, depth), BF16),
        grid=(rows // step,),
        in_specs=[
            pl.BlockSpec((step, term[4]), lambda i, column=term[1]: (i + ahead, column))
            for term in terms
        ]
        + [pl.BlockSpec((depth, term[4]), lambda i, column=term[3]: (0, column)) for term in terms]
        + [pl.BlockSpec((step, depth), lambda i: (i + ahead, 0))] * len(plus),
        out_specs=pl.BlockSpec((step, depth), lambda i: (i, 0)),
        compiler_params=params(),
        cost_estimate=cost(work),
        name="back",
    )(*[term[0] for term in terms], *[term[2] for term in terms], *plus)


def front_kernel(count, *refs):
    w_ref, o_ref, buffer, sems = refs[count:]
    x = next_piece(refs[:count], buffer, sems)
    o_ref[...] = jnp.dot(x, w_ref[...], preferred_element_type=F32).astype(BF16)


def front_product(x, w, width, column):
    step, depth = x[0].shape
    rows = len(x) * step
    return pl.pallas_call(
        functools.partial(front_kernel, len(x)),
        out_shape=jax.ShapeDtypeStruct((rows, width), BF16),
        grid=(len(x),),
        in_specs=[pl.BlockSpec(memory_space=pl.ANY)] * len(x)
        + [pl.BlockSpec((depth, width), lambda i: (0, column))],
        out_specs=pl.BlockSpec((step, width), lambda i: (i, 0)),
        scratch_shapes=stream_scratch(1, step, depth),
        compiler_params=params(),
        cost_estimate=cost(),
        name="front",
    )(*x, w)


def stack_heads(block):
    count = block.shape[1] // HEAD_DIM
    return jnp.concatenate(
        [block[:, h * HEAD_DIM : (h + 1) * HEAD_DIM] for h in range(count)], axis=0
    )


def unstack_heads(stacked):
    count = stacked.shape[0] // BLOCK
    return jnp.concatenate([stacked[h * BLOCK : (h + 1) * BLOCK] for h in range(count)], axis=1)


def allowed_of(i, j, start):
    row = i * BLOCK + lax.broadcasted_iota(jnp.int32, (BLOCK, BLOCK), 0)
    col = j * BLOCK + lax.broadcasted_iota(jnp.int32, (BLOCK, BLOCK), 1)
    return (col <= row) & (col >= start)


def attend_kernel(place, first, q_ref, kv_ref, start_ref, o_ref):
    i = pl.program_id(0)
    q = stack_heads(q_ref[...])
    heads = q.shape[0] // BLOCK
    start = start_ref[...]

    def step(j, carry):
        top, total, acc = carry
        at = pl.multiple_of(place[j] * BLOCK, BLOCK)
        kv = kv_ref[pl.ds(at, BLOCK), :]
        raw = lax.dot_general(
            q, kv[:, :HEAD_DIM], (((1,), (1,)), ((), ())), preferred_element_type=F32
        ) * (HEAD_DIM**-0.5 * LOG2_E)
        allowed = allowed_of(i, j, start)
        scores = jnp.where(allowed[None], raw.reshape(heads, BLOCK, BLOCK), MASKED).reshape(
            heads * BLOCK, BLOCK
        )
        new_top = jnp.maximum(top, jnp.max(scores, axis=-1, keepdims=True))
        keep = jnp.exp2(top - new_top)
        probs = jnp.exp2(scores - new_top)
        total = total * keep + jnp.sum(probs, axis=-1, keepdims=True)
        acc = acc * keep + jnp.dot(probs.astype(BF16), kv, preferred_element_type=F32)
        return (new_top, total, acc)

    size = heads * BLOCK
    top, total, acc = lax.fori_loop(
        first[i],
        i + 1,
        step,
        (
            jnp.full((size, 1), MASKED, F32),
            jnp.zeros((size, 1), F32),
            jnp.zeros((size, 2 * HEAD_DIM), F32),
        ),
    )
    out = acc[:, HEAD_DIM:] / total
    q_width = q_ref.shape[1]
    o_ref[:, :q_width] = unstack_heads(out)
    lse = top + jnp.log2(total)
    lane = lax.broadcasted_iota(jnp.int32, (BLOCK, 128), 1)
    packed = jnp.zeros((BLOCK, 128), F32)
    for h in range(heads):
        packed = jnp.where(lane == h, lse[h * BLOCK : (h + 1) * BLOCK], packed)
    o_ref[:, q_width:] = packed


def attend(qkv, depth, place, first, start, q_width):
    rows = qkv.shape[0]
    blocks = rows // BLOCK
    return pl.pallas_call(
        attend_kernel,
        out_shape=jax.ShapeDtypeStruct((rows, q_width + 128), F32),
        grid_spec=pltpu.PrefetchScalarGridSpec(
            num_scalar_prefetch=2,
            grid=(blocks,),
            in_specs=[
                pl.BlockSpec((BLOCK, q_width), lambda i, place, first: (place[i], depth // q_width)),
                pl.BlockSpec((rows, 128), lambda i, place, first: (0, (depth + q_width) // 128)),
                pl.BlockSpec((BLOCK, 1), lambda i, place, first: (i, 0)),
            ],
            out_specs=pl.BlockSpec((BLOCK, q_width + 128), lambda i, place, first: (place[i], 0)),
        ),
        compiler_params=params(),
        cost_estimate=cost(),
        name="attend",
    )(place, first, qkv, qkv, start)


def attend_back_kernel(
    place,
    first,
    q_ref,
    d_ref,
    h_ref,
    kv_ref,
    start_ref,
    cos_ref,
    sin_ref,
    o_ref,
    dkv_ref,
):
    i = pl.program_id(0)
    blocks = pl.num_programs(0)
    score_scale = HEAD_DIM**-0.5
    q_width = q_ref.shape[1]

    @pl.when(i == 0)
    def _():
        dkv_ref[...] = jnp.zeros_like(dkv_ref)

    q = stack_heads(q_ref[...])
    d_out = stack_heads(d_ref[...])
    heads = q.shape[0] // BLOCK
    out = stack_heads(h_ref[:, :q_width])
    delta = jnp.sum(d_out.astype(F32) * out, axis=-1, keepdims=True)
    lse_block = h_ref[:, q_width:]
    lse = jnp.concatenate([lse_block[:, h : h + 1] for h in range(heads)], axis=0)
    start = start_ref[...]

    def step(j, d_q):
        at = pl.multiple_of(place[j] * BLOCK, BLOCK)
        kv = kv_ref[pl.ds(at, BLOCK), :]
        k, v = kv[:, :HEAD_DIM], kv[:, HEAD_DIM:]
        across = (((1,), (1,)), ((), ()))
        down = (((0,), (0,)), ((), ()))
        raw = lax.dot_general(q, k, across, preferred_element_type=F32) * (score_scale * LOG2_E)
        allowed = allowed_of(i, j, start)
        scores = jnp.where(allowed[None], raw.reshape(heads, BLOCK, BLOCK), MASKED).reshape(
            heads * BLOCK, BLOCK
        )
        probs = jnp.exp2(scores - lse)
        d_probs = lax.dot_general(d_out, v, across, preferred_element_type=F32)
        d_scores = (probs * (d_probs - delta)).astype(BF16)
        d_k = lax.dot_general(d_scores, q, down, preferred_element_type=F32) * score_scale
        d_v = lax.dot_general(probs.astype(BF16), d_out, down, preferred_element_type=F32)
        here = pl.ds(pl.multiple_of(j * BLOCK, BLOCK), BLOCK)
        dkv_ref[here, :] += jnp.concatenate([d_k, d_v], axis=1)
        return d_q + jnp.dot(d_scores, k, preferred_element_type=F32)

    d_q = lax.fori_loop(first[i], i + 1, step, jnp.zeros((heads * BLOCK, HEAD_DIM), F32))
    d_q = unstack_heads(d_q * score_scale)
    lane = lax.broadcasted_iota(jnp.int32, (BLOCK, 128), 1)
    front = (lane % 64) < 32
    mine = pl.ds(pl.multiple_of(place[i] * BLOCK, BLOCK), BLOCK)
    cos, sin = cos_ref[mine, :], sin_ref[mine, :]
    for tile in range(q_width // 128):
        u = d_q[:, tile * 128 : (tile + 1) * 128]
        o_ref[mine, tile * 128 : (tile + 1) * 128] = (u * cos - turn_lanes(u, front) * sin).astype(
            BF16
        )

    @pl.when(i == blocks - 1)
    def _():
        for b in range(dkv_ref.shape[0] // BLOCK):
            there = pl.ds(pl.multiple_of(place[b] * BLOCK, BLOCK), BLOCK)
            u = dkv_ref[b * BLOCK : (b + 1) * BLOCK, :]
            turned = u * cos_ref[there, :] - turn_lanes(u, front) * sin_ref[there, :]
            o_ref[there, q_width:] = jnp.where(lane < HEAD_DIM, turned, u).astype(BF16)


def attend_back(qkv, depth, d_heads, heads, place, first, start, cos, sin):
    rows, q_width = d_heads.shape
    width = q_width + 128
    blocks = rows // BLOCK
    by_place = lambda i, place, first: (place[i], 0)
    whole = lambda i, place, first: (0, 0)
    return pl.pallas_call(
        attend_back_kernel,
        out_shape=jax.ShapeDtypeStruct((rows, width), BF16),
        grid_spec=pltpu.PrefetchScalarGridSpec(
            num_scalar_prefetch=2,
            grid=(blocks,),
            in_specs=[
                pl.BlockSpec((BLOCK, q_width), lambda i, place, first: (place[i], depth // q_width)),
                pl.BlockSpec((BLOCK, q_width), by_place),
                pl.BlockSpec((BLOCK, q_width + 128), by_place),
                pl.BlockSpec((rows, 128), lambda i, place, first: (0, (depth + q_width) // 128)),
                pl.BlockSpec((BLOCK, 1), lambda i, place, first: (i, 0)),
                pl.BlockSpec((rows, 128), whole),
                pl.BlockSpec((rows, 128), whole),
            ],
            out_specs=pl.BlockSpec((rows, width), whole),
            scratch_shapes=[pltpu.VMEM((rows, 128), F32)],
        ),
        compiler_params=params(),
        cost_estimate=cost(),
        name="attend_back",
    )(place, first, qkv, d_heads, heads, qkv, start, cos, sin)


def sum_cores(terms, pieces=2):
    sent = [back_product(terms, 2 * pieces - 1 - at, 2 * pieces) for at in range(pieces)]
    arrived = [swap_core(piece) for piece in sent]
    return add_blocks(back_product(terms, 0, 2), arrived)


def add_blocks(mine, arrived):
    rows = mine.shape[0] // 4
    each = 4 // len(arrived)
    blocks = []
    for at in range(4):
        other = arrived[len(arrived) - 1 - at // each]
        begin = (at % each) * rows
        blocks.append(mine[at * rows : (at + 1) * rows] + other[begin : begin + rows])
    return blocks


def sum_first(blocks, early=()):
    own, along_a, along_b, both = blocks
    along_a = along_a + after(swap_second(both), *early)
    return (own, *lax.optimization_barrier((along_a, along_b)))


def last_parts(own, along_a, along_b, beside=()):
    return own, swap_second(along_b), after(swap_first(along_a), *beside)


def halves_of_cores(terms, plus):
    arrived = swap_core(back_product(terms, 1, 2, plus))
    mine = back_product(terms, 0, 2, plus)
    rows = mine.shape[0] // 4
    return mine[2 * rows :] + arrived[2 * rows :], mine[: 2 * rows] + arrived[: 2 * rows]


def wide_first(far, near, between):
    return after(near + swap_second(far), *between)


def wide_last(near, beside):
    return near, after(swap_first(near[near.shape[0] // 2 :]), *beside)


def share_rows(own, beside=()):
    beside = list(beside) + [()] * (2 - len(beside))
    one, two, *_ = lax.optimization_barrier((swap_first(own), swap_second(own), *beside[0]))
    early = tuple(swap_core(part) for part in (own, one, two))
    last = after(swap_second(one), *early, *beside[1])
    return (own, one, two, last, *early, swap_core(last))


def ring_over(shard, count, held):
    cycle = [(at, (at + 1) % count) for at in range(count)]
    pieces = [shard]
    for step in range(count - 1):
        sent = after(pieces[-1], *held) if step == 1 else pieces[-1]
        pieces.append(lax.ppermute(sent, "fsdp", cycle))
    return pieces


def in_place(pieces, axis):
    count, size = len(pieces), pieces[0].shape[axis]
    here = lax.axis_index("fsdp")
    shape = list(pieces[0].shape)
    shape[axis] *= count
    whole = jnp.zeros(shape, pieces[0].dtype)
    for back, piece in enumerate(pieces):
        owner = lax.rem(here + count - back, count)
        whole = lax.dynamic_update_slice_in_dim(whole, piece, owner * size, axis)
    return whole


def share_in_ctx(own, beside, y, core):
    pair = jnp.stack([own, beside])
    other = jnp.stack([swap_core(own), swap_core(beside)])
    four = jnp.stack([pair, other])
    four = jnp.where(y == 1, four[:, ::-1], four)
    four = jnp.where(core == 1, four[::-1], four)
    return four.transpose(1, 0, 2, 3).reshape(-1, own.shape[1])


def both_halves(own, other, ctx):
    low = jnp.where(ctx == 0, own, other).astype(F32)
    high = jnp.where(ctx == 0, other, own).astype(F32)
    return low, high


def shards(
    tokens,
    q_weight,
    k_weight,
    v_weight,
    o_weight,
    attn_gain,
    gate_weight,
    up_weight,
    down_weight,
    ffn_gain,
    lengths,
    deal,
    cotangent,
):
    ctx = lax.axis_index("ctx")
    tp = lax.axis_index("tp")
    y, core = tp // 2, tp % 2
    row_count, depth = tokens.shape
    group_rows = row_count * lax.axis_size("ctx")
    own_rows = row_count // lax.axis_size("tp")

    def half(weight):
        width = weight.shape[1] // 2
        return lax.dynamic_slice_in_dim(weight, ctx * width, width, 1)

    length_row, deal_row = lengths[0], deal[0]
    spans = deal_row.shape[0]
    span_rows = group_rows // spans
    ends = jnp.cumsum(length_row, dtype=jnp.int32)
    starts = ends - length_row
    natural = jnp.arange(group_rows, dtype=jnp.int32)
    inside = (natural[:, None] >= starts[None]) & (natural[:, None] < ends[None])
    start_of = jnp.sum(jnp.where(inside, starts[None], 0), axis=1, dtype=jnp.int32)
    first = start_of[::BLOCK] // BLOCK
    rel = jnp.arange(group_rows // own_rows, dtype=jnp.int32)
    rel_core = core ^ (rel // 4)
    by_first, by_second = rel % 2, (rel // 2) % 2
    rel_ctx = ctx ^ jnp.where(rel_core == 0, by_first, by_second)
    rel_y = y ^ jnp.where(rel_core == 0, by_second, by_first)
    dealt_block = rel_ctx * (row_count // own_rows) + rel_y * 2 + rel_core
    per_span = span_rows // own_rows
    span_of = jnp.sum(
        jnp.where(
            (dealt_block // per_span)[:, None] == jnp.arange(spans, dtype=jnp.int32)[None],
            deal_row[None],
            0,
        ),
        axis=1,
        dtype=jnp.int32,
    )
    natural_block = span_of * per_span + dealt_block % per_span
    place = jnp.sum(
        jnp.where(natural_block[None, :] == rel[:, None], rel[None, :], 0), axis=1, dtype=jnp.int32
    )
    natural_rel = (
        natural_block[:, None] * own_rows + jnp.arange(own_rows, dtype=jnp.int32)[None]
    ).reshape(-1)
    inside_rel = (natural_rel[:, None] >= starts[None]) & (natural_rel[:, None] < ends[None])
    position = natural_rel - jnp.sum(
        jnp.where(inside_rel, starts[None], 0), axis=1, dtype=jnp.int32
    )
    lane = jnp.arange(128, dtype=jnp.int32)
    inverse = jnp.exp((lane % 32).astype(F32) * (-2.0 * math.log(ROPE_BASE) / HEAD_DIM))
    angles = position.astype(F32)[:, None] * inverse[None]
    cos = jnp.cos(angles)
    sin = jnp.where((lane % 64 < 32)[None], -jnp.sin(angles), jnp.sin(angles))
    start_column = start_of[:, None]

    q_half, k_half, v_half, o_half = map(half, (q_weight, k_weight, v_weight, o_weight))
    q_width, kv_width = q_half.shape[1], k_half.shape[1]
    attn_shard = jnp.concatenate([o_half, q_half, k_half, v_half], axis=1)
    fsdp = lax.axis_size("fsdp")
    gain_rows = jnp.stack([attn_gain, ffn_gain])
    gain_width = attn_gain.shape[0]
    extra = ((0, 14), (0, attn_shard.shape[1] - gain_width))
    tokens_low = lax.dynamic_slice_in_dim(tokens, tp * own_rows, own_rows, 0)
    cot_low = lax.dynamic_slice_in_dim(cotangent, tp * own_rows, own_rows, 0)
    tokens_one = swap_first(tokens_low)
    attn_ring = ring_over(
        jnp.concatenate([attn_shard, jnp.pad(gain_rows, extra)]),
        fsdp,
        (tokens_one, cos, sin, cot_low, place, first, start_column),
    )
    own_depth = attn_shard.shape[0]
    attn_full = in_place([piece[:own_depth] for piece in attn_ring], 0)
    gains = in_place([piece[own_depth : own_depth + 2, :gain_width] for piece in attn_ring], 1)
    gain_one = gains[0].astype(F32)[None]
    gain_two = gains[1].astype(F32)[None]
    ff_half = gate_weight.shape[1] // 2
    chunks = [ff_half * share // sum(SPLIT) for share in SPLIT]
    ffn_shards = []
    for part, chunk in enumerate(chunks):
        at = ctx * ff_half + sum(chunks[:part])
        ffn_shards.append(
            jnp.concatenate(
                [
                    lax.dynamic_slice_in_dim(weight, at, chunk, 1)
                    for weight in (gate_weight, up_weight, down_weight)
                ],
                axis=1,
            )
        )
    tokens_own, cot_own = tokens_low.astype(F32), cot_low.astype(F32)
    group_tokens = (tokens_low, tokens_one, swap_second(tokens_low), swap_second(tokens_one))
    first_shard = after(ffn_shards[0], attn_ring[-1], *group_tokens[2:])
    group_tokens = group_tokens + tuple(swap_core(part) for part in group_tokens)
    attn_full, cot_low, cos, sin, gain_one, *group_tokens = lax.optimization_barrier(
        (attn_full, cot_low, cos, sin, gain_one, *group_tokens)
    )
    qkv = project_qkv(group_tokens, gain_one, attn_full, q_width, cos, sin)
    heads = attend(qkv, depth, place, first, start_column, q_width)
    cot = share_rows(cot_low, [[qkv], [heads]])
    ffn_full = [
        lax.all_gather(shard, "fsdp", axis=0, tiled=True)
        for shard in (first_shard, after(ffn_shards[1], heads))
    ]
    heads = after(heads, *cot)
    attn_blocks = sum_cores([(heads, 0, attn_full, 0, q_width)])
    attn_parts = last_parts(*sum_first(attn_blocks), beside=ffn_full[:1])
    attn_sum = sum(part.astype(F32) for part in attn_parts)
    hidden = tokens_own + attn_sum
    normed_two = share_rows((hidden * inv_rms(hidden) * gain_two).astype(BF16))

    acts = []
    grad_parts = []
    d_norm_partial = ()

    def chunk_grads(part, held=()):
        chunk = chunks[part]
        act = after(acts[part], *held)
        grad_parts.append(weight_grads(normed_two, act, 2 * chunk, 0, cot, act, chunk, 2))

    last = len(chunks) - 1
    for part in range(len(chunks)):
        normed_two = (after(normed_two[0], *grad_parts, *d_norm_partial), *normed_two[1:])
        acts.append(ffn_chunk(normed_two, cot, ffn_full[part]))
        d_norm_term = (acts[part], 0, ffn_full[part], 0, 2 * chunks[part])
        if part < last:
            chunk_grads(part)
            d_norm_partial = (back_product([d_norm_term], plus=d_norm_partial),)
    ffn_terms = [(acts[part], 2, ffn_full[part], 2, chunk) for part, chunk in enumerate(chunks)]
    d_norm_far, d_norm_near = halves_of_cores([d_norm_term], d_norm_partial)
    chunk_grads(last, (d_norm_far,))
    reduced = [
        lax.psum_scatter(part, "fsdp", scatter_dimension=0, tiled=True) for part in grad_parts
    ]
    d_norm_near = wide_first(d_norm_far, d_norm_near, grad_parts)

    def ffn_rows(part, parts, held):
        (act, *rest), *others = ffn_terms
        return back_product([(after(act, held), *rest), *others], part, parts, work=7)

    ffn_sent = [ffn_rows(3, 4, d_norm_near)]
    d_own = norm_back(wide_last(d_norm_near, ffn_sent), hidden, gain_two, cot_low)
    ffn_sent.append(ffn_rows(2, 4, d_own))
    ffn_mine = ffn_rows(0, 2, d_own)
    ffn_own, ffn_a, ffn_b, ffn_both = add_blocks(ffn_mine, [swap_core(piece) for piece in ffn_sent])
    ffn_x, ffn_y = jnp.where(core == 0, ffn_a, ffn_b), jnp.where(core == 0, ffn_b, ffn_a)
    d_one, d_two, ffn_own, ffn_x, ffn_y, ffn_both = lax.optimization_barrier(
        (swap_first(d_own), swap_second(d_own), ffn_own, ffn_x, ffn_y, ffn_both)
    )
    d_early = [swap_core(part) for part in (d_own, d_one, d_two)]
    d_last = after(swap_second(d_one), *d_early, reduced[0])
    d_attn = (d_own, d_one, d_two, d_last, *d_early, swap_core(d_last))

    d_heads = front_product(d_attn, attn_full, q_width, 0)
    other_reduced = [swap_x(after(reduced[0], d_last))]
    d_qkv = attend_back(qkv, depth, d_heads, heads, place, first, start_column, cos, sin)
    y_both, y_own, d_qkv, other_reduced[0] = lax.optimization_barrier(
        (swap_y(ffn_both), swap_y(ffn_y), d_qkv, other_reduced[0])
    )
    ffn_x, ffn_own, d_qkv = lax.optimization_barrier((ffn_x + y_both, ffn_own + y_own, d_qkv))
    ffn_far = swap_x(ffn_x)
    normed_blocks = sum_cores(
        [
            (d_qkv, 0, attn_full, 1, q_width),
            (d_qkv, q_width // 128, attn_full, 2 * q_width // 128, 128),
        ]
    )
    attn_grad = weight_grads(
        d_attn, heads, q_width, 0, (qkv,), after(d_qkv, normed_blocks[3]), q_width + 128, 0
    )
    ffn_far = after(ffn_far, attn_grad)
    result_own = (hidden + (ffn_own.astype(F32) + ffn_far.astype(F32))).astype(BF16)
    result_beside = swap_y(result_own)
    normed_first = sum_first(normed_blocks, [attn_grad, result_own])
    for part in range(1, len(chunks)):
        reduced[part] = after(reduced[part], attn_grad)
        other_reduced.append(swap_x(reduced[part]))
    normed_parts = last_parts(*normed_first, beside=[result_beside, *other_reduced[1:]])
    tokens_grad_own = norm_back(normed_parts, tokens_low, gain_one, d_own)
    attn_reduced = lax.psum_scatter(attn_grad, "fsdp", scatter_dimension=0, tiled=True)
    attn_reduced = after(attn_reduced, tokens_grad_own)
    other_attn = swap_x(attn_reduced)
    result_own, result_beside, _ = lax.optimization_barrier(
        (result_own, result_beside, tokens_grad_own)
    )
    result = share_in_ctx(result_own, result_beside, y, core)

    def gain_part(pairs):
        return sum(jnp.sum(mine.astype(F32) * grad.astype(F32), axis=1) for mine, grad in pairs)

    gain_sums = jnp.stack(
        [
            gain_part([(attn_shard[:, q_width:], attn_reduced[:, q_width:])]),
            gain_part(
                [
                    (ffn_shards[part][:, : 2 * chunk], reduced[part][:, : 2 * chunk])
                    for part, chunk in enumerate(chunks)
                ]
            ),
        ]
    )
    gain_sums = gain_sums + swap_core(gain_sums)
    gain_sums = gain_sums + swap_y(gain_sums)
    gain_sums = gain_sums + swap_x(gain_sums)

    other_reduced[-1] = after(other_reduced[-1], attn_reduced)
    halves = [both_halves(mine, other, ctx) for mine, other in zip(reduced, other_reduced)]

    def ffn_out(which):
        return jnp.concatenate(
            [
                halves[part][side][:, which * chunk : (which + 1) * chunk]
                for side in range(2)
                for part, chunk in enumerate(chunks)
            ],
            axis=1,
        )

    ffn_grads = [ffn_out(which) for which in range(3)]
    tokens_grad_beside, gain_sums, other_attn, result, *ffn_grads = lax.optimization_barrier(
        (swap_y(tokens_grad_own), gain_sums, other_attn, result, *ffn_grads)
    )
    tokens_grad = share_in_ctx(tokens_grad_own, tokens_grad_beside, y, core)
    attn_gain_grad = gain_sums[0] / attn_gain.astype(F32)
    ffn_gain_grad = gain_sums[1] / ffn_gain.astype(F32)
    attn_low, attn_high = both_halves(attn_reduced, other_attn, ctx)

    def attn_out(begin, end):
        return jnp.concatenate([attn_low[:, begin:end], attn_high[:, begin:end]], axis=1)

    q_end, k_end = 2 * q_width, 2 * q_width + kv_width
    return (
        result,
        tokens_grad,
        attn_out(q_width, q_end),
        attn_out(q_end, k_end),
        attn_out(k_end, k_end + kv_width),
        attn_out(0, q_width),
        attn_gain_grad,
        *ffn_grads,
        ffn_gain_grad,
    )


def solution(mesh):
    rows = P(("fsdp", "ctx"), None)
    matrix = P("fsdp", "tp")
    vector = P("fsdp")
    return jax.shard_map(
        shards,
        mesh=mesh,
        in_specs=(
            rows,
            matrix,
            matrix,
            matrix,
            matrix,
            vector,
            matrix,
            matrix,
            matrix,
            vector,
            P("fsdp", None),
            P("fsdp", None),
            rows,
        ),
        out_specs=(
            rows,
            rows,
            matrix,
            matrix,
            matrix,
            matrix,
            vector,
            matrix,
            matrix,
            matrix,
            vector,
        ),
        check_vma=False,
    )
```

```python
import functools
import math

import jax
import jax.numpy as jnp
from jax import lax
from jax.experimental import pallas as pl
from jax.experimental.pallas import tpu as pltpu
from jax.sharding import PartitionSpec as P

HEAD_DIM = 64
EPSILON = 1e-05
ROPE_BASE = 500000.0
MASKED = -1e30
LOG2_E = 1.4426950408889634
BLOCK = 256
SPLIT = (5, 3)
VMEM = 56 * 2**20

F32 = jnp.float32
BF16 = jnp.bfloat16

PAIR = [(0, 1), (1, 0)]
CORE = [(0, 1), (1, 0), (2, 3), (3, 2)]
ACROSS = [(0, 2), (2, 0), (1, 3), (3, 1)]


def joint_pairs(x_core):
    pairs = []
    for ctx in range(2):
        for tp in range(4):
            there = (1 - ctx) * 4 + tp if tp % 2 == x_core else ctx * 4 + (tp ^ 2)
            pairs.append((ctx * 4 + tp, there))
    return pairs


FIRST = joint_pairs(0)
SECOND = joint_pairs(1)


def swap_core(v):
    return lax.ppermute(v, "tp", CORE)


def swap_y(v):
    return lax.ppermute(v, "tp", ACROSS)


def swap_x(v):
    return lax.ppermute(v, "ctx", PAIR)


def swap_first(v):
    return lax.ppermute(v, ("ctx", "tp"), FIRST)


def swap_second(v):
    return lax.ppermute(v, ("ctx", "tp"), SECOND)


def after(value, *others):
    return lax.optimization_barrier((value,) + others)[0]


def params(*semantics):
    return pltpu.CompilerParams(vmem_limit_bytes=VMEM)


def cost(gigaflops=0):
    return pl.CostEstimate(flops=int(gigaflops * 1e9) + 1, bytes_accessed=1, transcendentals=0)


def inv_rms(hidden):
    return lax.rsqrt(jnp.mean(hidden * hidden, axis=-1, keepdims=True) + EPSILON)


def rms_back(hidden, gain, grad):
    scale = inv_rms(hidden)
    weighted = grad * gain
    inner = jnp.mean(weighted * hidden, axis=-1, keepdims=True)
    return scale * weighted - hidden * (scale * scale * scale) * inner


def norm_back_kernel(count, *refs):
    hidden_ref, gain_ref, kept_ref, o_ref = refs[count:]
    grad = sum(ref[...].astype(F32) for ref in refs[:count])
    back = rms_back(hidden_ref[...].astype(F32), gain_ref[...], grad)
    o_ref[...] = (kept_ref[...].astype(F32) + back).astype(BF16)


def norm_back(parts, hidden, gain, kept):
    rows, depth = hidden.shape
    step = min(64, rows)
    block = pl.BlockSpec((step, depth), lambda i: (i, 0))
    return pl.pallas_call(
        functools.partial(norm_back_kernel, len(parts)),
        out_shape=jax.ShapeDtypeStruct((rows, depth), BF16),
        grid=(rows // step,),
        in_specs=[block] * (len(parts) + 1)
        + [pl.BlockSpec((1, depth), lambda i: (0, 0)), block],
        out_specs=block,
        compiler_params=params(),
        cost_estimate=cost(),
        name="norm_back",
    )(*parts, hidden, gain, kept)


def turn_lanes(u, first):
    return jnp.where(first, pltpu.roll(u, 96, 1), pltpu.roll(u, 32, 1))


def stream_scratch(count, rows, depth):
    return [pltpu.VMEM((2, rows, depth), BF16), pltpu.SemaphoreType.DMA((2,))] * count


def next_piece(refs, buffer, sems):
    i = pl.program_id(0)

    def copy_of(piece):
        return pltpu.make_async_copy(refs[piece], buffer.at[piece % 2], sems.at[piece % 2])

    @pl.when(i == 0)
    def _():
        copy_of(0).start()

    for piece in range(1, len(refs)):

        @pl.when(i == piece - 1)
        def _(piece=piece):
            copy_of(piece).start()

    for piece in range(len(refs)):

        @pl.when(i == piece)
        def _(piece=piece):
            copy_of(piece).wait()

    return buffer[lax.rem(i, 2)]


def qkv_kernel(count, *refs):
    gain_ref, wq_ref, wkv_ref, cos_ref, sin_ref, o_ref, buffer, sems = refs[count:]
    cos, sin = cos_ref[...], sin_ref[...]
    depth = gain_ref.shape[1]
    lane = lax.broadcasted_iota(jnp.int32, cos.shape, 1)
    first = (lane % 64) < 32
    x = next_piece(refs[:count], buffer, sems).astype(F32)
    x = (x * inv_rms(x) * gain_ref[...]).astype(BF16)
    o_ref[:, :depth] = x
    raw = jnp.dot(x, wq_ref[...], preferred_element_type=F32)
    tiles = raw.shape[1] // 128
    for tile in range(tiles):
        u = raw[:, tile * 128 : (tile + 1) * 128]
        turned = u * cos + turn_lanes(u, first) * sin
        o_ref[:, depth + tile * 128 : depth + (tile + 1) * 128] = turned.astype(BF16)
    u = jnp.dot(x, wkv_ref[...], preferred_element_type=F32)
    turned = u * cos + turn_lanes(u, first) * sin
    o_ref[:, depth + tiles * 128 :] = jnp.where(lane < 64, turned, u).astype(BF16)


def project_qkv(x, gain, w, q_width, cos, sin):
    step, depth = x[0].shape
    rows = len(x) * step
    width = depth + q_width + 128
    return pl.pallas_call(
        functools.partial(qkv_kernel, len(x)),
        out_shape=jax.ShapeDtypeStruct((rows, width), BF16),
        grid=(len(x),),
        in_specs=[pl.BlockSpec(memory_space=pl.ANY)] * len(x)
        + [
            pl.BlockSpec((1, depth), lambda i: (0, 0)),
            pl.BlockSpec((depth, q_width), lambda i: (0, 1)),
            pl.BlockSpec((depth, 128), lambda i: (0, 2 * q_width // 128)),
            pl.BlockSpec((step, 128), lambda i: (i, 0)),
            pl.BlockSpec((step, 128), lambda i: (i, 0)),
        ],
        out_specs=pl.BlockSpec((step, width), lambda i: (i, 0)),
        scratch_shapes=stream_scratch(1, step, depth),
        compiler_params=params(),
        cost_estimate=cost(),
        name="qkv",
    )(*x, gain, w, w, cos, sin)


def ffn_kernel(count, *refs):
    w_ref, o_ref, x_buffer, x_sems, c_buffer, c_sems = refs[2 * count :]
    n = w_ref.shape[1] // 3
    x = next_piece(refs[:count], x_buffer, x_sems)
    c = next_piece(refs[count : 2 * count], c_buffer, c_sems)
    gate = jnp.dot(x, w_ref[:, :n], preferred_element_type=F32)
    up = jnp.dot(x, w_ref[:, n : 2 * n], preferred_element_type=F32)
    d_mixed = jnp.dot(c, w_ref[:, 2 * n :], preferred_element_type=F32)
    sig = 1.0 / (1.0 + jnp.exp(-gate))
    silu = gate * sig
    o_ref[:, :n] = (d_mixed * up * (sig * (1.0 + gate * (1.0 - sig)))).astype(BF16)
    o_ref[:, n : 2 * n] = (d_mixed * silu).astype(BF16)
    o_ref[:, 2 * n :] = (silu * up).astype(BF16)


def ffn_chunk(x, cot, w):
    step, depth = x[0].shape
    rows = len(x) * step
    width = w.shape[1]
    return pl.pallas_call(
        functools.partial(ffn_kernel, len(x)),
        out_shape=jax.ShapeDtypeStruct((rows, width), BF16),
        grid=(len(x),),
        in_specs=[pl.BlockSpec(memory_space=pl.ANY)] * (2 * len(x))
        + [pl.BlockSpec((depth, width), lambda i: (0, 0))],
        out_specs=pl.BlockSpec((step, width), lambda i: (i, 0)),
        scratch_shapes=stream_scratch(2, step, depth),
        compiler_params=params(),
        cost_estimate=cost(),
        name="ffn",
    )(*x, *cot, w)


DOWN = (((0,), (0,)), ((), ()))


def grads_kernel(x_count, y_count, *refs):
    a_ref, b_ref, o_ref = refs[x_count + y_count :]
    split = a_ref.shape[1]

    def product(tall_refs, right_ref):
        tall = jnp.concatenate([ref[...] for ref in tall_refs], axis=0)
        return lax.dot_general(
            tall, right_ref[...].astype(BF16), DOWN, preferred_element_type=F32
        ).astype(BF16)

    o_ref[:, :split] = product(refs[:x_count], a_ref)
    o_ref[:, split:] = product(refs[x_count : x_count + y_count], b_ref)


def weight_grads(x, a, a_width, a_column, y, b, b_width, b_column):
    depth = x[0].shape[1]
    rows = a.shape[0]
    width = a_width + b_width
    step = 512
    return pl.pallas_call(
        functools.partial(grads_kernel, len(x), len(y)),
        out_shape=jax.ShapeDtypeStruct((depth, width), BF16),
        grid=(depth // step,),
        in_specs=[pl.BlockSpec((piece.shape[0], step), lambda i: (0, i)) for piece in (*x, *y)]
        + [
            pl.BlockSpec((rows, a_width), lambda i: (0, a_column)),
            pl.BlockSpec((rows, b_width), lambda i: (0, b_column)),
        ],
        out_specs=pl.BlockSpec((step, width), lambda i: (i, 0)),
        compiler_params=params(),
        cost_estimate=cost(20),
        name="weight_grads",
    )(*x, *y, a, b)


def back_kernel(count, *refs):
    o_ref = refs[-1]
    total = refs[2 * count][...].astype(F32) if len(refs) > 2 * count + 1 else None
    for part in range(count):
        term = lax.dot_general(
            refs[part][...].astype(BF16),
            refs[count + part][...],
            (((1,), (1,)), ((), ())),
            preferred_element_type=F32,
        )
        total = term if total is None else total + term
    o_ref[...] = total.astype(BF16)


def back_product(terms, part=0, parts=1, plus=(), work=0):
    rows = terms[0][0].shape[0] // parts
    depth = terms[0][2].shape[0]
    step = min(512, rows)
    ahead = part * (rows // step)
    return pl.pallas_call(
        functools.partial(back_kernel, len(terms)),
        out_shape=jax.ShapeDtypeStruct((rows, depth), BF16),
        grid=(rows // step,),
        in_specs=[
            pl.BlockSpec((step, term[4]), lambda i, column=term[1]: (i + ahead, column))
            for term in terms
        ]
        + [pl.BlockSpec((depth, term[4]), lambda i, column=term[3]: (0, column)) for term in terms]
        + [pl.BlockSpec((step, depth), lambda i: (i + ahead, 0))] * len(plus),
        out_specs=pl.BlockSpec((step, depth), lambda i: (i, 0)),
        compiler_params=params(),
        cost_estimate=cost(work),
        name="back",
    )(*[term[0] for term in terms], *[term[2] for term in terms], *plus)


def front_kernel(count, *refs):
    w_ref, o_ref, buffer, sems = refs[count:]
    x = next_piece(refs[:count], buffer, sems)
    o_ref[...] = jnp.dot(x, w_ref[...], preferred_element_type=F32).astype(BF16)


def front_product(x, w, width, column):
    step, depth = x[0].shape
    rows = len(x) * step
    return pl.pallas_call(
        functools.partial(front_kernel, len(x)),
        out_shape=jax.ShapeDtypeStruct((rows, width), BF16),
        grid=(len(x),),
        in_specs=[pl.BlockSpec(memory_space=pl.ANY)] * len(x)
        + [pl.BlockSpec((depth, width), lambda i: (0, column))],
        out_specs=pl.BlockSpec((step, width), lambda i: (i, 0)),
        scratch_shapes=stream_scratch(1, step, depth),
        compiler_params=params(),
        cost_estimate=cost(),
        name="front",
    )(*x, w)


def stack_heads(block):
    count = block.shape[1] // HEAD_DIM
    return jnp.concatenate(
        [block[:, h * HEAD_DIM : (h + 1) * HEAD_DIM] for h in range(count)], axis=0
    )


def unstack_heads(stacked):
    count = stacked.shape[0] // BLOCK
    return jnp.concatenate([stacked[h * BLOCK : (h + 1) * BLOCK] for h in range(count)], axis=1)


def allowed_of(i, j, start):
    row = i * BLOCK + lax.broadcasted_iota(jnp.int32, (BLOCK, BLOCK), 0)
    col = j * BLOCK + lax.broadcasted_iota(jnp.int32, (BLOCK, BLOCK), 1)
    return (col <= row) & (col >= start)


def attend_kernel(place, first, q_ref, kv_ref, start_ref, o_ref):
    i = pl.program_id(0)
    q = stack_heads(q_ref[...])
    heads = q.shape[0] // BLOCK
    start = start_ref[...]

    def step(j, carry):
        top, total, acc = carry
        at = pl.multiple_of(place[j] * BLOCK, BLOCK)
        kv = kv_ref[pl.ds(at, BLOCK), :]
        raw = lax.dot_general(
            q, kv[:, :HEAD_DIM], (((1,), (1,)), ((), ())), preferred_element_type=F32
        ) * (HEAD_DIM**-0.5 * LOG2_E)
        allowed = allowed_of(i, j, start)
        scores = jnp.where(allowed[None], raw.reshape(heads, BLOCK, BLOCK), MASKED).reshape(
            heads * BLOCK, BLOCK
        )
        new_top = jnp.maximum(top, jnp.max(scores, axis=-1, keepdims=True))
        keep = jnp.exp2(top - new_top)
        probs = jnp.exp2(scores - new_top)
        total = total * keep + jnp.sum(probs, axis=-1, keepdims=True)
        acc = acc * keep + jnp.dot(probs.astype(BF16), kv, preferred_element_type=F32)
        return (new_top, total, acc)

    size = heads * BLOCK
    top, total, acc = lax.fori_loop(
        first[i],
        i + 1,
        step,
        (
            jnp.full((size, 1), MASKED, F32),
            jnp.zeros((size, 1), F32),
            jnp.zeros((size, 2 * HEAD_DIM), F32),
        ),
    )
    out = acc[:, HEAD_DIM:] / total
    q_width = q_ref.shape[1]
    o_ref[:, :q_width] = unstack_heads(out)
    lse = top + jnp.log2(total)
    lane = lax.broadcasted_iota(jnp.int32, (BLOCK, 128), 1)
    packed = jnp.zeros((BLOCK, 128), F32)
    for h in range(heads):
        packed = jnp.where(lane == h, lse[h * BLOCK : (h + 1) * BLOCK], packed)
    o_ref[:, q_width:] = packed


def attend(qkv, depth, place, first, start, q_width):
    rows = qkv.shape[0]
    blocks = rows // BLOCK
    return pl.pallas_call(
        attend_kernel,
        out_shape=jax.ShapeDtypeStruct((rows, q_width + 128), F32),
        grid_spec=pltpu.PrefetchScalarGridSpec(
            num_scalar_prefetch=2,
            grid=(blocks,),
            in_specs=[
                pl.BlockSpec((BLOCK, q_width), lambda i, place, first: (place[i], depth // q_width)),
                pl.BlockSpec((rows, 128), lambda i, place, first: (0, (depth + q_width) // 128)),
                pl.BlockSpec((BLOCK, 1), lambda i, place, first: (i, 0)),
            ],
            out_specs=pl.BlockSpec((BLOCK, q_width + 128), lambda i, place, first: (place[i], 0)),
        ),
        compiler_params=params(),
        cost_estimate=cost(),
        name="attend",
    )(place, first, qkv, qkv, start)


def attend_back_kernel(
    place,
    first,
    q_ref,
    d_ref,
    h_ref,
    kv_ref,
    start_ref,
    cos_ref,
    sin_ref,
    o_ref,
    dkv_ref,
):
    i = pl.program_id(0)
    blocks = pl.num_programs(0)
    score_scale = HEAD_DIM**-0.5
    q_width = q_ref.shape[1]

    @pl.when(i == 0)
    def _():
        dkv_ref[...] = jnp.zeros_like(dkv_ref)

    q = stack_heads(q_ref[...])
    d_out = stack_heads(d_ref[...])
    heads = q.shape[0] // BLOCK
    out = stack_heads(h_ref[:, :q_width])
    delta = jnp.sum(d_out.astype(F32) * out, axis=-1, keepdims=True)
    lse_block = h_ref[:, q_width:]
    lse = jnp.concatenate([lse_block[:, h : h + 1] for h in range(heads)], axis=0)
    start = start_ref[...]

    def step(j, d_q):
        at = pl.multiple_of(place[j] * BLOCK, BLOCK)
        kv = kv_ref[pl.ds(at, BLOCK), :]
        k, v = kv[:, :HEAD_DIM], kv[:, HEAD_DIM:]
        across = (((1,), (1,)), ((), ()))
        down = (((0,), (0,)), ((), ()))
        raw = lax.dot_general(q, k, across, preferred_element_type=F32) * (score_scale * LOG2_E)
        allowed = allowed_of(i, j, start)
        scores = jnp.where(allowed[None], raw.reshape(heads, BLOCK, BLOCK), MASKED).reshape(
            heads * BLOCK, BLOCK
        )
        probs = jnp.exp2(scores - lse)
        d_probs = lax.dot_general(d_out, v, across, preferred_element_type=F32)
        d_scores = (probs * (d_probs - delta)).astype(BF16)
        d_k = lax.dot_general(d_scores, q, down, preferred_element_type=F32) * score_scale
        d_v = lax.dot_general(probs.astype(BF16), d_out, down, preferred_element_type=F32)
        here = pl.ds(pl.multiple_of(j * BLOCK, BLOCK), BLOCK)
        dkv_ref[here, :] += jnp.concatenate([d_k, d_v], axis=1)
        return d_q + jnp.dot(d_scores, k, preferred_element_type=F32)

    d_q = lax.fori_loop(first[i], i + 1, step, jnp.zeros((heads * BLOCK, HEAD_DIM), F32))
    d_q = unstack_heads(d_q * score_scale)
    lane = lax.broadcasted_iota(jnp.int32, (BLOCK, 128), 1)
    front = (lane % 64) < 32
    mine = pl.ds(pl.multiple_of(place[i] * BLOCK, BLOCK), BLOCK)
    cos, sin = cos_ref[mine, :], sin_ref[mine, :]
    for tile in range(q_width // 128):
        u = d_q[:, tile * 128 : (tile + 1) * 128]
        o_ref[mine, tile * 128 : (tile + 1) * 128] = (u * cos - turn_lanes(u, front) * sin).astype(
            BF16
        )

    @pl.when(i == blocks - 1)
    def _():
        for b in range(dkv_ref.shape[0] // BLOCK):
            there = pl.ds(pl.multiple_of(place[b] * BLOCK, BLOCK), BLOCK)
            u = dkv_ref[b * BLOCK : (b + 1) * BLOCK, :]
            turned = u * cos_ref[there, :] - turn_lanes(u, front) * sin_ref[there, :]
            o_ref[there, q_width:] = jnp.where(lane < HEAD_DIM, turned, u).astype(BF16)


def attend_back(qkv, depth, d_heads, heads, place, first, start, cos, sin):
    rows, q_width = d_heads.shape
    width = q_width + 128
    blocks = rows // BLOCK
    by_place = lambda i, place, first: (place[i], 0)
    whole = lambda i, place, first: (0, 0)
    return pl.pallas_call(
        attend_back_kernel,
        out_shape=jax.ShapeDtypeStruct((rows, width), BF16),
        grid_spec=pltpu.PrefetchScalarGridSpec(
            num_scalar_prefetch=2,
            grid=(blocks,),
            in_specs=[
                pl.BlockSpec((BLOCK, q_width), lambda i, place, first: (place[i], depth // q_width)),
                pl.BlockSpec((BLOCK, q_width), by_place),
                pl.BlockSpec((BLOCK, q_width + 128), by_place),
                pl.BlockSpec((rows, 128), lambda i, place, first: (0, (depth + q_width) // 128)),
                pl.BlockSpec((BLOCK, 1), lambda i, place, first: (i, 0)),
                pl.BlockSpec((rows, 128), whole),
                pl.BlockSpec((rows, 128), whole),
            ],
            out_specs=pl.BlockSpec((rows, width), whole),
            scratch_shapes=[pltpu.VMEM((rows, 128), F32)],
        ),
        compiler_params=params(),
        cost_estimate=cost(),
        name="attend_back",
    )(place, first, qkv, d_heads, heads, qkv, start, cos, sin)


def sum_cores(terms, pieces=2):
    sent = [back_product(terms, 2 * pieces - 1 - at, 2 * pieces) for at in range(pieces)]
    arrived = [swap_core(piece) for piece in sent]
    return add_blocks(back_product(terms, 0, 2), arrived)


def add_blocks(mine, arrived):
    rows = mine.shape[0] // 4
    each = 4 // len(arrived)
    blocks = []
    for at in range(4):
        other = arrived[len(arrived) - 1 - at // each]
        begin = (at % each) * rows
        blocks.append(mine[at * rows : (at + 1) * rows] + other[begin : begin + rows])
    return blocks


def sum_first(blocks, early=()):
    own, along_a, along_b, both = blocks
    along_a = along_a + after(swap_second(both), *early)
    return (own, *lax.optimization_barrier((along_a, along_b)))


def last_parts(own, along_a, along_b, beside=()):
    return own, swap_second(along_b), after(swap_first(along_a), *beside)


def halves_of_cores(terms, plus):
    arrived = swap_core(back_product(terms, 1, 2, plus))
    mine = back_product(terms, 0, 2, plus)
    rows = mine.shape[0] // 4
    return mine[2 * rows :] + arrived[2 * rows :], mine[: 2 * rows] + arrived[: 2 * rows]


def wide_first(far, near, between):
    return after(near + swap_second(far), *between)


def wide_last(near, beside):
    return near, after(swap_first(near[near.shape[0] // 2 :]), *beside)


def share_rows(own, beside=()):
    beside = list(beside) + [()] * (2 - len(beside))
    one, two, *_ = lax.optimization_barrier((swap_first(own), swap_second(own), *beside[0]))
    early = tuple(swap_core(part) for part in (own, one, two))
    last = after(swap_second(one), *early, *beside[1])
    return (own, one, two, last, *early, swap_core(last))


def ring_over(shard, count, held):
    cycle = [(at, (at + 1) % count) for at in range(count)]
    pieces = [shard]
    for step in range(count - 1):
        sent = after(pieces[-1], *held) if step == 1 else pieces[-1]
        pieces.append(lax.ppermute(sent, "fsdp", cycle))
    return pieces


def in_place(pieces, axis):
    count, size = len(pieces), pieces[0].shape[axis]
    here = lax.axis_index("fsdp")
    shape = list(pieces[0].shape)
    shape[axis] *= count
    whole = jnp.zeros(shape, pieces[0].dtype)
    for back, piece in enumerate(pieces):
        owner = lax.rem(here + count - back, count)
        whole = lax.dynamic_update_slice_in_dim(whole, piece, owner * size, axis)
    return whole


def share_in_ctx(own, beside, y, core):
    pair = jnp.stack([own, beside])
    other = jnp.stack([swap_core(own), swap_core(beside)])
    four = jnp.stack([pair, other])
    four = jnp.where(y == 1, four[:, ::-1], four)
    four = jnp.where(core == 1, four[::-1], four)
    return four.transpose(1, 0, 2, 3).reshape(-1, own.shape[1])


def both_halves(own, other, ctx):
    low = jnp.where(ctx == 0, own, other).astype(F32)
    high = jnp.where(ctx == 0, other, own).astype(F32)
    return low, high


def shards(
    tokens,
    q_weight,
    k_weight,
    v_weight,
    o_weight,
    attn_gain,
    gate_weight,
    up_weight,
    down_weight,
    ffn_gain,
    lengths,
    deal,
    cotangent,
):
    ctx = lax.axis_index("ctx")
    tp = lax.axis_index("tp")
    y, core = tp // 2, tp % 2
    row_count, depth = tokens.shape
    group_rows = row_count * lax.axis_size("ctx")
    own_rows = row_count // lax.axis_size("tp")

    def half(weight):
        width = weight.shape[1] // 2
        return lax.dynamic_slice_in_dim(weight, ctx * width, width, 1)

    length_row, deal_row = lengths[0], deal[0]
    spans = deal_row.shape[0]
    span_rows = group_rows // spans
    ends = jnp.cumsum(length_row, dtype=jnp.int32)
    starts = ends - length_row
    natural = jnp.arange(group_rows, dtype=jnp.int32)
    inside = (natural[:, None] >= starts[None]) & (natural[:, None] < ends[None])
    start_of = jnp.sum(jnp.where(inside, starts[None], 0), axis=1, dtype=jnp.int32)
    first = start_of[::BLOCK] // BLOCK
    rel = jnp.arange(group_rows // own_rows, dtype=jnp.int32)
    rel_core = core ^ (rel // 4)
    by_first, by_second = rel % 2, (rel // 2) % 2
    rel_ctx = ctx ^ jnp.where(rel_core == 0, by_first, by_second)
    rel_y = y ^ jnp.where(rel_core == 0, by_second, by_first)
    dealt_block = rel_ctx * (row_count // own_rows) + rel_y * 2 + rel_core
    per_span = span_rows // own_rows
    span_of = jnp.sum(
        jnp.where(
            (dealt_block // per_span)[:, None] == jnp.arange(spans, dtype=jnp.int32)[None],
            deal_row[None],
            0,
        ),
        axis=1,
        dtype=jnp.int32,
    )
    natural_block = span_of * per_span + dealt_block % per_span
    place = jnp.sum(
        jnp.where(natural_block[None, :] == rel[:, None], rel[None, :], 0), axis=1, dtype=jnp.int32
    )
    natural_rel = (
        natural_block[:, None] * own_rows + jnp.arange(own_rows, dtype=jnp.int32)[None]
    ).reshape(-1)
    inside_rel = (natural_rel[:, None] >= starts[None]) & (natural_rel[:, None] < ends[None])
    position = natural_rel - jnp.sum(
        jnp.where(inside_rel, starts[None], 0), axis=1, dtype=jnp.int32
    )
    lane = jnp.arange(128, dtype=jnp.int32)
    inverse = jnp.exp((lane % 32).astype(F32) * (-2.0 * math.log(ROPE_BASE) / HEAD_DIM))
    angles = position.astype(F32)[:, None] * inverse[None]
    cos = jnp.cos(angles)
    sin = jnp.where((lane % 64 < 32)[None], -jnp.sin(angles), jnp.sin(angles))
    start_column = start_of[:, None]

    q_half, k_half, v_half, o_half = map(half, (q_weight, k_weight, v_weight, o_weight))
    q_width, kv_width = q_half.shape[1], k_half.shape[1]
    attn_shard = jnp.concatenate([o_half, q_half, k_half, v_half], axis=1)
    fsdp = lax.axis_size("fsdp")
    gain_rows = jnp.stack([attn_gain, ffn_gain])
    gain_width = attn_gain.shape[0]
    extra = ((0, 14), (0, attn_shard.shape[1] - gain_width))
    tokens_low = lax.dynamic_slice_in_dim(tokens, tp * own_rows, own_rows, 0)
    cot_low = lax.dynamic_slice_in_dim(cotangent, tp * own_rows, own_rows, 0)
    tokens_one = swap_first(tokens_low)
    attn_ring = ring_over(
        jnp.concatenate([attn_shard, jnp.pad(gain_rows, extra)]),
        fsdp,
        (tokens_one, cos, sin, cot_low, place, first, start_column),
    )
    own_depth = attn_shard.shape[0]
    attn_full = in_place([piece[:own_depth] for piece in attn_ring], 0)
    gains = in_place([piece[own_depth : own_depth + 2, :gain_width] for piece in attn_ring], 1)
    gain_one = gains[0].astype(F32)[None]
    gain_two = gains[1].astype(F32)[None]
    ff_half = gate_weight.shape[1] // 2
    chunks = [ff_half * share // sum(SPLIT) for share in SPLIT]
    ffn_shards = []
    for part, chunk in enumerate(chunks):
        at = ctx * ff_half + sum(chunks[:part])
        ffn_shards.append(
            jnp.concatenate(
                [
                    lax.dynamic_slice_in_dim(weight, at, chunk, 1)
                    for weight in (gate_weight, up_weight, down_weight)
                ],
                axis=1,
            )
        )
    tokens_own, cot_own = tokens_low.astype(F32), cot_low.astype(F32)
    group_tokens = (tokens_low, tokens_one, swap_second(tokens_low), swap_second(tokens_one))
    first_shard = after(ffn_shards[0], attn_ring[-1], *group_tokens[2:])
    group_tokens = group_tokens + tuple(swap_core(part) for part in group_tokens)
    attn_full, cot_low, cos, sin, gain_one, *group_tokens = lax.optimization_barrier(
        (attn_full, cot_low, cos, sin, gain_one, *group_tokens)
    )
    qkv = project_qkv(group_tokens, gain_one, attn_full, q_width, cos, sin)
    heads = attend(qkv, depth, place, first, start_column, q_width)
    cot = share_rows(cot_low, [[qkv], [heads]])
    ffn_full = [
        lax.all_gather(shard, "fsdp", axis=0, tiled=True)
        for shard in (first_shard, after(ffn_shards[1], heads))
    ]
    heads = after(heads, *cot)
    attn_blocks = sum_cores([(heads, 0, attn_full, 0, q_width)])
    attn_parts = last_parts(*sum_first(attn_blocks))
    attn_sum = sum(part.astype(F32) for part in attn_parts)
    hidden = tokens_own + attn_sum
    normed_two = share_rows(
        (hidden * inv_rms(hidden) * gain_two).astype(BF16), [(), ffn_full[:1]]
    )

    acts = []
    grad_parts = []
    d_norm_partial = ()

    def chunk_grads(part, held=()):
        chunk = chunks[part]
        act = after(acts[part], *held)
        grad_parts.append(weight_grads(normed_two, act, 2 * chunk, 0, cot, act, chunk, 2))

    last = len(chunks) - 1
    for part in range(len(chunks)):
        normed_two = (after(normed_two[0], *grad_parts, *d_norm_partial), *normed_two[1:])
        acts.append(ffn_chunk(normed_two, cot, ffn_full[part]))
        d_norm_term = (acts[part], 0, ffn_full[part], 0, 2 * chunks[part])
        if part < last:
            chunk_grads(part)
            d_norm_partial = (back_product([d_norm_term], plus=d_norm_partial),)
    ffn_terms = [(acts[part], 2, ffn_full[part], 2, chunk) for part, chunk in enumerate(chunks)]
    d_norm_far, d_norm_near = halves_of_cores([d_norm_term], d_norm_partial)
    chunk_grads(last, (d_norm_far,))
    reduced = [
        lax.psum_scatter(part, "fsdp", scatter_dimension=0, tiled=True) for part in grad_parts
    ]
    d_norm_near = wide_first(d_norm_far, d_norm_near, grad_parts)

    def ffn_rows(part, parts, held):
        (act, *rest), *others = ffn_terms
        return back_product([(after(act, held), *rest), *others], part, parts, work=7)

    ffn_sent = [ffn_rows(3, 4, d_norm_near)]
    d_own = norm_back(wide_last(d_norm_near, ffn_sent), hidden, gain_two, cot_low)
    ffn_sent.append(ffn_rows(2, 4, d_own))
    ffn_mine = ffn_rows(0, 2, d_own)
    ffn_own, ffn_a, ffn_b, ffn_both = add_blocks(ffn_mine, [swap_core(piece) for piece in ffn_sent])
    ffn_x, ffn_y = jnp.where(core == 0, ffn_a, ffn_b), jnp.where(core == 0, ffn_b, ffn_a)
    d_one, d_two, ffn_own, ffn_x, ffn_y, ffn_both = lax.optimization_barrier(
        (swap_first(d_own), swap_second(d_own), ffn_own, ffn_x, ffn_y, ffn_both)
    )
    d_early = [swap_core(part) for part in (d_own, d_one, d_two)]
    d_last = after(swap_second(d_one), *d_early, reduced[0])
    d_attn = (d_own, d_one, d_two, d_last, *d_early, swap_core(d_last))

    d_heads = front_product(d_attn, attn_full, q_width, 0)
    other_reduced = [swap_x(after(reduced[0], d_last))]
    d_qkv = attend_back(qkv, depth, d_heads, heads, place, first, start_column, cos, sin)
    y_both, y_own, d_qkv, other_reduced[0] = lax.optimization_barrier(
        (swap_y(ffn_both), swap_y(ffn_y), d_qkv, other_reduced[0])
    )
    ffn_x, ffn_own, d_qkv = lax.optimization_barrier((ffn_x + y_both, ffn_own + y_own, d_qkv))
    ffn_far = swap_x(ffn_x)
    normed_blocks = sum_cores(
        [
            (d_qkv, 0, attn_full, 1, q_width),
            (d_qkv, q_width // 128, attn_full, 2 * q_width // 128, 128),
        ]
    )
    attn_grad = weight_grads(
        d_attn, heads, q_width, 0, (qkv,), after(d_qkv, normed_blocks[3]), q_width + 128, 0
    )
    ffn_far = after(ffn_far, attn_grad)
    result_own = (hidden + (ffn_own.astype(F32) + ffn_far.astype(F32))).astype(BF16)
    result_beside = swap_y(result_own)
    normed_first = sum_first(normed_blocks, [attn_grad, result_own])
    for part in range(1, len(chunks)):
        reduced[part] = after(reduced[part], attn_grad)
        other_reduced.append(swap_x(reduced[part]))
    normed_parts = last_parts(*normed_first, beside=[result_beside, *other_reduced[1:]])
    tokens_grad_own = norm_back(normed_parts, tokens_low, gain_one, d_own)
    attn_reduced = lax.psum_scatter(attn_grad, "fsdp", scatter_dimension=0, tiled=True)
    attn_reduced = after(attn_reduced, tokens_grad_own)
    other_attn = swap_x(attn_reduced)
    result_own, result_beside, _ = lax.optimization_barrier(
        (result_own, result_beside, tokens_grad_own)
    )
    result = share_in_ctx(result_own, result_beside, y, core)

    def gain_part(pairs):
        return sum(jnp.sum(mine.astype(F32) * grad.astype(F32), axis=1) for mine, grad in pairs)

    gain_sums = jnp.stack(
        [
            gain_part([(attn_shard[:, q_width:], attn_reduced[:, q_width:])]),
            gain_part(
                [
                    (ffn_shards[part][:, : 2 * chunk], reduced[part][:, : 2 * chunk])
                    for part, chunk in enumerate(chunks)
                ]
            ),
        ]
    )
    gain_sums = gain_sums + swap_core(gain_sums)
    gain_sums = gain_sums + swap_y(gain_sums)
    gain_sums = gain_sums + swap_x(gain_sums)

    other_reduced[-1] = after(other_reduced[-1], attn_reduced)
    halves = [both_halves(mine, other, ctx) for mine, other in zip(reduced, other_reduced)]

    def ffn_out(which):
        return jnp.concatenate(
            [
                halves[part][side][:, which * chunk : (which + 1) * chunk]
                for side in range(2)
                for part, chunk in enumerate(chunks)
            ],
            axis=1,
        )

    ffn_grads = [ffn_out(which) for which in range(3)]
    tokens_grad_beside, gain_sums, other_attn, result, *ffn_grads = lax.optimization_barrier(
        (swap_y(tokens_grad_own), gain_sums, other_attn, result, *ffn_grads)
    )
    tokens_grad = share_in_ctx(tokens_grad_own, tokens_grad_beside, y, core)
    attn_gain_grad = gain_sums[0] / attn_gain.astype(F32)
    ffn_gain_grad = gain_sums[1] / ffn_gain.astype(F32)
    attn_low, attn_high = both_halves(attn_reduced, other_attn, ctx)

    def attn_out(begin, end):
        return jnp.concatenate([attn_low[:, begin:end], attn_high[:, begin:end]], axis=1)

    q_end, k_end = 2 * q_width, 2 * q_width + kv_width
    return (
        result,
        tokens_grad,
        attn_out(q_width, q_end),
        attn_out(q_end, k_end),
        attn_out(k_end, k_end + kv_width),
        attn_out(0, q_width),
        attn_gain_grad,
        *ffn_grads,
        ffn_gain_grad,
    )


def solution(mesh):
    rows = P(("fsdp", "ctx"), None)
    matrix = P("fsdp", "tp")
    vector = P("fsdp")
    return jax.shard_map(
        shards,
        mesh=mesh,
        in_specs=(
            rows,
            matrix,
            matrix,
            matrix,
            matrix,
            vector,
            matrix,
            matrix,
            matrix,
            vector,
            P("fsdp", None),
            P("fsdp", None),
            rows,
        ),
        out_specs=(
            rows,
            rows,
            matrix,
            matrix,
            matrix,
            matrix,
            vector,
            matrix,
            matrix,
            matrix,
            vector,
        ),
        check_vma=False,
    )
```

```python
import functools
import math

import jax
import jax.numpy as jnp
from jax import lax
from jax.experimental import pallas as pl
from jax.experimental.pallas import tpu as pltpu
from jax.sharding import PartitionSpec as P

HEAD_DIM = 64
EPSILON = 1e-05
ROPE_BASE = 500000.0
MASKED = -1e30
LOG2_E = 1.4426950408889634
BLOCK = 256
SPLIT = (1, 1)
VMEM = 56 * 2**20

F32 = jnp.float32
BF16 = jnp.bfloat16

PAIR = [(0, 1), (1, 0)]
CORE = [(0, 1), (1, 0), (2, 3), (3, 2)]
ACROSS = [(0, 2), (2, 0), (1, 3), (3, 1)]


def joint_pairs(x_core):
    pairs = []
    for ctx in range(2):
        for tp in range(4):
            there = (1 - ctx) * 4 + tp if tp % 2 == x_core else ctx * 4 + (tp ^ 2)
            pairs.append((ctx * 4 + tp, there))
    return pairs


FIRST = joint_pairs(0)
SECOND = joint_pairs(1)


def swap_core(v):
    return lax.ppermute(v, "tp", CORE)


def swap_y(v):
    return lax.ppermute(v, "tp", ACROSS)


def swap_x(v):
    return lax.ppermute(v, "ctx", PAIR)


def swap_first(v):
    return lax.ppermute(v, ("ctx", "tp"), FIRST)


def swap_second(v):
    return lax.ppermute(v, ("ctx", "tp"), SECOND)


def after(value, *others):
    return lax.optimization_barrier((value,) + others)[0]


def params(*semantics):
    return pltpu.CompilerParams(vmem_limit_bytes=VMEM)


def cost(gigaflops=0):
    return pl.CostEstimate(flops=int(gigaflops * 1e9) + 1, bytes_accessed=1, transcendentals=0)


def inv_rms(hidden):
    return lax.rsqrt(jnp.mean(hidden * hidden, axis=-1, keepdims=True) + EPSILON)


def rms_back(hidden, gain, grad):
    scale = inv_rms(hidden)
    weighted = grad * gain
    inner = jnp.mean(weighted * hidden, axis=-1, keepdims=True)
    return scale * weighted - hidden * (scale * scale * scale) * inner


def norm_back_kernel(count, *refs):
    hidden_ref, gain_ref, kept_ref, o_ref = refs[count:]
    grad = sum(ref[...].astype(F32) for ref in refs[:count])
    back = rms_back(hidden_ref[...].astype(F32), gain_ref[...], grad)
    o_ref[...] = (kept_ref[...].astype(F32) + back).astype(BF16)


def norm_back(parts, hidden, gain, kept):
    rows, depth = hidden.shape
    step = min(64, rows)
    block = pl.BlockSpec((step, depth), lambda i: (i, 0))
    return pl.pallas_call(
        functools.partial(norm_back_kernel, len(parts)),
        out_shape=jax.ShapeDtypeStruct((rows, depth), BF16),
        grid=(rows // step,),
        in_specs=[block] * (len(parts) + 1)
        + [pl.BlockSpec((1, depth), lambda i: (0, 0)), block],
        out_specs=block,
        compiler_params=params(),
        cost_estimate=cost(),
        name="norm_back",
    )(*parts, hidden, gain, kept)


def turn_lanes(u, first):
    return jnp.where(first, pltpu.roll(u, 96, 1), pltpu.roll(u, 32, 1))


def stream_scratch(count, rows, depth):
    return [pltpu.VMEM((2, rows, depth), BF16), pltpu.SemaphoreType.DMA((2,))] * count


def next_piece(refs, buffer, sems):
    i = pl.program_id(0)

    def copy_of(piece):
        return pltpu.make_async_copy(refs[piece], buffer.at[piece % 2], sems.at[piece % 2])

    @pl.when(i == 0)
    def _():
        copy_of(0).start()

    for piece in range(1, len(refs)):

        @pl.when(i == piece - 1)
        def _(piece=piece):
            copy_of(piece).start()

    for piece in range(len(refs)):

        @pl.when(i == piece)
        def _(piece=piece):
            copy_of(piece).wait()

    return buffer[lax.rem(i, 2)]


def qkv_kernel(count, *refs):
    gain_ref, wq_ref, wkv_ref, cos_ref, sin_ref, o_ref, buffer, sems = refs[count:]
    cos, sin = cos_ref[...], sin_ref[...]
    depth = gain_ref.shape[1]
    lane = lax.broadcasted_iota(jnp.int32, cos.shape, 1)
    first = (lane % 64) < 32
    x = next_piece(refs[:count], buffer, sems).astype(F32)
    x = (x * inv_rms(x) * gain_ref[...]).astype(BF16)
    o_ref[:, :depth] = x
    raw = jnp.dot(x, wq_ref[...], preferred_element_type=F32)
    tiles = raw.shape[1] // 128
    for tile in range(tiles):
        u = raw[:, tile * 128 : (tile + 1) * 128]
        turned = u * cos + turn_lanes(u, first) * sin
        o_ref[:, depth + tile * 128 : depth + (tile + 1) * 128] = turned.astype(BF16)
    u = jnp.dot(x, wkv_ref[...], preferred_element_type=F32)
    turned = u * cos + turn_lanes(u, first) * sin
    o_ref[:, depth + tiles * 128 :] = jnp.where(lane < 64, turned, u).astype(BF16)


def project_qkv(x, gain, w, q_width, cos, sin):
    step, depth = x[0].shape
    rows = len(x) * step
    width = depth + q_width + 128
    return pl.pallas_call(
        functools.partial(qkv_kernel, len(x)),
        out_shape=jax.ShapeDtypeStruct((rows, width), BF16),
        grid=(len(x),),
        in_specs=[pl.BlockSpec(memory_space=pl.ANY)] * len(x)
        + [
            pl.BlockSpec((1, depth), lambda i: (0, 0)),
            pl.BlockSpec((depth, q_width), lambda i: (0, 1)),
            pl.BlockSpec((depth, 128), lambda i: (0, 2 * q_width // 128)),
            pl.BlockSpec((step, 128), lambda i: (i, 0)),
            pl.BlockSpec((step, 128), lambda i: (i, 0)),
        ],
        out_specs=pl.BlockSpec((step, width), lambda i: (i, 0)),
        scratch_shapes=stream_scratch(1, step, depth),
        compiler_params=params(),
        cost_estimate=cost(),
        name="qkv",
    )(*x, gain, w, w, cos, sin)


def ffn_kernel(count, *refs):
    w_ref, o_ref, x_buffer, x_sems, c_buffer, c_sems = refs[2 * count :]
    n = w_ref.shape[1] // 3
    x = next_piece(refs[:count], x_buffer, x_sems)
    c = next_piece(refs[count : 2 * count], c_buffer, c_sems)
    gate = jnp.dot(x, w_ref[:, :n], preferred_element_type=F32)
    up = jnp.dot(x, w_ref[:, n : 2 * n], preferred_element_type=F32)
    d_mixed = jnp.dot(c, w_ref[:, 2 * n :], preferred_element_type=F32)
    sig = 1.0 / (1.0 + jnp.exp(-gate))
    silu = gate * sig
    o_ref[:, :n] = (d_mixed * up * (sig * (1.0 + gate * (1.0 - sig)))).astype(BF16)
    o_ref[:, n : 2 * n] = (d_mixed * silu).astype(BF16)
    o_ref[:, 2 * n :] = (silu * up).astype(BF16)


def ffn_chunk(x, cot, w):
    step, depth = x[0].shape
    rows = len(x) * step
    width = w.shape[1]
    return pl.pallas_call(
        functools.partial(ffn_kernel, len(x)),
        out_shape=jax.ShapeDtypeStruct((rows, width), BF16),
        grid=(len(x),),
        in_specs=[pl.BlockSpec(memory_space=pl.ANY)] * (2 * len(x))
        + [pl.BlockSpec((depth, width), lambda i: (0, 0))],
        out_specs=pl.BlockSpec((step, width), lambda i: (i, 0)),
        scratch_shapes=stream_scratch(2, step, depth),
        compiler_params=params(),
        cost_estimate=cost(),
        name="ffn",
    )(*x, *cot, w)


DOWN = (((0,), (0,)), ((), ()))


def grads_kernel(x_count, y_count, *refs):
    a_ref, b_ref, o_ref = refs[x_count + y_count :]
    split = a_ref.shape[1]

    def product(tall_refs, right_ref):
        tall = jnp.concatenate([ref[...] for ref in tall_refs], axis=0)
        return lax.dot_general(
            tall, right_ref[...].astype(BF16), DOWN, preferred_element_type=F32
        ).astype(BF16)

    o_ref[:, :split] = product(refs[:x_count], a_ref)
    o_ref[:, split:] = product(refs[x_count : x_count + y_count], b_ref)


def weight_grads(x, a, a_width, a_column, y, b, b_width, b_column):
    depth = x[0].shape[1]
    rows = a.shape[0]
    width = a_width + b_width
    step = 512
    return pl.pallas_call(
        functools.partial(grads_kernel, len(x), len(y)),
        out_shape=jax.ShapeDtypeStruct((depth, width), BF16),
        grid=(depth // step,),
        in_specs=[pl.BlockSpec((piece.shape[0], step), lambda i: (0, i)) for piece in (*x, *y)]
        + [
            pl.BlockSpec((rows, a_width), lambda i: (0, a_column)),
            pl.BlockSpec((rows, b_width), lambda i: (0, b_column)),
        ],
        out_specs=pl.BlockSpec((step, width), lambda i: (i, 0)),
        compiler_params=params(),
        cost_estimate=cost(20),
        name="weight_grads",
    )(*x, *y, a, b)


def back_kernel(count, *refs):
    o_ref = refs[-1]
    total = refs[2 * count][...].astype(F32) if len(refs) > 2 * count + 1 else None
    for part in range(count):
        term = lax.dot_general(
            refs[part][...].astype(BF16),
            refs[count + part][...],
            (((1,), (1,)), ((), ())),
            preferred_element_type=F32,
        )
        total = term if total is None else total + term
    o_ref[...] = total.astype(BF16)


def back_product(terms, part=0, parts=1, plus=(), work=0):
    rows = terms[0][0].shape[0] // parts
    depth = terms[0][2].shape[0]
    step = min(512, rows)
    ahead = part * (rows // step)
    return pl.pallas_call(
        functools.partial(back_kernel, len(terms)),
        out_shape=jax.ShapeDtypeStruct((rows, depth), BF16),
        grid=(rows // step,),
        in_specs=[
            pl.BlockSpec((step, term[4]), lambda i, column=term[1]: (i + ahead, column))
            for term in terms
        ]
        + [pl.BlockSpec((depth, term[4]), lambda i, column=term[3]: (0, column)) for term in terms]
        + [pl.BlockSpec((step, depth), lambda i: (i + ahead, 0))] * len(plus),
        out_specs=pl.BlockSpec((step, depth), lambda i: (i, 0)),
        compiler_params=params(),
        cost_estimate=cost(work),
        name="back",
    )(*[term[0] for term in terms], *[term[2] for term in terms], *plus)


def front_kernel(count, *refs):
    w_ref, o_ref, buffer, sems = refs[count:]
    x = next_piece(refs[:count], buffer, sems)
    o_ref[...] = jnp.dot(x, w_ref[...], preferred_element_type=F32).astype(BF16)


def front_product(x, w, width, column):
    step, depth = x[0].shape
    rows = len(x) * step
    return pl.pallas_call(
        functools.partial(front_kernel, len(x)),
        out_shape=jax.ShapeDtypeStruct((rows, width), BF16),
        grid=(len(x),),
        in_specs=[pl.BlockSpec(memory_space=pl.ANY)] * len(x)
        + [pl.BlockSpec((depth, width), lambda i: (0, column))],
        out_specs=pl.BlockSpec((step, width), lambda i: (i, 0)),
        scratch_shapes=stream_scratch(1, step, depth),
        compiler_params=params(),
        cost_estimate=cost(),
        name="front",
    )(*x, w)


def stack_heads(block):
    count = block.shape[1] // HEAD_DIM
    return jnp.concatenate(
        [block[:, h * HEAD_DIM : (h + 1) * HEAD_DIM] for h in range(count)], axis=0
    )


def unstack_heads(stacked):
    count = stacked.shape[0] // BLOCK
    return jnp.concatenate([stacked[h * BLOCK : (h + 1) * BLOCK] for h in range(count)], axis=1)


def allowed_of(i, j, start):
    row = i * BLOCK + lax.broadcasted_iota(jnp.int32, (BLOCK, BLOCK), 0)
    col = j * BLOCK + lax.broadcasted_iota(jnp.int32, (BLOCK, BLOCK), 1)
    return (col <= row) & (col >= start)


def attend_kernel(place, first, q_ref, kv_ref, start_ref, o_ref):
    i = pl.program_id(0)
    q = stack_heads(q_ref[...])
    heads = q.shape[0] // BLOCK
    start = start_ref[...]

    def step(j, carry):
        top, total, acc = carry
        at = pl.multiple_of(place[j] * BLOCK, BLOCK)
        kv = kv_ref[pl.ds(at, BLOCK), :]
        raw = lax.dot_general(
            q, kv[:, :HEAD_DIM], (((1,), (1,)), ((), ())), preferred_element_type=F32
        ) * (HEAD_DIM**-0.5 * LOG2_E)
        allowed = allowed_of(i, j, start)
        scores = jnp.where(allowed[None], raw.reshape(heads, BLOCK, BLOCK), MASKED).reshape(
            heads * BLOCK, BLOCK
        )
        new_top = jnp.maximum(top, jnp.max(scores, axis=-1, keepdims=True))
        keep = jnp.exp2(top - new_top)
        probs = jnp.exp2(scores - new_top)
        total = total * keep + jnp.sum(probs, axis=-1, keepdims=True)
        acc = acc * keep + jnp.dot(probs.astype(BF16), kv, preferred_element_type=F32)
        return (new_top, total, acc)

    size = heads * BLOCK
    top, total, acc = lax.fori_loop(
        first[i],
        i + 1,
        step,
        (
            jnp.full((size, 1), MASKED, F32),
            jnp.zeros((size, 1), F32),
            jnp.zeros((size, 2 * HEAD_DIM), F32),
        ),
    )
    out = acc[:, HEAD_DIM:] / total
    q_width = q_ref.shape[1]
    o_ref[:, :q_width] = unstack_heads(out)
    lse = top + jnp.log2(total)
    lane = lax.broadcasted_iota(jnp.int32, (BLOCK, 128), 1)
    packed = jnp.zeros((BLOCK, 128), F32)
    for h in range(heads):
        packed = jnp.where(lane == h, lse[h * BLOCK : (h + 1) * BLOCK], packed)
    o_ref[:, q_width:] = packed


def attend(qkv, depth, place, first, start, q_width):
    rows = qkv.shape[0]
    blocks = rows // BLOCK
    return pl.pallas_call(
        attend_kernel,
        out_shape=jax.ShapeDtypeStruct((rows, q_width + 128), F32),
        grid_spec=pltpu.PrefetchScalarGridSpec(
            num_scalar_prefetch=2,
            grid=(blocks,),
            in_specs=[
                pl.BlockSpec((BLOCK, q_width), lambda i, place, first: (place[i], depth // q_width)),
                pl.BlockSpec((rows, 128), lambda i, place, first: (0, (depth + q_width) // 128)),
                pl.BlockSpec((BLOCK, 1), lambda i, place, first: (i, 0)),
            ],
            out_specs=pl.BlockSpec((BLOCK, q_width + 128), lambda i, place, first: (place[i], 0)),
        ),
        compiler_params=params(),
        cost_estimate=cost(),
        name="attend",
    )(place, first, qkv, qkv, start)


def attend_back_kernel(
    place,
    first,
    q_ref,
    d_ref,
    h_ref,
    kv_ref,
    start_ref,
    cos_ref,
    sin_ref,
    o_ref,
    dkv_ref,
):
    i = pl.program_id(0)
    blocks = pl.num_programs(0)
    score_scale = HEAD_DIM**-0.5
    q_width = q_ref.shape[1]

    @pl.when(i == 0)
    def _():
        dkv_ref[...] = jnp.zeros_like(dkv_ref)

    q = stack_heads(q_ref[...])
    d_out = stack_heads(d_ref[...])
    heads = q.shape[0] // BLOCK
    out = stack_heads(h_ref[:, :q_width])
    delta = jnp.sum(d_out.astype(F32) * out, axis=-1, keepdims=True)
    lse_block = h_ref[:, q_width:]
    lse = jnp.concatenate([lse_block[:, h : h + 1] for h in range(heads)], axis=0)
    start = start_ref[...]

    def step(j, d_q):
        at = pl.multiple_of(place[j] * BLOCK, BLOCK)
        kv = kv_ref[pl.ds(at, BLOCK), :]
        k, v = kv[:, :HEAD_DIM], kv[:, HEAD_DIM:]
        across = (((1,), (1,)), ((), ()))
        down = (((0,), (0,)), ((), ()))
        raw = lax.dot_general(q, k, across, preferred_element_type=F32) * (score_scale * LOG2_E)
        allowed = allowed_of(i, j, start)
        scores = jnp.where(allowed[None], raw.reshape(heads, BLOCK, BLOCK), MASKED).reshape(
            heads * BLOCK, BLOCK
        )
        probs = jnp.exp2(scores - lse)
        d_probs = lax.dot_general(d_out, v, across, preferred_element_type=F32)
        d_scores = (probs * (d_probs - delta)).astype(BF16)
        d_k = lax.dot_general(d_scores, q, down, preferred_element_type=F32) * score_scale
        d_v = lax.dot_general(probs.astype(BF16), d_out, down, preferred_element_type=F32)
        here = pl.ds(pl.multiple_of(j * BLOCK, BLOCK), BLOCK)
        dkv_ref[here, :] += jnp.concatenate([d_k, d_v], axis=1)
        return d_q + jnp.dot(d_scores, k, preferred_element_type=F32)

    d_q = lax.fori_loop(first[i], i + 1, step, jnp.zeros((heads * BLOCK, HEAD_DIM), F32))
    d_q = unstack_heads(d_q * score_scale)
    lane = lax.broadcasted_iota(jnp.int32, (BLOCK, 128), 1)
    front = (lane % 64) < 32
    mine = pl.ds(pl.multiple_of(place[i] * BLOCK, BLOCK), BLOCK)
    cos, sin = cos_ref[mine, :], sin_ref[mine, :]
    for tile in range(q_width // 128):
        u = d_q[:, tile * 128 : (tile + 1) * 128]
        o_ref[mine, tile * 128 : (tile + 1) * 128] = (u * cos - turn_lanes(u, front) * sin).astype(
            BF16
        )

    @pl.when(i == blocks - 1)
    def _():
        for b in range(dkv_ref.shape[0] // BLOCK):
            there = pl.ds(pl.multiple_of(place[b] * BLOCK, BLOCK), BLOCK)
            u = dkv_ref[b * BLOCK : (b + 1) * BLOCK, :]
            turned = u * cos_ref[there, :] - turn_lanes(u, front) * sin_ref[there, :]
            o_ref[there, q_width:] = jnp.where(lane < HEAD_DIM, turned, u).astype(BF16)


def attend_back(qkv, depth, d_heads, heads, place, first, start, cos, sin):
    rows, q_width = d_heads.shape
    width = q_width + 128
    blocks = rows // BLOCK
    by_place = lambda i, place, first: (place[i], 0)
    whole = lambda i, place, first: (0, 0)
    return pl.pallas_call(
        attend_back_kernel,
        out_shape=jax.ShapeDtypeStruct((rows, width), BF16),
        grid_spec=pltpu.PrefetchScalarGridSpec(
            num_scalar_prefetch=2,
            grid=(blocks,),
            in_specs=[
                pl.BlockSpec((BLOCK, q_width), lambda i, place, first: (place[i], depth // q_width)),
                pl.BlockSpec((BLOCK, q_width), by_place),
                pl.BlockSpec((BLOCK, q_width + 128), by_place),
                pl.BlockSpec((rows, 128), lambda i, place, first: (0, (depth + q_width) // 128)),
                pl.BlockSpec((BLOCK, 1), lambda i, place, first: (i, 0)),
                pl.BlockSpec((rows, 128), whole),
                pl.BlockSpec((rows, 128), whole),
            ],
            out_specs=pl.BlockSpec((rows, width), whole),
            scratch_shapes=[pltpu.VMEM((rows, 128), F32)],
        ),
        compiler_params=params(),
        cost_estimate=cost(),
        name="attend_back",
    )(place, first, qkv, d_heads, heads, qkv, start, cos, sin)


def sum_cores(terms, pieces=2):
    sent = [back_product(terms, 2 * pieces - 1 - at, 2 * pieces) for at in range(pieces)]
    arrived = [swap_core(piece) for piece in sent]
    return add_blocks(back_product(terms, 0, 2), arrived)


def add_blocks(mine, arrived):
    rows = mine.shape[0] // 4
    each = 4 // len(arrived)
    blocks = []
    for at in range(4):
        other = arrived[len(arrived) - 1 - at // each]
        begin = (at % each) * rows
        blocks.append(mine[at * rows : (at + 1) * rows] + other[begin : begin + rows])
    return blocks


def sum_first(blocks, early=()):
    own, along_a, along_b, both = blocks
    along_a = along_a + after(swap_second(both), *early)
    return (own, *lax.optimization_barrier((along_a, along_b)))


def last_parts(own, along_a, along_b, beside=()):
    return own, swap_second(along_b), after(swap_first(along_a), *beside)


def halves_of_cores(terms, plus):
    arrived = swap_core(back_product(terms, 1, 2, plus))
    mine = back_product(terms, 0, 2, plus)
    rows = mine.shape[0] // 4
    return mine[2 * rows :] + arrived[2 * rows :], mine[: 2 * rows] + arrived[: 2 * rows]


def wide_first(far, near, between):
    return after(near + swap_second(far), *between)


def wide_last(near, beside):
    return near, after(swap_first(near[near.shape[0] // 2 :]), *beside)


def share_rows(own, beside=()):
    beside = list(beside) + [()] * (2 - len(beside))
    one, two, *_ = lax.optimization_barrier((swap_first(own), swap_second(own), *beside[0]))
    early = tuple(swap_core(part) for part in (own, one, two))
    last = after(swap_second(one), *early, *beside[1])
    return (own, one, two, last, *early, swap_core(last))


def ring_over(shard, count, held):
    cycle = [(at, (at + 1) % count) for at in range(count)]
    pieces = [shard]
    for step in range(count - 1):
        sent = after(pieces[-1], *held) if step == 1 else pieces[-1]
        pieces.append(lax.ppermute(sent, "fsdp", cycle))
    return pieces


def in_place(pieces, axis):
    count, size = len(pieces), pieces[0].shape[axis]
    here = lax.axis_index("fsdp")
    shape = list(pieces[0].shape)
    shape[axis] *= count
    whole = jnp.zeros(shape, pieces[0].dtype)
    for back, piece in enumerate(pieces):
        owner = lax.rem(here + count - back, count)
        whole = lax.dynamic_update_slice_in_dim(whole, piece, owner * size, axis)
    return whole


def share_in_ctx(own, beside, y, core):
    pair = jnp.stack([own, beside])
    other = jnp.stack([swap_core(own), swap_core(beside)])
    four = jnp.stack([pair, other])
    four = jnp.where(y == 1, four[:, ::-1], four)
    four = jnp.where(core == 1, four[::-1], four)
    return four.transpose(1, 0, 2, 3).reshape(-1, own.shape[1])


def both_halves(own, other, ctx):
    low = jnp.where(ctx == 0, own, other).astype(F32)
    high = jnp.where(ctx == 0, other, own).astype(F32)
    return low, high


def shards(
    tokens,
    q_weight,
    k_weight,
    v_weight,
    o_weight,
    attn_gain,
    gate_weight,
    up_weight,
    down_weight,
    ffn_gain,
    lengths,
    deal,
    cotangent,
):
    ctx = lax.axis_index("ctx")
    tp = lax.axis_index("tp")
    y, core = tp // 2, tp % 2
    row_count, depth = tokens.shape
    group_rows = row_count * lax.axis_size("ctx")
    own_rows = row_count // lax.axis_size("tp")

    def half(weight):
        width = weight.shape[1] // 2
        return lax.dynamic_slice_in_dim(weight, ctx * width, width, 1)

    length_row, deal_row = lengths[0], deal[0]
    spans = deal_row.shape[0]
    span_rows = group_rows // spans
    ends = jnp.cumsum(length_row, dtype=jnp.int32)
    starts = ends - length_row
    natural = jnp.arange(group_rows, dtype=jnp.int32)
    inside = (natural[:, None] >= starts[None]) & (natural[:, None] < ends[None])
    start_of = jnp.sum(jnp.where(inside, starts[None], 0), axis=1, dtype=jnp.int32)
    first = start_of[::BLOCK] // BLOCK
    rel = jnp.arange(group_rows // own_rows, dtype=jnp.int32)
    rel_core = core ^ (rel // 4)
    by_first, by_second = rel % 2, (rel // 2) % 2
    rel_ctx = ctx ^ jnp.where(rel_core == 0, by_first, by_second)
    rel_y = y ^ jnp.where(rel_core == 0, by_second, by_first)
    dealt_block = rel_ctx * (row_count // own_rows) + rel_y * 2 + rel_core
    per_span = span_rows // own_rows
    span_of = jnp.sum(
        jnp.where(
            (dealt_block // per_span)[:, None] == jnp.arange(spans, dtype=jnp.int32)[None],
            deal_row[None],
            0,
        ),
        axis=1,
        dtype=jnp.int32,
    )
    natural_block = span_of * per_span + dealt_block % per_span
    place = jnp.sum(
        jnp.where(natural_block[None, :] == rel[:, None], rel[None, :], 0), axis=1, dtype=jnp.int32
    )
    natural_rel = (
        natural_block[:, None] * own_rows + jnp.arange(own_rows, dtype=jnp.int32)[None]
    ).reshape(-1)
    inside_rel = (natural_rel[:, None] >= starts[None]) & (natural_rel[:, None] < ends[None])
    position = natural_rel - jnp.sum(
        jnp.where(inside_rel, starts[None], 0), axis=1, dtype=jnp.int32
    )
    lane = jnp.arange(128, dtype=jnp.int32)
    inverse = jnp.exp((lane % 32).astype(F32) * (-2.0 * math.log(ROPE_BASE) / HEAD_DIM))
    angles = position.astype(F32)[:, None] * inverse[None]
    cos = jnp.cos(angles)
    sin = jnp.where((lane % 64 < 32)[None], -jnp.sin(angles), jnp.sin(angles))
    start_column = start_of[:, None]

    q_half, k_half, v_half, o_half = map(half, (q_weight, k_weight, v_weight, o_weight))
    q_width, kv_width = q_half.shape[1], k_half.shape[1]
    attn_shard = jnp.concatenate([o_half, q_half, k_half, v_half], axis=1)
    fsdp = lax.axis_size("fsdp")
    gain_rows = jnp.stack([attn_gain, ffn_gain])
    gain_width = attn_gain.shape[0]
    extra = ((0, 14), (0, attn_shard.shape[1] - gain_width))
    tokens_low = lax.dynamic_slice_in_dim(tokens, tp * own_rows, own_rows, 0)
    cot_low = lax.dynamic_slice_in_dim(cotangent, tp * own_rows, own_rows, 0)
    tokens_one = swap_first(tokens_low)
    attn_ring = ring_over(
        jnp.concatenate([attn_shard, jnp.pad(gain_rows, extra)]),
        fsdp,
        (tokens_one, cos, sin, cot_low, place, first, start_column),
    )
    own_depth = attn_shard.shape[0]
    attn_full = in_place([piece[:own_depth] for piece in attn_ring], 0)
    gains = in_place([piece[own_depth : own_depth + 2, :gain_width] for piece in attn_ring], 1)
    gain_one = gains[0].astype(F32)[None]
    gain_two = gains[1].astype(F32)[None]
    ff_half = gate_weight.shape[1] // 2
    chunks = [ff_half * share // sum(SPLIT) for share in SPLIT]
    ffn_shards = []
    for part, chunk in enumerate(chunks):
        at = ctx * ff_half + sum(chunks[:part])
        ffn_shards.append(
            jnp.concatenate(
                [
                    lax.dynamic_slice_in_dim(weight, at, chunk, 1)
                    for weight in (gate_weight, up_weight, down_weight)
                ],
                axis=1,
            )
        )
    tokens_own, cot_own = tokens_low.astype(F32), cot_low.astype(F32)
    group_tokens = (tokens_low, tokens_one, swap_second(tokens_low), swap_second(tokens_one))
    first_shard = after(ffn_shards[0], attn_ring[-1], *group_tokens[2:])
    group_tokens = group_tokens + tuple(swap_core(part) for part in group_tokens)
    attn_full, cot_low, cos, sin, gain_one, *group_tokens = lax.optimization_barrier(
        (attn_full, cot_low, cos, sin, gain_one, *group_tokens)
    )
    qkv = project_qkv(group_tokens, gain_one, attn_full, q_width, cos, sin)
    heads = attend(qkv, depth, place, first, start_column, q_width)
    cot = share_rows(cot_low, [[qkv], [heads]])
    ffn_full = [
        lax.all_gather(shard, "fsdp", axis=0, tiled=True)
        for shard in (first_shard, after(ffn_shards[1], heads))
    ]
    heads = after(heads, *cot)
    attn_blocks = sum_cores([(heads, 0, attn_full, 0, q_width)])
    attn_parts = last_parts(*sum_first(attn_blocks), beside=ffn_full[:1])
    attn_sum = sum(part.astype(F32) for part in attn_parts)
    hidden = tokens_own + attn_sum
    normed_two = share_rows((hidden * inv_rms(hidden) * gain_two).astype(BF16))

    acts = []
    grad_parts = []
    d_norm_partial = ()

    def chunk_grads(part, held=()):
        chunk = chunks[part]
        act = after(acts[part], *held)
        grad_parts.append(weight_grads(normed_two, act, 2 * chunk, 0, cot, act, chunk, 2))

    last = len(chunks) - 1
    for part in range(len(chunks)):
        normed_two = (after(normed_two[0], *grad_parts, *d_norm_partial), *normed_two[1:])
        acts.append(ffn_chunk(normed_two, cot, ffn_full[part]))
        d_norm_term = (acts[part], 0, ffn_full[part], 0, 2 * chunks[part])
        if part < last:
            chunk_grads(part)
            d_norm_partial = (back_product([d_norm_term], plus=d_norm_partial),)
    ffn_terms = [(acts[part], 2, ffn_full[part], 2, chunk) for part, chunk in enumerate(chunks)]
    d_norm_far, d_norm_near = halves_of_cores([d_norm_term], d_norm_partial)
    chunk_grads(last, (d_norm_far,))
    reduced = [
        lax.psum_scatter(part, "fsdp", scatter_dimension=0, tiled=True) for part in grad_parts
    ]
    d_norm_near = wide_first(d_norm_far, d_norm_near, grad_parts)

    def ffn_rows(part, parts, held):
        (act, *rest), *others = ffn_terms
        return back_product([(after(act, held), *rest), *others], part, parts, work=7)

    ffn_sent = [ffn_rows(3, 4, d_norm_near)]
    d_own = norm_back(wide_last(d_norm_near, ffn_sent), hidden, gain_two, cot_low)
    ffn_sent.append(ffn_rows(2, 4, d_own))
    ffn_mine = ffn_rows(0, 2, d_own)
    ffn_own, ffn_a, ffn_b, ffn_both = add_blocks(ffn_mine, [swap_core(piece) for piece in ffn_sent])
    ffn_x, ffn_y = jnp.where(core == 0, ffn_a, ffn_b), jnp.where(core == 0, ffn_b, ffn_a)
    d_one, d_two, ffn_own, ffn_x, ffn_y, ffn_both = lax.optimization_barrier(
        (swap_first(d_own), swap_second(d_own), ffn_own, ffn_x, ffn_y, ffn_both)
    )
    d_early = [swap_core(part) for part in (d_own, d_one, d_two)]
    d_last = after(swap_second(d_one), *d_early, reduced[0])
    d_attn = (d_own, d_one, d_two, d_last, *d_early, swap_core(d_last))

    d_heads = front_product(d_attn, attn_full, q_width, 0)
    other_reduced = [swap_x(after(reduced[0], d_last))]
    d_qkv = attend_back(qkv, depth, d_heads, heads, place, first, start_column, cos, sin)
    y_both, y_own, d_qkv, other_reduced[0] = lax.optimization_barrier(
        (swap_y(ffn_both), swap_y(ffn_y), d_qkv, other_reduced[0])
    )
    ffn_x, ffn_own, d_qkv = lax.optimization_barrier((ffn_x + y_both, ffn_own + y_own, d_qkv))
    ffn_far = swap_x(ffn_x)
    normed_blocks = sum_cores(
        [
            (d_qkv, 0, attn_full, 1, q_width),
            (d_qkv, q_width // 128, attn_full, 2 * q_width // 128, 128),
        ]
    )
    attn_grad = weight_grads(
        d_attn, heads, q_width, 0, (qkv,), after(d_qkv, normed_blocks[3]), q_width + 128, 0
    )
    ffn_far = after(ffn_far, attn_grad)
    result_own = (hidden + (ffn_own.astype(F32) + ffn_far.astype(F32))).astype(BF16)
    result_beside = swap_y(result_own)
    normed_first = sum_first(normed_blocks, [attn_grad, result_own])
    for part in range(1, len(chunks)):
        reduced[part] = after(reduced[part], attn_grad)
        other_reduced.append(swap_x(reduced[part]))
    halves = [both_halves(mine, other, ctx) for mine, other in zip(reduced, other_reduced)]

    def ffn_out(which):
        return jnp.concatenate(
            [
                halves[part][side][:, which * chunk : (which + 1) * chunk]
                for side in range(2)
                for part, chunk in enumerate(chunks)
            ],
            axis=1,
        )

    ffn_grads = [ffn_out(which) for which in range(3)]
    result = share_in_ctx(result_own, result_beside, y, core)
    normed_parts = last_parts(*normed_first, beside=[result, *ffn_grads])
    tokens_grad_own = norm_back(normed_parts, tokens_low, gain_one, d_own)
    attn_reduced = lax.psum_scatter(attn_grad, "fsdp", scatter_dimension=0, tiled=True)
    attn_reduced = after(attn_reduced, tokens_grad_own)
    other_attn = swap_x(attn_reduced)
    def gain_part(pairs):
        return sum(jnp.sum(mine.astype(F32) * grad.astype(F32), axis=1) for mine, grad in pairs)

    gain_sums = jnp.stack(
        [
            gain_part([(attn_shard[:, q_width:], attn_reduced[:, q_width:])]),
            gain_part(
                [
                    (ffn_shards[part][:, : 2 * chunk], reduced[part][:, : 2 * chunk])
                    for part, chunk in enumerate(chunks)
                ]
            ),
        ]
    )
    gain_sums = gain_sums + swap_core(gain_sums)
    gain_sums = gain_sums + swap_y(gain_sums)
    gain_sums = gain_sums + swap_x(gain_sums)

    tokens_grad_beside, gain_sums, other_attn, result, *ffn_grads = lax.optimization_barrier(
        (swap_y(tokens_grad_own), gain_sums, other_attn, result, *ffn_grads)
    )
    tokens_grad = share_in_ctx(tokens_grad_own, tokens_grad_beside, y, core)
    attn_gain_grad = gain_sums[0] / attn_gain.astype(F32)
    ffn_gain_grad = gain_sums[1] / ffn_gain.astype(F32)
    attn_low, attn_high = both_halves(attn_reduced, other_attn, ctx)

    def attn_out(begin, end):
        return jnp.concatenate([attn_low[:, begin:end], attn_high[:, begin:end]], axis=1)

    q_end, k_end = 2 * q_width, 2 * q_width + kv_width
    return (
        result,
        tokens_grad,
        attn_out(q_width, q_end),
        attn_out(q_end, k_end),
        attn_out(k_end, k_end + kv_width),
        attn_out(0, q_width),
        attn_gain_grad,
        *ffn_grads,
        ffn_gain_grad,
    )


def solution(mesh):
    rows = P(("fsdp", "ctx"), None)
    matrix = P("fsdp", "tp")
    vector = P("fsdp")
    return jax.shard_map(
        shards,
        mesh=mesh,
        in_specs=(
            rows,
            matrix,
            matrix,
            matrix,
            matrix,
            vector,
            matrix,
            matrix,
            matrix,
            vector,
            P("fsdp", None),
            P("fsdp", None),
            rows,
        ),
        out_specs=(
            rows,
            rows,
            matrix,
            matrix,
            matrix,
            matrix,
            vector,
            matrix,
            matrix,
            matrix,
            vector,
        ),
        check_vma=False,
    )
```

```python
import functools
import math

import jax
import jax.numpy as jnp
from jax import lax
from jax.experimental import pallas as pl
from jax.experimental.pallas import tpu as pltpu
from jax.sharding import PartitionSpec as P

HEAD_DIM = 64
EPSILON = 1e-05
ROPE_BASE = 500000.0
MASKED = -1e30
LOG2_E = 1.4426950408889634
BLOCK = 256
SPLIT = (1, 1)
VMEM = 56 * 2**20

F32 = jnp.float32
BF16 = jnp.bfloat16

PAIR = [(0, 1), (1, 0)]
CORE = [(0, 1), (1, 0), (2, 3), (3, 2)]
ACROSS = [(0, 2), (2, 0), (1, 3), (3, 1)]


def joint_pairs(x_core):
    pairs = []
    for ctx in range(2):
        for tp in range(4):
            there = (1 - ctx) * 4 + tp if tp % 2 == x_core else ctx * 4 + (tp ^ 2)
            pairs.append((ctx * 4 + tp, there))
    return pairs


FIRST = joint_pairs(0)
SECOND = joint_pairs(1)


def swap_core(v):
    return lax.ppermute(v, "tp", CORE)


def swap_y(v):
    return lax.ppermute(v, "tp", ACROSS)


def swap_x(v):
    return lax.ppermute(v, "ctx", PAIR)


def swap_first(v):
    return lax.ppermute(v, ("ctx", "tp"), FIRST)


def swap_second(v):
    return lax.ppermute(v, ("ctx", "tp"), SECOND)


def after(value, *others):
    return lax.optimization_barrier((value,) + others)[0]


def params(*semantics):
    return pltpu.CompilerParams(vmem_limit_bytes=VMEM)


def cost(gigaflops=0):
    return pl.CostEstimate(flops=int(gigaflops * 1e9) + 1, bytes_accessed=1, transcendentals=0)


def inv_rms(hidden):
    return lax.rsqrt(jnp.mean(hidden * hidden, axis=-1, keepdims=True) + EPSILON)


def rms_back(hidden, gain, grad):
    scale = inv_rms(hidden)
    weighted = grad * gain
    inner = jnp.mean(weighted * hidden, axis=-1, keepdims=True)
    return scale * weighted - hidden * (scale * scale * scale) * inner


def norm_back_kernel(count, *refs):
    hidden_ref, gain_ref, kept_ref, o_ref = refs[count:]
    grad = sum(ref[...].astype(F32) for ref in refs[:count])
    back = rms_back(hidden_ref[...].astype(F32), gain_ref[...], grad)
    o_ref[...] = (kept_ref[...].astype(F32) + back).astype(BF16)


def norm_back(parts, hidden, gain, kept):
    rows, depth = hidden.shape
    step = min(64, rows)
    block = pl.BlockSpec((step, depth), lambda i: (i, 0))
    return pl.pallas_call(
        functools.partial(norm_back_kernel, len(parts)),
        out_shape=jax.ShapeDtypeStruct((rows, depth), BF16),
        grid=(rows // step,),
        in_specs=[block] * (len(parts) + 1)
        + [pl.BlockSpec((1, depth), lambda i: (0, 0)), block],
        out_specs=block,
        compiler_params=params(),
        cost_estimate=cost(),
        name="norm_back",
    )(*parts, hidden, gain, kept)


def turn_lanes(u, first):
    return jnp.where(first, pltpu.roll(u, 96, 1), pltpu.roll(u, 32, 1))


def stream_scratch(count, rows, depth):
    return [pltpu.VMEM((2, rows, depth), BF16), pltpu.SemaphoreType.DMA((2,))] * count


def next_piece(refs, buffer, sems):
    i = pl.program_id(0)

    def copy_of(piece):
        return pltpu.make_async_copy(refs[piece], buffer.at[piece % 2], sems.at[piece % 2])

    @pl.when(i == 0)
    def _():
        copy_of(0).start()

    for piece in range(1, len(refs)):

        @pl.when(i == piece - 1)
        def _(piece=piece):
            copy_of(piece).start()

    for piece in range(len(refs)):

        @pl.when(i == piece)
        def _(piece=piece):
            copy_of(piece).wait()

    return buffer[lax.rem(i, 2)]


def qkv_kernel(count, *refs):
    gain_ref, wq_ref, wkv_ref, cos_ref, sin_ref, o_ref, buffer, sems = refs[count:]
    cos, sin = cos_ref[...], sin_ref[...]
    depth = gain_ref.shape[1]
    lane = lax.broadcasted_iota(jnp.int32, cos.shape, 1)
    first = (lane % 64) < 32
    x = next_piece(refs[:count], buffer, sems).astype(F32)
    x = (x * inv_rms(x) * gain_ref[...]).astype(BF16)
    o_ref[:, :depth] = x
    raw = jnp.dot(x, wq_ref[...], preferred_element_type=F32)
    tiles = raw.shape[1] // 128
    for tile in range(tiles):
        u = raw[:, tile * 128 : (tile + 1) * 128]
        turned = u * cos + turn_lanes(u, first) * sin
        o_ref[:, depth + tile * 128 : depth + (tile + 1) * 128] = turned.astype(BF16)
    u = jnp.dot(x, wkv_ref[...], preferred_element_type=F32)
    turned = u * cos + turn_lanes(u, first) * sin
    o_ref[:, depth + tiles * 128 :] = jnp.where(lane < 64, turned, u).astype(BF16)


def project_qkv(x, gain, w, q_width, cos, sin):
    step, depth = x[0].shape
    rows = len(x) * step
    width = depth + q_width + 128
    return pl.pallas_call(
        functools.partial(qkv_kernel, len(x)),
        out_shape=jax.ShapeDtypeStruct((rows, width), BF16),
        grid=(len(x),),
        in_specs=[pl.BlockSpec(memory_space=pl.ANY)] * len(x)
        + [
            pl.BlockSpec((1, depth), lambda i: (0, 0)),
            pl.BlockSpec((depth, q_width), lambda i: (0, 1)),
            pl.BlockSpec((depth, 128), lambda i: (0, 2 * q_width // 128)),
            pl.BlockSpec((step, 128), lambda i: (i, 0)),
            pl.BlockSpec((step, 128), lambda i: (i, 0)),
        ],
        out_specs=pl.BlockSpec((step, width), lambda i: (i, 0)),
        scratch_shapes=stream_scratch(1, step, depth),
        compiler_params=params(),
        cost_estimate=cost(),
        name="qkv",
    )(*x, gain, w, w, cos, sin)


def ffn_kernel(count, *refs):
    w_ref, o_ref, x_buffer, x_sems, c_buffer, c_sems = refs[2 * count :]
    n = w_ref.shape[1] // 3
    x = next_piece(refs[:count], x_buffer, x_sems)
    c = next_piece(refs[count : 2 * count], c_buffer, c_sems)
    gate = jnp.dot(x, w_ref[:, :n], preferred_element_type=F32)
    up = jnp.dot(x, w_ref[:, n : 2 * n], preferred_element_type=F32)
    d_mixed = jnp.dot(c, w_ref[:, 2 * n :], preferred_element_type=F32)
    sig = 1.0 / (1.0 + jnp.exp(-gate))
    silu = gate * sig
    o_ref[:, :n] = (d_mixed * up * (sig * (1.0 + gate * (1.0 - sig)))).astype(BF16)
    o_ref[:, n : 2 * n] = (d_mixed * silu).astype(BF16)
    o_ref[:, 2 * n :] = (silu * up).astype(BF16)


def ffn_chunk(x, cot, w):
    step, depth = x[0].shape
    rows = len(x) * step
    width = w.shape[1]
    return pl.pallas_call(
        functools.partial(ffn_kernel, len(x)),
        out_shape=jax.ShapeDtypeStruct((rows, width), BF16),
        grid=(len(x),),
        in_specs=[pl.BlockSpec(memory_space=pl.ANY)] * (2 * len(x))
        + [pl.BlockSpec((depth, width), lambda i: (0, 0))],
        out_specs=pl.BlockSpec((step, width), lambda i: (i, 0)),
        scratch_shapes=stream_scratch(2, step, depth),
        compiler_params=params(),
        cost_estimate=cost(),
        name="ffn",
    )(*x, *cot, w)


DOWN = (((0,), (0,)), ((), ()))


def grads_kernel(x_count, y_count, *refs):
    a_ref, b_ref, o_ref = refs[x_count + y_count :]
    split = a_ref.shape[1]

    def product(tall_refs, right_ref):
        tall = jnp.concatenate([ref[...] for ref in tall_refs], axis=0)
        return lax.dot_general(
            tall, right_ref[...].astype(BF16), DOWN, preferred_element_type=F32
        ).astype(BF16)

    o_ref[:, :split] = product(refs[:x_count], a_ref)
    o_ref[:, split:] = product(refs[x_count : x_count + y_count], b_ref)


def weight_grads(x, a, a_width, a_column, y, b, b_width, b_column):
    depth = x[0].shape[1]
    rows = a.shape[0]
    width = a_width + b_width
    step = 512
    return pl.pallas_call(
        functools.partial(grads_kernel, len(x), len(y)),
        out_shape=jax.ShapeDtypeStruct((depth, width), BF16),
        grid=(depth // step,),
        in_specs=[pl.BlockSpec((piece.shape[0], step), lambda i: (0, i)) for piece in (*x, *y)]
        + [
            pl.BlockSpec((rows, a_width), lambda i: (0, a_column)),
            pl.BlockSpec((rows, b_width), lambda i: (0, b_column)),
        ],
        out_specs=pl.BlockSpec((step, width), lambda i: (i, 0)),
        compiler_params=params(),
        cost_estimate=cost(20),
        name="weight_grads",
    )(*x, *y, a, b)


def back_kernel(count, *refs):
    o_ref = refs[-1]
    total = refs[2 * count][...].astype(F32) if len(refs) > 2 * count + 1 else None
    for part in range(count):
        term = lax.dot_general(
            refs[part][...].astype(BF16),
            refs[count + part][...],
            (((1,), (1,)), ((), ())),
            preferred_element_type=F32,
        )
        total = term if total is None else total + term
    o_ref[...] = total.astype(BF16)


def back_product(terms, part=0, parts=1, plus=(), work=0):
    rows = terms[0][0].shape[0] // parts
    depth = terms[0][2].shape[0]
    step = min(512, rows)
    ahead = part * (rows // step)
    return pl.pallas_call(
        functools.partial(back_kernel, len(terms)),
        out_shape=jax.ShapeDtypeStruct((rows, depth), BF16),
        grid=(rows // step,),
        in_specs=[
            pl.BlockSpec((step, term[4]), lambda i, column=term[1]: (i + ahead, column))
            for term in terms
        ]
        + [pl.BlockSpec((depth, term[4]), lambda i, column=term[3]: (0, column)) for term in terms]
        + [pl.BlockSpec((step, depth), lambda i: (i + ahead, 0))] * len(plus),
        out_specs=pl.BlockSpec((step, depth), lambda i: (i, 0)),
        compiler_params=params(),
        cost_estimate=cost(work),
        name="back",
    )(*[term[0] for term in terms], *[term[2] for term in terms], *plus)


def front_kernel(count, *refs):
    w_ref, o_ref, buffer, sems = refs[count:]
    x = next_piece(refs[:count], buffer, sems)
    o_ref[...] = jnp.dot(x, w_ref[...], preferred_element_type=F32).astype(BF16)


def front_product(x, w, width, column):
    step, depth = x[0].shape
    rows = len(x) * step
    return pl.pallas_call(
        functools.partial(front_kernel, len(x)),
        out_shape=jax.ShapeDtypeStruct((rows, width), BF16),
        grid=(len(x),),
        in_specs=[pl.BlockSpec(memory_space=pl.ANY)] * len(x)
        + [pl.BlockSpec((depth, width), lambda i: (0, column))],
        out_specs=pl.BlockSpec((step, width), lambda i: (i, 0)),
        scratch_shapes=stream_scratch(1, step, depth),
        compiler_params=params(),
        cost_estimate=cost(),
        name="front",
    )(*x, w)


def stack_heads(block):
    count = block.shape[1] // HEAD_DIM
    return jnp.concatenate(
        [block[:, h * HEAD_DIM : (h + 1) * HEAD_DIM] for h in range(count)], axis=0
    )


def unstack_heads(stacked):
    count = stacked.shape[0] // BLOCK
    return jnp.concatenate([stacked[h * BLOCK : (h + 1) * BLOCK] for h in range(count)], axis=1)


def allowed_of(i, j, start):
    row = i * BLOCK + lax.broadcasted_iota(jnp.int32, (BLOCK, BLOCK), 0)
    col = j * BLOCK + lax.broadcasted_iota(jnp.int32, (BLOCK, BLOCK), 1)
    return (col <= row) & (col >= start)


def attend_kernel(place, first, q_ref, kv_ref, start_ref, o_ref):
    i = pl.program_id(0)
    q = stack_heads(q_ref[...])
    heads = q.shape[0] // BLOCK
    start = start_ref[...]

    def step(j, carry):
        top, total, acc = carry
        at = pl.multiple_of(place[j] * BLOCK, BLOCK)
        kv = kv_ref[pl.ds(at, BLOCK), :]
        raw = lax.dot_general(
            q, kv[:, :HEAD_DIM], (((1,), (1,)), ((), ())), preferred_element_type=F32
        ) * (HEAD_DIM**-0.5 * LOG2_E)
        allowed = allowed_of(i, j, start)
        scores = jnp.where(allowed[None], raw.reshape(heads, BLOCK, BLOCK), MASKED).reshape(
            heads * BLOCK, BLOCK
        )
        new_top = jnp.maximum(top, jnp.max(scores, axis=-1, keepdims=True))
        keep = jnp.exp2(top - new_top)
        probs = jnp.exp2(scores - new_top)
        total = total * keep + jnp.sum(probs, axis=-1, keepdims=True)
        acc = acc * keep + jnp.dot(probs.astype(BF16), kv, preferred_element_type=F32)
        return (new_top, total, acc)

    size = heads * BLOCK
    top, total, acc = lax.fori_loop(
        first[i],
        i + 1,
        step,
        (
            jnp.full((size, 1), MASKED, F32),
            jnp.zeros((size, 1), F32),
            jnp.zeros((size, 2 * HEAD_DIM), F32),
        ),
    )
    out = acc[:, HEAD_DIM:] / total
    q_width = q_ref.shape[1]
    o_ref[:, :q_width] = unstack_heads(out)
    lse = top + jnp.log2(total)
    lane = lax.broadcasted_iota(jnp.int32, (BLOCK, 128), 1)
    packed = jnp.zeros((BLOCK, 128), F32)
    for h in range(heads):
        packed = jnp.where(lane == h, lse[h * BLOCK : (h + 1) * BLOCK], packed)
    o_ref[:, q_width:] = packed


def attend(qkv, depth, place, first, start, q_width):
    rows = qkv.shape[0]
    blocks = rows // BLOCK
    return pl.pallas_call(
        attend_kernel,
        out_shape=jax.ShapeDtypeStruct((rows, q_width + 128), F32),
        grid_spec=pltpu.PrefetchScalarGridSpec(
            num_scalar_prefetch=2,
            grid=(blocks,),
            in_specs=[
                pl.BlockSpec((BLOCK, q_width), lambda i, place, first: (place[i], depth // q_width)),
                pl.BlockSpec((rows, 128), lambda i, place, first: (0, (depth + q_width) // 128)),
                pl.BlockSpec((BLOCK, 1), lambda i, place, first: (i, 0)),
            ],
            out_specs=pl.BlockSpec((BLOCK, q_width + 128), lambda i, place, first: (place[i], 0)),
        ),
        compiler_params=params(),
        cost_estimate=cost(),
        name="attend",
    )(place, first, qkv, qkv, start)


def attend_back_kernel(
    place,
    first,
    q_ref,
    d_ref,
    h_ref,
    kv_ref,
    start_ref,
    cos_ref,
    sin_ref,
    o_ref,
    dkv_ref,
):
    i = pl.program_id(0)
    blocks = pl.num_programs(0)
    score_scale = HEAD_DIM**-0.5
    q_width = q_ref.shape[1]

    @pl.when(i == 0)
    def _():
        dkv_ref[...] = jnp.zeros_like(dkv_ref)

    q = stack_heads(q_ref[...])
    d_out = stack_heads(d_ref[...])
    heads = q.shape[0] // BLOCK
    out = stack_heads(h_ref[:, :q_width])
    delta = jnp.sum(d_out.astype(F32) * out, axis=-1, keepdims=True)
    lse_block = h_ref[:, q_width:]
    lse = jnp.concatenate([lse_block[:, h : h + 1] for h in range(heads)], axis=0)
    start = start_ref[...]

    def step(j, d_q):
        at = pl.multiple_of(place[j] * BLOCK, BLOCK)
        kv = kv_ref[pl.ds(at, BLOCK), :]
        k, v = kv[:, :HEAD_DIM], kv[:, HEAD_DIM:]
        across = (((1,), (1,)), ((), ()))
        down = (((0,), (0,)), ((), ()))
        raw = lax.dot_general(q, k, across, preferred_element_type=F32) * (score_scale * LOG2_E)
        allowed = allowed_of(i, j, start)
        scores = jnp.where(allowed[None], raw.reshape(heads, BLOCK, BLOCK), MASKED).reshape(
            heads * BLOCK, BLOCK
        )
        probs = jnp.exp2(scores - lse)
        d_probs = lax.dot_general(d_out, v, across, preferred_element_type=F32)
        d_scores = (probs * (d_probs - delta)).astype(BF16)
        d_k = lax.dot_general(d_scores, q, down, preferred_element_type=F32) * score_scale
        d_v = lax.dot_general(probs.astype(BF16), d_out, down, preferred_element_type=F32)
        here = pl.ds(pl.multiple_of(j * BLOCK, BLOCK), BLOCK)
        dkv_ref[here, :] += jnp.concatenate([d_k, d_v], axis=1)
        return d_q + jnp.dot(d_scores, k, preferred_element_type=F32)

    d_q = lax.fori_loop(first[i], i + 1, step, jnp.zeros((heads * BLOCK, HEAD_DIM), F32))
    d_q = unstack_heads(d_q * score_scale)
    lane = lax.broadcasted_iota(jnp.int32, (BLOCK, 128), 1)
    front = (lane % 64) < 32
    mine = pl.ds(pl.multiple_of(place[i] * BLOCK, BLOCK), BLOCK)
    cos, sin = cos_ref[mine, :], sin_ref[mine, :]
    for tile in range(q_width // 128):
        u = d_q[:, tile * 128 : (tile + 1) * 128]
        o_ref[mine, tile * 128 : (tile + 1) * 128] = (u * cos - turn_lanes(u, front) * sin).astype(
            BF16
        )

    @pl.when(i == blocks - 1)
    def _():
        for b in range(dkv_ref.shape[0] // BLOCK):
            there = pl.ds(pl.multiple_of(place[b] * BLOCK, BLOCK), BLOCK)
            u = dkv_ref[b * BLOCK : (b + 1) * BLOCK, :]
            turned = u * cos_ref[there, :] - turn_lanes(u, front) * sin_ref[there, :]
            o_ref[there, q_width:] = jnp.where(lane < HEAD_DIM, turned, u).astype(BF16)


def attend_back(qkv, depth, d_heads, heads, place, first, start, cos, sin):
    rows, q_width = d_heads.shape
    width = q_width + 128
    blocks = rows // BLOCK
    by_place = lambda i, place, first: (place[i], 0)
    whole = lambda i, place, first: (0, 0)
    return pl.pallas_call(
        attend_back_kernel,
        out_shape=jax.ShapeDtypeStruct((rows, width), BF16),
        grid_spec=pltpu.PrefetchScalarGridSpec(
            num_scalar_prefetch=2,
            grid=(blocks,),
            in_specs=[
                pl.BlockSpec((BLOCK, q_width), lambda i, place, first: (place[i], depth // q_width)),
                pl.BlockSpec((BLOCK, q_width), by_place),
                pl.BlockSpec((BLOCK, q_width + 128), by_place),
                pl.BlockSpec((rows, 128), lambda i, place, first: (0, (depth + q_width) // 128)),
                pl.BlockSpec((BLOCK, 1), lambda i, place, first: (i, 0)),
                pl.BlockSpec((rows, 128), whole),
                pl.BlockSpec((rows, 128), whole),
            ],
            out_specs=pl.BlockSpec((rows, width), whole),
            scratch_shapes=[pltpu.VMEM((rows, 128), F32)],
        ),
        compiler_params=params(),
        cost_estimate=cost(),
        name="attend_back",
    )(place, first, qkv, d_heads, heads, qkv, start, cos, sin)


def sum_cores(terms, pieces=2):
    sent = [back_product(terms, 2 * pieces - 1 - at, 2 * pieces) for at in range(pieces)]
    arrived = [swap_core(piece) for piece in sent]
    return add_blocks(back_product(terms, 0, 2), arrived)


def add_blocks(mine, arrived):
    rows = mine.shape[0] // 4
    each = 4 // len(arrived)
    blocks = []
    for at in range(4):
        other = arrived[len(arrived) - 1 - at // each]
        begin = (at % each) * rows
        blocks.append(mine[at * rows : (at + 1) * rows] + other[begin : begin + rows])
    return blocks


def sum_first(blocks, early=()):
    own, along_a, along_b, both = blocks
    along_a = along_a + after(swap_second(both), *early)
    return (own, *lax.optimization_barrier((along_a, along_b)))


def last_parts(own, along_a, along_b, beside=()):
    return own, swap_second(along_b), after(swap_first(along_a), *beside)


def halves_of_cores(terms, plus):
    arrived = swap_core(back_product(terms, 1, 2, plus))
    mine = back_product(terms, 0, 2, plus)
    rows = mine.shape[0] // 4
    return mine[2 * rows :] + arrived[2 * rows :], mine[: 2 * rows] + arrived[: 2 * rows]


def wide_first(far, near, between):
    return after(near + swap_second(far), *between)


def wide_last(near, beside):
    return near, after(swap_first(near[near.shape[0] // 2 :]), *beside)


def share_rows(own, beside=()):
    beside = list(beside) + [()] * (2 - len(beside))
    one, two, *_ = lax.optimization_barrier((swap_first(own), swap_second(own), *beside[0]))
    early = tuple(swap_core(part) for part in (own, one, two))
    last = after(swap_second(one), *early, *beside[1])
    return (own, one, two, last, *early, swap_core(last))


def ring_over(shard, count, held):
    cycle = [(at, (at + 1) % count) for at in range(count)]
    pieces = [shard]
    for step in range(count - 1):
        sent = after(pieces[-1], *held) if step == 1 else pieces[-1]
        pieces.append(lax.ppermute(sent, "fsdp", cycle))
    return pieces


def in_place(pieces, axis):
    count, size = len(pieces), pieces[0].shape[axis]
    here = lax.axis_index("fsdp")
    shape = list(pieces[0].shape)
    shape[axis] *= count
    whole = jnp.zeros(shape, pieces[0].dtype)
    for back, piece in enumerate(pieces):
        owner = lax.rem(here + count - back, count)
        whole = lax.dynamic_update_slice_in_dim(whole, piece, owner * size, axis)
    return whole


def share_in_ctx(own, beside, y, core):
    pair = jnp.stack([own, beside])
    other = jnp.stack([swap_core(own), swap_core(beside)])
    four = jnp.stack([pair, other])
    four = jnp.where(y == 1, four[:, ::-1], four)
    four = jnp.where(core == 1, four[::-1], four)
    return four.transpose(1, 0, 2, 3).reshape(-1, own.shape[1])


def both_halves(own, other, ctx):
    low = jnp.where(ctx == 0, own, other).astype(F32)
    high = jnp.where(ctx == 0, other, own).astype(F32)
    return low, high


def shards(
    tokens,
    q_weight,
    k_weight,
    v_weight,
    o_weight,
    attn_gain,
    gate_weight,
    up_weight,
    down_weight,
    ffn_gain,
    lengths,
    deal,
    cotangent,
):
    ctx = lax.axis_index("ctx")
    tp = lax.axis_index("tp")
    y, core = tp // 2, tp % 2
    row_count, depth = tokens.shape
    group_rows = row_count * lax.axis_size("ctx")
    own_rows = row_count // lax.axis_size("tp")

    def half(weight):
        width = weight.shape[1] // 2
        return lax.dynamic_slice_in_dim(weight, ctx * width, width, 1)

    length_row, deal_row = lengths[0], deal[0]
    spans = deal_row.shape[0]
    span_rows = group_rows // spans
    ends = jnp.cumsum(length_row, dtype=jnp.int32)
    starts = ends - length_row
    natural = jnp.arange(group_rows, dtype=jnp.int32)
    inside = (natural[:, None] >= starts[None]) & (natural[:, None] < ends[None])
    start_of = jnp.sum(jnp.where(inside, starts[None], 0), axis=1, dtype=jnp.int32)
    first = start_of[::BLOCK] // BLOCK
    rel = jnp.arange(group_rows // own_rows, dtype=jnp.int32)
    rel_core = core ^ (rel // 4)
    by_first, by_second = rel % 2, (rel // 2) % 2
    rel_ctx = ctx ^ jnp.where(rel_core == 0, by_first, by_second)
    rel_y = y ^ jnp.where(rel_core == 0, by_second, by_first)
    dealt_block = rel_ctx * (row_count // own_rows) + rel_y * 2 + rel_core
    per_span = span_rows // own_rows
    span_of = jnp.sum(
        jnp.where(
            (dealt_block // per_span)[:, None] == jnp.arange(spans, dtype=jnp.int32)[None],
            deal_row[None],
            0,
        ),
        axis=1,
        dtype=jnp.int32,
    )
    natural_block = span_of * per_span + dealt_block % per_span
    place = jnp.sum(
        jnp.where(natural_block[None, :] == rel[:, None], rel[None, :], 0), axis=1, dtype=jnp.int32
    )
    natural_rel = (
        natural_block[:, None] * own_rows + jnp.arange(own_rows, dtype=jnp.int32)[None]
    ).reshape(-1)
    inside_rel = (natural_rel[:, None] >= starts[None]) & (natural_rel[:, None] < ends[None])
    position = natural_rel - jnp.sum(
        jnp.where(inside_rel, starts[None], 0), axis=1, dtype=jnp.int32
    )
    lane = jnp.arange(128, dtype=jnp.int32)
    inverse = jnp.exp((lane % 32).astype(F32) * (-2.0 * math.log(ROPE_BASE) / HEAD_DIM))
    angles = position.astype(F32)[:, None] * inverse[None]
    cos = jnp.cos(angles)
    sin = jnp.where((lane % 64 < 32)[None], -jnp.sin(angles), jnp.sin(angles))
    start_column = start_of[:, None]

    q_half, k_half, v_half, o_half = map(half, (q_weight, k_weight, v_weight, o_weight))
    q_width, kv_width = q_half.shape[1], k_half.shape[1]
    attn_shard = jnp.concatenate([o_half, q_half, k_half, v_half], axis=1)
    fsdp = lax.axis_size("fsdp")
    gain_rows = jnp.stack([attn_gain, ffn_gain])
    gain_width = attn_gain.shape[0]
    extra = ((0, 14), (0, attn_shard.shape[1] - gain_width))
    tokens_low = lax.dynamic_slice_in_dim(tokens, tp * own_rows, own_rows, 0)
    cot_low = lax.dynamic_slice_in_dim(cotangent, tp * own_rows, own_rows, 0)
    tokens_one = swap_first(tokens_low)
    attn_ring = ring_over(
        jnp.concatenate([attn_shard, jnp.pad(gain_rows, extra)]),
        fsdp,
        (tokens_one, cos, sin, cot_low, place, first, start_column),
    )
    own_depth = attn_shard.shape[0]
    attn_full = in_place([piece[:own_depth] for piece in attn_ring], 0)
    gains = in_place([piece[own_depth : own_depth + 2, :gain_width] for piece in attn_ring], 1)
    gain_one = gains[0].astype(F32)[None]
    gain_two = gains[1].astype(F32)[None]
    ff_half = gate_weight.shape[1] // 2
    chunks = [ff_half * share // sum(SPLIT) for share in SPLIT]
    ffn_shards = []
    for part, chunk in enumerate(chunks):
        at = ctx * ff_half + sum(chunks[:part])
        ffn_shards.append(
            jnp.concatenate(
                [
                    lax.dynamic_slice_in_dim(weight, at, chunk, 1)
                    for weight in (gate_weight, up_weight, down_weight)
                ],
                axis=1,
            )
        )
    tokens_own, cot_own = tokens_low.astype(F32), cot_low.astype(F32)
    group_tokens = (tokens_low, tokens_one, swap_second(tokens_low), swap_second(tokens_one))
    first_shard = after(ffn_shards[0], attn_ring[-1], *group_tokens[2:])
    group_tokens = group_tokens + tuple(swap_core(part) for part in group_tokens)
    attn_full, cot_low, cos, sin, gain_one, *group_tokens = lax.optimization_barrier(
        (attn_full, cot_low, cos, sin, gain_one, *group_tokens)
    )
    qkv = project_qkv(group_tokens, gain_one, attn_full, q_width, cos, sin)
    heads = attend(qkv, depth, place, first, start_column, q_width)
    cot = share_rows(cot_low, [[qkv], [heads]])
    ffn_full = [
        lax.all_gather(shard, "fsdp", axis=0, tiled=True)
        for shard in (first_shard, after(ffn_shards[1], heads))
    ]
    heads = after(heads, *cot)
    attn_blocks = sum_cores([(heads, 0, attn_full, 0, q_width)])
    attn_parts = last_parts(*sum_first(attn_blocks), beside=ffn_full[:1])
    attn_sum = sum(part.astype(F32) for part in attn_parts)
    hidden = tokens_own + attn_sum
    normed_two = share_rows((hidden * inv_rms(hidden) * gain_two).astype(BF16))

    acts = []
    grad_parts = []
    d_norm_partial = ()

    def chunk_grads(part, held=()):
        chunk = chunks[part]
        act = after(acts[part], *held)
        grad_parts.append(weight_grads(normed_two, act, 2 * chunk, 0, cot, act, chunk, 2))

    last = len(chunks) - 1
    for part in range(len(chunks)):
        normed_two = (after(normed_two[0], *grad_parts, *d_norm_partial), *normed_two[1:])
        acts.append(ffn_chunk(normed_two, cot, ffn_full[part]))
        d_norm_term = (acts[part], 0, ffn_full[part], 0, 2 * chunks[part])
        if part < last:
            chunk_grads(part)
            d_norm_partial = (back_product([d_norm_term], plus=d_norm_partial),)
    ffn_terms = [(acts[part], 2, ffn_full[part], 2, chunk) for part, chunk in enumerate(chunks)]
    d_norm_far, d_norm_near = halves_of_cores([d_norm_term], d_norm_partial)
    chunk_grads(last, (d_norm_far,))
    reduced = [
        lax.psum_scatter(part, "fsdp", scatter_dimension=0, tiled=True) for part in grad_parts
    ]
    d_norm_near = wide_first(d_norm_far, d_norm_near, grad_parts)

    def ffn_rows(part, parts, held):
        (act, *rest), *others = ffn_terms
        return back_product([(after(act, held), *rest), *others], part, parts, work=7)

    ffn_sent = [ffn_rows(3, 4, d_norm_near)]
    d_own = norm_back(wide_last(d_norm_near, ffn_sent), hidden, gain_two, cot_low)
    ffn_sent.append(ffn_rows(2, 4, d_own))
    ffn_mine = ffn_rows(0, 2, d_own)
    d_one, d_two, ffn_mine, ffn_sent[1] = lax.optimization_barrier(
        (swap_first(d_own), swap_second(d_own), ffn_mine, ffn_sent[1])
    )
    ffn_own, ffn_a, ffn_b, ffn_both = add_blocks(ffn_mine, [swap_core(piece) for piece in ffn_sent])
    ffn_x, ffn_y = jnp.where(core == 0, ffn_a, ffn_b), jnp.where(core == 0, ffn_b, ffn_a)
    d_early = [swap_core(part) for part in (d_own, d_one, d_two)]
    d_last = after(swap_second(d_one), *d_early, ffn_own, ffn_x, ffn_y, ffn_both, reduced[0])
    d_attn = (d_own, d_one, d_two, d_last, *d_early, swap_core(d_last))

    d_heads = front_product(d_attn, attn_full, q_width, 0)
    other_reduced = [swap_x(after(reduced[0], d_last))]
    d_qkv = attend_back(qkv, depth, d_heads, heads, place, first, start_column, cos, sin)
    y_both, y_own, d_qkv, other_reduced[0] = lax.optimization_barrier(
        (swap_y(ffn_both), swap_y(ffn_y), d_qkv, other_reduced[0])
    )
    ffn_x, ffn_own, d_qkv = lax.optimization_barrier((ffn_x + y_both, ffn_own + y_own, d_qkv))
    ffn_far = swap_x(ffn_x)
    normed_blocks = sum_cores(
        [
            (d_qkv, 0, attn_full, 1, q_width),
            (d_qkv, q_width // 128, attn_full, 2 * q_width // 128, 128),
        ]
    )
    attn_grad = weight_grads(
        d_attn, heads, q_width, 0, (qkv,), after(d_qkv, normed_blocks[3]), q_width + 128, 0
    )
    ffn_far = after(ffn_far, attn_grad)
    result_own = (hidden + (ffn_own.astype(F32) + ffn_far.astype(F32))).astype(BF16)
    result_beside = swap_y(result_own)
    normed_first = sum_first(normed_blocks, [attn_grad, result_own])
    for part in range(1, len(chunks)):
        reduced[part] = after(reduced[part], attn_grad)
        other_reduced.append(swap_x(reduced[part]))
    late = [after(part, normed_first[1]) for part in other_reduced]
    halves = [both_halves(mine, other, ctx) for mine, other in zip(reduced, late)]

    def ffn_out(which):
        return jnp.concatenate(
            [
                halves[part][side][:, which * chunk : (which + 1) * chunk]
                for side in range(2)
                for part, chunk in enumerate(chunks)
            ],
            axis=1,
        )

    ffn_grads = [ffn_out(which) for which in range(3)]
    result = share_in_ctx(result_own, result_beside, y, core)
    normed_parts = last_parts(*normed_first, beside=[result, *ffn_grads])
    tokens_grad_own = norm_back(normed_parts, tokens_low, gain_one, d_own)
    attn_reduced = lax.psum_scatter(attn_grad, "fsdp", scatter_dimension=0, tiled=True)
    attn_reduced = after(attn_reduced, tokens_grad_own)
    other_attn = swap_x(attn_reduced)
    def gain_part(pairs):
        return sum(jnp.sum(mine.astype(F32) * grad.astype(F32), axis=1) for mine, grad in pairs)

    gain_sums = jnp.stack(
        [
            gain_part([(attn_shard[:, q_width:], attn_reduced[:, q_width:])]),
            gain_part(
                [
                    (ffn_shards[part][:, : 2 * chunk], reduced[part][:, : 2 * chunk])
                    for part, chunk in enumerate(chunks)
                ]
            ),
        ]
    )
    gain_sums = gain_sums + swap_core(gain_sums)
    gain_sums = gain_sums + swap_y(gain_sums)
    gain_sums = gain_sums + swap_x(gain_sums)

    tokens_grad_beside, gain_sums, other_attn, result, *ffn_grads = lax.optimization_barrier(
        (swap_y(tokens_grad_own), gain_sums, other_attn, result, *ffn_grads)
    )
    tokens_grad = share_in_ctx(tokens_grad_own, tokens_grad_beside, y, core)
    attn_gain_grad = gain_sums[0] / attn_gain.astype(F32)
    ffn_gain_grad = gain_sums[1] / ffn_gain.astype(F32)
    attn_low, attn_high = both_halves(attn_reduced, other_attn, ctx)

    def attn_out(begin, end):
        return jnp.concatenate([attn_low[:, begin:end], attn_high[:, begin:end]], axis=1)

    q_end, k_end = 2 * q_width, 2 * q_width + kv_width
    return (
        result,
        tokens_grad,
        attn_out(q_width, q_end),
        attn_out(q_end, k_end),
        attn_out(k_end, k_end + kv_width),
        attn_out(0, q_width),
        attn_gain_grad,
        *ffn_grads,
        ffn_gain_grad,
    )


def solution(mesh):
    rows = P(("fsdp", "ctx"), None)
    matrix = P("fsdp", "tp")
    vector = P("fsdp")
    return jax.shard_map(
        shards,
        mesh=mesh,
        in_specs=(
            rows,
            matrix,
            matrix,
            matrix,
            matrix,
            vector,
            matrix,
            matrix,
            matrix,
            vector,
            P("fsdp", None),
            P("fsdp", None),
            rows,
        ),
        out_specs=(
            rows,
            rows,
            matrix,
            matrix,
            matrix,
            matrix,
            vector,
            matrix,
            matrix,
            matrix,
            vector,
        ),
        check_vma=False,
    )
```

```python
import functools
import math

import jax
import jax.numpy as jnp
from jax import lax
from jax.experimental import pallas as pl
from jax.experimental.pallas import tpu as pltpu
from jax.sharding import PartitionSpec as P

HEAD_DIM = 64
EPSILON = 1e-05
ROPE_BASE = 500000.0
MASKED = -1e30
LOG2_E = 1.4426950408889634
BLOCK = 256
SPLIT = (1, 1)
VMEM = 56 * 2**20

F32 = jnp.float32
BF16 = jnp.bfloat16

PAIR = [(0, 1), (1, 0)]
CORE = [(0, 1), (1, 0), (2, 3), (3, 2)]
ACROSS = [(0, 2), (2, 0), (1, 3), (3, 1)]


def joint_pairs(x_core):
    pairs = []
    for ctx in range(2):
        for tp in range(4):
            there = (1 - ctx) * 4 + tp if tp % 2 == x_core else ctx * 4 + (tp ^ 2)
            pairs.append((ctx * 4 + tp, there))
    return pairs


FIRST = joint_pairs(0)
SECOND = joint_pairs(1)


def swap_core(v):
    return lax.ppermute(v, "tp", CORE)


def swap_y(v):
    return lax.ppermute(v, "tp", ACROSS)


def swap_x(v):
    return lax.ppermute(v, "ctx", PAIR)


def swap_first(v):
    return lax.ppermute(v, ("ctx", "tp"), FIRST)


def swap_second(v):
    return lax.ppermute(v, ("ctx", "tp"), SECOND)


def after(value, *others):
    return lax.optimization_barrier((value,) + others)[0]


def params(*semantics):
    return pltpu.CompilerParams(vmem_limit_bytes=VMEM)


def cost(gigaflops=0):
    return pl.CostEstimate(flops=int(gigaflops * 1e9) + 1, bytes_accessed=1, transcendentals=0)


def inv_rms(hidden):
    return lax.rsqrt(jnp.mean(hidden * hidden, axis=-1, keepdims=True) + EPSILON)


def rms_back(hidden, gain, grad):
    scale = inv_rms(hidden)
    weighted = grad * gain
    inner = jnp.mean(weighted * hidden, axis=-1, keepdims=True)
    return scale * weighted - hidden * (scale * scale * scale) * inner


def norm_back_kernel(count, *refs):
    hidden_ref, gain_ref, kept_ref, o_ref = refs[count:]
    grad = sum(ref[...].astype(F32) for ref in refs[:count])
    back = rms_back(hidden_ref[...].astype(F32), gain_ref[...], grad)
    o_ref[...] = (kept_ref[...].astype(F32) + back).astype(BF16)


def norm_back(parts, hidden, gain, kept):
    rows, depth = hidden.shape
    step = min(64, rows)
    block = pl.BlockSpec((step, depth), lambda i: (i, 0))
    return pl.pallas_call(
        functools.partial(norm_back_kernel, len(parts)),
        out_shape=jax.ShapeDtypeStruct((rows, depth), BF16),
        grid=(rows // step,),
        in_specs=[block] * (len(parts) + 1)
        + [pl.BlockSpec((1, depth), lambda i: (0, 0)), block],
        out_specs=block,
        compiler_params=params(),
        cost_estimate=cost(),
        name="norm_back",
    )(*parts, hidden, gain, kept)


def turn_lanes(u, first):
    return jnp.where(first, pltpu.roll(u, 96, 1), pltpu.roll(u, 32, 1))


def stream_scratch(count, rows, depth):
    return [pltpu.VMEM((2, rows, depth), BF16), pltpu.SemaphoreType.DMA((2,))] * count


def next_piece(refs, buffer, sems):
    i = pl.program_id(0)

    def copy_of(piece):
        return pltpu.make_async_copy(refs[piece], buffer.at[piece % 2], sems.at[piece % 2])

    @pl.when(i == 0)
    def _():
        copy_of(0).start()

    for piece in range(1, len(refs)):

        @pl.when(i == piece - 1)
        def _(piece=piece):
            copy_of(piece).start()

    for piece in range(len(refs)):

        @pl.when(i == piece)
        def _(piece=piece):
            copy_of(piece).wait()

    return buffer[lax.rem(i, 2)]


def qkv_kernel(count, *refs):
    gain_ref, wq_ref, wkv_ref, cos_ref, sin_ref, o_ref, buffer, sems = refs[count:]
    cos, sin = cos_ref[...], sin_ref[...]
    depth = gain_ref.shape[1]
    lane = lax.broadcasted_iota(jnp.int32, cos.shape, 1)
    first = (lane % 64) < 32
    x = next_piece(refs[:count], buffer, sems).astype(F32)
    x = (x * inv_rms(x) * gain_ref[...]).astype(BF16)
    o_ref[:, :depth] = x
    raw = jnp.dot(x, wq_ref[...], preferred_element_type=F32)
    tiles = raw.shape[1] // 128
    for tile in range(tiles):
        u = raw[:, tile * 128 : (tile + 1) * 128]
        turned = u * cos + turn_lanes(u, first) * sin
        o_ref[:, depth + tile * 128 : depth + (tile + 1) * 128] = turned.astype(BF16)
    u = jnp.dot(x, wkv_ref[...], preferred_element_type=F32)
    turned = u * cos + turn_lanes(u, first) * sin
    o_ref[:, depth + tiles * 128 :] = jnp.where(lane < 64, turned, u).astype(BF16)


def project_qkv(x, gain, w, q_width, cos, sin):
    step, depth = x[0].shape
    rows = len(x) * step
    width = depth + q_width + 128
    return pl.pallas_call(
        functools.partial(qkv_kernel, len(x)),
        out_shape=jax.ShapeDtypeStruct((rows, width), BF16),
        grid=(len(x),),
        in_specs=[pl.BlockSpec(memory_space=pl.ANY)] * len(x)
        + [
            pl.BlockSpec((1, depth), lambda i: (0, 0)),
            pl.BlockSpec((depth, q_width), lambda i: (0, 1)),
            pl.BlockSpec((depth, 128), lambda i: (0, 2 * q_width // 128)),
            pl.BlockSpec((step, 128), lambda i: (i, 0)),
            pl.BlockSpec((step, 128), lambda i: (i, 0)),
        ],
        out_specs=pl.BlockSpec((step, width), lambda i: (i, 0)),
        scratch_shapes=stream_scratch(1, step, depth),
        compiler_params=params(),
        cost_estimate=cost(),
        name="qkv",
    )(*x, gain, w, w, cos, sin)


def ffn_kernel(count, *refs):
    w_ref, o_ref, x_buffer, x_sems, c_buffer, c_sems = refs[2 * count :]
    n = w_ref.shape[1] // 3
    x = next_piece(refs[:count], x_buffer, x_sems)
    c = next_piece(refs[count : 2 * count], c_buffer, c_sems)
    gate = jnp.dot(x, w_ref[:, :n], preferred_element_type=F32)
    up = jnp.dot(x, w_ref[:, n : 2 * n], preferred_element_type=F32)
    d_mixed = jnp.dot(c, w_ref[:, 2 * n :], preferred_element_type=F32)
    sig = 1.0 / (1.0 + jnp.exp(-gate))
    silu = gate * sig
    o_ref[:, :n] = (d_mixed * up * (sig * (1.0 + gate * (1.0 - sig)))).astype(BF16)
    o_ref[:, n : 2 * n] = (d_mixed * silu).astype(BF16)
    o_ref[:, 2 * n :] = (silu * up).astype(BF16)


def ffn_chunk(x, cot, w):
    step, depth = x[0].shape
    rows = len(x) * step
    width = w.shape[1]
    return pl.pallas_call(
        functools.partial(ffn_kernel, len(x)),
        out_shape=jax.ShapeDtypeStruct((rows, width), BF16),
        grid=(len(x),),
        in_specs=[pl.BlockSpec(memory_space=pl.ANY)] * (2 * len(x))
        + [pl.BlockSpec((depth, width), lambda i: (0, 0))],
        out_specs=pl.BlockSpec((step, width), lambda i: (i, 0)),
        scratch_shapes=stream_scratch(2, step, depth),
        compiler_params=params(),
        cost_estimate=cost(),
        name="ffn",
    )(*x, *cot, w)


DOWN = (((0,), (0,)), ((), ()))


def grads_kernel(x_count, y_count, *refs):
    a_ref, b_ref, o_ref = refs[x_count + y_count :]
    split = a_ref.shape[1]

    def product(tall_refs, right_ref):
        tall = jnp.concatenate([ref[...] for ref in tall_refs], axis=0)
        return lax.dot_general(
            tall, right_ref[...].astype(BF16), DOWN, preferred_element_type=F32
        ).astype(BF16)

    o_ref[:, :split] = product(refs[:x_count], a_ref)
    o_ref[:, split:] = product(refs[x_count : x_count + y_count], b_ref)


def weight_grads(x, a, a_width, a_column, y, b, b_width, b_column, work=20):
    depth = x[0].shape[1]
    rows = a.shape[0]
    width = a_width + b_width
    step = 512
    return pl.pallas_call(
        functools.partial(grads_kernel, len(x), len(y)),
        out_shape=jax.ShapeDtypeStruct((depth, width), BF16),
        grid=(depth // step,),
        in_specs=[pl.BlockSpec((piece.shape[0], step), lambda i: (0, i)) for piece in (*x, *y)]
        + [
            pl.BlockSpec((rows, a_width), lambda i: (0, a_column)),
            pl.BlockSpec((rows, b_width), lambda i: (0, b_column)),
        ],
        out_specs=pl.BlockSpec((step, width), lambda i: (i, 0)),
        compiler_params=params(),
        cost_estimate=cost(work),
        name="weight_grads",
    )(*x, *y, a, b)


def back_kernel(count, *refs):
    o_ref = refs[-1]
    total = refs[2 * count][...].astype(F32) if len(refs) > 2 * count + 1 else None
    for part in range(count):
        term = lax.dot_general(
            refs[part][...].astype(BF16),
            refs[count + part][...],
            (((1,), (1,)), ((), ())),
            preferred_element_type=F32,
        )
        total = term if total is None else total + term
    o_ref[...] = total.astype(BF16)


def back_product(terms, part=0, parts=1, plus=(), work=0):
    rows = terms[0][0].shape[0] // parts
    depth = terms[0][2].shape[0]
    step = min(512, rows)
    ahead = part * (rows // step)
    return pl.pallas_call(
        functools.partial(back_kernel, len(terms)),
        out_shape=jax.ShapeDtypeStruct((rows, depth), BF16),
        grid=(rows // step,),
        in_specs=[
            pl.BlockSpec((step, term[4]), lambda i, column=term[1]: (i + ahead, column))
            for term in terms
        ]
        + [pl.BlockSpec((depth, term[4]), lambda i, column=term[3]: (0, column)) for term in terms]
        + [pl.BlockSpec((step, depth), lambda i: (i + ahead, 0))] * len(plus),
        out_specs=pl.BlockSpec((step, depth), lambda i: (i, 0)),
        compiler_params=params(),
        cost_estimate=cost(work),
        name="back",
    )(*[term[0] for term in terms], *[term[2] for term in terms], *plus)


def front_kernel(count, *refs):
    w_ref, o_ref, buffer, sems = refs[count:]
    x = next_piece(refs[:count], buffer, sems)
    o_ref[...] = jnp.dot(x, w_ref[...], preferred_element_type=F32).astype(BF16)


def front_product(x, w, width, column):
    step, depth = x[0].shape
    rows = len(x) * step
    return pl.pallas_call(
        functools.partial(front_kernel, len(x)),
        out_shape=jax.ShapeDtypeStruct((rows, width), BF16),
        grid=(len(x),),
        in_specs=[pl.BlockSpec(memory_space=pl.ANY)] * len(x)
        + [pl.BlockSpec((depth, width), lambda i: (0, column))],
        out_specs=pl.BlockSpec((step, width), lambda i: (i, 0)),
        scratch_shapes=stream_scratch(1, step, depth),
        compiler_params=params(),
        cost_estimate=cost(),
        name="front",
    )(*x, w)


def stack_heads(block):
    count = block.shape[1] // HEAD_DIM
    return jnp.concatenate(
        [block[:, h * HEAD_DIM : (h + 1) * HEAD_DIM] for h in range(count)], axis=0
    )


def unstack_heads(stacked):
    count = stacked.shape[0] // BLOCK
    return jnp.concatenate([stacked[h * BLOCK : (h + 1) * BLOCK] for h in range(count)], axis=1)


def allowed_of(i, j, start):
    row = i * BLOCK + lax.broadcasted_iota(jnp.int32, (BLOCK, BLOCK), 0)
    col = j * BLOCK + lax.broadcasted_iota(jnp.int32, (BLOCK, BLOCK), 1)
    return (col <= row) & (col >= start)


def attend_kernel(place, first, q_ref, kv_ref, start_ref, o_ref):
    i = pl.program_id(0)
    q = stack_heads(q_ref[...])
    heads = q.shape[0] // BLOCK
    start = start_ref[...]

    def step(j, carry):
        top, total, acc = carry
        at = pl.multiple_of(place[j] * BLOCK, BLOCK)
        kv = kv_ref[pl.ds(at, BLOCK), :]
        raw = lax.dot_general(
            q, kv[:, :HEAD_DIM], (((1,), (1,)), ((), ())), preferred_element_type=F32
        ) * (HEAD_DIM**-0.5 * LOG2_E)
        allowed = allowed_of(i, j, start)
        scores = jnp.where(allowed[None], raw.reshape(heads, BLOCK, BLOCK), MASKED).reshape(
            heads * BLOCK, BLOCK
        )
        new_top = jnp.maximum(top, jnp.max(scores, axis=-1, keepdims=True))
        keep = jnp.exp2(top - new_top)
        probs = jnp.exp2(scores - new_top)
        total = total * keep + jnp.sum(probs, axis=-1, keepdims=True)
        acc = acc * keep + jnp.dot(probs.astype(BF16), kv, preferred_element_type=F32)
        return (new_top, total, acc)

    size = heads * BLOCK
    top, total, acc = lax.fori_loop(
        first[i],
        i + 1,
        step,
        (
            jnp.full((size, 1), MASKED, F32),
            jnp.zeros((size, 1), F32),
            jnp.zeros((size, 2 * HEAD_DIM), F32),
        ),
    )
    out = acc[:, HEAD_DIM:] / total
    q_width = q_ref.shape[1]
    o_ref[:, :q_width] = unstack_heads(out)
    lse = top + jnp.log2(total)
    lane = lax.broadcasted_iota(jnp.int32, (BLOCK, 128), 1)
    packed = jnp.zeros((BLOCK, 128), F32)
    for h in range(heads):
        packed = jnp.where(lane == h, lse[h * BLOCK : (h + 1) * BLOCK], packed)
    o_ref[:, q_width:] = packed


def attend(qkv, depth, place, first, start, q_width):
    rows = qkv.shape[0]
    blocks = rows // BLOCK
    return pl.pallas_call(
        attend_kernel,
        out_shape=jax.ShapeDtypeStruct((rows, q_width + 128), F32),
        grid_spec=pltpu.PrefetchScalarGridSpec(
            num_scalar_prefetch=2,
            grid=(blocks,),
            in_specs=[
                pl.BlockSpec((BLOCK, q_width), lambda i, place, first: (place[i], depth // q_width)),
                pl.BlockSpec((rows, 128), lambda i, place, first: (0, (depth + q_width) // 128)),
                pl.BlockSpec((BLOCK, 1), lambda i, place, first: (i, 0)),
            ],
            out_specs=pl.BlockSpec((BLOCK, q_width + 128), lambda i, place, first: (place[i], 0)),
        ),
        compiler_params=params(),
        cost_estimate=cost(),
        name="attend",
    )(place, first, qkv, qkv, start)


def attend_back_kernel(
    place,
    first,
    q_ref,
    d_ref,
    h_ref,
    kv_ref,
    start_ref,
    cos_ref,
    sin_ref,
    o_ref,
    dkv_ref,
):
    i = pl.program_id(0)
    blocks = pl.num_programs(0)
    score_scale = HEAD_DIM**-0.5
    q_width = q_ref.shape[1]

    @pl.when(i == 0)
    def _():
        dkv_ref[...] = jnp.zeros_like(dkv_ref)

    q = stack_heads(q_ref[...])
    d_out = stack_heads(d_ref[...])
    heads = q.shape[0] // BLOCK
    out = stack_heads(h_ref[:, :q_width])
    delta = jnp.sum(d_out.astype(F32) * out, axis=-1, keepdims=True)
    lse_block = h_ref[:, q_width:]
    lse = jnp.concatenate([lse_block[:, h : h + 1] for h in range(heads)], axis=0)
    start = start_ref[...]

    def step(j, d_q):
        at = pl.multiple_of(place[j] * BLOCK, BLOCK)
        kv = kv_ref[pl.ds(at, BLOCK), :]
        k, v = kv[:, :HEAD_DIM], kv[:, HEAD_DIM:]
        across = (((1,), (1,)), ((), ()))
        down = (((0,), (0,)), ((), ()))
        raw = lax.dot_general(q, k, across, preferred_element_type=F32) * (score_scale * LOG2_E)
        allowed = allowed_of(i, j, start)
        scores = jnp.where(allowed[None], raw.reshape(heads, BLOCK, BLOCK), MASKED).reshape(
            heads * BLOCK, BLOCK
        )
        probs = jnp.exp2(scores - lse)
        d_probs = lax.dot_general(d_out, v, across, preferred_element_type=F32)
        d_scores = (probs * (d_probs - delta)).astype(BF16)
        d_k = lax.dot_general(d_scores, q, down, preferred_element_type=F32) * score_scale
        d_v = lax.dot_general(probs.astype(BF16), d_out, down, preferred_element_type=F32)
        here = pl.ds(pl.multiple_of(j * BLOCK, BLOCK), BLOCK)
        dkv_ref[here, :] += jnp.concatenate([d_k, d_v], axis=1)
        return d_q + jnp.dot(d_scores, k, preferred_element_type=F32)

    d_q = lax.fori_loop(first[i], i + 1, step, jnp.zeros((heads * BLOCK, HEAD_DIM), F32))
    d_q = unstack_heads(d_q * score_scale)
    lane = lax.broadcasted_iota(jnp.int32, (BLOCK, 128), 1)
    front = (lane % 64) < 32
    mine = pl.ds(pl.multiple_of(place[i] * BLOCK, BLOCK), BLOCK)
    cos, sin = cos_ref[mine, :], sin_ref[mine, :]
    for tile in range(q_width // 128):
        u = d_q[:, tile * 128 : (tile + 1) * 128]
        o_ref[mine, tile * 128 : (tile + 1) * 128] = (u * cos - turn_lanes(u, front) * sin).astype(
            BF16
        )

    @pl.when(i == blocks - 1)
    def _():
        for b in range(dkv_ref.shape[0] // BLOCK):
            there = pl.ds(pl.multiple_of(place[b] * BLOCK, BLOCK), BLOCK)
            u = dkv_ref[b * BLOCK : (b + 1) * BLOCK, :]
            turned = u * cos_ref[there, :] - turn_lanes(u, front) * sin_ref[there, :]
            o_ref[there, q_width:] = jnp.where(lane < HEAD_DIM, turned, u).astype(BF16)


def attend_back(qkv, depth, d_heads, heads, place, first, start, cos, sin):
    rows, q_width = d_heads.shape
    width = q_width + 128
    blocks = rows // BLOCK
    by_place = lambda i, place, first: (place[i], 0)
    whole = lambda i, place, first: (0, 0)
    return pl.pallas_call(
        attend_back_kernel,
        out_shape=jax.ShapeDtypeStruct((rows, width), BF16),
        grid_spec=pltpu.PrefetchScalarGridSpec(
            num_scalar_prefetch=2,
            grid=(blocks,),
            in_specs=[
                pl.BlockSpec((BLOCK, q_width), lambda i, place, first: (place[i], depth // q_width)),
                pl.BlockSpec((BLOCK, q_width), by_place),
                pl.BlockSpec((BLOCK, q_width + 128), by_place),
                pl.BlockSpec((rows, 128), lambda i, place, first: (0, (depth + q_width) // 128)),
                pl.BlockSpec((BLOCK, 1), lambda i, place, first: (i, 0)),
                pl.BlockSpec((rows, 128), whole),
                pl.BlockSpec((rows, 128), whole),
            ],
            out_specs=pl.BlockSpec((rows, width), whole),
            scratch_shapes=[pltpu.VMEM((rows, 128), F32)],
        ),
        compiler_params=params(),
        cost_estimate=cost(),
        name="attend_back",
    )(place, first, qkv, d_heads, heads, qkv, start, cos, sin)


def sum_cores(terms, pieces=2):
    sent = [back_product(terms, 2 * pieces - 1 - at, 2 * pieces) for at in range(pieces)]
    arrived = [swap_core(piece) for piece in sent]
    return add_blocks(back_product(terms, 0, 2), arrived)


def add_blocks(mine, arrived):
    rows = mine.shape[0] // 4
    each = 4 // len(arrived)
    blocks = []
    for at in range(4):
        other = arrived[len(arrived) - 1 - at // each]
        begin = (at % each) * rows
        blocks.append(mine[at * rows : (at + 1) * rows] + other[begin : begin + rows])
    return blocks


def sum_first(blocks, early=()):
    own, along_a, along_b, both = blocks
    along_a = along_a + after(swap_second(both), *early)
    return (own, *lax.optimization_barrier((along_a, along_b)))


def last_parts(own, along_a, along_b, beside=()):
    return own, swap_second(along_b), after(swap_first(along_a), *beside)


def halves_of_cores(terms, plus):
    arrived = swap_core(back_product(terms, 1, 2, plus))
    mine = back_product(terms, 0, 2, plus)
    rows = mine.shape[0] // 4
    return mine[2 * rows :] + arrived[2 * rows :], mine[: 2 * rows] + arrived[: 2 * rows]


def wide_first(far, near, between):
    return after(near + swap_second(far), *between)


def wide_last(near, beside):
    return near, after(swap_first(near[near.shape[0] // 2 :]), *beside)


def share_rows(own, beside=()):
    beside = list(beside) + [()] * (2 - len(beside))
    one, two, *_ = lax.optimization_barrier((swap_first(own), swap_second(own), *beside[0]))
    early = tuple(swap_core(part) for part in (own, one, two))
    last = after(swap_second(one), *early, *beside[1])
    return (own, one, two, last, *early, swap_core(last))


def ring_over(shard, count, held):
    cycle = [(at, (at + 1) % count) for at in range(count)]
    pieces = [shard]
    for step in range(count - 1):
        sent = after(pieces[-1], *held) if step == 1 else pieces[-1]
        pieces.append(lax.ppermute(sent, "fsdp", cycle))
    return pieces


def in_place(pieces, axis):
    count, size = len(pieces), pieces[0].shape[axis]
    here = lax.axis_index("fsdp")
    shape = list(pieces[0].shape)
    shape[axis] *= count
    whole = jnp.zeros(shape, pieces[0].dtype)
    for back, piece in enumerate(pieces):
        owner = lax.rem(here + count - back, count)
        whole = lax.dynamic_update_slice_in_dim(whole, piece, owner * size, axis)
    return whole


def share_in_ctx(own, beside, y, core):
    pair = jnp.stack([own, beside])
    other = jnp.stack([swap_core(own), swap_core(beside)])
    four = jnp.stack([pair, other])
    four = jnp.where(y == 1, four[:, ::-1], four)
    four = jnp.where(core == 1, four[::-1], four)
    return four.transpose(1, 0, 2, 3).reshape(-1, own.shape[1])


def both_halves(own, other, ctx):
    low = jnp.where(ctx == 0, own, other).astype(F32)
    high = jnp.where(ctx == 0, other, own).astype(F32)
    return low, high


def shards(
    tokens,
    q_weight,
    k_weight,
    v_weight,
    o_weight,
    attn_gain,
    gate_weight,
    up_weight,
    down_weight,
    ffn_gain,
    lengths,
    deal,
    cotangent,
):
    ctx = lax.axis_index("ctx")
    tp = lax.axis_index("tp")
    y, core = tp // 2, tp % 2
    row_count, depth = tokens.shape
    group_rows = row_count * lax.axis_size("ctx")
    own_rows = row_count // lax.axis_size("tp")

    def half(weight):
        width = weight.shape[1] // 2
        return lax.dynamic_slice_in_dim(weight, ctx * width, width, 1)

    length_row, deal_row = lengths[0], deal[0]
    spans = deal_row.shape[0]
    span_rows = group_rows // spans
    ends = jnp.cumsum(length_row, dtype=jnp.int32)
    starts = ends - length_row
    natural = jnp.arange(group_rows, dtype=jnp.int32)
    inside = (natural[:, None] >= starts[None]) & (natural[:, None] < ends[None])
    start_of = jnp.sum(jnp.where(inside, starts[None], 0), axis=1, dtype=jnp.int32)
    first = start_of[::BLOCK] // BLOCK
    rel = jnp.arange(group_rows // own_rows, dtype=jnp.int32)
    rel_core = core ^ (rel // 4)
    by_first, by_second = rel % 2, (rel // 2) % 2
    rel_ctx = ctx ^ jnp.where(rel_core == 0, by_first, by_second)
    rel_y = y ^ jnp.where(rel_core == 0, by_second, by_first)
    dealt_block = rel_ctx * (row_count // own_rows) + rel_y * 2 + rel_core
    per_span = span_rows // own_rows
    span_of = jnp.sum(
        jnp.where(
            (dealt_block // per_span)[:, None] == jnp.arange(spans, dtype=jnp.int32)[None],
            deal_row[None],
            0,
        ),
        axis=1,
        dtype=jnp.int32,
    )
    natural_block = span_of * per_span + dealt_block % per_span
    place = jnp.sum(
        jnp.where(natural_block[None, :] == rel[:, None], rel[None, :], 0), axis=1, dtype=jnp.int32
    )
    natural_rel = (
        natural_block[:, None] * own_rows + jnp.arange(own_rows, dtype=jnp.int32)[None]
    ).reshape(-1)
    inside_rel = (natural_rel[:, None] >= starts[None]) & (natural_rel[:, None] < ends[None])
    position = natural_rel - jnp.sum(
        jnp.where(inside_rel, starts[None], 0), axis=1, dtype=jnp.int32
    )
    lane = jnp.arange(128, dtype=jnp.int32)
    inverse = jnp.exp((lane % 32).astype(F32) * (-2.0 * math.log(ROPE_BASE) / HEAD_DIM))
    angles = position.astype(F32)[:, None] * inverse[None]
    cos = jnp.cos(angles)
    sin = jnp.where((lane % 64 < 32)[None], -jnp.sin(angles), jnp.sin(angles))
    start_column = start_of[:, None]

    q_half, k_half, v_half, o_half = map(half, (q_weight, k_weight, v_weight, o_weight))
    q_width, kv_width = q_half.shape[1], k_half.shape[1]
    attn_shard = jnp.concatenate([o_half, q_half, k_half, v_half], axis=1)
    fsdp = lax.axis_size("fsdp")
    gain_rows = jnp.stack([attn_gain, ffn_gain])
    gain_width = attn_gain.shape[0]
    extra = ((0, 14), (0, attn_shard.shape[1] - gain_width))
    tokens_low = lax.dynamic_slice_in_dim(tokens, tp * own_rows, own_rows, 0)
    cot_low = lax.dynamic_slice_in_dim(cotangent, tp * own_rows, own_rows, 0)
    tokens_one = swap_first(tokens_low)
    attn_ring = ring_over(
        jnp.concatenate([attn_shard, jnp.pad(gain_rows, extra)]),
        fsdp,
        (tokens_one, cos, sin, cot_low, place, first, start_column),
    )
    own_depth = attn_shard.shape[0]
    attn_full = in_place([piece[:own_depth] for piece in attn_ring], 0)
    gains = in_place([piece[own_depth : own_depth + 2, :gain_width] for piece in attn_ring], 1)
    gain_one = gains[0].astype(F32)[None]
    gain_two = gains[1].astype(F32)[None]
    ff_half = gate_weight.shape[1] // 2
    chunks = [ff_half * share // sum(SPLIT) for share in SPLIT]
    ffn_shards = []
    for part, chunk in enumerate(chunks):
        at = ctx * ff_half + sum(chunks[:part])
        ffn_shards.append(
            jnp.concatenate(
                [
                    lax.dynamic_slice_in_dim(weight, at, chunk, 1)
                    for weight in (gate_weight, up_weight, down_weight)
                ],
                axis=1,
            )
        )
    tokens_own, cot_own = tokens_low.astype(F32), cot_low.astype(F32)
    group_tokens = (tokens_low, tokens_one, swap_second(tokens_low), swap_second(tokens_one))
    first_shard = after(ffn_shards[0], attn_ring[-1], *group_tokens[2:])
    group_tokens = group_tokens + tuple(swap_core(part) for part in group_tokens)
    attn_full, cot_low, cos, sin, gain_one, *group_tokens = lax.optimization_barrier(
        (attn_full, cot_low, cos, sin, gain_one, *group_tokens)
    )
    qkv = project_qkv(group_tokens, gain_one, attn_full, q_width, cos, sin)
    heads = attend(qkv, depth, place, first, start_column, q_width)
    cot = share_rows(cot_low, [[qkv], [heads]])
    ffn_full = [
        lax.all_gather(shard, "fsdp", axis=0, tiled=True)
        for shard in (first_shard, after(ffn_shards[1], heads))
    ]
    heads = after(heads, *cot)
    attn_blocks = sum_cores([(heads, 0, attn_full, 0, q_width)])
    attn_parts = last_parts(*sum_first(attn_blocks), beside=ffn_full[:1])
    attn_sum = sum(part.astype(F32) for part in attn_parts)
    hidden = tokens_own + attn_sum
    normed_two = share_rows((hidden * inv_rms(hidden) * gain_two).astype(BF16))

    acts = []
    grad_parts = []
    d_norm_partial = ()

    def chunk_grads(part, held=()):
        chunk = chunks[part]
        act = after(acts[part], *held)
        grad_parts.append(weight_grads(normed_two, act, 2 * chunk, 0, cot, act, chunk, 2))

    last = len(chunks) - 1
    for part in range(len(chunks)):
        normed_two = (after(normed_two[0], *grad_parts, *d_norm_partial), *normed_two[1:])
        acts.append(ffn_chunk(normed_two, cot, ffn_full[part]))
        d_norm_term = (acts[part], 0, ffn_full[part], 0, 2 * chunks[part])
        if part < last:
            chunk_grads(part)
            d_norm_partial = (back_product([d_norm_term], plus=d_norm_partial),)
    ffn_terms = [(acts[part], 2, ffn_full[part], 2, chunk) for part, chunk in enumerate(chunks)]
    d_norm_far, d_norm_near = halves_of_cores([d_norm_term], d_norm_partial)
    chunk_grads(last, (d_norm_far,))
    reduced = [
        lax.psum_scatter(part, "fsdp", scatter_dimension=0, tiled=True) for part in grad_parts
    ]
    d_norm_near = wide_first(d_norm_far, d_norm_near, grad_parts)

    def ffn_rows(part, parts, held):
        (act, *rest), *others = ffn_terms
        return back_product([(after(act, held), *rest), *others], part, parts, work=7)

    ffn_sent = [ffn_rows(3, 4, d_norm_near)]
    d_own = norm_back(wide_last(d_norm_near, ffn_sent), hidden, gain_two, cot_low)
    ffn_sent.append(ffn_rows(2, 4, d_own))
    ffn_mine = ffn_rows(0, 2, d_own)
    d_one, d_two, ffn_mine, ffn_sent[1] = lax.optimization_barrier(
        (swap_first(d_own), swap_second(d_own), ffn_mine, ffn_sent[1])
    )
    ffn_own, ffn_a, ffn_b, ffn_both = add_blocks(ffn_mine, [swap_core(piece) for piece in ffn_sent])
    ffn_x, ffn_y = jnp.where(core == 0, ffn_a, ffn_b), jnp.where(core == 0, ffn_b, ffn_a)
    d_early = [swap_core(part) for part in (d_own, d_one, d_two)]
    d_last = after(swap_second(d_one), *d_early, ffn_own, ffn_x, ffn_y, ffn_both, reduced[0])
    d_attn = (d_own, d_one, d_two, d_last, *d_early, swap_core(d_last))

    d_heads = front_product(d_attn, attn_full, q_width, 0)
    other_reduced = [swap_x(after(reduced[0], d_last))]
    d_qkv = attend_back(qkv, depth, d_heads, heads, place, first, start_column, cos, sin)
    y_both, y_own, d_qkv, other_reduced[0] = lax.optimization_barrier(
        (swap_y(ffn_both), swap_y(ffn_y), d_qkv, other_reduced[0])
    )
    ffn_x, ffn_own, d_qkv = lax.optimization_barrier((ffn_x + y_both, ffn_own + y_own, d_qkv))
    ffn_far = swap_x(ffn_x)
    normed_blocks = sum_cores(
        [
            (d_qkv, 0, attn_full, 1, q_width),
            (d_qkv, q_width // 128, attn_full, 2 * q_width // 128, 128),
        ]
    )
    attn_grad = weight_grads(
        d_attn, heads, q_width, 0, (qkv,), after(d_qkv, normed_blocks[3]), q_width + 128, 0, 0
    )
    ffn_far = after(ffn_far, attn_grad)
    result_own = (hidden + (ffn_own.astype(F32) + ffn_far.astype(F32))).astype(BF16)
    result_beside = swap_y(result_own)
    normed_first = sum_first(normed_blocks, [attn_grad, result_own])
    for part in range(1, len(chunks)):
        reduced[part] = after(reduced[part], attn_grad)
        other_reduced.append(swap_x(reduced[part]))
    late = [after(part, normed_first[1]) for part in other_reduced]
    halves = [both_halves(mine, other, ctx) for mine, other in zip(reduced, late)]

    def ffn_out(which):
        return jnp.concatenate(
            [
                halves[part][side][:, which * chunk : (which + 1) * chunk]
                for side in range(2)
                for part, chunk in enumerate(chunks)
            ],
            axis=1,
        )

    ffn_grads = [ffn_out(which) for which in range(3)]
    result = share_in_ctx(result_own, result_beside, y, core)
    normed_parts = last_parts(*normed_first, beside=[result, *ffn_grads])
    tokens_grad_own = norm_back(normed_parts, tokens_low, gain_one, d_own)
    attn_reduced = lax.psum_scatter(attn_grad, "fsdp", scatter_dimension=0, tiled=True)
    attn_reduced = after(attn_reduced, tokens_grad_own)
    other_attn = swap_x(attn_reduced)
    def gain_part(pairs):
        return sum(jnp.sum(mine.astype(F32) * grad.astype(F32), axis=1) for mine, grad in pairs)

    gain_sums = jnp.stack(
        [
            gain_part([(attn_shard[:, q_width:], attn_reduced[:, q_width:])]),
            gain_part(
                [
                    (ffn_shards[part][:, : 2 * chunk], reduced[part][:, : 2 * chunk])
                    for part, chunk in enumerate(chunks)
                ]
            ),
        ]
    )
    gain_sums = gain_sums + swap_core(gain_sums)
    gain_sums = gain_sums + swap_y(gain_sums)
    gain_sums = gain_sums + swap_x(gain_sums)

    tokens_grad_beside, gain_sums, other_attn, result, *ffn_grads = lax.optimization_barrier(
        (swap_y(tokens_grad_own), gain_sums, other_attn, result, *ffn_grads)
    )
    tokens_grad = share_in_ctx(tokens_grad_own, tokens_grad_beside, y, core)
    attn_gain_grad = gain_sums[0] / attn_gain.astype(F32)
    ffn_gain_grad = gain_sums[1] / ffn_gain.astype(F32)
    attn_low, attn_high = both_halves(attn_reduced, other_attn, ctx)

    def attn_out(begin, end):
        return jnp.concatenate([attn_low[:, begin:end], attn_high[:, begin:end]], axis=1)

    q_end, k_end = 2 * q_width, 2 * q_width + kv_width
    return (
        result,
        tokens_grad,
        attn_out(q_width, q_end),
        attn_out(q_end, k_end),
        attn_out(k_end, k_end + kv_width),
        attn_out(0, q_width),
        attn_gain_grad,
        *ffn_grads,
        ffn_gain_grad,
    )


def solution(mesh):
    rows = P(("fsdp", "ctx"), None)
    matrix = P("fsdp", "tp")
    vector = P("fsdp")
    return jax.shard_map(
        shards,
        mesh=mesh,
        in_specs=(
            rows,
            matrix,
            matrix,
            matrix,
            matrix,
            vector,
            matrix,
            matrix,
            matrix,
            vector,
            P("fsdp", None),
            P("fsdp", None),
            rows,
        ),
        out_specs=(
            rows,
            rows,
            matrix,
            matrix,
            matrix,
            matrix,
            vector,
            matrix,
            matrix,
            matrix,
            vector,
        ),
        check_vma=False,
    )
```

```python
import functools
import math

import jax
import jax.numpy as jnp
from jax import lax
from jax.experimental import pallas as pl
from jax.experimental.pallas import tpu as pltpu
from jax.sharding import PartitionSpec as P

HEAD_DIM = 64
EPSILON = 1e-05
ROPE_BASE = 500000.0
MASKED = -1e30
LOG2_E = 1.4426950408889634
BLOCK = 256
SPLIT = (1, 1)
VMEM = 56 * 2**20

F32 = jnp.float32
BF16 = jnp.bfloat16

PAIR = [(0, 1), (1, 0)]
CORE = [(0, 1), (1, 0), (2, 3), (3, 2)]
ACROSS = [(0, 2), (2, 0), (1, 3), (3, 1)]


def joint_pairs(x_core):
    pairs = []
    for ctx in range(2):
        for tp in range(4):
            there = (1 - ctx) * 4 + tp if tp % 2 == x_core else ctx * 4 + (tp ^ 2)
            pairs.append((ctx * 4 + tp, there))
    return pairs


FIRST = joint_pairs(0)
SECOND = joint_pairs(1)


def swap_core(v):
    return lax.ppermute(v, "tp", CORE)


def swap_y(v):
    return lax.ppermute(v, "tp", ACROSS)


def swap_x(v):
    return lax.ppermute(v, "ctx", PAIR)


def swap_first(v):
    return lax.ppermute(v, ("ctx", "tp"), FIRST)


def swap_second(v):
    return lax.ppermute(v, ("ctx", "tp"), SECOND)


def after(value, *others):
    return lax.optimization_barrier((value,) + others)[0]


def params(*semantics):
    return pltpu.CompilerParams(vmem_limit_bytes=VMEM)


def cost(gigaflops=0):
    return pl.CostEstimate(flops=int(gigaflops * 1e9) + 1, bytes_accessed=1, transcendentals=0)


def inv_rms(hidden):
    return lax.rsqrt(jnp.mean(hidden * hidden, axis=-1, keepdims=True) + EPSILON)


def rms_back(hidden, gain, grad):
    scale = inv_rms(hidden)
    weighted = grad * gain
    inner = jnp.mean(weighted * hidden, axis=-1, keepdims=True)
    return scale * weighted - hidden * (scale * scale * scale) * inner


def norm_back_kernel(count, *refs):
    hidden_ref, gain_ref, kept_ref, o_ref = refs[count:]
    grad = sum(ref[...].astype(F32) for ref in refs[:count])
    back = rms_back(hidden_ref[...].astype(F32), gain_ref[...], grad)
    o_ref[...] = (kept_ref[...].astype(F32) + back).astype(BF16)


def norm_back(parts, hidden, gain, kept):
    rows, depth = hidden.shape
    step = min(64, rows)
    block = pl.BlockSpec((step, depth), lambda i: (i, 0))
    return pl.pallas_call(
        functools.partial(norm_back_kernel, len(parts)),
        out_shape=jax.ShapeDtypeStruct((rows, depth), BF16),
        grid=(rows // step,),
        in_specs=[block] * (len(parts) + 1)
        + [pl.BlockSpec((1, depth), lambda i: (0, 0)), block],
        out_specs=block,
        compiler_params=params(),
        cost_estimate=cost(),
        name="norm_back",
    )(*parts, hidden, gain, kept)


def turn_lanes(u, first):
    return jnp.where(first, pltpu.roll(u, 96, 1), pltpu.roll(u, 32, 1))


def stream_scratch(count, rows, depth):
    return [pltpu.VMEM((2, rows, depth), BF16), pltpu.SemaphoreType.DMA((2,))] * count


def next_piece(refs, buffer, sems):
    i = pl.program_id(0)

    def copy_of(piece):
        return pltpu.make_async_copy(refs[piece], buffer.at[piece % 2], sems.at[piece % 2])

    @pl.when(i == 0)
    def _():
        copy_of(0).start()

    for piece in range(1, len(refs)):

        @pl.when(i == piece - 1)
        def _(piece=piece):
            copy_of(piece).start()

    for piece in range(len(refs)):

        @pl.when(i == piece)
        def _(piece=piece):
            copy_of(piece).wait()

    return buffer[lax.rem(i, 2)]


def qkv_kernel(count, *refs):
    gain_ref, wq_ref, wkv_ref, cos_ref, sin_ref, o_ref, buffer, sems = refs[count:]
    cos, sin = cos_ref[...], sin_ref[...]
    depth = gain_ref.shape[1]
    lane = lax.broadcasted_iota(jnp.int32, cos.shape, 1)
    first = (lane % 64) < 32
    x = next_piece(refs[:count], buffer, sems).astype(F32)
    x = (x * inv_rms(x) * gain_ref[...]).astype(BF16)
    o_ref[:, :depth] = x
    raw = jnp.dot(x, wq_ref[...], preferred_element_type=F32)
    tiles = raw.shape[1] // 128
    for tile in range(tiles):
        u = raw[:, tile * 128 : (tile + 1) * 128]
        turned = u * cos + turn_lanes(u, first) * sin
        o_ref[:, depth + tile * 128 : depth + (tile + 1) * 128] = turned.astype(BF16)
    u = jnp.dot(x, wkv_ref[...], preferred_element_type=F32)
    turned = u * cos + turn_lanes(u, first) * sin
    o_ref[:, depth + tiles * 128 :] = jnp.where(lane < 64, turned, u).astype(BF16)


def project_qkv(x, gain, w, q_width, cos, sin):
    step, depth = x[0].shape
    rows = len(x) * step
    width = depth + q_width + 128
    return pl.pallas_call(
        functools.partial(qkv_kernel, len(x)),
        out_shape=jax.ShapeDtypeStruct((rows, width), BF16),
        grid=(len(x),),
        in_specs=[pl.BlockSpec(memory_space=pl.ANY)] * len(x)
        + [
            pl.BlockSpec((1, depth), lambda i: (0, 0)),
            pl.BlockSpec((depth, q_width), lambda i: (0, 1)),
            pl.BlockSpec((depth, 128), lambda i: (0, 2 * q_width // 128)),
            pl.BlockSpec((step, 128), lambda i: (i, 0)),
            pl.BlockSpec((step, 128), lambda i: (i, 0)),
        ],
        out_specs=pl.BlockSpec((step, width), lambda i: (i, 0)),
        scratch_shapes=stream_scratch(1, step, depth),
        compiler_params=params(),
        cost_estimate=cost(),
        name="qkv",
    )(*x, gain, w, w, cos, sin)


def ffn_kernel(count, *refs):
    w_ref, o_ref, x_buffer, x_sems, c_buffer, c_sems = refs[2 * count :]
    n = w_ref.shape[1] // 3
    x = next_piece(refs[:count], x_buffer, x_sems)
    c = next_piece(refs[count : 2 * count], c_buffer, c_sems)
    gate = jnp.dot(x, w_ref[:, :n], preferred_element_type=F32)
    up = jnp.dot(x, w_ref[:, n : 2 * n], preferred_element_type=F32)
    d_mixed = jnp.dot(c, w_ref[:, 2 * n :], preferred_element_type=F32)
    sig = 1.0 / (1.0 + jnp.exp(-gate))
    silu = gate * sig
    o_ref[:, :n] = (d_mixed * up * (sig * (1.0 + gate * (1.0 - sig)))).astype(BF16)
    o_ref[:, n : 2 * n] = (d_mixed * silu).astype(BF16)
    o_ref[:, 2 * n :] = (silu * up).astype(BF16)


def ffn_chunk(x, cot, w):
    step, depth = x[0].shape
    rows = len(x) * step
    width = w.shape[1]
    return pl.pallas_call(
        functools.partial(ffn_kernel, len(x)),
        out_shape=jax.ShapeDtypeStruct((rows, width), BF16),
        grid=(len(x),),
        in_specs=[pl.BlockSpec(memory_space=pl.ANY)] * (2 * len(x))
        + [pl.BlockSpec((depth, width), lambda i: (0, 0))],
        out_specs=pl.BlockSpec((step, width), lambda i: (i, 0)),
        scratch_shapes=stream_scratch(2, step, depth),
        compiler_params=params(),
        cost_estimate=cost(),
        name="ffn",
    )(*x, *cot, w)


DOWN = (((0,), (0,)), ((), ()))


def grads_kernel(x_count, y_count, *refs):
    a_ref, b_ref, o_ref = refs[x_count + y_count :]
    split = a_ref.shape[1]

    def product(tall_refs, right_ref):
        tall = jnp.concatenate([ref[...] for ref in tall_refs], axis=0)
        return lax.dot_general(
            tall, right_ref[...].astype(BF16), DOWN, preferred_element_type=F32
        ).astype(BF16)

    o_ref[:, :split] = product(refs[:x_count], a_ref)
    o_ref[:, split:] = product(refs[x_count : x_count + y_count], b_ref)


def weight_grads(x, a, a_width, a_column, y, b, b_width, b_column, work=20):
    depth = x[0].shape[1]
    rows = a.shape[0]
    width = a_width + b_width
    step = 512
    return pl.pallas_call(
        functools.partial(grads_kernel, len(x), len(y)),
        out_shape=jax.ShapeDtypeStruct((depth, width), BF16),
        grid=(depth // step,),
        in_specs=[pl.BlockSpec((piece.shape[0], step), lambda i: (0, i)) for piece in (*x, *y)]
        + [
            pl.BlockSpec((rows, a_width), lambda i: (0, a_column)),
            pl.BlockSpec((rows, b_width), lambda i: (0, b_column)),
        ],
        out_specs=pl.BlockSpec((step, width), lambda i: (i, 0)),
        compiler_params=params(),
        cost_estimate=cost(work),
        name="weight_grads",
    )(*x, *y, a, b)


def back_kernel(count, *refs):
    o_ref = refs[-1]
    total = refs[2 * count][...].astype(F32) if len(refs) > 2 * count + 1 else None
    for part in range(count):
        term = lax.dot_general(
            refs[part][...].astype(BF16),
            refs[count + part][...],
            (((1,), (1,)), ((), ())),
            preferred_element_type=F32,
        )
        total = term if total is None else total + term
    o_ref[...] = total.astype(BF16)


def back_product(terms, part=0, parts=1, plus=(), work=0):
    rows = terms[0][0].shape[0] // parts
    depth = terms[0][2].shape[0]
    step = min(512, rows)
    ahead = part * (rows // step)
    return pl.pallas_call(
        functools.partial(back_kernel, len(terms)),
        out_shape=jax.ShapeDtypeStruct((rows, depth), BF16),
        grid=(rows // step,),
        in_specs=[
            pl.BlockSpec((step, term[4]), lambda i, column=term[1]: (i + ahead, column))
            for term in terms
        ]
        + [pl.BlockSpec((depth, term[4]), lambda i, column=term[3]: (0, column)) for term in terms]
        + [pl.BlockSpec((step, depth), lambda i: (i + ahead, 0))] * len(plus),
        out_specs=pl.BlockSpec((step, depth), lambda i: (i, 0)),
        compiler_params=params(),
        cost_estimate=cost(work),
        name="back",
    )(*[term[0] for term in terms], *[term[2] for term in terms], *plus)


def front_kernel(count, *refs):
    w_ref, o_ref, buffer, sems = refs[count:]
    x = next_piece(refs[:count], buffer, sems)
    o_ref[...] = jnp.dot(x, w_ref[...], preferred_element_type=F32).astype(BF16)


def front_product(x, w, width, column):
    step, depth = x[0].shape
    rows = len(x) * step
    return pl.pallas_call(
        functools.partial(front_kernel, len(x)),
        out_shape=jax.ShapeDtypeStruct((rows, width), BF16),
        grid=(len(x),),
        in_specs=[pl.BlockSpec(memory_space=pl.ANY)] * len(x)
        + [pl.BlockSpec((depth, width), lambda i: (0, column))],
        out_specs=pl.BlockSpec((step, width), lambda i: (i, 0)),
        scratch_shapes=stream_scratch(1, step, depth),
        compiler_params=params(),
        cost_estimate=cost(),
        name="front",
    )(*x, w)


def stack_heads(block):
    count = block.shape[1] // HEAD_DIM
    return jnp.concatenate(
        [block[:, h * HEAD_DIM : (h + 1) * HEAD_DIM] for h in range(count)], axis=0
    )


def unstack_heads(stacked):
    count = stacked.shape[0] // BLOCK
    return jnp.concatenate([stacked[h * BLOCK : (h + 1) * BLOCK] for h in range(count)], axis=1)


def allowed_of(i, j, start):
    row = i * BLOCK + lax.broadcasted_iota(jnp.int32, (BLOCK, BLOCK), 0)
    col = j * BLOCK + lax.broadcasted_iota(jnp.int32, (BLOCK, BLOCK), 1)
    return (col <= row) & (col >= start)


def attend_kernel(place, first, q_ref, kv_ref, start_ref, o_ref):
    i = pl.program_id(0)
    q = stack_heads(q_ref[...])
    heads = q.shape[0] // BLOCK
    start = start_ref[...]

    def step(j, carry):
        top, total, acc = carry
        at = pl.multiple_of(place[j] * BLOCK, BLOCK)
        kv = kv_ref[pl.ds(at, BLOCK), :]
        raw = lax.dot_general(
            q, kv[:, :HEAD_DIM], (((1,), (1,)), ((), ())), preferred_element_type=F32
        ) * (HEAD_DIM**-0.5 * LOG2_E)
        allowed = allowed_of(i, j, start)
        scores = jnp.where(allowed[None], raw.reshape(heads, BLOCK, BLOCK), MASKED).reshape(
            heads * BLOCK, BLOCK
        )
        new_top = jnp.maximum(top, jnp.max(scores, axis=-1, keepdims=True))
        keep = jnp.exp2(top - new_top)
        probs = jnp.exp2(scores - new_top)
        total = total * keep + jnp.sum(probs, axis=-1, keepdims=True)
        acc = acc * keep + jnp.dot(probs.astype(BF16), kv, preferred_element_type=F32)
        return (new_top, total, acc)

    size = heads * BLOCK
    top, total, acc = lax.fori_loop(
        first[i],
        i + 1,
        step,
        (
            jnp.full((size, 1), MASKED, F32),
            jnp.zeros((size, 1), F32),
            jnp.zeros((size, 2 * HEAD_DIM), F32),
        ),
    )
    out = acc[:, HEAD_DIM:] / total
    q_width = q_ref.shape[1]
    o_ref[:, :q_width] = unstack_heads(out)
    lse = top + jnp.log2(total)
    lane = lax.broadcasted_iota(jnp.int32, (BLOCK, 128), 1)
    packed = jnp.zeros((BLOCK, 128), F32)
    for h in range(heads):
        packed = jnp.where(lane == h, lse[h * BLOCK : (h + 1) * BLOCK], packed)
    o_ref[:, q_width:] = packed


def attend(qkv, depth, place, first, start, q_width):
    rows = qkv.shape[0]
    blocks = rows // BLOCK
    return pl.pallas_call(
        attend_kernel,
        out_shape=jax.ShapeDtypeStruct((rows, q_width + 128), F32),
        grid_spec=pltpu.PrefetchScalarGridSpec(
            num_scalar_prefetch=2,
            grid=(blocks,),
            in_specs=[
                pl.BlockSpec((BLOCK, q_width), lambda i, place, first: (place[i], depth // q_width)),
                pl.BlockSpec((rows, 128), lambda i, place, first: (0, (depth + q_width) // 128)),
                pl.BlockSpec((BLOCK, 1), lambda i, place, first: (i, 0)),
            ],
            out_specs=pl.BlockSpec((BLOCK, q_width + 128), lambda i, place, first: (place[i], 0)),
        ),
        compiler_params=params(),
        cost_estimate=cost(),
        name="attend",
    )(place, first, qkv, qkv, start)


def attend_back_kernel(
    place,
    first,
    q_ref,
    d_ref,
    h_ref,
    kv_ref,
    start_ref,
    cos_ref,
    sin_ref,
    o_ref,
    dkv_ref,
):
    i = pl.program_id(0)
    blocks = pl.num_programs(0)
    score_scale = HEAD_DIM**-0.5
    q_width = q_ref.shape[1]

    @pl.when(i == 0)
    def _():
        dkv_ref[...] = jnp.zeros_like(dkv_ref)

    q = stack_heads(q_ref[...])
    d_out = stack_heads(d_ref[...])
    heads = q.shape[0] // BLOCK
    out = stack_heads(h_ref[:, :q_width])
    delta = jnp.sum(d_out.astype(F32) * out, axis=-1, keepdims=True)
    lse_block = h_ref[:, q_width:]
    lse = jnp.concatenate([lse_block[:, h : h + 1] for h in range(heads)], axis=0)
    start = start_ref[...]

    def step(j, d_q):
        at = pl.multiple_of(place[j] * BLOCK, BLOCK)
        kv = kv_ref[pl.ds(at, BLOCK), :]
        k, v = kv[:, :HEAD_DIM], kv[:, HEAD_DIM:]
        across = (((1,), (1,)), ((), ()))
        down = (((0,), (0,)), ((), ()))
        raw = lax.dot_general(q, k, across, preferred_element_type=F32) * (score_scale * LOG2_E)
        allowed = allowed_of(i, j, start)
        scores = jnp.where(allowed[None], raw.reshape(heads, BLOCK, BLOCK), MASKED).reshape(
            heads * BLOCK, BLOCK
        )
        probs = jnp.exp2(scores - lse)
        d_probs = lax.dot_general(d_out, v, across, preferred_element_type=F32)
        d_scores = (probs * (d_probs - delta)).astype(BF16)
        d_k = lax.dot_general(d_scores, q, down, preferred_element_type=F32) * score_scale
        d_v = lax.dot_general(probs.astype(BF16), d_out, down, preferred_element_type=F32)
        here = pl.ds(pl.multiple_of(j * BLOCK, BLOCK), BLOCK)
        dkv_ref[here, :] += jnp.concatenate([d_k, d_v], axis=1)
        return d_q + jnp.dot(d_scores, k, preferred_element_type=F32)

    d_q = lax.fori_loop(first[i], i + 1, step, jnp.zeros((heads * BLOCK, HEAD_DIM), F32))
    d_q = unstack_heads(d_q * score_scale)
    lane = lax.broadcasted_iota(jnp.int32, (BLOCK, 128), 1)
    front = (lane % 64) < 32
    mine = pl.ds(pl.multiple_of(place[i] * BLOCK, BLOCK), BLOCK)
    cos, sin = cos_ref[mine, :], sin_ref[mine, :]
    for tile in range(q_width // 128):
        u = d_q[:, tile * 128 : (tile + 1) * 128]
        o_ref[mine, tile * 128 : (tile + 1) * 128] = (u * cos - turn_lanes(u, front) * sin).astype(
            BF16
        )

    @pl.when(i == blocks - 1)
    def _():
        for b in range(dkv_ref.shape[0] // BLOCK):
            there = pl.ds(pl.multiple_of(place[b] * BLOCK, BLOCK), BLOCK)
            u = dkv_ref[b * BLOCK : (b + 1) * BLOCK, :]
            turned = u * cos_ref[there, :] - turn_lanes(u, front) * sin_ref[there, :]
            o_ref[there, q_width:] = jnp.where(lane < HEAD_DIM, turned, u).astype(BF16)


def attend_back(qkv, depth, d_heads, heads, place, first, start, cos, sin):
    rows, q_width = d_heads.shape
    width = q_width + 128
    blocks = rows // BLOCK
    by_place = lambda i, place, first: (place[i], 0)
    whole = lambda i, place, first: (0, 0)
    return pl.pallas_call(
        attend_back_kernel,
        out_shape=jax.ShapeDtypeStruct((rows, width), BF16),
        grid_spec=pltpu.PrefetchScalarGridSpec(
            num_scalar_prefetch=2,
            grid=(blocks,),
            in_specs=[
                pl.BlockSpec((BLOCK, q_width), lambda i, place, first: (place[i], depth // q_width)),
                pl.BlockSpec((BLOCK, q_width), by_place),
                pl.BlockSpec((BLOCK, q_width + 128), by_place),
                pl.BlockSpec((rows, 128), lambda i, place, first: (0, (depth + q_width) // 128)),
                pl.BlockSpec((BLOCK, 1), lambda i, place, first: (i, 0)),
                pl.BlockSpec((rows, 128), whole),
                pl.BlockSpec((rows, 128), whole),
            ],
            out_specs=pl.BlockSpec((rows, width), whole),
            scratch_shapes=[pltpu.VMEM((rows, 128), F32)],
        ),
        compiler_params=params(),
        cost_estimate=cost(),
        name="attend_back",
    )(place, first, qkv, d_heads, heads, qkv, start, cos, sin)


def sum_cores(terms, pieces=2):
    sent = [back_product(terms, 2 * pieces - 1 - at, 2 * pieces) for at in range(pieces)]
    arrived = [swap_core(piece) for piece in sent]
    return add_blocks(back_product(terms, 0, 2), arrived)


def add_blocks(mine, arrived):
    rows = mine.shape[0] // 4
    each = 4 // len(arrived)
    blocks = []
    for at in range(4):
        other = arrived[len(arrived) - 1 - at // each]
        begin = (at % each) * rows
        blocks.append(mine[at * rows : (at + 1) * rows] + other[begin : begin + rows])
    return blocks


def sum_first(blocks, early=()):
    own, along_a, along_b, both = blocks
    along_a = along_a + after(swap_second(both), *early)
    return (own, *lax.optimization_barrier((along_a, along_b)))


def last_parts(own, along_a, along_b, beside=()):
    return own, swap_second(along_b), after(swap_first(along_a), *beside)


def halves_of_cores(terms, plus):
    arrived = swap_core(back_product(terms, 1, 2, plus))
    mine = back_product(terms, 0, 2, plus)
    rows = mine.shape[0] // 4
    return mine[2 * rows :] + arrived[2 * rows :], mine[: 2 * rows] + arrived[: 2 * rows]


def wide_first(far, near, between):
    return after(near + swap_second(far), *between)


def wide_last(near, beside):
    return near, after(swap_first(near[near.shape[0] // 2 :]), *beside)


def share_rows(own, beside=()):
    beside = list(beside) + [()] * (2 - len(beside))
    one, two, *_ = lax.optimization_barrier((swap_first(own), swap_second(own), *beside[0]))
    early = tuple(swap_core(part) for part in (own, one, two))
    last = after(swap_second(one), *early, *beside[1])
    return (own, one, two, last, *early, swap_core(last))


def ring_over(shard, count, held):
    cycle = [(at, (at + 1) % count) for at in range(count)]
    pieces = [shard]
    for step in range(count - 1):
        sent = after(pieces[-1], *held) if step == 1 else pieces[-1]
        pieces.append(lax.ppermute(sent, "fsdp", cycle))
    return pieces


def in_place(pieces, axis):
    count, size = len(pieces), pieces[0].shape[axis]
    here = lax.axis_index("fsdp")
    shape = list(pieces[0].shape)
    shape[axis] *= count
    whole = jnp.zeros(shape, pieces[0].dtype)
    for back, piece in enumerate(pieces):
        owner = lax.rem(here + count - back, count)
        whole = lax.dynamic_update_slice_in_dim(whole, piece, owner * size, axis)
    return whole


def share_in_ctx(own, beside, y, core):
    pair = jnp.stack([own, beside])
    other = jnp.stack([swap_core(own), swap_core(beside)])
    four = jnp.stack([pair, other])
    four = jnp.where(y == 1, four[:, ::-1], four)
    four = jnp.where(core == 1, four[::-1], four)
    return four.transpose(1, 0, 2, 3).reshape(-1, own.shape[1])


def both_halves(own, other, ctx):
    low = jnp.where(ctx == 0, own, other).astype(F32)
    high = jnp.where(ctx == 0, other, own).astype(F32)
    return low, high


def shards(
    tokens,
    q_weight,
    k_weight,
    v_weight,
    o_weight,
    attn_gain,
    gate_weight,
    up_weight,
    down_weight,
    ffn_gain,
    lengths,
    deal,
    cotangent,
):
    ctx = lax.axis_index("ctx")
    tp = lax.axis_index("tp")
    y, core = tp // 2, tp % 2
    row_count, depth = tokens.shape
    group_rows = row_count * lax.axis_size("ctx")
    own_rows = row_count // lax.axis_size("tp")

    def half(weight):
        width = weight.shape[1] // 2
        return lax.dynamic_slice_in_dim(weight, ctx * width, width, 1)

    length_row, deal_row = lengths[0], deal[0]
    spans = deal_row.shape[0]
    span_rows = group_rows // spans
    ends = jnp.cumsum(length_row, dtype=jnp.int32)
    starts = ends - length_row
    natural = jnp.arange(group_rows, dtype=jnp.int32)
    inside = (natural[:, None] >= starts[None]) & (natural[:, None] < ends[None])
    start_of = jnp.sum(jnp.where(inside, starts[None], 0), axis=1, dtype=jnp.int32)
    first = start_of[::BLOCK] // BLOCK
    rel = jnp.arange(group_rows // own_rows, dtype=jnp.int32)
    rel_core = core ^ (rel // 4)
    by_first, by_second = rel % 2, (rel // 2) % 2
    rel_ctx = ctx ^ jnp.where(rel_core == 0, by_first, by_second)
    rel_y = y ^ jnp.where(rel_core == 0, by_second, by_first)
    dealt_block = rel_ctx * (row_count // own_rows) + rel_y * 2 + rel_core
    per_span = span_rows // own_rows
    span_of = jnp.sum(
        jnp.where(
            (dealt_block // per_span)[:, None] == jnp.arange(spans, dtype=jnp.int32)[None],
            deal_row[None],
            0,
        ),
        axis=1,
        dtype=jnp.int32,
    )
    natural_block = span_of * per_span + dealt_block % per_span
    place = jnp.sum(
        jnp.where(natural_block[None, :] == rel[:, None], rel[None, :], 0), axis=1, dtype=jnp.int32
    )
    natural_rel = (
        natural_block[:, None] * own_rows + jnp.arange(own_rows, dtype=jnp.int32)[None]
    ).reshape(-1)
    inside_rel = (natural_rel[:, None] >= starts[None]) & (natural_rel[:, None] < ends[None])
    position = natural_rel - jnp.sum(
        jnp.where(inside_rel, starts[None], 0), axis=1, dtype=jnp.int32
    )
    lane = jnp.arange(128, dtype=jnp.int32)
    inverse = jnp.exp((lane % 32).astype(F32) * (-2.0 * math.log(ROPE_BASE) / HEAD_DIM))
    angles = position.astype(F32)[:, None] * inverse[None]
    cos = jnp.cos(angles)
    sin = jnp.where((lane % 64 < 32)[None], -jnp.sin(angles), jnp.sin(angles))
    start_column = start_of[:, None]

    q_half, k_half, v_half, o_half = map(half, (q_weight, k_weight, v_weight, o_weight))
    q_width, kv_width = q_half.shape[1], k_half.shape[1]
    attn_shard = jnp.concatenate([o_half, q_half, k_half, v_half], axis=1)
    fsdp = lax.axis_size("fsdp")
    gain_rows = jnp.stack([attn_gain, ffn_gain])
    gain_width = attn_gain.shape[0]
    extra = ((0, 14), (0, attn_shard.shape[1] - gain_width))
    tokens_low = lax.dynamic_slice_in_dim(tokens, tp * own_rows, own_rows, 0)
    cot_low = lax.dynamic_slice_in_dim(cotangent, tp * own_rows, own_rows, 0)
    tokens_one = swap_first(tokens_low)
    attn_ring = ring_over(
        jnp.concatenate([attn_shard, jnp.pad(gain_rows, extra)]),
        fsdp,
        (tokens_one, cos, sin, cot_low, place, first, start_column),
    )
    own_depth = attn_shard.shape[0]
    attn_full = in_place([piece[:own_depth] for piece in attn_ring], 0)
    gains = in_place([piece[own_depth : own_depth + 2, :gain_width] for piece in attn_ring], 1)
    gain_one = gains[0].astype(F32)[None]
    gain_two = gains[1].astype(F32)[None]
    ff_half = gate_weight.shape[1] // 2
    chunks = [ff_half * share // sum(SPLIT) for share in SPLIT]
    ffn_shards = []
    for part, chunk in enumerate(chunks):
        at = ctx * ff_half + sum(chunks[:part])
        ffn_shards.append(
            jnp.concatenate(
                [
                    lax.dynamic_slice_in_dim(weight, at, chunk, 1)
                    for weight in (gate_weight, up_weight, down_weight)
                ],
                axis=1,
            )
        )
    tokens_own, cot_own = tokens_low.astype(F32), cot_low.astype(F32)
    group_tokens = (tokens_low, tokens_one, swap_second(tokens_low), swap_second(tokens_one))
    first_shard = after(ffn_shards[0], attn_ring[-1], *group_tokens[2:])
    group_tokens = group_tokens + tuple(swap_core(part) for part in group_tokens)
    attn_full, cot_low, cos, sin, gain_one, *group_tokens = lax.optimization_barrier(
        (attn_full, cot_low, cos, sin, gain_one, *group_tokens)
    )
    qkv = project_qkv(group_tokens, gain_one, attn_full, q_width, cos, sin)
    heads = attend(qkv, depth, place, first, start_column, q_width)
    cot = share_rows(cot_low, [[qkv], [heads]])
    ffn_full = [
        lax.all_gather(shard, "fsdp", axis=0, tiled=True)
        for shard in (first_shard, after(ffn_shards[1], heads))
    ]
    heads = after(heads, *cot)
    attn_blocks = sum_cores([(heads, 0, attn_full, 0, q_width)])
    attn_parts = last_parts(*sum_first(attn_blocks), beside=ffn_full[:1])
    attn_sum = sum(part.astype(F32) for part in attn_parts)
    hidden = tokens_own + attn_sum
    normed_two = share_rows((hidden * inv_rms(hidden) * gain_two).astype(BF16))

    acts = []
    grad_parts = []
    d_norm_partial = ()

    def chunk_grads(part, held=()):
        chunk = chunks[part]
        act = after(acts[part], *held)
        grad_parts.append(weight_grads(normed_two, act, 2 * chunk, 0, cot, act, chunk, 2))

    last = len(chunks) - 1
    for part in range(len(chunks)):
        normed_two = (after(normed_two[0], *grad_parts, *d_norm_partial), *normed_two[1:])
        acts.append(ffn_chunk(normed_two, cot, ffn_full[part]))
        d_norm_term = (acts[part], 0, ffn_full[part], 0, 2 * chunks[part])
        if part < last:
            chunk_grads(part)
            d_norm_partial = (back_product([d_norm_term], plus=d_norm_partial),)
    ffn_terms = [(acts[part], 2, ffn_full[part], 2, chunk) for part, chunk in enumerate(chunks)]
    d_norm_far, d_norm_near = halves_of_cores([d_norm_term], d_norm_partial)
    chunk_grads(last, (d_norm_far,))
    reduced = [
        lax.psum_scatter(part, "fsdp", scatter_dimension=0, tiled=True) for part in grad_parts
    ]
    d_norm_near = wide_first(d_norm_far, d_norm_near, grad_parts)

    def ffn_rows(part, parts, held):
        (act, *rest), *others = ffn_terms
        return back_product([(after(act, held), *rest), *others], part, parts, work=7)

    ffn_sent = [ffn_rows(3, 4, d_norm_near)]
    d_own = norm_back(wide_last(d_norm_near, ffn_sent), hidden, gain_two, cot_low)
    ffn_sent.append(ffn_rows(2, 4, d_own))
    ffn_mine = ffn_rows(0, 2, d_own)
    d_one, d_two, ffn_mine, ffn_sent[1] = lax.optimization_barrier(
        (swap_first(d_own), swap_second(d_own), ffn_mine, ffn_sent[1])
    )
    ffn_own, ffn_a, ffn_b, ffn_both = add_blocks(ffn_mine, [swap_core(piece) for piece in ffn_sent])
    ffn_x, ffn_y = jnp.where(core == 0, ffn_a, ffn_b), jnp.where(core == 0, ffn_b, ffn_a)
    d_early = [swap_core(part) for part in (d_own, d_one, d_two)]
    d_last = after(swap_second(d_one), *d_early, ffn_own, ffn_x, ffn_y, ffn_both, reduced[0])
    d_attn = (d_own, d_one, d_two, d_last, *d_early, swap_core(d_last))

    d_heads = front_product(d_attn, attn_full, q_width, 0)
    other_reduced = [swap_x(after(reduced[0], d_last))]
    d_qkv = attend_back(qkv, depth, d_heads, heads, place, first, start_column, cos, sin)
    y_both, y_own, d_qkv, other_reduced[0] = lax.optimization_barrier(
        (swap_y(ffn_both), swap_y(ffn_y), d_qkv, other_reduced[0])
    )
    ffn_x, ffn_own, d_qkv = lax.optimization_barrier((ffn_x + y_both, ffn_own + y_own, d_qkv))
    ffn_far = swap_x(ffn_x)
    normed_blocks = sum_cores(
        [
            (d_qkv, 0, attn_full, 1, q_width),
            (d_qkv, q_width // 128, attn_full, 2 * q_width // 128, 128),
        ]
    )
    attn_grad = weight_grads(
        d_attn, heads, q_width, 0, (qkv,), after(d_qkv, normed_blocks[3]), q_width + 128, 0, 0
    )
    ffn_far = after(ffn_far, attn_grad)
    result_own = (hidden + (ffn_own.astype(F32) + ffn_far.astype(F32))).astype(BF16)
    result_beside = swap_y(result_own)
    normed_first = sum_first(normed_blocks, [attn_grad, result_own])
    for part in range(1, len(chunks)):
        reduced[part] = after(reduced[part], attn_grad)
        other_reduced.append(swap_x(reduced[part]))
    late = [after(part, normed_first[1]) for part in other_reduced]
    halves = [both_halves(mine, other, ctx) for mine, other in zip(reduced, late)]

    def ffn_out(which):
        return jnp.concatenate(
            [
                halves[part][side][:, which * chunk : (which + 1) * chunk]
                for side in range(2)
                for part, chunk in enumerate(chunks)
            ],
            axis=1,
        )

    ffn_grads = [ffn_out(which) for which in range(3)]
    result = share_in_ctx(result_own, result_beside, y, core)
    normed_parts = last_parts(*normed_first, beside=[result, *ffn_grads])
    tokens_grad_own = norm_back(normed_parts, tokens_low, gain_one, d_own)
    attn_reduced = lax.psum_scatter(attn_grad, "fsdp", scatter_dimension=0, tiled=True)
    attn_reduced = after(attn_reduced, tokens_grad_own)
    other_attn = swap_x(attn_reduced)
    def gain_part(pairs):
        return sum(jnp.sum(mine.astype(F32) * grad.astype(F32), axis=1) for mine, grad in pairs)

    gain_sums = jnp.stack(
        [
            gain_part([(attn_shard[:, q_width:], attn_reduced[:, q_width:])]),
            gain_part(
                [
                    (ffn_shards[part][:, : 2 * chunk], reduced[part][:, : 2 * chunk])
                    for part, chunk in enumerate(chunks)
                ]
            ),
        ]
    )
    gain_sums = gain_sums + swap_core(gain_sums)
    gain_sums = gain_sums + swap_y(gain_sums)

    tokens_grad_beside, gain_sums, other_attn, result, *ffn_grads = lax.optimization_barrier(
        (swap_y(tokens_grad_own), gain_sums, other_attn, result, *ffn_grads)
    )
    tokens_grad = share_in_ctx(tokens_grad_own, tokens_grad_beside, y, core)
    gain_sums = gain_sums + swap_x(gain_sums)
    attn_gain_grad = gain_sums[0] / attn_gain.astype(F32)
    ffn_gain_grad = gain_sums[1] / ffn_gain.astype(F32)
    attn_low, attn_high = both_halves(attn_reduced, other_attn, ctx)

    def attn_out(begin, end):
        return jnp.concatenate([attn_low[:, begin:end], attn_high[:, begin:end]], axis=1)

    q_end, k_end = 2 * q_width, 2 * q_width + kv_width
    return (
        result,
        tokens_grad,
        attn_out(q_width, q_end),
        attn_out(q_end, k_end),
        attn_out(k_end, k_end + kv_width),
        attn_out(0, q_width),
        attn_gain_grad,
        *ffn_grads,
        ffn_gain_grad,
    )


def solution(mesh):
    rows = P(("fsdp", "ctx"), None)
    matrix = P("fsdp", "tp")
    vector = P("fsdp")
    return jax.shard_map(
        shards,
        mesh=mesh,
        in_specs=(
            rows,
            matrix,
            matrix,
            matrix,
            matrix,
            vector,
            matrix,
            matrix,
            matrix,
            vector,
            P("fsdp", None),
            P("fsdp", None),
            rows,
        ),
        out_specs=(
            rows,
            rows,
            matrix,
            matrix,
            matrix,
            matrix,
            vector,
            matrix,
            matrix,
            matrix,
            vector,
        ),
        check_vma=False,
    )
```

```python
import functools
import math

import jax
import jax.numpy as jnp
from jax import lax
from jax.experimental import pallas as pl
from jax.experimental.pallas import tpu as pltpu
from jax.sharding import PartitionSpec as P

HEAD_DIM = 64
EPSILON = 1e-05
ROPE_BASE = 500000.0
MASKED = -1e30
LOG2_E = 1.4426950408889634
BLOCK = 256
SPLIT = (1, 1)
VMEM = 56 * 2**20

F32 = jnp.float32
BF16 = jnp.bfloat16

PAIR = [(0, 1), (1, 0)]
CORE = [(0, 1), (1, 0), (2, 3), (3, 2)]
ACROSS = [(0, 2), (2, 0), (1, 3), (3, 1)]


def joint_pairs(x_core):
    pairs = []
    for ctx in range(2):
        for tp in range(4):
            there = (1 - ctx) * 4 + tp if tp % 2 == x_core else ctx * 4 + (tp ^ 2)
            pairs.append((ctx * 4 + tp, there))
    return pairs


FIRST = joint_pairs(0)
SECOND = joint_pairs(1)


def swap_core(v):
    return lax.ppermute(v, "tp", CORE)


def swap_y(v):
    return lax.ppermute(v, "tp", ACROSS)


def swap_x(v):
    return lax.ppermute(v, "ctx", PAIR)


def swap_first(v):
    return lax.ppermute(v, ("ctx", "tp"), FIRST)


def swap_second(v):
    return lax.ppermute(v, ("ctx", "tp"), SECOND)


def after(value, *others):
    return lax.optimization_barrier((value,) + others)[0]


def params(*semantics):
    return pltpu.CompilerParams(vmem_limit_bytes=VMEM)


def cost(gigaflops=0):
    return pl.CostEstimate(flops=int(gigaflops * 1e9) + 1, bytes_accessed=1, transcendentals=0)


def inv_rms(hidden):
    return lax.rsqrt(jnp.mean(hidden * hidden, axis=-1, keepdims=True) + EPSILON)


def rms_back(hidden, gain, grad):
    scale = inv_rms(hidden)
    weighted = grad * gain
    inner = jnp.mean(weighted * hidden, axis=-1, keepdims=True)
    return scale * weighted - hidden * (scale * scale * scale) * inner


def norm_back_kernel(count, *refs):
    hidden_ref, gain_ref, kept_ref, o_ref = refs[count:]
    grad = sum(ref[...].astype(F32) for ref in refs[:count])
    back = rms_back(hidden_ref[...].astype(F32), gain_ref[...], grad)
    o_ref[...] = (kept_ref[...].astype(F32) + back).astype(BF16)


def norm_back(parts, hidden, gain, kept):
    rows, depth = hidden.shape
    step = min(128, rows)
    block = pl.BlockSpec((step, depth), lambda i: (i, 0))
    return pl.pallas_call(
        functools.partial(norm_back_kernel, len(parts)),
        out_shape=jax.ShapeDtypeStruct((rows, depth), BF16),
        grid=(rows // step,),
        in_specs=[block] * (len(parts) + 1)
        + [pl.BlockSpec((1, depth), lambda i: (0, 0)), block],
        out_specs=block,
        compiler_params=params(),
        cost_estimate=cost(),
        name="norm_back",
    )(*parts, hidden, gain, kept)


def turn_lanes(u, first):
    return jnp.where(first, pltpu.roll(u, 96, 1), pltpu.roll(u, 32, 1))


def stream_scratch(count, rows, depth):
    return [pltpu.VMEM((2, rows, depth), BF16), pltpu.SemaphoreType.DMA((2,))] * count


def next_piece(refs, buffer, sems):
    i = pl.program_id(0)

    def copy_of(piece):
        return pltpu.make_async_copy(refs[piece], buffer.at[piece % 2], sems.at[piece % 2])

    @pl.when(i == 0)
    def _():
        copy_of(0).start()

    for piece in range(1, len(refs)):

        @pl.when(i == piece - 1)
        def _(piece=piece):
            copy_of(piece).start()

    for piece in range(len(refs)):

        @pl.when(i == piece)
        def _(piece=piece):
            copy_of(piece).wait()

    return buffer[lax.rem(i, 2)]


def qkv_kernel(count, *refs):
    gain_ref, wq_ref, wkv_ref, cos_ref, sin_ref, o_ref, buffer, sems = refs[count:]
    cos, sin = cos_ref[...], sin_ref[...]
    depth = gain_ref.shape[1]
    lane = lax.broadcasted_iota(jnp.int32, cos.shape, 1)
    first = (lane % 64) < 32
    x = next_piece(refs[:count], buffer, sems).astype(F32)
    x = (x * inv_rms(x) * gain_ref[...]).astype(BF16)
    o_ref[:, :depth] = x
    raw = jnp.dot(x, wq_ref[...], preferred_element_type=F32)
    tiles = raw.shape[1] // 128
    for tile in range(tiles):
        u = raw[:, tile * 128 : (tile + 1) * 128]
        turned = u * cos + turn_lanes(u, first) * sin
        o_ref[:, depth + tile * 128 : depth + (tile + 1) * 128] = turned.astype(BF16)
    u = jnp.dot(x, wkv_ref[...], preferred_element_type=F32)
    turned = u * cos + turn_lanes(u, first) * sin
    o_ref[:, depth + tiles * 128 :] = jnp.where(lane < 64, turned, u).astype(BF16)


def project_qkv(x, gain, w, q_width, cos, sin):
    step, depth = x[0].shape
    rows = len(x) * step
    width = depth + q_width + 128
    return pl.pallas_call(
        functools.partial(qkv_kernel, len(x)),
        out_shape=jax.ShapeDtypeStruct((rows, width), BF16),
        grid=(len(x),),
        in_specs=[pl.BlockSpec(memory_space=pl.ANY)] * len(x)
        + [
            pl.BlockSpec((1, depth), lambda i: (0, 0)),
            pl.BlockSpec((depth, q_width), lambda i: (0, 1)),
            pl.BlockSpec((depth, 128), lambda i: (0, 2 * q_width // 128)),
            pl.BlockSpec((step, 128), lambda i: (i, 0)),
            pl.BlockSpec((step, 128), lambda i: (i, 0)),
        ],
        out_specs=pl.BlockSpec((step, width), lambda i: (i, 0)),
        scratch_shapes=stream_scratch(1, step, depth),
        compiler_params=params(),
        cost_estimate=cost(),
        name="qkv",
    )(*x, gain, w, w, cos, sin)


def ffn_kernel(count, *refs):
    w_ref, o_ref, x_buffer, x_sems, c_buffer, c_sems = refs[2 * count :]
    n = w_ref.shape[1] // 3
    x = next_piece(refs[:count], x_buffer, x_sems)
    c = next_piece(refs[count : 2 * count], c_buffer, c_sems)
    gate = jnp.dot(x, w_ref[:, :n], preferred_element_type=F32)
    up = jnp.dot(x, w_ref[:, n : 2 * n], preferred_element_type=F32)
    d_mixed = jnp.dot(c, w_ref[:, 2 * n :], preferred_element_type=F32)
    sig = 1.0 / (1.0 + jnp.exp(-gate))
    silu = gate * sig
    o_ref[:, :n] = (d_mixed * up * (sig * (1.0 + gate * (1.0 - sig)))).astype(BF16)
    o_ref[:, n : 2 * n] = (d_mixed * silu).astype(BF16)
    o_ref[:, 2 * n :] = (silu * up).astype(BF16)


def ffn_chunk(x, cot, w):
    step, depth = x[0].shape
    rows = len(x) * step
    width = w.shape[1]
    return pl.pallas_call(
        functools.partial(ffn_kernel, len(x)),
        out_shape=jax.ShapeDtypeStruct((rows, width), BF16),
        grid=(len(x),),
        in_specs=[pl.BlockSpec(memory_space=pl.ANY)] * (2 * len(x))
        + [pl.BlockSpec((depth, width), lambda i: (0, 0))],
        out_specs=pl.BlockSpec((step, width), lambda i: (i, 0)),
        scratch_shapes=stream_scratch(2, step, depth),
        compiler_params=params(),
        cost_estimate=cost(),
        name="ffn",
    )(*x, *cot, w)


DOWN = (((0,), (0,)), ((), ()))


def grads_kernel(x_count, y_count, *refs):
    a_ref, b_ref, o_ref = refs[x_count + y_count :]
    split = a_ref.shape[1]

    def product(tall_refs, right_ref):
        tall = jnp.concatenate([ref[...] for ref in tall_refs], axis=0)
        return lax.dot_general(
            tall, right_ref[...].astype(BF16), DOWN, preferred_element_type=F32
        ).astype(BF16)

    o_ref[:, :split] = product(refs[:x_count], a_ref)
    o_ref[:, split:] = product(refs[x_count : x_count + y_count], b_ref)


def weight_grads(x, a, a_width, a_column, y, b, b_width, b_column, work=20):
    depth = x[0].shape[1]
    rows = a.shape[0]
    width = a_width + b_width
    step = 512
    return pl.pallas_call(
        functools.partial(grads_kernel, len(x), len(y)),
        out_shape=jax.ShapeDtypeStruct((depth, width), BF16),
        grid=(depth // step,),
        in_specs=[pl.BlockSpec((piece.shape[0], step), lambda i: (0, i)) for piece in (*x, *y)]
        + [
            pl.BlockSpec((rows, a_width), lambda i: (0, a_column)),
            pl.BlockSpec((rows, b_width), lambda i: (0, b_column)),
        ],
        out_specs=pl.BlockSpec((step, width), lambda i: (i, 0)),
        compiler_params=params(),
        cost_estimate=cost(work),
        name="weight_grads",
    )(*x, *y, a, b)


def back_kernel(count, *refs):
    o_ref = refs[-1]
    total = refs[2 * count][...].astype(F32) if len(refs) > 2 * count + 1 else None
    for part in range(count):
        term = lax.dot_general(
            refs[part][...].astype(BF16),
            refs[count + part][...],
            (((1,), (1,)), ((), ())),
            preferred_element_type=F32,
        )
        total = term if total is None else total + term
    o_ref[...] = total.astype(BF16)


def back_product(terms, part=0, parts=1, plus=(), work=0):
    rows = terms[0][0].shape[0] // parts
    depth = terms[0][2].shape[0]
    step = min(512, rows)
    ahead = part * (rows // step)
    return pl.pallas_call(
        functools.partial(back_kernel, len(terms)),
        out_shape=jax.ShapeDtypeStruct((rows, depth), BF16),
        grid=(rows // step,),
        in_specs=[
            pl.BlockSpec((step, term[4]), lambda i, column=term[1]: (i + ahead, column))
            for term in terms
        ]
        + [pl.BlockSpec((depth, term[4]), lambda i, column=term[3]: (0, column)) for term in terms]
        + [pl.BlockSpec((step, depth), lambda i: (i + ahead, 0))] * len(plus),
        out_specs=pl.BlockSpec((step, depth), lambda i: (i, 0)),
        compiler_params=params(),
        cost_estimate=cost(work),
        name="back",
    )(*[term[0] for term in terms], *[term[2] for term in terms], *plus)


def front_kernel(count, *refs):
    w_ref, o_ref, buffer, sems = refs[count:]
    x = next_piece(refs[:count], buffer, sems)
    o_ref[...] = jnp.dot(x, w_ref[...], preferred_element_type=F32).astype(BF16)


def front_product(x, w, width, column):
    step, depth = x[0].shape
    rows = len(x) * step
    return pl.pallas_call(
        functools.partial(front_kernel, len(x)),
        out_shape=jax.ShapeDtypeStruct((rows, width), BF16),
        grid=(len(x),),
        in_specs=[pl.BlockSpec(memory_space=pl.ANY)] * len(x)
        + [pl.BlockSpec((depth, width), lambda i: (0, column))],
        out_specs=pl.BlockSpec((step, width), lambda i: (i, 0)),
        scratch_shapes=stream_scratch(1, step, depth),
        compiler_params=params(),
        cost_estimate=cost(),
        name="front",
    )(*x, w)


def stack_heads(block):
    count = block.shape[1] // HEAD_DIM
    return jnp.concatenate(
        [block[:, h * HEAD_DIM : (h + 1) * HEAD_DIM] for h in range(count)], axis=0
    )


def unstack_heads(stacked):
    count = stacked.shape[0] // BLOCK
    return jnp.concatenate([stacked[h * BLOCK : (h + 1) * BLOCK] for h in range(count)], axis=1)


def allowed_of(i, j, start):
    row = i * BLOCK + lax.broadcasted_iota(jnp.int32, (BLOCK, BLOCK), 0)
    col = j * BLOCK + lax.broadcasted_iota(jnp.int32, (BLOCK, BLOCK), 1)
    return (col <= row) & (col >= start)


def attend_kernel(place, first, q_ref, kv_ref, start_ref, o_ref):
    i = pl.program_id(0)
    q = stack_heads(q_ref[...])
    heads = q.shape[0] // BLOCK
    start = start_ref[...]

    def step(j, carry):
        top, total, acc = carry
        at = pl.multiple_of(place[j] * BLOCK, BLOCK)
        kv = kv_ref[pl.ds(at, BLOCK), :]
        raw = lax.dot_general(
            q, kv[:, :HEAD_DIM], (((1,), (1,)), ((), ())), preferred_element_type=F32
        ) * (HEAD_DIM**-0.5 * LOG2_E)
        allowed = allowed_of(i, j, start)
        scores = jnp.where(allowed[None], raw.reshape(heads, BLOCK, BLOCK), MASKED).reshape(
            heads * BLOCK, BLOCK
        )
        new_top = jnp.maximum(top, jnp.max(scores, axis=-1, keepdims=True))
        keep = jnp.exp2(top - new_top)
        probs = jnp.exp2(scores - new_top)
        total = total * keep + jnp.sum(probs, axis=-1, keepdims=True)
        acc = acc * keep + jnp.dot(probs.astype(BF16), kv, preferred_element_type=F32)
        return (new_top, total, acc)

    size = heads * BLOCK
    top, total, acc = lax.fori_loop(
        first[i],
        i + 1,
        step,
        (
            jnp.full((size, 1), MASKED, F32),
            jnp.zeros((size, 1), F32),
            jnp.zeros((size, 2 * HEAD_DIM), F32),
        ),
    )
    out = acc[:, HEAD_DIM:] / total
    q_width = q_ref.shape[1]
    o_ref[:, :q_width] = unstack_heads(out)
    lse = top + jnp.log2(total)
    lane = lax.broadcasted_iota(jnp.int32, (BLOCK, 128), 1)
    packed = jnp.zeros((BLOCK, 128), F32)
    for h in range(heads):
        packed = jnp.where(lane == h, lse[h * BLOCK : (h + 1) * BLOCK], packed)
    o_ref[:, q_width:] = packed


def attend(qkv, depth, place, first, start, q_width):
    rows = qkv.shape[0]
    blocks = rows // BLOCK
    return pl.pallas_call(
        attend_kernel,
        out_shape=jax.ShapeDtypeStruct((rows, q_width + 128), F32),
        grid_spec=pltpu.PrefetchScalarGridSpec(
            num_scalar_prefetch=2,
            grid=(blocks,),
            in_specs=[
                pl.BlockSpec((BLOCK, q_width), lambda i, place, first: (place[i], depth // q_width)),
                pl.BlockSpec((rows, 128), lambda i, place, first: (0, (depth + q_width) // 128)),
                pl.BlockSpec((BLOCK, 1), lambda i, place, first: (i, 0)),
            ],
            out_specs=pl.BlockSpec((BLOCK, q_width + 128), lambda i, place, first: (place[i], 0)),
        ),
        compiler_params=params(),
        cost_estimate=cost(),
        name="attend",
    )(place, first, qkv, qkv, start)


def attend_back_kernel(
    place,
    first,
    q_ref,
    d_ref,
    h_ref,
    kv_ref,
    start_ref,
    cos_ref,
    sin_ref,
    o_ref,
    dkv_ref,
):
    i = pl.program_id(0)
    blocks = pl.num_programs(0)
    score_scale = HEAD_DIM**-0.5
    q_width = q_ref.shape[1]

    @pl.when(i == 0)
    def _():
        dkv_ref[...] = jnp.zeros_like(dkv_ref)

    q = stack_heads(q_ref[...])
    d_out = stack_heads(d_ref[...])
    heads = q.shape[0] // BLOCK
    out = stack_heads(h_ref[:, :q_width])
    delta = jnp.sum(d_out.astype(F32) * out, axis=-1, keepdims=True)
    lse_block = h_ref[:, q_width:]
    lse = jnp.concatenate([lse_block[:, h : h + 1] for h in range(heads)], axis=0)
    start = start_ref[...]

    def step(j, d_q):
        at = pl.multiple_of(place[j] * BLOCK, BLOCK)
        kv = kv_ref[pl.ds(at, BLOCK), :]
        k, v = kv[:, :HEAD_DIM], kv[:, HEAD_DIM:]
        across = (((1,), (1,)), ((), ()))
        down = (((0,), (0,)), ((), ()))
        raw = lax.dot_general(q, k, across, preferred_element_type=F32) * (score_scale * LOG2_E)
        allowed = allowed_of(i, j, start)
        scores = jnp.where(allowed[None], raw.reshape(heads, BLOCK, BLOCK), MASKED).reshape(
            heads * BLOCK, BLOCK
        )
        probs = jnp.exp2(scores - lse)
        d_probs = lax.dot_general(d_out, v, across, preferred_element_type=F32)
        d_scores = (probs * (d_probs - delta)).astype(BF16)
        d_k = lax.dot_general(d_scores, q, down, preferred_element_type=F32) * score_scale
        d_v = lax.dot_general(probs.astype(BF16), d_out, down, preferred_element_type=F32)
        here = pl.ds(pl.multiple_of(j * BLOCK, BLOCK), BLOCK)
        dkv_ref[here, :] += jnp.concatenate([d_k, d_v], axis=1)
        return d_q + jnp.dot(d_scores, k, preferred_element_type=F32)

    d_q = lax.fori_loop(first[i], i + 1, step, jnp.zeros((heads * BLOCK, HEAD_DIM), F32))
    d_q = unstack_heads(d_q * score_scale)
    lane = lax.broadcasted_iota(jnp.int32, (BLOCK, 128), 1)
    front = (lane % 64) < 32
    mine = pl.ds(pl.multiple_of(place[i] * BLOCK, BLOCK), BLOCK)
    cos, sin = cos_ref[mine, :], sin_ref[mine, :]
    for tile in range(q_width // 128):
        u = d_q[:, tile * 128 : (tile + 1) * 128]
        o_ref[mine, tile * 128 : (tile + 1) * 128] = (u * cos - turn_lanes(u, front) * sin).astype(
            BF16
        )

    @pl.when(i == blocks - 1)
    def _():
        for b in range(dkv_ref.shape[0] // BLOCK):
            there = pl.ds(pl.multiple_of(place[b] * BLOCK, BLOCK), BLOCK)
            u = dkv_ref[b * BLOCK : (b + 1) * BLOCK, :]
            turned = u * cos_ref[there, :] - turn_lanes(u, front) * sin_ref[there, :]
            o_ref[there, q_width:] = jnp.where(lane < HEAD_DIM, turned, u).astype(BF16)


def attend_back(qkv, depth, d_heads, heads, place, first, start, cos, sin):
    rows, q_width = d_heads.shape
    width = q_width + 128
    blocks = rows // BLOCK
    by_place = lambda i, place, first: (place[i], 0)
    whole = lambda i, place, first: (0, 0)
    return pl.pallas_call(
        attend_back_kernel,
        out_shape=jax.ShapeDtypeStruct((rows, width), BF16),
        grid_spec=pltpu.PrefetchScalarGridSpec(
            num_scalar_prefetch=2,
            grid=(blocks,),
            in_specs=[
                pl.BlockSpec((BLOCK, q_width), lambda i, place, first: (place[i], depth // q_width)),
                pl.BlockSpec((BLOCK, q_width), by_place),
                pl.BlockSpec((BLOCK, q_width + 128), by_place),
                pl.BlockSpec((rows, 128), lambda i, place, first: (0, (depth + q_width) // 128)),
                pl.BlockSpec((BLOCK, 1), lambda i, place, first: (i, 0)),
                pl.BlockSpec((rows, 128), whole),
                pl.BlockSpec((rows, 128), whole),
            ],
            out_specs=pl.BlockSpec((rows, width), whole),
            scratch_shapes=[pltpu.VMEM((rows, 128), F32)],
        ),
        compiler_params=params(),
        cost_estimate=cost(),
        name="attend_back",
    )(place, first, qkv, d_heads, heads, qkv, start, cos, sin)


def sum_cores(terms, pieces=2):
    sent = [back_product(terms, 2 * pieces - 1 - at, 2 * pieces) for at in range(pieces)]
    arrived = [swap_core(piece) for piece in sent]
    return add_blocks(back_product(terms, 0, 2), arrived)


def add_blocks(mine, arrived):
    rows = mine.shape[0] // 4
    each = 4 // len(arrived)
    blocks = []
    for at in range(4):
        other = arrived[len(arrived) - 1 - at // each]
        begin = (at % each) * rows
        blocks.append(mine[at * rows : (at + 1) * rows] + other[begin : begin + rows])
    return blocks


def sum_first(blocks, early=()):
    own, along_a, along_b, both = blocks
    along_a = along_a + after(swap_second(both), *early)
    return (own, *lax.optimization_barrier((along_a, along_b)))


def last_parts(own, along_a, along_b, beside=()):
    return own, swap_second(along_b), after(swap_first(along_a), *beside)


def halves_of_cores(terms, plus):
    arrived = swap_core(back_product(terms, 1, 2, plus))
    mine = back_product(terms, 0, 2, plus)
    rows = mine.shape[0] // 4
    return mine[2 * rows :] + arrived[2 * rows :], mine[: 2 * rows] + arrived[: 2 * rows]


def wide_first(far, near, between):
    return after(near + swap_second(far), *between)


def wide_last(near, beside):
    return near, after(swap_first(near[near.shape[0] // 2 :]), *beside)


def share_rows(own, beside=()):
    beside = list(beside) + [()] * (2 - len(beside))
    one, two, *_ = lax.optimization_barrier((swap_first(own), swap_second(own), *beside[0]))
    early = tuple(swap_core(part) for part in (own, one, two))
    last = after(swap_second(one), *early, *beside[1])
    return (own, one, two, last, *early, swap_core(last))


def ring_over(shard, count, held):
    cycle = [(at, (at + 1) % count) for at in range(count)]
    pieces = [shard]
    for step in range(count - 1):
        sent = after(pieces[-1], *held) if step == 1 else pieces[-1]
        pieces.append(lax.ppermute(sent, "fsdp", cycle))
    return pieces


def in_place(pieces, axis):
    count, size = len(pieces), pieces[0].shape[axis]
    here = lax.axis_index("fsdp")
    shape = list(pieces[0].shape)
    shape[axis] *= count
    whole = jnp.zeros(shape, pieces[0].dtype)
    for back, piece in enumerate(pieces):
        owner = lax.rem(here + count - back, count)
        whole = lax.dynamic_update_slice_in_dim(whole, piece, owner * size, axis)
    return whole


def share_in_ctx(own, beside, y, core):
    pair = jnp.stack([own, beside])
    other = jnp.stack([swap_core(own), swap_core(beside)])
    four = jnp.stack([pair, other])
    four = jnp.where(y == 1, four[:, ::-1], four)
    four = jnp.where(core == 1, four[::-1], four)
    return four.transpose(1, 0, 2, 3).reshape(-1, own.shape[1])


def both_halves(own, other, ctx):
    low = jnp.where(ctx == 0, own, other).astype(F32)
    high = jnp.where(ctx == 0, other, own).astype(F32)
    return low, high


def shards(
    tokens,
    q_weight,
    k_weight,
    v_weight,
    o_weight,
    attn_gain,
    gate_weight,
    up_weight,
    down_weight,
    ffn_gain,
    lengths,
    deal,
    cotangent,
):
    ctx = lax.axis_index("ctx")
    tp = lax.axis_index("tp")
    y, core = tp // 2, tp % 2
    row_count, depth = tokens.shape
    group_rows = row_count * lax.axis_size("ctx")
    own_rows = row_count // lax.axis_size("tp")

    def half(weight):
        width = weight.shape[1] // 2
        return lax.dynamic_slice_in_dim(weight, ctx * width, width, 1)

    length_row, deal_row = lengths[0], deal[0]
    spans = deal_row.shape[0]
    span_rows = group_rows // spans
    ends = jnp.cumsum(length_row, dtype=jnp.int32)
    starts = ends - length_row
    natural = jnp.arange(group_rows, dtype=jnp.int32)
    inside = (natural[:, None] >= starts[None]) & (natural[:, None] < ends[None])
    start_of = jnp.sum(jnp.where(inside, starts[None], 0), axis=1, dtype=jnp.int32)
    first = start_of[::BLOCK] // BLOCK
    rel = jnp.arange(group_rows // own_rows, dtype=jnp.int32)
    rel_core = core ^ (rel // 4)
    by_first, by_second = rel % 2, (rel // 2) % 2
    rel_ctx = ctx ^ jnp.where(rel_core == 0, by_first, by_second)
    rel_y = y ^ jnp.where(rel_core == 0, by_second, by_first)
    dealt_block = rel_ctx * (row_count // own_rows) + rel_y * 2 + rel_core
    per_span = span_rows // own_rows
    span_of = jnp.sum(
        jnp.where(
            (dealt_block // per_span)[:, None] == jnp.arange(spans, dtype=jnp.int32)[None],
            deal_row[None],
            0,
        ),
        axis=1,
        dtype=jnp.int32,
    )
    natural_block = span_of * per_span + dealt_block % per_span
    place = jnp.sum(
        jnp.where(natural_block[None, :] == rel[:, None], rel[None, :], 0), axis=1, dtype=jnp.int32
    )
    natural_rel = (
        natural_block[:, None] * own_rows + jnp.arange(own_rows, dtype=jnp.int32)[None]
    ).reshape(-1)
    inside_rel = (natural_rel[:, None] >= starts[None]) & (natural_rel[:, None] < ends[None])
    position = natural_rel - jnp.sum(
        jnp.where(inside_rel, starts[None], 0), axis=1, dtype=jnp.int32
    )
    lane = jnp.arange(128, dtype=jnp.int32)
    inverse = jnp.exp((lane % 32).astype(F32) * (-2.0 * math.log(ROPE_BASE) / HEAD_DIM))
    angles = position.astype(F32)[:, None] * inverse[None]
    cos = jnp.cos(angles)
    sin = jnp.where((lane % 64 < 32)[None], -jnp.sin(angles), jnp.sin(angles))
    start_column = start_of[:, None]

    q_half, k_half, v_half, o_half = map(half, (q_weight, k_weight, v_weight, o_weight))
    q_width, kv_width = q_half.shape[1], k_half.shape[1]
    attn_shard = jnp.concatenate([o_half, q_half, k_half, v_half], axis=1)
    fsdp = lax.axis_size("fsdp")
    gain_rows = jnp.stack([attn_gain, ffn_gain])
    gain_width = attn_gain.shape[0]
    extra = ((0, 14), (0, attn_shard.shape[1] - gain_width))
    tokens_low = lax.dynamic_slice_in_dim(tokens, tp * own_rows, own_rows, 0)
    cot_low = lax.dynamic_slice_in_dim(cotangent, tp * own_rows, own_rows, 0)
    tokens_one = swap_first(tokens_low)
    attn_ring = ring_over(
        jnp.concatenate([attn_shard, jnp.pad(gain_rows, extra)]),
        fsdp,
        (tokens_one, cos, sin, cot_low, place, first, start_column),
    )
    own_depth = attn_shard.shape[0]
    attn_full = in_place([piece[:own_depth] for piece in attn_ring], 0)
    gains = in_place([piece[own_depth : own_depth + 2, :gain_width] for piece in attn_ring], 1)
    gain_one = gains[0].astype(F32)[None]
    gain_two = gains[1].astype(F32)[None]
    ff_half = gate_weight.shape[1] // 2
    chunks = [ff_half * share // sum(SPLIT) for share in SPLIT]
    ffn_shards = []
    for part, chunk in enumerate(chunks):
        at = ctx * ff_half + sum(chunks[:part])
        ffn_shards.append(
            jnp.concatenate(
                [
                    lax.dynamic_slice_in_dim(weight, at, chunk, 1)
                    for weight in (gate_weight, up_weight, down_weight)
                ],
                axis=1,
            )
        )
    tokens_own, cot_own = tokens_low.astype(F32), cot_low.astype(F32)
    group_tokens = (tokens_low, tokens_one, swap_second(tokens_low), swap_second(tokens_one))
    first_shard = after(ffn_shards[0], attn_ring[-1], *group_tokens[2:])
    group_tokens = group_tokens + tuple(swap_core(part) for part in group_tokens)
    attn_full, cot_low, cos, sin, gain_one, *group_tokens = lax.optimization_barrier(
        (attn_full, cot_low, cos, sin, gain_one, *group_tokens)
    )
    qkv = project_qkv(group_tokens, gain_one, attn_full, q_width, cos, sin)
    heads = attend(qkv, depth, place, first, start_column, q_width)
    cot = share_rows(cot_low, [[qkv], [heads]])
    ffn_full = [
        lax.all_gather(shard, "fsdp", axis=0, tiled=True)
        for shard in (first_shard, after(ffn_shards[1], heads))
    ]
    heads = after(heads, *cot)
    attn_blocks = sum_cores([(heads, 0, attn_full, 0, q_width)])
    attn_parts = last_parts(*sum_first(attn_blocks), beside=ffn_full[:1])
    attn_sum = sum(part.astype(F32) for part in attn_parts)
    hidden = tokens_own + attn_sum
    normed_two = share_rows((hidden * inv_rms(hidden) * gain_two).astype(BF16))

    acts = []
    grad_parts = []
    d_norm_partial = ()

    def chunk_grads(part, held=()):
        chunk = chunks[part]
        act = after(acts[part], *held)
        grad_parts.append(weight_grads(normed_two, act, 2 * chunk, 0, cot, act, chunk, 2))

    last = len(chunks) - 1
    for part in range(len(chunks)):
        normed_two = (after(normed_two[0], *grad_parts, *d_norm_partial), *normed_two[1:])
        acts.append(ffn_chunk(normed_two, cot, ffn_full[part]))
        d_norm_term = (acts[part], 0, ffn_full[part], 0, 2 * chunks[part])
        if part < last:
            chunk_grads(part)
            d_norm_partial = (back_product([d_norm_term], plus=d_norm_partial),)
    ffn_terms = [(acts[part], 2, ffn_full[part], 2, chunk) for part, chunk in enumerate(chunks)]
    d_norm_far, d_norm_near = halves_of_cores([d_norm_term], d_norm_partial)
    chunk_grads(last, (d_norm_far,))
    reduced = [
        lax.psum_scatter(part, "fsdp", scatter_dimension=0, tiled=True) for part in grad_parts
    ]
    d_norm_near = wide_first(d_norm_far, d_norm_near, grad_parts)

    def ffn_rows(part, parts, held):
        (act, *rest), *others = ffn_terms
        return back_product([(after(act, held), *rest), *others], part, parts, work=7)

    ffn_sent = [ffn_rows(3, 4, d_norm_near)]
    d_own = norm_back(wide_last(d_norm_near, ffn_sent), hidden, gain_two, cot_low)
    ffn_sent.append(ffn_rows(2, 4, d_own))
    ffn_mine = ffn_rows(0, 2, d_own)
    d_one, d_two, ffn_mine, ffn_sent[1] = lax.optimization_barrier(
        (swap_first(d_own), swap_second(d_own), ffn_mine, ffn_sent[1])
    )
    ffn_own, ffn_a, ffn_b, ffn_both = add_blocks(ffn_mine, [swap_core(piece) for piece in ffn_sent])
    ffn_x, ffn_y = jnp.where(core == 0, ffn_a, ffn_b), jnp.where(core == 0, ffn_b, ffn_a)
    d_early = [swap_core(part) for part in (d_own, d_one, d_two)]
    d_last = after(swap_second(d_one), *d_early, ffn_own, ffn_x, ffn_y, ffn_both, reduced[0])
    d_attn = (d_own, d_one, d_two, d_last, *d_early, swap_core(d_last))

    d_heads = front_product(d_attn, attn_full, q_width, 0)
    other_reduced = [swap_x(after(reduced[0], d_last))]
    d_qkv = attend_back(qkv, depth, d_heads, heads, place, first, start_column, cos, sin)
    y_both, y_own, d_qkv, other_reduced[0] = lax.optimization_barrier(
        (swap_y(ffn_both), swap_y(ffn_y), d_qkv, other_reduced[0])
    )
    ffn_x, ffn_own, d_qkv = lax.optimization_barrier((ffn_x + y_both, ffn_own + y_own, d_qkv))
    ffn_far = swap_x(ffn_x)
    normed_blocks = sum_cores(
        [
            (d_qkv, 0, attn_full, 1, q_width),
            (d_qkv, q_width // 128, attn_full, 2 * q_width // 128, 128),
        ]
    )
    attn_grad = weight_grads(
        d_attn, heads, q_width, 0, (qkv,), after(d_qkv, normed_blocks[3]), q_width + 128, 0, 0
    )
    ffn_far = after(ffn_far, attn_grad)
    result_own = (hidden + (ffn_own.astype(F32) + ffn_far.astype(F32))).astype(BF16)
    result_beside = swap_y(result_own)
    normed_first = sum_first(normed_blocks, [attn_grad, result_own])
    for part in range(1, len(chunks)):
        reduced[part] = after(reduced[part], attn_grad)
        other_reduced.append(swap_x(reduced[part]))
    late = [after(part, normed_first[1]) for part in other_reduced]
    halves = [both_halves(mine, other, ctx) for mine, other in zip(reduced, late)]

    def ffn_out(which):
        return jnp.concatenate(
            [
                halves[part][side][:, which * chunk : (which + 1) * chunk]
                for side in range(2)
                for part, chunk in enumerate(chunks)
            ],
            axis=1,
        )

    ffn_grads = [ffn_out(which) for which in range(3)]
    result = share_in_ctx(result_own, result_beside, y, core)
    normed_parts = last_parts(*normed_first, beside=[result, *ffn_grads])
    tokens_grad_own = norm_back(normed_parts, tokens_low, gain_one, d_own)
    attn_reduced = lax.psum_scatter(attn_grad, "fsdp", scatter_dimension=0, tiled=True)
    attn_reduced = after(attn_reduced, tokens_grad_own)
    other_attn = swap_x(attn_reduced)
    def gain_part(pairs):
        return sum(jnp.sum(mine.astype(F32) * grad.astype(F32), axis=1) for mine, grad in pairs)

    gain_sums = jnp.stack(
        [
            gain_part([(attn_shard[:, q_width:], attn_reduced[:, q_width:])]),
            gain_part(
                [
                    (ffn_shards[part][:, : 2 * chunk], reduced[part][:, : 2 * chunk])
                    for part, chunk in enumerate(chunks)
                ]
            ),
        ]
    )
    gain_sums = gain_sums + swap_core(gain_sums)
    gain_sums = gain_sums + swap_y(gain_sums)

    tokens_grad_beside, gain_sums, other_attn, result, *ffn_grads = lax.optimization_barrier(
        (swap_y(tokens_grad_own), gain_sums, other_attn, result, *ffn_grads)
    )
    tokens_grad = share_in_ctx(tokens_grad_own, tokens_grad_beside, y, core)
    gain_sums = gain_sums + swap_x(gain_sums)
    attn_gain_grad = gain_sums[0] / attn_gain.astype(F32)
    ffn_gain_grad = gain_sums[1] / ffn_gain.astype(F32)
    attn_low, attn_high = both_halves(attn_reduced, other_attn, ctx)

    def attn_out(begin, end):
        return jnp.concatenate([attn_low[:, begin:end], attn_high[:, begin:end]], axis=1)

    q_end, k_end = 2 * q_width, 2 * q_width + kv_width
    return (
        result,
        tokens_grad,
        attn_out(q_width, q_end),
        attn_out(q_end, k_end),
        attn_out(k_end, k_end + kv_width),
        attn_out(0, q_width),
        attn_gain_grad,
        *ffn_grads,
        ffn_gain_grad,
    )


def solution(mesh):
    rows = P(("fsdp", "ctx"), None)
    matrix = P("fsdp", "tp")
    vector = P("fsdp")
    return jax.shard_map(
        shards,
        mesh=mesh,
        in_specs=(
            rows,
            matrix,
            matrix,
            matrix,
            matrix,
            vector,
            matrix,
            matrix,
            matrix,
            vector,
            P("fsdp", None),
            P("fsdp", None),
            rows,
        ),
        out_specs=(
            rows,
            rows,
            matrix,
            matrix,
            matrix,
            matrix,
            vector,
            matrix,
            matrix,
            matrix,
            vector,
        ),
        check_vma=False,
    )
```
